32 devices in a mesh: lat: 2 (over x), lon: 16 (over z, y, core).
Axes of the slice: x: 2, y: 2, z: 4, core: 2. Of those that a mesh axis runs over, the one named last changes fastest.
Arguments:
- field: bfloat16 [16, 256, 256], P('lat', 'lon'), may hold values from -6 to 6
- dw_weight: bfloat16 [7, 7, 256], replicated, may hold values from -0.875 to 0.875
- w_expand: bfloat16 [256, 1024], replicated, may hold values from -0.375 to 0.375
- w_reduce: bfloat16 [1024, 256], replicated, may hold values from -0.1875 to 0.1875
- lat_attn: bfloat16 [4, 256, 256], replicated, as said below
- lon_attn: bfloat16 [4, 256, 256], replicated, as said below
Outputs:
- result: bfloat16 [16, 256, 256], P('lat', 'lon')
The draws below stay inside these ranges and needn't reach their ends.
Inputs may be any that keep to these rules, and one draw needn't show every extreme that they name: `lat_attn`: query, key, value and output projections in this order. `lon_attn`: query, key, value and output projections in this order.
All inputs are finite; a program needn't handle non-finite values.
Results may differ from the reference program's by a relative error of at most 0.03.
Values may be sent and summed in bfloat16 or wider, within the bound.
No kernel may reach another device: no remote copies, remote signals or barrier semaphores. Data moves between devices by JAX's collectives and lax.ppermute only.
A program may use at most 64 MiB of HBM per device.

```python
import jax
import jax.numpy as jnp
from jax import lax

C = 256
HEADS = 8
HID = 1024
NLAT = 16
NLON = 256


def attention_weights(key, marker):
    base = jax.random.fold_in(key, marker)
    entries = jax.random.normal(base, (4, C, C), jnp.float32) * C ** (-0.5)
    return entries.astype(jnp.bfloat16)


def draw_lat_attn(key, part):
    return attention_weights(key, 11)


def draw_lon_attn(key, part):
    return attention_weights(key, 23)


def level_of(stream_key, dims, split, low, largest):
    loudness = 1.0
    for position, blocks in split:
        draws = jax.random.uniform(jax.random.fold_in(jax.random.fold_in(stream_key, 6), position), (blocks,), jnp.float32, low / len(split), largest / len(split))
        loudness = loudness * jnp.repeat(jnp.exp(draws), dims[position] // blocks).reshape((-1,) + (1,) * (len(dims) - 1 - position))
    return loudness


def normal_values(key, extent, spread, bound, shards=(), kind=jnp.bfloat16):
    values = spread * jax.random.normal(key, extent, jnp.float32)
    if shards:
        values = values * level_of(key, extent, shards, -0.22, 0.18)
    return jnp.clip(values, -bound, bound).astype(kind)


def setup_inputs(seed: int = 0) -> dict:
    keys = jax.random.split(jax.random.key(seed), 7)
    return {
        "field": normal_values(keys[0], (NLAT, NLON, C), 1.0, 6.0, ((0, 2), (1, 16))),
        "dw_weight": normal_values(keys[1], (7, 7, C), 49 ** -0.5, 0.875),
        "w_expand": normal_values(keys[2], (C, HID), C ** -0.5, 0.375),
        "w_reduce": normal_values(keys[3], (HID, C), HID ** -0.5, 0.1875),
        "lat_attn": draw_lat_attn(jax.random.fold_in(keys[6], 71), 0),
        "lon_attn": draw_lon_attn(jax.random.fold_in(keys[6], 71), 0),
    }


EPSILON = 1e-06

def layer_norm(values):
    average = lax.optimization_barrier(jnp.mean(values, axis=-1, keepdims=True))
    centered = values - average
    variance = lax.optimization_barrier(jnp.mean(centered * centered, axis=-1, keepdims=True))
    return centered * lax.rsqrt(variance + EPSILON)

def project(rows, matrix):
    shape = rows.shape
    flat_rows = rows.reshape(-1, shape[-1])
    product = jnp.dot(flat_rows, matrix, preferred_element_type=jnp.float32)
    return product.reshape(shape[:-1] + (matrix.shape[1],))

def row_attention(sequence, weights):
    count, length, channels = sequence.shape
    head_size = channels // HEADS
    queries = project(sequence, weights[0]).astype(jnp.bfloat16).reshape(count, length, HEADS, head_size)
    key_all = project(sequence, weights[1]).astype(jnp.bfloat16).reshape(count, length, HEADS, head_size)
    value_all = project(sequence, weights[2]).astype(jnp.bfloat16).reshape(count, length, HEADS, head_size)

    def single_row(operands):
        query_row, key_row, value_row = operands
        scores = jnp.einsum('qhd,khd->hqk', query_row.astype(jnp.float32), key_row.astype(jnp.float32), precision=lax.Precision.HIGHEST) * head_size ** (-0.5)
        top = lax.optimization_barrier(jnp.max(scores, axis=-1, keepdims=True))
        raw_weights = jnp.exp(scores - top)
        totals = lax.optimization_barrier(jnp.sum(raw_weights, axis=-1))
        rounded = lax.optimization_barrier(raw_weights.astype(jnp.bfloat16)).astype(jnp.float32)
        mixed = jnp.einsum('hqk,khd->hqd', rounded, value_row.astype(jnp.float32), precision=lax.Precision.HIGHEST)
        mixed = mixed / totals[..., None]
        return jnp.swapaxes(mixed, 0, 1).reshape(length, channels).astype(jnp.bfloat16)
    return lax.map(single_row, (queries, key_all, value_all))

def reference(field, dw_weight, w_expand, w_reduce, lat_attn, lon_attn):
    field_wide = field.astype(jnp.float32)
    padded = jnp.pad(field_wide, ((3, 3), (0, 0), (0, 0)))
    padded = jnp.concatenate([padded[:, -3:], padded, padded[:, :3]], axis=1)
    taps = dw_weight.astype(jnp.float32)
    convolved = jnp.zeros_like(field_wide)
    for row_off in range(7):
        for col_off in range(7):
            convolved = convolved + padded[row_off:row_off + NLAT, col_off:col_off + NLON] * taps[row_off, col_off]
    normed = layer_norm(convolved).astype(jnp.bfloat16)
    expanded = jax.nn.gelu(project(normed, w_expand), approximate=False).astype(jnp.bfloat16)
    block_one = (field_wide + project(expanded, w_reduce)).astype(jnp.bfloat16)
    lat_in = layer_norm(block_one.astype(jnp.float32)).astype(jnp.bfloat16)
    lat_mix = jnp.swapaxes(row_attention(jnp.swapaxes(lat_in, 0, 1), lat_attn), 0, 1)
    block_two = (block_one.astype(jnp.float32) + project(lat_mix, lat_attn[3])).astype(jnp.bfloat16)
    lon_in = layer_norm(block_two.astype(jnp.float32)).astype(jnp.bfloat16)
    lon_mix = row_attention(lon_in, lon_attn)
    return (block_two.astype(jnp.float32) + project(lon_mix, lon_attn[3])).astype(jnp.bfloat16)
```

```python
import jax
import jax.numpy as jnp
from jax import lax
from jax.sharding import PartitionSpec as P

HEADS = 8
HALO = 3
EPSILON = 1e-06


def layer_norm(values):
    average = jnp.mean(values, axis=-1, keepdims=True)
    centered = values - average
    variance = jnp.mean(centered * centered, axis=-1, keepdims=True)
    return centered * lax.rsqrt(variance + EPSILON)


def dot(rows, matrix):
    return jnp.dot(rows, matrix, preferred_element_type=jnp.float32)


def dot_t(rows, matrix):
    return lax.dot_general(
        rows, matrix, (((1,), (1,)), ((), ())), preferred_element_type=jnp.float32
    )


def attend(queries, keys, values, heads, head_size, mask):
    count = queries.shape[0]
    lane_head = lax.broadcasted_iota(jnp.int32, (1, queries.shape[1]), 1) // head_size
    stacked = jnp.concatenate(
        [jnp.where(lane_head == h, queries, jnp.zeros_like(queries)) for h in range(heads)], axis=0
    )
    scores = dot_t(stacked, keys) * head_size ** (-0.5)
    if mask is not None:
        scores = jnp.where(mask, scores, -1e30)
    top = jnp.max(scores, axis=-1, keepdims=True)
    probs = jnp.exp(scores - top)
    totals = jnp.sum(probs, axis=-1, keepdims=True)
    mixed = dot(probs.astype(jnp.bfloat16), values) / totals
    out = mixed[:count]
    for h in range(1, heads):
        out = jnp.where(lane_head == h, mixed[h * count : (h + 1) * count], out)
    return out.astype(jnp.bfloat16)


def gather_windows(field):
    nlat, nlon = lax.axis_size("lat"), lax.axis_size("lon")
    rows, cols, channels = field.shape

    def shift(piece, dlat, dlon):
        pairs = [
            (((i + dlat) % nlat) * nlon + (j + dlon) % nlon, i * nlon + j)
            for i in range(nlat)
            for j in range(nlon)
        ]
        return lax.ppermute(piece, ("lat", "lon"), pairs)

    first, last = field[:, :HALO], field[:, cols - HALO :]
    windows = []
    for s in range(nlat):
        middle = field if s == 0 else shift(field, s, 0)
        windows.append(jnp.concatenate([shift(last, s, -1), middle, shift(first, s, 1)], axis=1))
    return windows


def shards(field, dw_weight, w_expand, w_reduce, lat_attn, lon_attn):
    rows, cols, channels = field.shape
    head_size = channels // HEADS
    nlat, nlon = lax.axis_size("lat"), lax.axis_size("lon")
    my_lat, my_lon = lax.axis_index("lat"), lax.axis_index("lon")
    split = max(1, nlon // rows)
    group = HEADS // split
    group_channels = group * head_size
    my_group = my_lon % split
    lon_qkv = lax.dynamic_slice_in_dim(lon_attn[:3], my_group * group_channels, group_channels, 2)

    windows = gather_windows(field)
    whole = jnp.concatenate(windows, axis=0)
    whole = jnp.roll(whole, my_lat * rows, axis=0)
    all_rows = rows * nlat
    padded = jnp.pad(whole, ((HALO, HALO), (0, 0), (0, 0))).astype(jnp.float32)
    taps = dw_weight.astype(jnp.float32)
    conv = jnp.zeros((all_rows, cols, channels), jnp.float32)
    for a in range(2 * HALO + 1):
        for b in range(2 * HALO + 1):
            conv = conv + padded[a : a + all_rows, b : b + cols] * taps[a, b]
    normed = layer_norm(conv).astype(jnp.bfloat16).reshape(-1, channels)
    expanded = jax.nn.gelu(dot(normed, w_expand), approximate=False).astype(jnp.bfloat16)
    center = whole[:, HALO : HALO + cols].reshape(-1, channels).astype(jnp.float32)
    block_one = (center + dot(expanded, w_reduce)).astype(jnp.bfloat16)
    lat_in = layer_norm(block_one.astype(jnp.float32)).astype(jnp.bfloat16)
    cells = rows * cols
    own_in = lax.dynamic_slice_in_dim(lat_in, my_lat * cells, cells, 0)
    own_one = lax.dynamic_slice_in_dim(block_one, my_lat * cells, cells, 0)
    queries = dot(own_in, lat_attn[0]).astype(jnp.bfloat16)
    keys = dot(lat_in, lat_attn[1]).astype(jnp.bfloat16)
    values = dot(lat_in, lat_attn[2]).astype(jnp.bfloat16)
    row_col = lax.broadcasted_iota(jnp.int32, (HEADS * cells, 1), 0) % cols
    key_col = lax.broadcasted_iota(jnp.int32, (1, all_rows * cols), 1) % cols
    lat_mix = attend(queries, keys, values, HEADS, head_size, row_col == key_col)
    block_two = (own_one.astype(jnp.float32) + dot(lat_mix, lat_attn[3])).astype(jnp.bfloat16)
    lon_in = layer_norm(block_two.astype(jnp.float32)).astype(jnp.bfloat16)

    sent = lon_in.reshape(rows, 1, cols, channels)
    sent = jnp.broadcast_to(sent, (rows, split, cols, channels)).reshape(
        rows * split, cols, channels
    )
    circle = lax.all_to_all(sent, "lon", 0, 0, tiled=True).reshape(nlon * cols, channels)
    lon_q = dot(circle, lon_qkv[0]).astype(jnp.bfloat16)
    lon_k = dot(circle, lon_qkv[1]).astype(jnp.bfloat16)
    lon_v = dot(circle, lon_qkv[2]).astype(jnp.bfloat16)
    lon_mix = attend(lon_q, lon_k, lon_v, group, head_size, None)
    back = lax.all_to_all(lon_mix.reshape(nlon, cols, group_channels), "lon", 0, 0, tiled=True)
    back = back.reshape(rows, split, cols, group_channels)
    back = jnp.concatenate([back[:, s] for s in range(split)], axis=-1).reshape(cells, channels)
    out = block_two.astype(jnp.float32) + dot(back, lon_attn[3])
    return out.astype(jnp.bfloat16).reshape(rows, cols, channels)


def solution(mesh):
    return jax.shard_map(
        shards,
        mesh=mesh,
        in_specs=(P("lat", "lon", None), P(), P(), P(), P(), P()),
        out_specs=P("lat", "lon", None),
        check_vma=False,
    )
```

```python
import functools

import jax
import jax.numpy as jnp
from jax import lax
from jax.experimental import pallas as pl
from jax.experimental.pallas import tpu as pltpu
from jax.sharding import PartitionSpec as P

HEADS = 8
HALO = 3
STRIP = 8
EPSILON = 1e-06
VMEM_BYTES = 24 * 1024 * 1024


def layer_norm(values):
    average = jnp.mean(values, axis=-1, keepdims=True)
    centered = values - average
    variance = jnp.mean(centered * centered, axis=-1, keepdims=True)
    return centered * lax.rsqrt(variance + EPSILON)


def dot(rows, matrix):
    return jnp.dot(rows, matrix, preferred_element_type=jnp.float32)


def dot_t(rows, matrix):
    return lax.dot_general(
        rows, matrix, (((1,), (1,)), ((), ())), preferred_element_type=jnp.float32
    )


def gelu(values):
    return 0.5 * values * (1.0 + lax.erf(values * 0.5**0.5))


def attend(queries, keys, values, heads, head_size, mask):
    scale = head_size ** (-0.5)
    lane_head = lax.broadcasted_iota(jnp.int32, (1, queries.shape[1]), 1) // head_size
    out = jnp.zeros(queries.shape, jnp.float32)
    for h in range(heads):
        mine = lane_head == h
        scores = dot_t(jnp.where(mine, queries, jnp.zeros_like(queries)), keys) * scale
        if mask is not None:
            scores = jnp.where(mask, scores, -1e30)
        top = jnp.max(scores, axis=-1, keepdims=True)
        probs = jnp.exp(scores - top)
        totals = jnp.sum(probs, axis=-1, keepdims=True)
        mixed = dot(probs.astype(jnp.bfloat16), values) / totals
        out = jnp.where(mine, mixed, out)
    return out.astype(jnp.bfloat16)


def cell_kernel(
    nlat,
    split,
    lat_ref,
    *refs,
):
    pieces = refs[: 3 * nlat]
    dw_ref, expand_ref, reduce_ref, attn_ref = refs[3 * nlat : 3 * nlat + 4]
    two_ref, sent_ref, padded, taps, normed, one, lat_in = refs[3 * nlat + 4 :]
    rows, cols, channels = pieces[1].shape
    cells = rows * cols
    all_rows = rows * nlat
    my_lat = lat_ref[0]
    lanes = 128

    padded[:HALO] = jnp.zeros((HALO,) + padded.shape[1:], jnp.float32)
    padded[HALO + all_rows :] = jnp.zeros((HALO,) + padded.shape[1:], jnp.float32)
    for s in range(nlat):
        source = lax.rem(my_lat + s, nlat)
        place = pl.ds(HALO + source * rows, rows)
        left, middle, right = pieces[3 * s : 3 * s + 3]
        padded[place, :STRIP] = left[...].astype(jnp.float32)
        padded[place, STRIP : STRIP + cols] = middle[...].astype(jnp.float32)
        padded[place, STRIP + cols :] = right[...].astype(jnp.float32)
    taps[...] = dw_ref[...].astype(jnp.float32)

    def conv_block(block, carry):
        start = block * rows
        parts = []
        for c in range(0, channels, lanes):
            acc = jnp.zeros((rows, cols, lanes), jnp.float32)
            for b in range(2 * HALO + 1):
                first = STRIP - HALO + b
                slab = padded[
                    pl.ds(start, rows + 2 * HALO), first : first + cols, c : c + lanes
                ]
                for a in range(2 * HALO + 1):
                    tap = taps[a, b : b + 1, c : c + lanes].reshape(1, 1, lanes)
                    acc = acc + slab[a : a + rows] * tap
            parts.append(acc.reshape(cells, lanes))
        conv = jnp.concatenate(parts, axis=-1)
        normed[pl.ds(pl.multiple_of(block * cells, cells), cells)] = layer_norm(conv).astype(
            jnp.bfloat16
        )
        return carry

    def mlp_block(block, size):
        place = pl.ds(pl.multiple_of(block * size, size), size)
        inputs = normed[place]
        hidden = expand_ref.shape[1]
        total = jnp.zeros((size, channels), jnp.float32)
        for k in range(0, hidden, channels):
            wide = gelu(dot(inputs, expand_ref[:, k : k + channels])).astype(jnp.bfloat16)
            total = total + dot(wide, reduce_ref[k : k + channels])
        lats = size // cols
        center = padded[
            pl.ds(HALO + block * lats, lats), STRIP : STRIP + cols, :
        ].reshape(size, channels)
        block_one = (center + total).astype(jnp.bfloat16)
        one[place] = block_one
        lat_in[place] = layer_norm(block_one.astype(jnp.float32)).astype(jnp.bfloat16)

    if nlat <= 2:
        for block in range(nlat):
            conv_block(block, 0)
        mlp_block(0, nlat * cells)
    else:
        lax.fori_loop(0, nlat, conv_block, 0)

        def mlp_step(block, carry):
            mlp_block(block, cells)
            return carry

        lax.fori_loop(0, nlat, mlp_step, 0)

    own = pl.ds(pl.multiple_of(my_lat * cells, cells), cells)
    every = lat_in[...]
    queries = dot(lat_in[own], attn_ref[0]).astype(jnp.bfloat16)
    keys = dot(every, attn_ref[1]).astype(jnp.bfloat16)
    values = dot(every, attn_ref[2]).astype(jnp.bfloat16)
    row_col = lax.broadcasted_iota(jnp.int32, (cells, 1), 0) % cols
    key_col = lax.broadcasted_iota(jnp.int32, (1, all_rows * cols), 1) % cols
    mix = attend(queries, keys, values, HEADS, channels // HEADS, row_col == key_col)
    block_two = (one[own].astype(jnp.float32) + dot(mix, attn_ref[3])).astype(jnp.bfloat16)
    two_ref[...] = block_two
    lon_in = layer_norm(block_two.astype(jnp.float32)).astype(jnp.bfloat16)
    lon_in = lon_in.reshape(rows, cols, channels)
    for s in range(split):
        for r in range(rows):
            sent_ref[r * split + s] = lon_in[r]


def circle_kernel(group, head_size, circle_ref, weights_ref, mix_ref):
    circle = circle_ref[...]
    queries = dot(circle, weights_ref[0]).astype(jnp.bfloat16)
    keys = dot(circle, weights_ref[1]).astype(jnp.bfloat16)
    values = dot(circle, weights_ref[2]).astype(jnp.bfloat16)
    mix_ref[...] = attend(queries, keys, values, group, head_size, None)


def last_kernel(split, back_ref, two_ref, weight_ref, out_ref):
    rows, cols = out_ref.shape[:2]
    width = back_ref.shape[-1]
    total = two_ref[...].astype(jnp.float32)
    for s in range(split):
        part = jnp.concatenate([back_ref[r * split + s] for r in range(rows)], axis=0)
        total = total + dot(part, weight_ref[s * width : (s + 1) * width])
    out_ref[...] = total.astype(jnp.bfloat16).reshape(out_ref.shape)


def call(kernel, out_shape, count, scratch=(), prefetch=0):
    smem = [pl.BlockSpec(memory_space=pltpu.SMEM)] * prefetch
    vmem = pl.BlockSpec(memory_space=pltpu.VMEM)
    return pl.pallas_call(
        kernel,
        out_shape=out_shape,
        in_specs=smem + [vmem] * count,
        out_specs=jax.tree.map(lambda _: vmem, out_shape),
        scratch_shapes=list(scratch),
        compiler_params=pltpu.CompilerParams(vmem_limit_bytes=VMEM_BYTES),
    )


def gather_windows(field):
    nlat, nlon = lax.axis_size("lat"), lax.axis_size("lon")
    cols = field.shape[1]

    def shift(piece, dlat, dlon):
        pairs = [
            (((i + dlat) % nlat) * nlon + (j + dlon) % nlon, i * nlon + j)
            for i in range(nlat)
            for j in range(nlon)
        ]
        return lax.ppermute(piece, ("lat", "lon"), pairs)

    first, last = field[:, :STRIP], field[:, cols - STRIP :]
    pieces = []
    for s in range(nlat):
        middle = field if s == 0 else shift(field, s, 0)
        pieces += [shift(last, s, -1), middle, shift(first, s, 1)]
    return pieces


def shards(field, dw_weight, w_expand, w_reduce, lat_attn, lon_attn):
    rows, cols, channels = field.shape
    head_size = channels // HEADS
    nlat, nlon = lax.axis_size("lat"), lax.axis_size("lon")
    my_lat, my_lon = lax.axis_index("lat"), lax.axis_index("lon")
    split = nlon // rows
    group = HEADS // split
    width = group * head_size
    cells = rows * cols
    all_rows = rows * nlat
    lon_qkv = lax.dynamic_slice_in_dim(lon_attn[:3], (my_lon % split) * width, width, 2)

    pieces = gather_windows(field)
    bf16, f32 = jnp.bfloat16, jnp.float32
    block_two, sent = call(
        functools.partial(cell_kernel, nlat, split),
        (
            jax.ShapeDtypeStruct((cells, channels), bf16),
            jax.ShapeDtypeStruct((rows * split, cols, channels), bf16),
        ),
        len(pieces) + 4,
        [
            pltpu.VMEM((all_rows + 2 * HALO, cols + 2 * STRIP, channels), f32),
            pltpu.VMEM(dw_weight.shape, f32),
            pltpu.VMEM((all_rows * cols, channels), bf16),
            pltpu.VMEM((all_rows * cols, channels), bf16),
            pltpu.VMEM((all_rows * cols, channels), bf16),
        ],
        prefetch=1,
    )(my_lat.astype(jnp.int32).reshape(1), *pieces, dw_weight, w_expand, w_reduce, lat_attn)

    circle = lax.all_to_all(sent, "lon", 0, 0, tiled=True).reshape(nlon * cols, channels)
    lon_mix = call(
        functools.partial(circle_kernel, group, head_size),
        jax.ShapeDtypeStruct((nlon * cols, width), bf16),
        2,
    )(circle, lon_qkv)
    back = lax.all_to_all(lon_mix.reshape(nlon, cols, width), "lon", 0, 0, tiled=True)
    return call(
        functools.partial(last_kernel, split),
        jax.ShapeDtypeStruct((rows, cols, channels), bf16),
        3,
    )(back, block_two, lon_attn[3])


def solution(mesh):
    return jax.shard_map(
        shards,
        mesh=mesh,
        in_specs=(P("lat", "lon", None), P(), P(), P(), P(), P()),
        out_specs=P("lat", "lon", None),
        check_vma=False,
    )
```

```python
import functools

import jax
import jax.numpy as jnp
from jax import lax
from jax.experimental import pallas as pl
from jax.experimental.pallas import tpu as pltpu
from jax.sharding import PartitionSpec as P

HEADS = 8
HALO = 3
TAPS = 2 * HALO + 1
STRIP = 8
SIDE = 4
LANES = 128
EPSILON = 1e-06
VMEM_BYTES = 24 * 1024 * 1024
STAGE_BYTES = 103 * 512 * 1024
bf16, f32 = jnp.bfloat16, jnp.float32


def layer_norm(values):
    average = jnp.mean(values, axis=-1, keepdims=True)
    centered = values - average
    variance = jnp.mean(centered * centered, axis=-1, keepdims=True)
    return centered * lax.rsqrt(variance + EPSILON)


def dot(rows, matrix):
    return jnp.dot(rows, matrix, preferred_element_type=f32)


def dot_t(rows, matrix):
    return lax.dot_general(rows, matrix, (((1,), (1,)), ((), ())), preferred_element_type=f32)


def gelu(values):
    return 0.5 * values * (1.0 + lax.erf(values * 0.5**0.5))


def attend(queries, keys, values, mask):
    head_size = queries.shape[1] // HEADS
    scale = head_size ** (-0.5)
    lane_head = lax.broadcasted_iota(jnp.int32, (1, queries.shape[1]), 1) // head_size
    out = jnp.zeros(queries.shape, f32)
    for h in range(HEADS):
        mine = lane_head == h
        scores = dot_t(jnp.where(mine, queries, jnp.zeros_like(queries)), keys) * scale
        if mask is not None:
            scores = jnp.where(mask, scores, -1e30)
        top = jnp.max(scores, axis=-1, keepdims=True)
        probs = jnp.exp(scores - top)
        totals = jnp.sum(probs, axis=-1, keepdims=True)
        mixed = dot(probs.astype(bf16), values) / totals
        out = jnp.where(mine, mixed, out)
    return out.astype(bf16)


def stage_kernel(*refs):
    count = (len(refs) - 1) // 2
    sems = refs[-1]
    copies = []
    for i in range(count):
        source, target = refs[i], refs[count + i]
        pieces = sems.shape[1]
        size = source.shape[0] // pieces
        for k in range(pieces):
            part = pl.ds(k * size, size)
            copies.append(pltpu.make_async_copy(source.at[part], target.at[part], sems.at[i, k]))
    for copy in copies:
        copy.start()
    for copy in copies:
        copy.wait()


def strip_kernel(nlat, place_ref, *refs):
    tiles = refs[:nlat]
    whole_ref, near_ref, far_ref, whole = refs[nlat + 1 :]
    rows, cols, channels = tiles[0].shape
    for s in range(nlat):
        source = lax.rem(place_ref[0] + s, nlat)
        whole[pl.ds(source * rows, rows)] = tiles[s][...].astype(f32)
    values = whole[...]
    whole_ref[...] = values.astype(bf16)
    first, last = values[:, :STRIP], values[:, cols - STRIP :]
    even = place_ref[1] == 0
    near_ref[...] = jnp.where(even, last, first).reshape(near_ref.shape).astype(bf16)
    far_ref[...] = jnp.where(even, first, last).reshape(far_ref.shape).astype(bf16)


def chain(my_lat, slab, shape, dw_ref, expand_ref, reduce_ref, attn_ref, center, scratch):
    taps, one, lat_in = scratch
    rows, all_rows, columns, channels = shape
    cells = all_rows * columns
    taps[...] = dw_ref[...].astype(f32)
    parts = []
    for c in range(0, channels, LANES):
        acc = jnp.zeros((all_rows, columns, LANES), f32)
        for b in range(TAPS):
            block = slab(b, c)
            for a in range(TAPS):
                tap = taps[a, b : b + 1, c : c + LANES].reshape(1, 1, LANES)
                acc = acc + block[a : a + all_rows] * tap
        parts.append(acc.reshape(cells, LANES))
    normed = layer_norm(jnp.concatenate(parts, axis=-1)).astype(bf16)
    total = center.reshape(cells, channels)
    for k in range(0, expand_ref.shape[1], channels):
        wide = gelu(dot(normed, expand_ref[:, k : k + channels])).astype(bf16)
        total = total + dot(wide, reduce_ref[k : k + channels])
    block_one = total.astype(bf16)
    one[...] = block_one
    every = layer_norm(block_one.astype(f32)).astype(bf16)
    lat_in[...] = every
    count = rows * columns
    own = pl.ds(pl.multiple_of(my_lat * count, count), count)
    queries = dot(lat_in[own], attn_ref[0]).astype(bf16)
    keys = dot(every, attn_ref[1]).astype(bf16)
    values = dot(every, attn_ref[2]).astype(bf16)
    row_col = lax.broadcasted_iota(jnp.int32, (count, 1), 0) % columns
    key_col = lax.broadcasted_iota(jnp.int32, (1, cells), 1) % columns
    mix = attend(queries, keys, values, row_col == key_col)
    block_two = (one[own].astype(f32) + dot(mix, attn_ref[3])).astype(bf16)
    return block_two, layer_norm(block_two.astype(f32))


def fill(padded, all_rows, first, values):
    width = values.shape[1]
    padded[HALO : HALO + all_rows, first : first + width] = values


def clear(padded, all_rows):
    edge = jnp.zeros((HALO,) + padded.shape[1:], f32)
    padded[:HALO] = edge
    padded[HALO + all_rows :] = edge


def inner_kernel(
    rows, place_ref, whole_ref, dw_ref, expand_ref, reduce_ref, attn_ref,
    two_ref, in_ref, padded, *scratch
):
    all_rows, cols, channels = whole_ref.shape
    columns = cols - 2 * SIDE
    clear(padded, all_rows)
    fill(padded, all_rows, 0, whole_ref[...].astype(f32))

    def slab(b, c):
        first = SIDE - HALO + b
        return padded[:, first : first + columns, c : c + LANES]

    center = padded[HALO : HALO + all_rows, SIDE : SIDE + columns]
    shape = (rows, all_rows, columns, channels)
    block_two, lon_in = chain(
        place_ref[0], slab, shape, dw_ref, expand_ref, reduce_ref, attn_ref, center, scratch
    )
    two_ref[...] = block_two
    in_ref[...] = lon_in.astype(bf16)


def outer_kernel(
    rows, place_ref, whole_ref, near_ref, far_ref, inner_in_ref,
    dw_ref, expand_ref, reduce_ref, attn_ref,
    two_ref, sent_ref, padded, *scratch
):
    all_rows, cols, channels = whole_ref.shape
    columns = 2 * SIDE
    strip_shape = (all_rows, STRIP, channels)
    near = near_ref[...].astype(f32).reshape(strip_shape)
    far = far_ref[...].astype(f32).reshape(strip_shape)
    even = place_ref[1] == 0
    clear(padded, all_rows)
    fill(padded, all_rows, 0, jnp.where(even, far, near))
    fill(padded, all_rows, STRIP, whole_ref[...].astype(f32))
    fill(padded, all_rows, STRIP + cols, jnp.where(even, near, far))
    sublane = lax.broadcasted_iota(jnp.int32, (1, columns, 1), 1)

    def halves(shift, rows_of, c, width):
        right = STRIP + cols - SIDE + shift
        left = STRIP - SIDE + shift
        return jnp.where(
            sublane < SIDE,
            padded[rows_of, right : right + columns, c : c + width],
            padded[rows_of, left : left + columns, c : c + width],
        )

    def slab(b, c):
        return halves(b - HALO, slice(None), c, LANES)

    center = halves(0, slice(HALO, HALO + all_rows), 0, channels)
    shape = (rows, all_rows, columns, channels)
    block_two, lon_in = chain(
        place_ref[0], slab, shape, dw_ref, expand_ref, reduce_ref, attn_ref, center, scratch
    )
    two_ref[...] = block_two
    inner = inner_in_ref[...].astype(f32).reshape(rows, cols - columns, channels)
    outer = lon_in.reshape(rows, columns, channels)
    sent_ref[...] = jnp.concatenate([inner, outer], axis=1).astype(bf16)


def circle_kernel(count, *refs):
    parts = refs[:count]
    attn_ref, mix_ref = refs[count:]
    circle = jnp.concatenate([part[...] for part in parts], axis=0)
    queries = dot(parts[0][...], attn_ref[0]).astype(bf16)
    keys = dot(circle, attn_ref[1]).astype(bf16)
    values = dot(circle, attn_ref[2]).astype(bf16)
    mix_ref[...] = attend(queries, keys, values, None)


def last_kernel(back_ref, inner_ref, outer_ref, attn_ref, out_ref):
    rows, cols, channels = out_ref.shape
    columns = 2 * SIDE
    change = dot(back_ref[...], attn_ref[3]).reshape(rows, cols, channels)
    inner = inner_ref[...].astype(f32).reshape(rows, cols - columns, channels)
    outer = outer_ref[...].astype(f32).reshape(rows, columns, channels)
    inner = inner + change[:, : cols - columns]
    outer = outer + change[:, cols - columns :]
    total = jnp.concatenate([outer[:, SIDE:], inner, outer[:, :SIDE]], axis=1)
    out_ref[...] = total.astype(bf16)


def call(
    kernel, outs, operands, scratch=(), any_space=False, prefetch=0, flops=0, grant=VMEM_BYTES
):
    vmem = pl.BlockSpec(memory_space=pltpu.VMEM)
    given = pl.BlockSpec(memory_space=pl.ANY) if any_space else vmem
    smem = pl.BlockSpec(memory_space=pltpu.SMEM)
    shapes = [jax.ShapeDtypeStruct(shape, bf16) for shape in outs]
    moved = sum(x.size * x.dtype.itemsize for x in operands)
    result = pl.pallas_call(
        kernel,
        out_shape=shapes,
        in_specs=[smem] * prefetch + [given] * (len(operands) - prefetch),
        out_specs=[vmem] * len(outs),
        scratch_shapes=list(scratch),
        compiler_params=pltpu.CompilerParams(vmem_limit_bytes=grant),
        cost_estimate=pl.CostEstimate(flops=flops, bytes_accessed=moved, transcendentals=0),
    )(*operands)
    return result


def shards(field, dw_weight, w_expand, w_reduce, lat_attn, lon_attn):
    rows, cols, channels = field.shape
    nlat, nlon = lax.axis_size("lat"), lax.axis_size("lon")
    my_lat, my_lon = lax.axis_index("lat"), lax.axis_index("lon")
    split = nlon // rows
    all_rows = rows * nlat
    columns = 2 * SIDE
    place = jnp.stack([my_lat, my_lon % 2]).astype(jnp.int32)

    tiles = [field]
    for s in range(1, nlat):
        tiles.append(lax.ppermute(field, "lat", [((i + s) % nlat, i) for i in range(nlat)]))
    weights = (w_expand, w_reduce, lat_attn, lon_attn)
    staged = call(
        stage_kernel,
        [w.shape for w in weights],
        weights,
        [pltpu.SemaphoreType.DMA((len(weights), 4))],
        any_space=True,
        grant=STAGE_BYTES,
    )
    expand, reduce, lat_proj, lon_proj = staged

    strip = (all_rows * STRIP, channels)
    whole, near, far = call(
        functools.partial(strip_kernel, nlat),
        [(all_rows, cols, channels), strip, strip],
        [place, *tiles, reduce],
        [pltpu.VMEM((all_rows, cols, channels), f32)],
        prefetch=1,
    )
    near = lax.ppermute(near, "lon", [(j, j ^ 1) for j in range(nlon)])
    far = lax.ppermute(
        far, "lon", [(j, (j - 1) % nlon if j % 2 == 0 else (j + 1) % nlon) for j in range(nlon)]
    )

    def scratch(width, count):
        return [
            pltpu.VMEM((all_rows + 2 * HALO, width, channels), f32),
            pltpu.VMEM(dw_weight.shape, f32),
            pltpu.VMEM((all_rows * count, channels), bf16),
            pltpu.VMEM((all_rows * count, channels), bf16),
        ]

    work = 4 * all_rows * columns * channels * w_expand.shape[1]
    inner_two, inner_in = call(
        functools.partial(inner_kernel, rows),
        [(rows * (cols - columns), channels)] * 2,
        [place, whole, dw_weight, expand, reduce, lat_proj],
        scratch(cols, cols - columns),
        prefetch=1,
        flops=work,
    )
    outer_two, sent = call(
        functools.partial(outer_kernel, rows),
        [(rows * columns, channels), (rows, cols, channels)],
        [place, whole, near, far, inner_in, dw_weight, expand, reduce, lat_proj],
        scratch(cols + 2 * STRIP, columns),
        prefetch=1,
        flops=work,
    )

    groups = [[r * split + s for r in range(rows)] for s in range(split)]
    part = lax.all_to_all(sent, "lon", 0, 0, tiled=True, axis_index_groups=groups)
    part = part.reshape(rows * cols, channels)
    parts = [part]
    for s in range(1, split):
        pairs = [(j - j % split + (j + s) % split, j) for j in range(nlon)]
        parts.append(lax.ppermute(part, "lon", pairs))
    (mix,) = call(
        functools.partial(circle_kernel, split), [(rows * cols, channels)], [*parts, lon_proj]
    )
    mix = mix.reshape(rows, cols, channels)
    back = lax.all_to_all(mix, "lon", 0, 0, tiled=True, axis_index_groups=groups)
    (out,) = call(
        last_kernel,
        [(rows, cols, channels)],
        [back.reshape(rows * cols, channels), inner_two, outer_two, lon_proj],
    )
    return out


def solution(mesh):
    return jax.shard_map(
        shards,
        mesh=mesh,
        in_specs=(P("lat", "lon", None), P(), P(), P(), P(), P()),
        out_specs=P("lat", "lon", None),
        check_vma=False,
    )
```

```python
import functools

import jax
import jax.numpy as jnp
from jax import lax
from jax.experimental import pallas as pl
from jax.experimental.pallas import tpu as pltpu
from jax.sharding import PartitionSpec as P

HEADS = 8
HALO = 3
TAPS = 2 * HALO + 1
STRIP = 8
SIDE = 4
LANES = 128
LEVELS = 4
EPSILON = 1e-06
VMEM_BYTES = 24 * 1024 * 1024
STAGE_BYTES = 103 * 512 * 1024
bf16, f32 = jnp.bfloat16, jnp.float32


def layer_norm(values):
    average = jnp.mean(values, axis=-1, keepdims=True)
    centered = values - average
    variance = jnp.mean(centered * centered, axis=-1, keepdims=True)
    return centered * lax.rsqrt(variance + EPSILON)


def dot(rows, matrix):
    return jnp.dot(rows, matrix, preferred_element_type=f32)


def dot_t(rows, matrix):
    return lax.dot_general(rows, matrix, (((1,), (1,)), ((), ())), preferred_element_type=f32)


def gelu(values):
    return 0.5 * values * (1.0 + lax.erf(values * 0.5**0.5))


def attend(queries, keys, values, mask):
    count, channels = queries.shape
    head_size = channels // HEADS
    lane_head = lax.broadcasted_iota(jnp.int32, (1, channels), 1) // head_size
    picks = [lane_head == h for h in range(HEADS)]
    none = jnp.zeros_like(queries)
    stacked = jnp.concatenate([jnp.where(pick, queries, none) for pick in picks], axis=0)
    scores = dot_t(stacked, keys) * head_size ** (-0.5)
    if mask is not None:
        scores = scores.reshape(HEADS, count, keys.shape[0])
        scores = jnp.where(mask[None], scores, -1e30).reshape(HEADS * count, keys.shape[0])
    top = jnp.max(scores, axis=-1, keepdims=True)
    probs = jnp.exp(scores - top)
    totals = jnp.sum(probs, axis=-1, keepdims=True)
    mixed = dot(probs.astype(bf16), values) * (1.0 / totals)
    out = mixed[:count]
    for h in range(1, HEADS):
        out = jnp.where(picks[h], mixed[h * count : (h + 1) * count], out)
    return out.astype(bf16)


def stage_kernel(*refs):
    count = (len(refs) - 1) // 2
    sems = refs[-1]
    copies = []
    for i in range(count):
        source, target = refs[i], refs[count + i]
        pieces = sems.shape[1]
        size = source.shape[0] // pieces
        for k in range(pieces):
            part = pl.ds(k * size, size)
            copies.append(pltpu.make_async_copy(source.at[part], target.at[part], sems.at[i, k]))
    for copy in copies:
        copy.start()
    for copy in copies:
        copy.wait()


def strip_kernel(nlat, place_ref, *refs):
    tiles = refs[:nlat]
    near_ref, far_ref, near, far = refs[nlat + 1 :]
    rows, cols, channels = tiles[0].shape
    even = place_ref[1] == 0
    for s in range(nlat):
        values = tiles[s][...].astype(f32)
        first, last = values[:, :STRIP], values[:, cols - STRIP :]
        where = pl.ds(lax.rem(place_ref[0] + s, nlat) * rows, rows)
        near[where] = jnp.where(even, last, first)
        far[where] = jnp.where(even, first, last)
    near_ref[...] = near[...].reshape(near_ref.shape).astype(bf16)
    far_ref[...] = far[...].reshape(far_ref.shape).astype(bf16)


def chain(my_lat, slab, shape, dw_ref, expand_ref, reduce_ref, attn_ref, center, scratch):
    taps, one, lat_in = scratch
    rows, all_rows, columns, channels = shape
    cells = all_rows * columns
    taps[...] = dw_ref[...].astype(f32)
    parts = []
    for c in range(0, channels, LANES):
        acc = jnp.zeros((all_rows, columns, LANES), f32)
        for b in range(TAPS):
            block = slab(b, c)
            for a in range(TAPS):
                tap = taps[a, b : b + 1, c : c + LANES].reshape(1, 1, LANES)
                acc = acc + block[a : a + all_rows] * tap
        parts.append(acc.reshape(cells, LANES))
    normed = layer_norm(jnp.concatenate(parts, axis=-1)).astype(bf16)
    total = center.reshape(cells, channels)
    for k in range(0, expand_ref.shape[1], channels):
        wide = gelu(dot(normed, expand_ref[:, k : k + channels])).astype(bf16)
        total = total + dot(wide, reduce_ref[k : k + channels])
    block_one = total.astype(bf16)
    one[...] = block_one
    every = layer_norm(block_one.astype(f32)).astype(bf16)
    lat_in[...] = every
    count = rows * columns
    own = pl.ds(pl.multiple_of(my_lat * count, count), count)
    queries = dot(lat_in[own], attn_ref[0]).astype(bf16)
    keys = dot(every, attn_ref[1]).astype(bf16)
    values = dot(every, attn_ref[2]).astype(bf16)
    row_col = lax.broadcasted_iota(jnp.int32, (count, 1), 0) % columns
    key_col = lax.broadcasted_iota(jnp.int32, (1, cells), 1) % columns
    mix = attend(queries, keys, values, row_col == key_col)
    block_two = (one[own].astype(f32) + dot(mix, attn_ref[3])).astype(bf16)
    return block_two, layer_norm(block_two.astype(f32))


def fill(padded, all_rows, first, values):
    width = values.shape[1]
    padded[HALO : HALO + all_rows, first : first + width] = values


def fill_tiles(padded, my_lat, first, tiles):
    rows, cols = tiles[0].shape[:2]
    for s in range(len(tiles)):
        place = HALO + lax.rem(my_lat + s, len(tiles)) * rows
        padded[pl.ds(place, rows), first : first + cols] = tiles[s][...].astype(f32)


def clear(padded, all_rows):
    edge = jnp.zeros((HALO,) + padded.shape[1:], f32)
    padded[:HALO] = edge
    padded[HALO + all_rows :] = edge


def inner_kernel(nlat, place_ref, *refs):
    tiles, refs = refs[:nlat], refs[nlat:]
    dw_ref, expand_ref, reduce_ref, attn_ref, two_ref, in_ref, padded, *scratch = refs
    rows, cols, channels = tiles[0].shape
    all_rows = rows * nlat
    columns = cols - 2 * SIDE
    clear(padded, all_rows)
    fill_tiles(padded, place_ref[0], 0, tiles)

    def slab(b, c):
        first = SIDE - HALO + b
        return padded[:, first : first + columns, c : c + LANES]

    center = padded[HALO : HALO + all_rows, SIDE : SIDE + columns]
    shape = (rows, all_rows, columns, channels)
    block_two, lon_in = chain(
        place_ref[0], slab, shape, dw_ref, expand_ref, reduce_ref, attn_ref, center, scratch
    )
    two_ref[...] = block_two
    in_ref[...] = lon_in.astype(bf16)


def outer_kernel(nlat, levels, place_ref, *refs):
    tiles, refs = refs[:nlat], refs[nlat:]
    near_ref, far_ref, inner_in_ref, dw_ref, expand_ref, reduce_ref, attn_ref = refs[:7]
    two_ref, *refs = refs[7:]
    sent_refs, (sent, padded, *scratch) = refs[:levels], refs[levels:]
    rows, cols, channels = tiles[0].shape
    all_rows = rows * nlat
    columns = 2 * SIDE
    strip_shape = (all_rows, STRIP, channels)
    near = near_ref[...].astype(f32).reshape(strip_shape)
    far = far_ref[...].astype(f32).reshape(strip_shape)
    even = place_ref[1] == 0
    clear(padded, all_rows)
    fill(padded, all_rows, 0, jnp.where(even, far, near))
    fill_tiles(padded, place_ref[0], STRIP, tiles)
    fill(padded, all_rows, STRIP + cols, jnp.where(even, near, far))
    sublane = lax.broadcasted_iota(jnp.int32, (1, columns, 1), 1)

    def halves(shift, rows_of, c, width):
        right = STRIP + cols - SIDE + shift
        left = STRIP - SIDE + shift
        return jnp.where(
            sublane < SIDE,
            padded[rows_of, right : right + columns, c : c + width],
            padded[rows_of, left : left + columns, c : c + width],
        )

    def slab(b, c):
        return halves(b - HALO, slice(None), c, LANES)

    center = halves(0, slice(HALO, HALO + all_rows), 0, channels)
    shape = (rows, all_rows, columns, channels)
    block_two, lon_in = chain(
        place_ref[0], slab, shape, dw_ref, expand_ref, reduce_ref, attn_ref, center, scratch
    )
    two_ref[...] = block_two
    inner = inner_in_ref[...].astype(f32).reshape(rows, cols - columns, channels)
    outer = lon_in.reshape(rows, columns, channels)
    sent[...] = jnp.concatenate([inner, outer], axis=1).astype(bf16)
    some = rows // levels
    for k in range(levels):
        part = sent[pl.ds((place_ref[2] ^ k) * some, some)]
        sent_refs[k][...] = part.reshape(sent_refs[k].shape)


def circle_kernel(levels, some, *refs):
    attn_ref, mix_refs = refs[-levels - 1], refs[-levels:]
    parts = refs[: -levels - 1]
    count = parts[0].shape[0] // (some * levels)

    def latitude(part, r):
        starts = [(k * some + r) * count for k in range(levels)]
        return jnp.concatenate([part[start : start + count] for start in starts], axis=0)

    for r in range(some):
        own = latitude(parts[0], r)
        every = jnp.concatenate([own] + [latitude(part, r) for part in parts[1:]], axis=0)
        queries = dot(own, attn_ref[0]).astype(bf16)
        keys = dot(every, attn_ref[1]).astype(bf16)
        values = dot(every, attn_ref[2]).astype(bf16)
        mix = attend(queries, keys, values, None)
        for k in range(levels):
            mix_refs[k][r * count : (r + 1) * count] = mix[k * count : (k + 1) * count]


def last_kernel(levels, place_ref, *refs):
    parts = refs[:levels]
    inner_ref, outer_ref, attn_ref, out_ref, back = refs[levels:]
    rows, cols, channels = out_ref.shape
    columns = 2 * SIDE
    some = parts[0].shape[0]
    for k in range(levels):
        start = (place_ref[2] ^ k) * some
        back[pl.ds(pl.multiple_of(start, some), some)] = parts[k][...]
    change = dot(back[...], attn_ref[3]).reshape(rows, cols, channels)
    inner = inner_ref[...].astype(f32).reshape(rows, cols - columns, channels)
    outer = outer_ref[...].astype(f32).reshape(rows, columns, channels)
    inner = inner + change[:, : cols - columns]
    outer = outer + change[:, cols - columns :]
    total = jnp.concatenate([outer[:, SIDE:], inner, outer[:, :SIDE]], axis=1)
    out_ref[...] = total.astype(bf16)


def call(
    kernel, outs, operands, scratch=(), any_space=False, prefetch=0, flops=0, grant=VMEM_BYTES
):
    vmem = pl.BlockSpec(memory_space=pltpu.VMEM)
    given = pl.BlockSpec(memory_space=pl.ANY) if any_space else vmem
    smem = pl.BlockSpec(memory_space=pltpu.SMEM)
    shapes = [jax.ShapeDtypeStruct(shape, bf16) for shape in outs]
    moved = sum(x.size * x.dtype.itemsize for x in operands)
    result = pl.pallas_call(
        kernel,
        out_shape=shapes,
        in_specs=[smem] * prefetch + [given] * (len(operands) - prefetch),
        out_specs=[vmem] * len(outs),
        scratch_shapes=list(scratch),
        compiler_params=pltpu.CompilerParams(vmem_limit_bytes=grant),
        cost_estimate=pl.CostEstimate(flops=flops, bytes_accessed=moved, transcendentals=0),
    )(*operands)
    return result


def shards(field, dw_weight, w_expand, w_reduce, lat_attn, lon_attn):
    rows, cols, channels = field.shape
    nlat, nlon = lax.axis_size("lat"), lax.axis_size("lon")
    my_lat, my_lon = lax.axis_index("lat"), lax.axis_index("lon")
    levels = min(LEVELS, nlon)
    column = nlon // levels
    some = rows // levels
    all_rows = rows * nlat
    columns = 2 * SIDE
    place = jnp.stack([my_lat, my_lon % 2, my_lon // column]).astype(jnp.int32)

    def swap(piece, mask):
        return lax.ppermute(piece, "lon", [(j, j ^ mask) for j in range(nlon)])

    tiles = [field]
    for s in range(1, nlat):
        tiles.append(lax.ppermute(field, "lat", [((i + s) % nlat, i) for i in range(nlat)]))
    weights = (w_expand, w_reduce, lat_attn, lon_attn)
    staged = call(
        stage_kernel,
        [w.shape for w in weights],
        weights,
        [pltpu.SemaphoreType.DMA((len(weights), 4))],
        any_space=True,
        grant=STAGE_BYTES,
    )
    expand, reduce, lat_proj, lon_proj = staged

    strip = (all_rows * STRIP, channels)
    strip_scratch = pltpu.VMEM((all_rows, STRIP, channels), f32)
    near, far = call(
        functools.partial(strip_kernel, nlat),
        [strip, strip],
        [place, *tiles, reduce],
        [strip_scratch, strip_scratch],
        prefetch=1,
    )
    near = swap(near, 1)
    far = lax.ppermute(
        far, "lon", [(j, (j - 1) % nlon if j % 2 == 0 else (j + 1) % nlon) for j in range(nlon)]
    )

    def scratch(width, count):
        return [
            pltpu.VMEM((all_rows + 2 * HALO, width, channels), f32),
            pltpu.VMEM(dw_weight.shape, f32),
            pltpu.VMEM((all_rows * count, channels), bf16),
            pltpu.VMEM((all_rows * count, channels), bf16),
        ]

    work = 4 * all_rows * columns * channels * w_expand.shape[1]
    inner_two, inner_in = call(
        functools.partial(inner_kernel, nlat),
        [(rows * (cols - columns), channels)] * 2,
        [place, *tiles, dw_weight, expand, reduce, lat_proj],
        scratch(cols, cols - columns),
        prefetch=1,
        flops=work,
    )
    piece = (some * cols, channels)
    outer_two, *parts = call(
        functools.partial(outer_kernel, nlat, levels),
        [(rows * columns, channels)] + [piece] * levels,
        [place, *tiles, near, far, inner_in, dw_weight, expand, reduce, lat_proj],
        [pltpu.VMEM((rows, cols, channels), bf16)] + scratch(cols + 2 * STRIP, columns),
        prefetch=1,
        flops=work,
    )

    parts = [parts[0]] + [swap(parts[k], k * column) for k in range(1, levels)]
    circle = [jnp.concatenate(parts, axis=0)]
    mask = column // 2
    while mask:
        circle = circle + [swap(part, mask) for part in circle]
        mask //= 2
    mixes = call(
        functools.partial(circle_kernel, levels, some), [piece] * levels, [*circle, lon_proj]
    )
    mixes = [mixes[0]] + [swap(mixes[k], k * column) for k in range(1, levels)]
    (out,) = call(
        functools.partial(last_kernel, levels),
        [(rows, cols, channels)],
        [place, *mixes, inner_two, outer_two, lon_proj],
        [pltpu.VMEM((rows * cols, channels), bf16)],
        prefetch=1,
    )
    return out


def solution(mesh):
    return jax.shard_map(
        shards,
        mesh=mesh,
        in_specs=(P("lat", "lon", None), P(), P(), P(), P(), P()),
        out_specs=P("lat", "lon", None),
        check_vma=False,
    )
```

```python
import functools

import jax
import jax.numpy as jnp
from jax import lax
from jax.experimental import pallas as pl
from jax.experimental.pallas import tpu as pltpu
from jax.sharding import PartitionSpec as P

HEADS = 8
HALO = 3
TAPS = 2 * HALO + 1
STRIP = 8
SIDE = 4
LANES = 128
LEVELS = 4
EPSILON = 1e-06
VMEM_BYTES = 24 * 1024 * 1024
STAGE_BYTES = 103 * 512 * 1024
bf16, f32 = jnp.bfloat16, jnp.float32


def layer_norm(values):
    average = jnp.mean(values, axis=-1, keepdims=True)
    centered = values - average
    variance = jnp.mean(centered * centered, axis=-1, keepdims=True)
    return centered * lax.rsqrt(variance + EPSILON)


def dot(rows, matrix):
    return jnp.dot(rows, matrix, preferred_element_type=f32)


def dot_t(rows, matrix):
    return lax.dot_general(rows, matrix, (((1,), (1,)), ((), ())), preferred_element_type=f32)


def gelu(values):
    size = jnp.abs(values)
    t = 1.0 / (1.0 + (0.3275911 * 0.5**0.5) * size)
    tail = 1.061405429 * t - 1.453152027
    for coefficient in (1.421413741, -0.284496736, 0.254829592):
        tail = tail * t + coefficient
    tail = (0.5 * size * t) * tail * jnp.exp(-0.5 * values * values)
    return jnp.maximum(values, 0.0) - tail


def attend(queries, keys, values, mask):
    count, channels = queries.shape
    head_size = channels // HEADS
    lane_head = lax.broadcasted_iota(jnp.int32, (1, channels), 1) // head_size
    picks = [lane_head == h for h in range(HEADS)]
    none = jnp.zeros_like(queries)
    stacked = jnp.concatenate([jnp.where(pick, queries, none) for pick in picks], axis=0)
    scores = dot_t(stacked, keys) * head_size ** (-0.5)
    if mask is not None:
        scores = scores.reshape(HEADS, count, keys.shape[0])
        scores = jnp.where(mask[None], scores, -1e30).reshape(HEADS * count, keys.shape[0])
    top = jnp.max(scores, axis=-1, keepdims=True)
    probs = jnp.exp(scores - top)
    totals = jnp.sum(probs, axis=-1, keepdims=True)
    mixed = dot(probs.astype(bf16), values) * (1.0 / totals)
    out = mixed[:count]
    for h in range(1, HEADS):
        out = jnp.where(picks[h], mixed[h * count : (h + 1) * count], out)
    return out.astype(bf16)


def stage_kernel(*refs):
    count = (len(refs) - 1) // 2
    sems = refs[-1]
    copies = []
    for i in range(count):
        source, target = refs[i], refs[count + i]
        pieces = sems.shape[1]
        size = source.shape[0] // pieces
        for k in range(pieces):
            part = pl.ds(k * size, size)
            copies.append(pltpu.make_async_copy(source.at[part], target.at[part], sems.at[i, k]))
    for copy in copies:
        copy.start()
    for copy in copies:
        copy.wait()


def strip_kernel(nlat, place_ref, *refs):
    tiles = refs[:nlat]
    near_ref, far_ref, near, far = refs[nlat + 1 :]
    rows, cols, channels = tiles[0].shape
    even = place_ref[1] == 0
    for s in range(nlat):
        values = tiles[s][...].astype(f32)
        first, last = values[:, :STRIP], values[:, cols - STRIP :]
        where = pl.ds(lax.rem(place_ref[0] + s, nlat) * rows, rows)
        near[where] = jnp.where(even, last, first)
        far[where] = jnp.where(even, first, last)
    near_ref[...] = near[...].reshape(near_ref.shape).astype(bf16)
    far_ref[...] = far[...].reshape(far_ref.shape).astype(bf16)


def chain(my_lat, slab, shape, dw_ref, expand_ref, reduce_ref, attn_ref, center, scratch):
    taps, one, lat_in = scratch
    rows, all_rows, columns, channels = shape
    cells = all_rows * columns
    taps[...] = dw_ref[...].astype(f32)
    parts = []
    for c in range(0, channels, LANES):
        acc = jnp.zeros((all_rows, columns, LANES), f32)
        for b in range(TAPS):
            block = slab(b, c)
            for a in range(TAPS):
                tap = taps[a, b : b + 1, c : c + LANES].reshape(1, 1, LANES)
                acc = acc + block[a : a + all_rows] * tap
        parts.append(acc.reshape(cells, LANES))
    normed = layer_norm(jnp.concatenate(parts, axis=-1)).astype(bf16)

    def widen(k, total):
        part = pl.ds(pl.multiple_of(k * channels, channels), channels)
        wide = gelu(dot(normed, expand_ref[:, part])).astype(bf16)
        return total + dot(wide, reduce_ref[part])

    total = lax.fori_loop(
        0, expand_ref.shape[1] // channels, widen, center.reshape(cells, channels)
    )
    block_one = total.astype(bf16)
    one[...] = block_one
    every = layer_norm(block_one.astype(f32)).astype(bf16)
    lat_in[...] = every
    count = rows * columns
    own = pl.ds(pl.multiple_of(my_lat * count, count), count)
    queries = dot(lat_in[own], attn_ref[0]).astype(bf16)
    keys = dot(every, attn_ref[1]).astype(bf16)
    values = dot(every, attn_ref[2]).astype(bf16)
    row_col = lax.broadcasted_iota(jnp.int32, (count, 1), 0) % columns
    key_col = lax.broadcasted_iota(jnp.int32, (1, cells), 1) % columns
    mix = attend(queries, keys, values, row_col == key_col)
    block_two = (one[own].astype(f32) + dot(mix, attn_ref[3])).astype(bf16)
    return block_two, layer_norm(block_two.astype(f32))


def fill(padded, all_rows, first, values):
    width = values.shape[1]
    padded[HALO : HALO + all_rows, first : first + width] = values


def fill_tiles(padded, my_lat, first, tiles):
    rows, cols = tiles[0].shape[:2]
    for s in range(len(tiles)):
        place = HALO + lax.rem(my_lat + s, len(tiles)) * rows
        padded[pl.ds(place, rows), first : first + cols] = tiles[s][...].astype(f32)


def clear(padded, all_rows):
    edge = jnp.zeros((HALO,) + padded.shape[1:], f32)
    padded[:HALO] = edge
    padded[HALO + all_rows :] = edge


def inner_kernel(nlat, place_ref, *refs):
    tiles, refs = refs[:nlat], refs[nlat:]
    dw_ref, expand_ref, reduce_ref, attn_ref, two_ref, in_ref, padded, *scratch = refs
    rows, cols, channels = tiles[0].shape
    all_rows = rows * nlat
    columns = cols - 2 * SIDE
    clear(padded, all_rows)
    fill_tiles(padded, place_ref[0], 0, tiles)

    def slab(b, c):
        first = SIDE - HALO + b
        return padded[:, first : first + columns, c : c + LANES]

    center = padded[HALO : HALO + all_rows, SIDE : SIDE + columns]
    shape = (rows, all_rows, columns, channels)
    block_two, lon_in = chain(
        place_ref[0], slab, shape, dw_ref, expand_ref, reduce_ref, attn_ref, center, scratch
    )
    two_ref[...] = block_two
    in_ref[...] = lon_in.astype(bf16)


def outer_kernel(nlat, levels, place_ref, *refs):
    tiles, refs = refs[:nlat], refs[nlat:]
    near_ref, far_ref, inner_in_ref, dw_ref, expand_ref, reduce_ref, attn_ref = refs[:7]
    two_ref, *refs = refs[7:]
    sent_refs, (sent, padded, *scratch) = refs[:levels], refs[levels:]
    rows, cols, channels = tiles[0].shape
    all_rows = rows * nlat
    columns = 2 * SIDE
    strip_shape = (all_rows, STRIP, channels)
    near = near_ref[...].astype(f32).reshape(strip_shape)
    far = far_ref[...].astype(f32).reshape(strip_shape)
    even = place_ref[1] == 0
    clear(padded, all_rows)
    fill(padded, all_rows, 0, jnp.where(even, far, near))
    fill_tiles(padded, place_ref[0], STRIP, tiles)
    fill(padded, all_rows, STRIP + cols, jnp.where(even, near, far))
    sublane = lax.broadcasted_iota(jnp.int32, (1, columns, 1), 1)

    def halves(shift, rows_of, c, width):
        right = STRIP + cols - SIDE + shift
        left = STRIP - SIDE + shift
        return jnp.where(
            sublane < SIDE,
            padded[rows_of, right : right + columns, c : c + width],
            padded[rows_of, left : left + columns, c : c + width],
        )

    def slab(b, c):
        return halves(b - HALO, slice(None), c, LANES)

    center = halves(0, slice(HALO, HALO + all_rows), 0, channels)
    shape = (rows, all_rows, columns, channels)
    block_two, lon_in = chain(
        place_ref[0], slab, shape, dw_ref, expand_ref, reduce_ref, attn_ref, center, scratch
    )
    two_ref[...] = block_two
    inner = inner_in_ref[...].astype(f32).reshape(rows, cols - columns, channels)
    outer = lon_in.reshape(rows, columns, channels)
    sent[...] = jnp.concatenate([inner, outer], axis=1).astype(bf16)
    some = rows // levels
    for k in range(levels):
        part = sent[pl.ds((place_ref[2] ^ k) * some, some)]
        sent_refs[k][...] = part.reshape(sent_refs[k].shape)


def circle_kernel(levels, some, *refs):
    attn_ref, mix_refs = refs[-levels - 1], refs[-levels:]
    parts = refs[: -levels - 1]
    count = parts[0].shape[0] // (some * levels)

    def latitude(part, r):
        starts = [(k * some + r) * count for k in range(levels)]
        return jnp.concatenate([part[start : start + count] for start in starts], axis=0)

    for r in range(some):
        own = latitude(parts[0], r)
        every = jnp.concatenate([own] + [latitude(part, r) for part in parts[1:]], axis=0)
        queries = dot(own, attn_ref[0]).astype(bf16)
        keys = dot(every, attn_ref[1]).astype(bf16)
        values = dot(every, attn_ref[2]).astype(bf16)
        mix = attend(queries, keys, values, None)
        for k in range(levels):
            mix_refs[k][r * count : (r + 1) * count] = mix[k * count : (k + 1) * count]


def last_kernel(levels, place_ref, *refs):
    parts = refs[:levels]
    inner_ref, outer_ref, attn_ref, out_ref = refs[levels:]
    rows, cols, channels = out_ref.shape
    columns = 2 * SIDE
    some = rows // levels
    every = jnp.concatenate([part[...] for part in parts], axis=0)
    change = dot(every, attn_ref[3]).reshape(levels, some, cols, channels)
    for k in range(levels):
        start = (place_ref[2] ^ k) * some

        def state(ref, width):
            count = some * width
            place = pl.ds(pl.multiple_of(start * width, count), count)
            return ref[place].astype(f32).reshape(some, width, channels)

        inner = state(inner_ref, cols - columns) + change[k, :, : cols - columns]
        outer = state(outer_ref, columns) + change[k, :, cols - columns :]
        total = jnp.concatenate([outer[:, SIDE:], inner, outer[:, :SIDE]], axis=1)
        out_ref[pl.ds(start, some)] = total.astype(bf16)


def call(
    kernel, outs, operands, scratch=(), any_space=False, prefetch=0, flops=0, grant=VMEM_BYTES
):
    vmem = pl.BlockSpec(memory_space=pltpu.VMEM)
    given = pl.BlockSpec(memory_space=pl.ANY) if any_space else vmem
    smem = pl.BlockSpec(memory_space=pltpu.SMEM)
    shapes = [jax.ShapeDtypeStruct(shape, bf16) for shape in outs]
    moved = sum(x.size * x.dtype.itemsize for x in operands)
    result = pl.pallas_call(
        kernel,
        out_shape=shapes,
        in_specs=[smem] * prefetch + [given] * (len(operands) - prefetch),
        out_specs=[vmem] * len(outs),
        scratch_shapes=list(scratch),
        compiler_params=pltpu.CompilerParams(vmem_limit_bytes=grant),
        cost_estimate=pl.CostEstimate(flops=flops, bytes_accessed=moved, transcendentals=0),
    )(*operands)
    return result


def shards(field, dw_weight, w_expand, w_reduce, lat_attn, lon_attn):
    rows, cols, channels = field.shape
    nlat, nlon = lax.axis_size("lat"), lax.axis_size("lon")
    my_lat, my_lon = lax.axis_index("lat"), lax.axis_index("lon")
    levels = min(LEVELS, nlon)
    column = nlon // levels
    some = rows // levels
    all_rows = rows * nlat
    columns = 2 * SIDE
    place = jnp.stack([my_lat, my_lon % 2, my_lon // column]).astype(jnp.int32)

    def swap(piece, mask):
        return lax.ppermute(piece, "lon", [(j, j ^ mask) for j in range(nlon)])

    def exchange(pieces):
        moved = [swap(pieces[k], k * column) for k in range(levels - 1, 0, -1)]
        return [pieces[0]] + moved[::-1]

    tiles = [field]
    for s in range(1, nlat):
        tiles.append(lax.ppermute(field, "lat", [((i + s) % nlat, i) for i in range(nlat)]))
    weights = (w_expand, w_reduce, lat_attn, lon_attn)
    staged = call(
        stage_kernel,
        [w.shape for w in weights],
        weights,
        [pltpu.SemaphoreType.DMA((len(weights), 4))],
        any_space=True,
        grant=STAGE_BYTES,
    )
    expand, reduce, lat_proj, lon_proj = staged

    strip = (all_rows * STRIP, channels)
    strip_scratch = pltpu.VMEM((all_rows, STRIP, channels), f32)
    near, far = call(
        functools.partial(strip_kernel, nlat),
        [strip, strip],
        [place, *tiles, reduce],
        [strip_scratch, strip_scratch],
        prefetch=1,
    )
    near = swap(near, 1)
    far = lax.ppermute(
        far, "lon", [(j, (j - 1) % nlon if j % 2 == 0 else (j + 1) % nlon) for j in range(nlon)]
    )

    def scratch(width, count):
        return [
            pltpu.VMEM((all_rows + 2 * HALO, width, channels), f32),
            pltpu.VMEM(dw_weight.shape, f32),
            pltpu.VMEM((all_rows * count, channels), bf16),
            pltpu.VMEM((all_rows * count, channels), bf16),
        ]

    work = 4 * all_rows * columns * channels * w_expand.shape[1]
    inner_two, inner_in = call(
        functools.partial(inner_kernel, nlat),
        [(rows * (cols - columns), channels)] * 2,
        [place, *tiles, dw_weight, expand, reduce, lat_proj],
        scratch(cols, cols - columns),
        prefetch=1,
        flops=work,
    )
    piece = (some * cols, channels)
    outer_two, *parts = call(
        functools.partial(outer_kernel, nlat, levels),
        [(rows * columns, channels)] + [piece] * levels,
        [place, *tiles, near, far, inner_in, dw_weight, expand, reduce, lat_proj],
        [pltpu.VMEM((rows, cols, channels), bf16)] + scratch(cols + 2 * STRIP, columns),
        prefetch=1,
        flops=work,
    )

    parts = exchange(parts)
    circle = [jnp.concatenate(parts, axis=0)]
    mask = column // 2
    while mask:
        circle = circle + [swap(part, mask) for part in circle]
        mask //= 2
    mixes = call(
        functools.partial(circle_kernel, levels, some), [piece] * levels, [*circle, lon_proj]
    )
    mixes = exchange(mixes)
    (out,) = call(
        functools.partial(last_kernel, levels),
        [(rows, cols, channels)],
        [place, *mixes, inner_two, outer_two, lon_proj],
        prefetch=1,
    )
    return out


def solution(mesh):
    return jax.shard_map(
        shards,
        mesh=mesh,
        in_specs=(P("lat", "lon", None), P(), P(), P(), P(), P()),
        out_specs=P("lat", "lon", None),
        check_vma=False,
    )
```

```python
import functools

import jax
import jax.numpy as jnp
from jax import lax
from jax.experimental import pallas as pl
from jax.experimental.pallas import tpu as pltpu
from jax.sharding import PartitionSpec as P

HEADS = 8
HALO = 3
TAPS = 2 * HALO + 1
STRIP = 8
SIDE = 4
LANES = 128
LEVELS = 4
EPSILON = 1e-06
VMEM_BYTES = 24 * 1024 * 1024
STAGE_BYTES = 103 * 512 * 1024
bf16, f32 = jnp.bfloat16, jnp.float32


def layer_norm(values):
    average = jnp.mean(values, axis=-1, keepdims=True)
    centered = values - average
    variance = jnp.mean(centered * centered, axis=-1, keepdims=True)
    return centered * lax.rsqrt(variance + EPSILON)


def dot(rows, matrix):
    return jnp.dot(rows, matrix, preferred_element_type=f32)


def dot_t(rows, matrix):
    return lax.dot_general(rows, matrix, (((1,), (1,)), ((), ())), preferred_element_type=f32)


def gelu(values):
    size = jnp.abs(values)
    t = 1.0 / (1.0 + (0.3275911 * 0.5**0.5) * size)
    tail = 1.061405429 * t - 1.453152027
    for coefficient in (1.421413741, -0.284496736, 0.254829592):
        tail = tail * t + coefficient
    tail = (0.5 * size * t) * tail * jnp.exp(-0.5 * values * values)
    return jnp.maximum(values, 0.0) - tail


def attend(queries, keys, values, mask):
    count, channels = queries.shape
    head_size = channels // HEADS
    lane_head = lax.broadcasted_iota(jnp.int32, (1, channels), 1) // head_size
    picks = [lane_head == h for h in range(HEADS)]
    none = jnp.zeros_like(queries)
    stacked = jnp.concatenate([jnp.where(pick, queries, none) for pick in picks], axis=0)
    scores = dot_t(stacked, keys) * head_size ** (-0.5)
    if mask is not None:
        scores = scores.reshape(HEADS, count, keys.shape[0])
        scores = jnp.where(mask[None], scores, -1e30).reshape(HEADS * count, keys.shape[0])
    top = jnp.max(scores, axis=-1, keepdims=True)
    probs = jnp.exp(scores - top)
    totals = jnp.sum(probs, axis=-1, keepdims=True)
    mixed = dot(probs.astype(bf16), values) * (1.0 / totals)
    out = mixed[:count]
    for h in range(1, HEADS):
        out = jnp.where(picks[h], mixed[h * count : (h + 1) * count], out)
    return out.astype(bf16)


def stage_kernel(*refs):
    count = (len(refs) - 1) // 2
    sems = refs[-1]
    copies = []
    for i in range(count):
        source, target = refs[i], refs[count + i]
        pieces = sems.shape[1]
        size = source.shape[0] // pieces
        for k in range(pieces):
            part = pl.ds(k * size, size)
            copies.append(pltpu.make_async_copy(source.at[part], target.at[part], sems.at[i, k]))
    for copy in copies:
        copy.start()
    for copy in copies:
        copy.wait()


def level_of(levels):
    return lax.axis_index("lon") // (lax.axis_size("lon") // levels)


def strip_kernel(nlat, *refs):
    tiles = refs[:nlat]
    near_ref, far_ref, near, far = refs[nlat + 1 :]
    rows, cols, channels = tiles[0].shape
    even = lax.axis_index("lon") % 2 == 0
    for s in range(nlat):
        values = tiles[s][...].astype(f32)
        first, last = values[:, :STRIP], values[:, cols - STRIP :]
        where = pl.ds(lax.rem(lax.axis_index("lat") + s, nlat) * rows, rows)
        near[where] = jnp.where(even, last, first)
        far[where] = jnp.where(even, first, last)
    near_ref[...] = near[...].reshape(near_ref.shape).astype(bf16)
    far_ref[...] = far[...].reshape(far_ref.shape).astype(bf16)


def chain(my_lat, slab, shape, dw_ref, expand_ref, reduce_ref, attn_ref, center, scratch):
    taps, one, lat_in = scratch
    rows, all_rows, columns, channels = shape
    cells = all_rows * columns
    taps[...] = dw_ref[...].astype(f32)
    parts = []
    for c in range(0, channels, LANES):
        acc = jnp.zeros((all_rows, columns, LANES), f32)
        for b in range(TAPS):
            block = slab(b, c)
            for a in range(TAPS):
                tap = taps[a, b : b + 1, c : c + LANES].reshape(1, 1, LANES)
                acc = acc + block[a : a + all_rows] * tap
        parts.append(acc.reshape(cells, LANES))
    normed = layer_norm(jnp.concatenate(parts, axis=-1)).astype(bf16)

    def widen(k, total):
        part = slice(k * channels, (k + 1) * channels)
        wide = gelu(dot(normed, expand_ref[:, part])).astype(bf16)
        return total + dot(wide, reduce_ref[part])

    total = center.reshape(cells, channels)
    for k in range(expand_ref.shape[1] // channels):
        total = widen(k, total)
    block_one = total.astype(bf16)
    one[...] = block_one
    every = layer_norm(block_one.astype(f32)).astype(bf16)
    lat_in[...] = every
    count = rows * columns
    own = pl.ds(pl.multiple_of(my_lat * count, count), count)
    queries = dot(lat_in[own], attn_ref[0]).astype(bf16)
    keys = dot(every, attn_ref[1]).astype(bf16)
    values = dot(every, attn_ref[2]).astype(bf16)
    row_col = lax.broadcasted_iota(jnp.int32, (count, 1), 0) % columns
    key_col = lax.broadcasted_iota(jnp.int32, (1, cells), 1) % columns
    mix = attend(queries, keys, values, row_col == key_col)
    block_two = (one[own].astype(f32) + dot(mix, attn_ref[3])).astype(bf16)
    return block_two, layer_norm(block_two.astype(f32))


def fill(padded, all_rows, first, values):
    width = values.shape[1]
    padded[HALO : HALO + all_rows, first : first + width] = values


def fill_tiles(padded, my_lat, first, tiles):
    rows, cols = tiles[0].shape[:2]
    for s in range(len(tiles)):
        place = HALO + lax.rem(my_lat + s, len(tiles)) * rows
        padded[pl.ds(place, rows), first : first + cols] = tiles[s][...].astype(f32)


def clear(padded, all_rows):
    edge = jnp.zeros((HALO,) + padded.shape[1:], f32)
    padded[:HALO] = edge
    padded[HALO + all_rows :] = edge


def inner_kernel(nlat, *refs):
    tiles, refs = refs[:nlat], refs[nlat:]
    dw_ref, expand_ref, reduce_ref, attn_ref, two_ref, in_ref, padded, *scratch = refs
    rows, cols, channels = tiles[0].shape
    all_rows = rows * nlat
    columns = cols - 2 * SIDE
    clear(padded, all_rows)
    my_lat = lax.axis_index("lat")
    fill_tiles(padded, my_lat, 0, tiles)

    def slab(b, c):
        first = SIDE - HALO + b
        return padded[:, first : first + columns, c : c + LANES]

    center = padded[HALO : HALO + all_rows, SIDE : SIDE + columns]
    shape = (rows, all_rows, columns, channels)
    block_two, lon_in = chain(
        my_lat, slab, shape, dw_ref, expand_ref, reduce_ref, attn_ref, center, scratch
    )
    two_ref[...] = block_two
    in_ref[...] = lon_in.astype(bf16)


def outer_kernel(nlat, levels, *refs):
    tiles, refs = refs[:nlat], refs[nlat:]
    near_ref, far_ref, inner_in_ref, dw_ref, expand_ref, reduce_ref, attn_ref = refs[:7]
    two_ref, *refs = refs[7:]
    sent_refs, (sent, padded, *scratch) = refs[:levels], refs[levels:]
    rows, cols, channels = tiles[0].shape
    all_rows = rows * nlat
    columns = 2 * SIDE
    strip_shape = (all_rows, STRIP, channels)
    near = near_ref[...].astype(f32).reshape(strip_shape)
    far = far_ref[...].astype(f32).reshape(strip_shape)
    even = lax.axis_index("lon") % 2 == 0
    clear(padded, all_rows)
    fill(padded, all_rows, 0, jnp.where(even, far, near))
    my_lat = lax.axis_index("lat")
    fill_tiles(padded, my_lat, STRIP, tiles)
    fill(padded, all_rows, STRIP + cols, jnp.where(even, near, far))
    sublane = lax.broadcasted_iota(jnp.int32, (1, columns, 1), 1)

    def halves(shift, rows_of, c, width):
        right = STRIP + cols - SIDE + shift
        left = STRIP - SIDE + shift
        return jnp.where(
            sublane < SIDE,
            padded[rows_of, right : right + columns, c : c + width],
            padded[rows_of, left : left + columns, c : c + width],
        )

    def slab(b, c):
        return halves(b - HALO, slice(None), c, LANES)

    center = halves(0, slice(HALO, HALO + all_rows), 0, channels)
    shape = (rows, all_rows, columns, channels)
    block_two, lon_in = chain(
        my_lat, slab, shape, dw_ref, expand_ref, reduce_ref, attn_ref, center, scratch
    )
    two_ref[...] = block_two
    inner = inner_in_ref[...].astype(f32).reshape(rows, cols - columns, channels)
    outer = lon_in.reshape(rows, columns, channels)
    sent[...] = jnp.concatenate([inner, outer], axis=1).astype(bf16)
    some = rows // levels
    for k in range(levels):
        part = sent[pl.ds((level_of(levels) ^ k) * some, some)]
        sent_refs[k][...] = part.reshape(sent_refs[k].shape)


def circle_kernel(levels, some, *refs):
    attn_ref, mix_refs = refs[-levels - 1], refs[-levels:]
    parts = refs[: -levels - 1]
    count = parts[0].shape[0] // (some * levels)

    def latitude(part, r):
        starts = [(k * some + r) * count for k in range(levels)]
        return jnp.concatenate([part[start : start + count] for start in starts], axis=0)

    for r in range(some):
        own = latitude(parts[0], r)
        every = jnp.concatenate([own] + [latitude(part, r) for part in parts[1:]], axis=0)
        queries = dot(own, attn_ref[0]).astype(bf16)
        keys = dot(every, attn_ref[1]).astype(bf16)
        values = dot(every, attn_ref[2]).astype(bf16)
        mix = attend(queries, keys, values, None)
        for k in range(levels):
            mix_refs[k][r * count : (r + 1) * count] = mix[k * count : (k + 1) * count]


def last_kernel(levels, *refs):
    parts = refs[:levels]
    inner_ref, outer_ref, attn_ref, out_ref = refs[levels:]
    rows, cols, channels = out_ref.shape
    columns = 2 * SIDE
    some = rows // levels
    every = jnp.concatenate([part[...] for part in parts], axis=0)
    change = dot(every, attn_ref[3]).reshape(levels, some, cols, channels)
    for k in range(levels):
        start = (level_of(levels) ^ k) * some

        def state(ref, width):
            count = some * width
            place = pl.ds(pl.multiple_of(start * width, count), count)
            return ref[place].astype(f32).reshape(some, width, channels)

        inner = state(inner_ref, cols - columns) + change[k, :, : cols - columns]
        outer = state(outer_ref, columns) + change[k, :, cols - columns :]
        total = jnp.concatenate([outer[:, SIDE:], inner, outer[:, :SIDE]], axis=1)
        out_ref[pl.ds(start, some)] = total.astype(bf16)


def call(
    kernel, outs, operands, scratch=(), any_space=False, flops=0, grant=VMEM_BYTES
):
    vmem = pl.BlockSpec(memory_space=pltpu.VMEM)
    given = pl.BlockSpec(memory_space=pl.ANY) if any_space else vmem
    shapes = [jax.ShapeDtypeStruct(shape, bf16) for shape in outs]
    moved = sum(x.size * x.dtype.itemsize for x in operands)
    result = pl.pallas_call(
        kernel,
        out_shape=shapes,
        in_specs=[given] * len(operands),
        out_specs=[vmem] * len(outs),
        scratch_shapes=list(scratch),
        compiler_params=pltpu.CompilerParams(vmem_limit_bytes=grant),
        cost_estimate=pl.CostEstimate(flops=flops, bytes_accessed=moved, transcendentals=0),
    )(*operands)
    return result


def shards(field, dw_weight, w_expand, w_reduce, lat_attn, lon_attn):
    rows, cols, channels = field.shape
    nlat, nlon = lax.axis_size("lat"), lax.axis_size("lon")
    levels = min(LEVELS, nlon)
    column = nlon // levels
    some = rows // levels
    all_rows = rows * nlat
    columns = 2 * SIDE

    def swap(piece, mask):
        return lax.ppermute(piece, "lon", [(j, j ^ mask) for j in range(nlon)])

    def exchange(pieces):
        moved = [swap(pieces[k], k * column) for k in range(levels - 1, 0, -1)]
        return [pieces[0]] + moved[::-1]

    tiles = [field]
    for s in range(1, nlat):
        tiles.append(lax.ppermute(field, "lat", [((i + s) % nlat, i) for i in range(nlat)]))
    weights = (w_expand, w_reduce, lat_attn, lon_attn)
    staged = call(
        stage_kernel,
        [w.shape for w in weights],
        weights,
        [pltpu.SemaphoreType.DMA((len(weights), 4))],
        any_space=True,
        grant=STAGE_BYTES,
    )
    expand, reduce, lat_proj, lon_proj = staged

    strip = (all_rows * STRIP, channels)
    strip_scratch = pltpu.VMEM((all_rows, STRIP, channels), f32)
    near, far = call(
        functools.partial(strip_kernel, nlat),
        [strip, strip],
        [*tiles, reduce],
        [strip_scratch, strip_scratch],
    )
    near = swap(near, 1)
    far = lax.ppermute(
        far, "lon", [(j, (j - 1) % nlon if j % 2 == 0 else (j + 1) % nlon) for j in range(nlon)]
    )

    def scratch(width, count):
        return [
            pltpu.VMEM((all_rows + 2 * HALO, width, channels), f32),
            pltpu.VMEM(dw_weight.shape, f32),
            pltpu.VMEM((all_rows * count, channels), bf16),
            pltpu.VMEM((all_rows * count, channels), bf16),
        ]

    work = 4 * all_rows * columns * channels * w_expand.shape[1]
    inner_two, inner_in = call(
        functools.partial(inner_kernel, nlat),
        [(rows * (cols - columns), channels)] * 2,
        [*tiles, dw_weight, expand, reduce, lat_proj],
        scratch(cols, cols - columns),
        flops=work,
    )
    piece = (some * cols, channels)
    outer_two, *parts = call(
        functools.partial(outer_kernel, nlat, levels),
        [(rows * columns, channels)] + [piece] * levels,
        [*tiles, near, far, inner_in, dw_weight, expand, reduce, lat_proj],
        [pltpu.VMEM((rows, cols, channels), bf16)] + scratch(cols + 2 * STRIP, columns),
        flops=work,
    )

    parts = exchange(parts)
    circle = [jnp.concatenate(parts, axis=0)]
    mask = column // 2
    while mask:
        circle = circle + [swap(part, mask) for part in circle]
        mask //= 2
    mixes = call(
        functools.partial(circle_kernel, levels, some), [piece] * levels, [*circle, lon_proj]
    )
    mixes = exchange(mixes)
    (out,) = call(
        functools.partial(last_kernel, levels),
        [(rows, cols, channels)],
        [*mixes, inner_two, outer_two, lon_proj],
    )
    return out


def solution(mesh):
    return jax.shard_map(
        shards,
        mesh=mesh,
        in_specs=(P("lat", "lon", None), P(), P(), P(), P(), P()),
        out_specs=P("lat", "lon", None),
        check_vma=False,
    )
```

```python
import functools

import jax
import jax.numpy as jnp
from jax import lax
from jax.experimental import pallas as pl
from jax.experimental.pallas import tpu as pltpu
from jax.sharding import PartitionSpec as P

HEADS = 8
HALO = 3
TAPS = 2 * HALO + 1
STRIP = 8
SIDE = 4
LANES = 128
LEVELS = 4
EPSILON = 1e-06
VMEM_BYTES = 24 * 1024 * 1024
STAGE_BYTES = 103 * 512 * 1024
bf16, f32 = jnp.bfloat16, jnp.float32


def layer_norm(values):
    average = jnp.mean(values, axis=-1, keepdims=True)
    centered = values - average
    variance = jnp.mean(centered * centered, axis=-1, keepdims=True)
    return centered * lax.rsqrt(variance + EPSILON)


def dot(rows, matrix):
    return jnp.dot(rows, matrix, preferred_element_type=f32)


def dot_t(rows, matrix):
    return lax.dot_general(rows, matrix, (((1,), (1,)), ((), ())), preferred_element_type=f32)


def gelu(values):
    size = jnp.abs(values)
    t = 1.0 / (1.0 + (0.3275911 * 0.5**0.5) * size)
    tail = 1.061405429 * t - 1.453152027
    for coefficient in (1.421413741, -0.284496736, 0.254829592):
        tail = tail * t + coefficient
    tail = (0.5 * size * t) * tail * jnp.exp(-0.5 * values * values)
    return jnp.maximum(values, 0.0) - tail


def attend(queries, keys, values, mask):
    count, channels = queries.shape
    head_size = channels // HEADS
    lane_head = lax.broadcasted_iota(jnp.int32, (1, channels), 1) // head_size
    picks = [lane_head == h for h in range(HEADS)]
    none = jnp.zeros_like(queries)
    stacked = jnp.concatenate([jnp.where(pick, queries, none) for pick in picks], axis=0)
    scores = dot_t(stacked, keys) * head_size ** (-0.5)
    if mask is not None:
        scores = scores.reshape(HEADS, count, keys.shape[0])
        scores = jnp.where(mask[None], scores, -1e30).reshape(HEADS * count, keys.shape[0])
    top = jnp.max(scores, axis=-1, keepdims=True)
    probs = jnp.exp(scores - top)
    totals = jnp.sum(probs, axis=-1, keepdims=True)
    mixed = dot(probs.astype(bf16), values) * (1.0 / totals)
    out = mixed[:count]
    for h in range(1, HEADS):
        out = jnp.where(picks[h], mixed[h * count : (h + 1) * count], out)
    return out.astype(bf16)


def stage_kernel(*refs):
    count = (len(refs) - 1) // 2
    sems = refs[-1]
    copies = []
    for i in range(count):
        source, target = refs[i], refs[count + i]
        pieces = sems.shape[1]
        size = source.shape[0] // pieces
        for k in range(pieces):
            part = pl.ds(k * size, size)
            copies.append(pltpu.make_async_copy(source.at[part], target.at[part], sems.at[i, k]))
    for copy in copies:
        copy.start()
    for copy in copies:
        copy.wait()


def peer(levels, k):
    level = lax.axis_index("lon") // (lax.axis_size("lon") // levels)
    return level ^ ((levels - k) % levels)


def strip_kernel(tile_ref, near_ref, far_ref):
    cols = tile_ref.shape[1]
    values = tile_ref[...].astype(f32)
    first, last = values[:, :STRIP], values[:, cols - STRIP :]
    even = lax.axis_index("lon") % 2 == 0
    near_ref[...] = jnp.where(even, last, first).reshape(near_ref.shape).astype(bf16)
    far_ref[...] = jnp.where(even, first, last).reshape(far_ref.shape).astype(bf16)


def merge_kernel(near_ref, far_ref, after_ref, sides_ref):
    near, far = near_ref[...].astype(f32), far_ref[...].astype(f32)
    even = lax.axis_index("lon") % 2 == 0
    left, right = jnp.where(even, far, near), jnp.where(even, near, far)
    place = lax.broadcasted_iota(jnp.int32, (near.shape[0], 1), 0) % STRIP
    sides_ref[...] = jnp.where(place < SIDE, right, left).astype(bf16)


def chain(my_lat, slab, shape, dw_ref, expand_ref, reduce_ref, attn_ref, center, scratch):
    taps, one, lat_in = scratch
    rows, all_rows, columns, channels = shape
    cells = all_rows * columns
    taps[...] = dw_ref[...].astype(f32)
    parts = []
    for c in range(0, channels, LANES):
        acc = jnp.zeros((all_rows, columns, LANES), f32)
        for b in range(TAPS):
            block = slab(b, c)
            for a in range(TAPS):
                tap = taps[a, b : b + 1, c : c + LANES].reshape(1, 1, LANES)
                acc = acc + block[a : a + all_rows] * tap
        parts.append(acc.reshape(cells, LANES))
    normed = layer_norm(jnp.concatenate(parts, axis=-1)).astype(bf16)

    def widen(k, total):
        part = slice(k * channels, (k + 1) * channels)
        wide = gelu(dot(normed, expand_ref[:, part])).astype(bf16)
        return total + dot(wide, reduce_ref[part])

    total = center.reshape(cells, channels)
    for k in range(expand_ref.shape[1] // channels):
        total = widen(k, total)
    block_one = total.astype(bf16)
    one[...] = block_one
    every = layer_norm(block_one.astype(f32)).astype(bf16)
    lat_in[...] = every
    count = rows * columns
    own = pl.ds(pl.multiple_of(my_lat * count, count), count)
    queries = dot(lat_in[own], attn_ref[0]).astype(bf16)
    keys = dot(every, attn_ref[1]).astype(bf16)
    values = dot(every, attn_ref[2]).astype(bf16)
    row_col = lax.broadcasted_iota(jnp.int32, (count, 1), 0) % columns
    key_col = lax.broadcasted_iota(jnp.int32, (1, cells), 1) % columns
    mix = attend(queries, keys, values, row_col == key_col)
    block_two = (one[own].astype(f32) + dot(mix, attn_ref[3])).astype(bf16)
    return block_two, layer_norm(block_two.astype(f32))


def fill_tiles(padded, my_lat, first, tiles):
    rows, cols = tiles[0].shape[:2]
    for s in range(len(tiles)):
        place = HALO + lax.rem(my_lat + s, len(tiles)) * rows
        padded[pl.ds(place, rows), first : first + cols] = tiles[s].astype(f32)


def clear(padded, all_rows):
    edge = jnp.zeros((HALO,) + padded.shape[1:], f32)
    padded[:HALO] = edge
    padded[HALO + all_rows :] = edge


def inner_kernel(nlat, *refs):
    tiles, refs = refs[:nlat], refs[nlat:]
    dw_ref, expand_ref, reduce_ref, attn_ref, two_ref, in_ref, padded, *scratch = refs
    rows, cols, channels = tiles[0].shape
    all_rows = rows * nlat
    columns = cols - 2 * SIDE
    clear(padded, all_rows)
    my_lat = lax.axis_index("lat")
    fill_tiles(padded, my_lat, 0, [tile[...] for tile in tiles])

    def slab(b, c):
        first = SIDE - HALO + b
        return padded[:, first : first + columns, c : c + LANES]

    center = padded[HALO : HALO + all_rows, SIDE : SIDE + columns]
    shape = (rows, all_rows, columns, channels)
    block_two, lon_in = chain(
        my_lat, slab, shape, dw_ref, expand_ref, reduce_ref, attn_ref, center, scratch
    )
    two_ref[...] = block_two
    in_ref[...] = lon_in.astype(bf16)


def outer_kernel(nlat, levels, *refs):
    tiles, sides, refs = refs[:nlat], refs[nlat : 2 * nlat], refs[2 * nlat :]
    inner_in_ref, dw_ref, expand_ref, reduce_ref, attn_ref = refs[:5]
    two_ref, *refs = refs[5:]
    sent_refs, (sent, padded, *scratch) = refs[:levels], refs[levels:]
    rows, cols, channels = tiles[0].shape
    all_rows = rows * nlat
    columns = 2 * SIDE
    my_lat = lax.axis_index("lat")
    tiles = [tile[...] for tile in tiles]
    sides = [side[...].astype(f32).reshape(rows, STRIP, channels) for side in sides]
    clear(padded, all_rows)
    fill_tiles(padded, my_lat, 0, sides)
    fill_tiles(padded, my_lat, STRIP, tiles)
    fill_tiles(padded, my_lat, STRIP + cols, sides)
    sublane = lax.broadcasted_iota(jnp.int32, (1, columns, 1), 1)

    def halves(shift, rows_of, c, width):
        right = STRIP + cols - SIDE + shift
        left = STRIP - SIDE + shift
        return jnp.where(
            sublane < SIDE,
            padded[rows_of, right : right + columns, c : c + width],
            padded[rows_of, left : left + columns, c : c + width],
        )

    def slab(b, c):
        return halves(b - HALO, slice(None), c, LANES)

    center = halves(0, slice(HALO, HALO + all_rows), 0, channels)
    shape = (rows, all_rows, columns, channels)
    block_two, lon_in = chain(
        my_lat, slab, shape, dw_ref, expand_ref, reduce_ref, attn_ref, center, scratch
    )
    two_ref[...] = block_two
    inner = inner_in_ref[...].astype(f32).reshape(rows, cols - columns, channels)
    outer = lon_in.reshape(rows, columns, channels)
    sent[...] = jnp.concatenate([inner, outer], axis=1).astype(bf16)
    some = rows // levels
    for k in range(levels):
        part = sent[pl.ds(peer(levels, k) * some, some)]
        sent_refs[k][...] = part.reshape(sent_refs[k].shape)


def circle_kernel(levels, some, *refs):
    attn_ref, mix_refs = refs[-levels - 1], refs[-levels:]
    parts = refs[: -levels - 1]
    count = parts[0].shape[0] // (some * levels)

    def latitude(part, r):
        starts = [(k * some + r) * count for k in range(levels)]
        return jnp.concatenate([part[start : start + count] for start in starts], axis=0)

    for r in range(some):
        own = latitude(parts[0], r)
        every = jnp.concatenate([own] + [latitude(part, r) for part in parts[1:]], axis=0)
        queries = dot(own, attn_ref[0]).astype(bf16)
        keys = dot(every, attn_ref[1]).astype(bf16)
        values = dot(every, attn_ref[2]).astype(bf16)
        mix = attend(queries, keys, values, None)
        for k in range(levels):
            mix_refs[k][r * count : (r + 1) * count] = mix[k * count : (k + 1) * count]


def last_kernel(levels, *refs):
    parts = refs[:levels]
    inner_ref, outer_ref, attn_ref, out_ref = refs[levels:]
    rows, cols, channels = out_ref.shape
    columns = 2 * SIDE
    some = rows // levels
    every = jnp.concatenate([part[...] for part in parts], axis=0)
    change = dot(every, attn_ref[3]).reshape(levels, some, cols, channels)
    for k in range(levels):
        start = peer(levels, k) * some

        def state(ref, width):
            count = some * width
            place = pl.ds(pl.multiple_of(start * width, count), count)
            return ref[place].astype(f32).reshape(some, width, channels)

        inner = state(inner_ref, cols - columns) + change[k, :, : cols - columns]
        outer = state(outer_ref, columns) + change[k, :, cols - columns :]
        total = jnp.concatenate([outer[:, SIDE:], inner, outer[:, :SIDE]], axis=1)
        out_ref[pl.ds(start, some)] = total.astype(bf16)


def call(
    kernel, outs, operands, scratch=(), any_space=False, flops=0, grant=VMEM_BYTES
):
    vmem = pl.BlockSpec(memory_space=pltpu.VMEM)
    given = pl.BlockSpec(memory_space=pl.ANY) if any_space else vmem
    shapes = [jax.ShapeDtypeStruct(shape, bf16) for shape in outs]
    moved = sum(x.size * x.dtype.itemsize for x in operands)
    result = pl.pallas_call(
        kernel,
        out_shape=shapes,
        in_specs=[given] * len(operands),
        out_specs=[vmem] * len(outs),
        scratch_shapes=list(scratch),
        compiler_params=pltpu.CompilerParams(vmem_limit_bytes=grant),
        cost_estimate=pl.CostEstimate(flops=flops, bytes_accessed=moved, transcendentals=0),
    )(*operands)
    return result


def shards(field, dw_weight, w_expand, w_reduce, lat_attn, lon_attn):
    rows, cols, channels = field.shape
    nlat, nlon = lax.axis_size("lat"), lax.axis_size("lon")
    levels = min(LEVELS, nlon)
    column = nlon // levels
    some = rows // levels
    all_rows = rows * nlat
    columns = 2 * SIDE

    def swap(piece, mask):
        return lax.ppermute(piece, "lon", [(j, j ^ mask) for j in range(nlon)])

    def exchange(pieces):
        moved = [swap(pieces[k], (levels - k) * column) for k in range(1, levels)]
        return [pieces[0]] + moved

    def gather(tile):
        pairs = [[((i + s) % nlat, i) for i in range(nlat)] for s in range(1, nlat)]
        return [tile] + [lax.ppermute(tile, "lat", pair) for pair in pairs]

    tiles = gather(field)
    strip = (rows * STRIP, channels)
    near, far = call(strip_kernel, [strip, strip], [field])
    near = swap(near, 1)
    far = lax.ppermute(
        far, "lon", [(j, (j - 1) % nlon if j % 2 == 0 else (j + 1) % nlon) for j in range(nlon)]
    )
    weights = (w_expand, w_reduce, lat_attn, lon_attn)
    staged = call(
        stage_kernel,
        [w.shape for w in weights],
        weights,
        [pltpu.SemaphoreType.DMA((len(weights), 4))],
        any_space=True,
        grant=STAGE_BYTES,
    )
    expand, reduce, lat_proj, lon_proj = staged

    def scratch(width, count):
        return [
            pltpu.VMEM((all_rows + 2 * HALO, width, channels), f32),
            pltpu.VMEM(dw_weight.shape, f32),
            pltpu.VMEM((all_rows * count, channels), bf16),
            pltpu.VMEM((all_rows * count, channels), bf16),
        ]

    work = 4 * all_rows * columns * channels * w_expand.shape[1]
    inner_two, inner_in = call(
        functools.partial(inner_kernel, nlat),
        [(rows * (cols - columns), channels)] * 2,
        [*tiles, dw_weight, expand, reduce, lat_proj],
        scratch(cols, cols - columns),
        flops=work,
    )
    (sides,) = call(merge_kernel, [strip], [near, far, inner_in])
    sides = gather(sides)
    piece = (some * cols, channels)
    outer_two, *parts = call(
        functools.partial(outer_kernel, nlat, levels),
        [(rows * columns, channels)] + [piece] * levels,
        [*tiles, *sides, inner_in, dw_weight, expand, reduce, lat_proj],
        [pltpu.VMEM((rows, cols, channels), bf16)] + scratch(cols + 2 * STRIP, columns),
        flops=work,
    )

    parts = exchange(parts)
    circle = [jnp.concatenate(parts, axis=0)]
    mask = column // 2
    while mask:
        circle = circle + [swap(part, mask) for part in circle]
        mask //= 2
    mixes = call(
        functools.partial(circle_kernel, levels, some), [piece] * levels, [*circle, lon_proj]
    )
    mixes = exchange(mixes)
    (out,) = call(
        functools.partial(last_kernel, levels),
        [(rows, cols, channels)],
        [*mixes, inner_two, outer_two, lon_proj],
    )
    return out


def solution(mesh):
    return jax.shard_map(
        shards,
        mesh=mesh,
        in_specs=(P("lat", "lon", None), P(), P(), P(), P(), P()),
        out_specs=P("lat", "lon", None),
        check_vma=False,
    )
```

```python
import functools

import jax
import jax.numpy as jnp
from jax import lax
from jax.experimental import pallas as pl
from jax.experimental.pallas import tpu as pltpu
from jax.sharding import PartitionSpec as P

HEADS = 8
HALO = 3
TAPS = 2 * HALO + 1
STRIP = 8
SIDE = 4
LANES = 128
LEVELS = 4
EPSILON = 1e-06
VMEM_BYTES = 24 * 1024 * 1024
STAGE_BYTES = 103 * 512 * 1024
bf16, f32 = jnp.bfloat16, jnp.float32


def layer_norm(values):
    average = jnp.mean(values, axis=-1, keepdims=True)
    centered = values - average
    variance = jnp.mean(centered * centered, axis=-1, keepdims=True)
    return centered * lax.rsqrt(variance + EPSILON)


def dot(rows, matrix):
    return jnp.dot(rows, matrix, preferred_element_type=f32)


def dot_t(rows, matrix):
    return lax.dot_general(rows, matrix, (((1,), (1,)), ((), ())), preferred_element_type=f32)


def gelu(values):
    size = jnp.abs(values)
    t = 1.0 / (1.0 + (0.3275911 * 0.5**0.5) * size)
    tail = 1.061405429 * t - 1.453152027
    for coefficient in (1.421413741, -0.284496736, 0.254829592):
        tail = tail * t + coefficient
    tail = (0.5 * size * t) * tail * jnp.exp(-0.5 * values * values)
    return jnp.maximum(values, 0.0) - tail


def attend(queries, keys, values, mask):
    count, channels = queries.shape
    head_size = channels // HEADS
    lane_head = lax.broadcasted_iota(jnp.int32, (1, channels), 1) // head_size
    picks = [lane_head == h for h in range(HEADS)]
    none = jnp.zeros_like(queries)
    stacked = jnp.concatenate([jnp.where(pick, queries, none) for pick in picks], axis=0)
    scores = dot_t(stacked, keys) * head_size ** (-0.5)
    if mask is not None:
        scores = scores.reshape(HEADS, count, keys.shape[0])
        scores = jnp.where(mask[None], scores, -1e30).reshape(HEADS * count, keys.shape[0])
    top = jnp.max(scores, axis=-1, keepdims=True)
    probs = jnp.exp(scores - top)
    totals = jnp.sum(probs, axis=-1, keepdims=True)
    mixed = dot(probs.astype(bf16), values) * (1.0 / totals)
    out = mixed[:count]
    for h in range(1, HEADS):
        out = jnp.where(picks[h], mixed[h * count : (h + 1) * count], out)
    return out.astype(bf16)


def stage_kernel(*refs):
    count = (len(refs) - 1) // 2
    sems = refs[-1]
    copies = []
    for i in range(count):
        source, target = refs[i], refs[count + i]
        pieces = sems.shape[1]
        size = source.shape[0] // pieces
        for k in range(pieces):
            part = pl.ds(k * size, size)
            copies.append(pltpu.make_async_copy(source.at[part], target.at[part], sems.at[i, k]))
    for copy in copies:
        copy.start()
    for copy in copies:
        copy.wait()


def peer(levels, k):
    level = lax.axis_index("lon") // (lax.axis_size("lon") // levels)
    return level ^ ((levels - k) % levels)


def strip_kernel(nlat, *refs):
    tiles = refs[:nlat]
    near_ref, far_ref, near, far = refs[nlat + 1 :]
    rows, cols, channels = tiles[0].shape
    even = lax.axis_index("lon") % 2 == 0
    for s in range(nlat):
        values = tiles[s][...].astype(f32)
        first, last = values[:, :STRIP], values[:, cols - STRIP :]
        where = pl.ds(lax.rem(lax.axis_index("lat") + s, nlat) * rows, rows)
        near[where] = jnp.where(even, last, first)
        far[where] = jnp.where(even, first, last)
    near_ref[...] = near[...].reshape(near_ref.shape).astype(bf16)
    far_ref[...] = far[...].reshape(far_ref.shape).astype(bf16)


def chain(my_lat, slab, shape, dw_ref, expand_ref, reduce_ref, attn_ref, center, scratch):
    taps, one, lat_in = scratch
    rows, all_rows, columns, channels = shape
    cells = all_rows * columns
    taps[...] = dw_ref[...].astype(f32)
    parts = []
    for c in range(0, channels, LANES):
        acc = jnp.zeros((all_rows, columns, LANES), f32)
        for b in range(TAPS):
            block = slab(b, c)
            for a in range(TAPS):
                tap = taps[a, b : b + 1, c : c + LANES].reshape(1, 1, LANES)
                acc = acc + block[a : a + all_rows] * tap
        parts.append(acc.reshape(cells, LANES))
    normed = layer_norm(jnp.concatenate(parts, axis=-1)).astype(bf16)

    def widen(k, total):
        part = slice(k * channels, (k + 1) * channels)
        wide = gelu(dot(normed, expand_ref[:, part])).astype(bf16)
        return total + dot(wide, reduce_ref[part])

    total = center.reshape(cells, channels)
    for k in range(expand_ref.shape[1] // channels):
        total = widen(k, total)
    block_one = total.astype(bf16)
    one[...] = block_one
    every = layer_norm(block_one.astype(f32)).astype(bf16)
    lat_in[...] = every
    count = rows * columns
    own = pl.ds(pl.multiple_of(my_lat * count, count), count)
    queries = dot(lat_in[own], attn_ref[0]).astype(bf16)
    keys = dot(every, attn_ref[1]).astype(bf16)
    values = dot(every, attn_ref[2]).astype(bf16)
    row_col = lax.broadcasted_iota(jnp.int32, (count, 1), 0) % columns
    key_col = lax.broadcasted_iota(jnp.int32, (1, cells), 1) % columns
    mix = attend(queries, keys, values, row_col == key_col)
    block_two = (one[own].astype(f32) + dot(mix, attn_ref[3])).astype(bf16)
    return block_two, layer_norm(block_two.astype(f32))


def fill(padded, all_rows, first, values):
    width = values.shape[1]
    padded[HALO : HALO + all_rows, first : first + width] = values


def fill_tiles(padded, my_lat, first, tiles):
    rows, cols = tiles[0].shape[:2]
    for s in range(len(tiles)):
        place = HALO + lax.rem(my_lat + s, len(tiles)) * rows
        padded[pl.ds(place, rows), first : first + cols] = tiles[s][...].astype(f32)


def clear(padded, all_rows):
    edge = jnp.zeros((HALO,) + padded.shape[1:], f32)
    padded[:HALO] = edge
    padded[HALO + all_rows :] = edge


def inner_kernel(nlat, *refs):
    tiles, refs = refs[:nlat], refs[nlat:]
    dw_ref, expand_ref, reduce_ref, attn_ref, two_ref, in_ref, padded, *scratch = refs
    rows, cols, channels = tiles[0].shape
    all_rows = rows * nlat
    columns = cols - 2 * SIDE
    clear(padded, all_rows)
    my_lat = lax.axis_index("lat")
    fill_tiles(padded, my_lat, 0, tiles)

    def slab(b, c):
        first = SIDE - HALO + b
        return padded[:, first : first + columns, c : c + LANES]

    center = padded[HALO : HALO + all_rows, SIDE : SIDE + columns]
    shape = (rows, all_rows, columns, channels)
    block_two, lon_in = chain(
        my_lat, slab, shape, dw_ref, expand_ref, reduce_ref, attn_ref, center, scratch
    )
    two_ref[...] = block_two
    in_ref[...] = lon_in.astype(bf16)


def outer_kernel(nlat, levels, *refs):
    tiles, refs = refs[:nlat], refs[nlat:]
    near_ref, far_ref, inner_in_ref, dw_ref, expand_ref, reduce_ref, attn_ref = refs[:7]
    two_ref, *refs = refs[7:]
    sent_refs, (sent, padded, *scratch) = refs[:levels], refs[levels:]
    rows, cols, channels = tiles[0].shape
    all_rows = rows * nlat
    columns = 2 * SIDE
    strip_shape = (all_rows, STRIP, channels)
    near = near_ref[...].astype(f32).reshape(strip_shape)
    far = far_ref[...].astype(f32).reshape(strip_shape)
    even = lax.axis_index("lon") % 2 == 0
    clear(padded, all_rows)
    fill(padded, all_rows, 0, jnp.where(even, far, near))
    my_lat = lax.axis_index("lat")
    fill_tiles(padded, my_lat, STRIP, tiles)
    fill(padded, all_rows, STRIP + cols, jnp.where(even, near, far))
    sublane = lax.broadcasted_iota(jnp.int32, (1, columns, 1), 1)

    def halves(shift, rows_of, c, width):
        right = STRIP + cols - SIDE + shift
        left = STRIP - SIDE + shift
        return jnp.where(
            sublane < SIDE,
            padded[rows_of, right : right + columns, c : c + width],
            padded[rows_of, left : left + columns, c : c + width],
        )

    def slab(b, c):
        return halves(b - HALO, slice(None), c, LANES)

    center = halves(0, slice(HALO, HALO + all_rows), 0, channels)
    shape = (rows, all_rows, columns, channels)
    block_two, lon_in = chain(
        my_lat, slab, shape, dw_ref, expand_ref, reduce_ref, attn_ref, center, scratch
    )
    two_ref[...] = block_two
    inner = inner_in_ref[...].astype(f32).reshape(rows, cols - columns, channels)
    outer = lon_in.reshape(rows, columns, channels)
    sent[...] = jnp.concatenate([inner, outer], axis=1).astype(bf16)
    some = rows // levels
    for k in range(levels):
        part = sent[pl.ds(peer(levels, k) * some, some)]
        sent_refs[k][...] = part.reshape(sent_refs[k].shape)


def circle_kernel(levels, some, *refs):
    attn_ref, mix_refs = refs[-levels - 1], refs[-levels:]
    parts = refs[: -levels - 1]
    count = parts[0].shape[0] // (some * levels)

    def latitude(part, r):
        starts = [(k * some + r) * count for k in range(levels)]
        return jnp.concatenate([part[start : start + count] for start in starts], axis=0)

    for r in range(some):
        own = latitude(parts[0], r)
        every = jnp.concatenate([own] + [latitude(part, r) for part in parts[1:]], axis=0)
        queries = dot(own, attn_ref[0]).astype(bf16)
        keys = dot(every, attn_ref[1]).astype(bf16)
        values = dot(every, attn_ref[2]).astype(bf16)
        mix = attend(queries, keys, values, None)
        for k in range(levels):
            mix_refs[k][r * count : (r + 1) * count] = mix[k * count : (k + 1) * count]


def last_kernel(levels, *refs):
    parts = refs[:levels]
    inner_ref, outer_ref, attn_ref, out_ref = refs[levels:]
    rows, cols, channels = out_ref.shape
    columns = 2 * SIDE
    some = rows // levels
    every = jnp.concatenate([part[...] for part in parts], axis=0)
    change = dot(every, attn_ref[3]).reshape(levels, some, cols, channels)
    for k in range(levels):
        start = peer(levels, k) * some

        def state(ref, width):
            count = some * width
            place = pl.ds(pl.multiple_of(start * width, count), count)
            return ref[place].astype(f32).reshape(some, width, channels)

        inner = state(inner_ref, cols - columns) + change[k, :, : cols - columns]
        outer = state(outer_ref, columns) + change[k, :, cols - columns :]
        total = jnp.concatenate([outer[:, SIDE:], inner, outer[:, :SIDE]], axis=1)
        out_ref[pl.ds(start, some)] = total.astype(bf16)


def call(
    kernel, outs, operands, scratch=(), any_space=False, flops=0, grant=VMEM_BYTES
):
    vmem = pl.BlockSpec(memory_space=pltpu.VMEM)
    given = pl.BlockSpec(memory_space=pl.ANY) if any_space else vmem
    shapes = [jax.ShapeDtypeStruct(shape, bf16) for shape in outs]
    moved = sum(x.size * x.dtype.itemsize for x in operands)
    result = pl.pallas_call(
        kernel,
        out_shape=shapes,
        in_specs=[given] * len(operands),
        out_specs=[vmem] * len(outs),
        scratch_shapes=list(scratch),
        compiler_params=pltpu.CompilerParams(vmem_limit_bytes=grant),
        cost_estimate=pl.CostEstimate(flops=flops, bytes_accessed=moved, transcendentals=0),
    )(*operands)
    return result


def shards(field, dw_weight, w_expand, w_reduce, lat_attn, lon_attn):
    rows, cols, channels = field.shape
    nlat, nlon = lax.axis_size("lat"), lax.axis_size("lon")
    levels = min(LEVELS, nlon)
    column = nlon // levels
    some = rows // levels
    all_rows = rows * nlat
    columns = 2 * SIDE

    def swap(piece, mask):
        return lax.ppermute(piece, "lon", [(j, j ^ mask) for j in range(nlon)])

    def exchange(pieces):
        moved = []
        for k in range(1, levels):
            level = levels - k
            moved.append(swap(pieces[k], level * column + level * 2 // levels))
        return [pieces[0]] + moved

    tiles = [field]
    for s in range(1, nlat):
        tiles.append(lax.ppermute(field, "lat", [((i + s) % nlat, i) for i in range(nlat)]))
    weights = (w_expand, w_reduce, lat_attn, lon_attn)
    staged = call(
        stage_kernel,
        [w.shape for w in weights],
        weights,
        [pltpu.SemaphoreType.DMA((len(weights), 4))],
        any_space=True,
        grant=STAGE_BYTES,
    )
    expand, reduce, lat_proj, lon_proj = staged

    strip = (all_rows * STRIP, channels)
    strip_scratch = pltpu.VMEM((all_rows, STRIP, channels), f32)
    near, far = call(
        functools.partial(strip_kernel, nlat),
        [strip, strip],
        [*tiles, reduce],
        [strip_scratch, strip_scratch],
    )
    near = swap(near, 1)
    far = lax.ppermute(
        far, "lon", [(j, (j - 1) % nlon if j % 2 == 0 else (j + 1) % nlon) for j in range(nlon)]
    )

    def scratch(width, count):
        return [
            pltpu.VMEM((all_rows + 2 * HALO, width, channels), f32),
            pltpu.VMEM(dw_weight.shape, f32),
            pltpu.VMEM((all_rows * count, channels), bf16),
            pltpu.VMEM((all_rows * count, channels), bf16),
        ]

    work = 4 * all_rows * columns * channels * w_expand.shape[1]
    inner_two, inner_in = call(
        functools.partial(inner_kernel, nlat),
        [(rows * (cols - columns), channels)] * 2,
        [*tiles, dw_weight, expand, reduce, lat_proj],
        scratch(cols, cols - columns),
        flops=work,
    )
    piece = (some * cols, channels)
    outer_two, *parts = call(
        functools.partial(outer_kernel, nlat, levels),
        [(rows * columns, channels)] + [piece] * levels,
        [*tiles, near, far, inner_in, dw_weight, expand, reduce, lat_proj],
        [pltpu.VMEM((rows, cols, channels), bf16)] + scratch(cols + 2 * STRIP, columns),
        flops=work,
    )

    parts = exchange(parts)
    circle = [jnp.concatenate(parts, axis=0)]
    mask = column // 2
    while mask:
        circle = circle + [swap(part, mask + mask // 2) for part in circle]
        mask //= 2
    mixes = call(
        functools.partial(circle_kernel, levels, some), [piece] * levels, [*circle, lon_proj]
    )
    mixes = exchange(mixes)
    (out,) = call(
        functools.partial(last_kernel, levels),
        [(rows, cols, channels)],
        [*mixes, inner_two, outer_two, lon_proj],
    )
    return out


def solution(mesh):
    return jax.shard_map(
        shards,
        mesh=mesh,
        in_specs=(P("lat", "lon", None), P(), P(), P(), P(), P()),
        out_specs=P("lat", "lon", None),
        check_vma=False,
    )
```

```python
import functools

import jax
import jax.numpy as jnp
from jax import lax
from jax.experimental import pallas as pl
from jax.experimental.pallas import tpu as pltpu
from jax.sharding import PartitionSpec as P

HEADS = 8
HALO = 3
TAPS = 2 * HALO + 1
STRIP = 8
SIDE = 4
LANES = 128
LEVELS = 4
STAGES = 4
EPSILON = 1e-06
VMEM_BYTES = 24 * 1024 * 1024
STAGE_BYTES = 103 * 512 * 1024
bf16, f32 = jnp.bfloat16, jnp.float32


def layer_norm(values):
    average = jnp.mean(values, axis=-1, keepdims=True)
    centered = values - average
    variance = jnp.mean(centered * centered, axis=-1, keepdims=True)
    return centered * lax.rsqrt(variance + EPSILON)


def dot(rows, matrix):
    return jnp.dot(rows, matrix, preferred_element_type=f32)


def dot_t(rows, matrix):
    return lax.dot_general(rows, matrix, (((1,), (1,)), ((), ())), preferred_element_type=f32)


def gelu(values):
    size = jnp.abs(values)
    t = 1.0 / (1.0 + (0.3275911 * 0.5**0.5) * size)
    tail = 1.061405429 * t - 1.453152027
    for coefficient in (1.421413741, -0.284496736, 0.254829592):
        tail = tail * t + coefficient
    tail = (0.5 * size * t) * tail * jnp.exp(-0.5 * values * values)
    return jnp.maximum(values, 0.0) - tail


def attend(queries, keys, values, mask):
    count, channels = queries.shape
    head_size = channels // HEADS
    lane_head = lax.broadcasted_iota(jnp.int32, (1, channels), 1) // head_size
    picks = [lane_head == h for h in range(HEADS)]
    none = jnp.zeros_like(queries)
    stacked = jnp.concatenate([jnp.where(pick, queries, none) for pick in picks], axis=0)
    scores = dot_t(stacked, keys) * head_size ** (-0.5)
    if mask is not None:
        scores = scores.reshape(HEADS, count, keys.shape[0])
        scores = jnp.where(mask[None], scores, -1e30).reshape(HEADS * count, keys.shape[0])
    top = jnp.max(scores, axis=-1, keepdims=True)
    probs = jnp.exp(scores - top)
    totals = jnp.sum(probs, axis=-1, keepdims=True)
    mixed = dot(probs.astype(bf16), values) * (1.0 / totals)
    out = mixed[:count]
    for h in range(1, HEADS):
        out = jnp.where(picks[h], mixed[h * count : (h + 1) * count], out)
    return out.astype(bf16)


def stage(sources, targets, sems):
    copies = []
    for i, (source, target) in enumerate(zip(sources, targets)):
        size = source.shape[0] // STAGES
        pieces = []
        for k in range(STAGES):
            part = pl.ds(k * size, size)
            pieces.append(pltpu.make_async_copy(source.at[part], target.at[part], sems.at[i, k]))
        copies.append(pieces)
    for pieces in copies:
        for piece in pieces:
            piece.start()

    def ready(i):
        for piece in copies[i]:
            piece.wait()

    return ready


def peer(levels, k):
    level = lax.axis_index("lon") // (lax.axis_size("lon") // levels)
    return level ^ ((levels - k) % levels)


def copy_kernel(source_ref, target_ref):
    target_ref[...] = source_ref[...]


def strip_kernel(nlat, *refs):
    tiles = refs[:nlat]
    near_ref, far_ref, near, far = refs[nlat:]
    rows, cols, channels = tiles[0].shape
    even = lax.axis_index("lon") % 2 == 0
    for s in range(nlat):
        values = tiles[s][...].astype(f32)
        first, last = values[:, :STRIP], values[:, cols - STRIP :]
        where = pl.ds(lax.rem(lax.axis_index("lat") + s, nlat) * rows, rows)
        near[where] = jnp.where(even, last, first)
        far[where] = jnp.where(even, first, last)
    for strip, strip_ref, is_last in ((near, near_ref, even), (far, far_ref, ~even)):
        strip_ref[...] = pack(strip[...], is_last).reshape(strip_ref.shape).astype(bf16)


def lower_half():
    return lax.broadcasted_iota(jnp.int32, (1, STRIP, 1), 1) < SIDE


def turn(values):
    return jnp.concatenate([values[:, SIDE:], values[:, :SIDE]], axis=1)


def pack(strip, is_last):
    half = strip.shape[0] // 2
    turned = turn(strip)
    low = jnp.where(is_last, turned, strip)
    high = jnp.where(is_last, strip, turned)
    return jnp.where(lower_half(), low[:half], high[half:])


def unpack(packed, is_left):
    turned = turn(packed)
    low = jnp.where(is_left, turned, packed)
    high = jnp.where(is_left, packed, turned)
    return jnp.concatenate([low, high], axis=0)


def chain(my_lat, slab, shape, weights, center, scratch, ready=lambda i: None):
    dw_ref, expand_ref, reduce_ref, attn_ref = weights
    taps, one, lat_in = scratch
    rows, all_rows, columns, channels = shape
    cells = all_rows * columns
    taps[...] = dw_ref[...].astype(f32)
    parts = []
    for c in range(0, channels, LANES):
        acc = jnp.zeros((all_rows, columns, LANES), f32)
        for b in range(TAPS):
            block = slab(b, c)
            for a in range(TAPS):
                tap = taps[a, b : b + 1, c : c + LANES].reshape(1, 1, LANES)
                acc = acc + block[a : a + all_rows] * tap
        parts.append(acc.reshape(cells, LANES))
    normed = layer_norm(jnp.concatenate(parts, axis=-1)).astype(bf16)

    ready(0)
    ready(1)

    def widen(k, total):
        part = slice(k * channels, (k + 1) * channels)
        wide = gelu(dot(normed, expand_ref[:, part])).astype(bf16)
        return total + dot(wide, reduce_ref[part])

    total = center.reshape(cells, channels)
    for k in range(expand_ref.shape[1] // channels):
        total = widen(k, total)
    block_one = total.astype(bf16)
    one[...] = block_one
    every = layer_norm(block_one.astype(f32)).astype(bf16)
    lat_in[...] = every
    ready(2)
    count = rows * columns
    own = pl.ds(pl.multiple_of(my_lat * count, count), count)
    queries = dot(lat_in[own], attn_ref[0]).astype(bf16)
    keys = dot(every, attn_ref[1]).astype(bf16)
    values = dot(every, attn_ref[2]).astype(bf16)
    row_col = lax.broadcasted_iota(jnp.int32, (count, 1), 0) % columns
    key_col = lax.broadcasted_iota(jnp.int32, (1, cells), 1) % columns
    mix = attend(queries, keys, values, row_col == key_col)
    block_two = (one[own].astype(f32) + dot(mix, attn_ref[3])).astype(bf16)
    return block_two, layer_norm(block_two.astype(f32))


def fill(padded, all_rows, first, values):
    width = values.shape[1]
    padded[HALO : HALO + all_rows, first : first + width] = values


def fill_tiles(padded, my_lat, first, tiles):
    rows, cols = tiles[0].shape[:2]
    for s in range(len(tiles)):
        place = HALO + lax.rem(my_lat + s, len(tiles)) * rows
        padded[pl.ds(place, rows), first : first + cols] = tiles[s][...].astype(f32)


def clear(padded, all_rows):
    edge = jnp.zeros((HALO,) + padded.shape[1:], f32)
    padded[:HALO] = edge
    padded[HALO + all_rows :] = edge


def inner_kernel(nlat, *refs):
    tiles, dw_ref, sources, refs = refs[:nlat], refs[nlat], refs[nlat + 1 : nlat + 5], refs[nlat + 5 :]
    two_ref, in_ref, *targets = refs[:6]
    padded, sems, *scratch = refs[6:]
    ready = stage(sources, targets, sems)
    rows, cols, channels = tiles[0].shape
    all_rows = rows * nlat
    columns = cols - 2 * SIDE
    my_lat = lax.axis_index("lat")
    clear(padded, all_rows)
    fill_tiles(padded, my_lat, 0, tiles)

    def slab(b, c):
        first = SIDE - HALO + b
        return padded[:, first : first + columns, c : c + LANES]

    center = padded[HALO : HALO + all_rows, SIDE : SIDE + columns]
    shape = (rows, all_rows, columns, channels)
    weights = (dw_ref, *targets[:3])
    block_two, lon_in = chain(my_lat, slab, shape, weights, center, scratch, ready)
    two_ref[...] = block_two
    in_ref[...] = lon_in.astype(bf16)
    ready(3)


def outer_kernel(nlat, levels, *refs):
    tiles, refs = refs[:nlat], refs[nlat:]
    near_ref, far_ref, inner_in_ref = refs[:3]
    ends, weights = refs[3 : nlat + 3], refs[nlat + 3 : nlat + 7]
    two_ref, *refs = refs[nlat + 7 :]
    sent_refs, (sent, padded, *scratch) = refs[:levels], refs[levels:]
    rows, cols, channels = tiles[0].shape
    all_rows = rows * nlat
    columns = 2 * SIDE
    packed = (all_rows // 2, STRIP, channels)
    near = near_ref[...].astype(f32).reshape(packed)
    far = far_ref[...].astype(f32).reshape(packed)
    even = lax.axis_index("lon") % 2 == 0
    my_lat = lax.axis_index("lat")
    clear(padded, all_rows)
    fill(padded, all_rows, 0, unpack(jnp.where(even, far, near), True))
    fill_tiles(padded, my_lat, STRIP, tiles)
    fill(padded, all_rows, STRIP + cols, unpack(jnp.where(even, near, far), False))

    @pl.when(lax.axis_index("lon") == 0)
    def _():
        fill_tiles(padded, my_lat, 0, [end[...].astype(f32)[:, cols - STRIP :] for end in ends])

    @pl.when(lax.axis_index("lon") == lax.axis_size("lon") - 1)
    def _():
        fill_tiles(padded, my_lat, STRIP + cols, [end[...].astype(f32)[:, :STRIP] for end in ends])

    sublane = lax.broadcasted_iota(jnp.int32, (1, columns, 1), 1)

    def halves(shift, rows_of, c, width):
        right = STRIP + cols - SIDE + shift
        left = STRIP - SIDE + shift
        return jnp.where(
            sublane < SIDE,
            padded[rows_of, right : right + columns, c : c + width],
            padded[rows_of, left : left + columns, c : c + width],
        )

    def slab(b, c):
        return halves(b - HALO, slice(None), c, LANES)

    center = halves(0, slice(HALO, HALO + all_rows), 0, channels)
    shape = (rows, all_rows, columns, channels)
    block_two, lon_in = chain(my_lat, slab, shape, weights, center, scratch)
    two_ref[...] = block_two
    inner = inner_in_ref[...].astype(f32).reshape(rows, cols - columns, channels)
    outer = lon_in.reshape(rows, columns, channels)
    sent[...] = jnp.concatenate([inner, outer], axis=1).astype(bf16)
    some = rows // levels
    for k in range(levels):
        part = sent[pl.ds(peer(levels, k) * some, some)]
        sent_refs[k][...] = part.reshape(sent_refs[k].shape)


def circle_kernel(levels, some, *refs):
    attn_ref, mix_refs = refs[-levels - 1], refs[-levels:]
    parts = refs[: -levels - 1]
    count = parts[0].shape[0] // (some * levels)

    def latitude(part, r):
        starts = [(k * some + r) * count for k in range(levels)]
        return jnp.concatenate([part[start : start + count] for start in starts], axis=0)

    for r in range(some):
        own = latitude(parts[0], r)
        every = jnp.concatenate([own] + [latitude(part, r) for part in parts[1:]], axis=0)
        queries = dot(own, attn_ref[0]).astype(bf16)
        keys = dot(every, attn_ref[1]).astype(bf16)
        values = dot(every, attn_ref[2]).astype(bf16)
        mix = attend(queries, keys, values, None)
        for k in range(levels):
            mix_refs[k][r * count : (r + 1) * count] = mix[k * count : (k + 1) * count]


def last_kernel(levels, *refs):
    parts = refs[:levels]
    inner_ref, outer_ref, attn_ref, out_ref = refs[levels:]
    rows, cols, channels = out_ref.shape
    columns = 2 * SIDE
    some = rows // levels
    every = jnp.concatenate([part[...] for part in parts], axis=0)
    change = dot(every, attn_ref[3]).reshape(levels, some, cols, channels)
    for k in range(levels):
        start = peer(levels, k) * some

        def state(ref, width):
            count = some * width
            place = pl.ds(pl.multiple_of(start * width, count), count)
            return ref[place].astype(f32).reshape(some, width, channels)

        inner = state(inner_ref, cols - columns) + change[k, :, : cols - columns]
        outer = state(outer_ref, columns) + change[k, :, cols - columns :]
        total = jnp.concatenate([outer[:, SIDE:], inner, outer[:, :SIDE]], axis=1)
        out_ref[pl.ds(start, some)] = total.astype(bf16)


def call(kernel, outs, operands, scratch=(), kept=0, flops=0, grant=VMEM_BYTES):
    vmem = pl.BlockSpec(memory_space=pltpu.VMEM)
    given = [vmem] * (len(operands) - kept) + [pl.BlockSpec(memory_space=pl.ANY)] * kept
    shapes = [jax.ShapeDtypeStruct(shape, bf16) for shape in outs]
    moved = sum(x.size * x.dtype.itemsize for x in operands)
    result = pl.pallas_call(
        kernel,
        out_shape=shapes,
        in_specs=given,
        out_specs=[vmem] * len(outs),
        scratch_shapes=list(scratch),
        compiler_params=pltpu.CompilerParams(vmem_limit_bytes=grant),
        cost_estimate=pl.CostEstimate(flops=flops, bytes_accessed=moved, transcendentals=0),
    )(*operands)
    return result


def shards(field, dw_weight, w_expand, w_reduce, lat_attn, lon_attn):
    rows, cols, channels = field.shape
    nlat, nlon = lax.axis_size("lat"), lax.axis_size("lon")
    levels = min(LEVELS, nlon)
    column = nlon // levels
    some = rows // levels
    all_rows = rows * nlat
    columns = 2 * SIDE

    def swap(piece, mask):
        return lax.ppermute(piece, "lon", [(j, j ^ mask) for j in range(nlon)])

    def exchange(pieces):
        moved = []
        for k in range(1, levels):
            level = levels - k
            moved.append(swap(pieces[k], level * column + level * 2 // levels))
        return [pieces[0]] + moved

    tiles = [field]
    for s in range(1, nlat):
        tiles.append(lax.ppermute(field, "lat", [((i + s) % nlat, i) for i in range(nlat)]))
    tiles[0] = call(copy_kernel, [field.shape], [field])[0]
    last = nlon - 1
    ends = []
    for s in range(nlat):
        pairs = []
        for i in range(nlat):
            here, there = i * nlon, (i + s) % nlat * nlon
            pairs += [(there + last, here), (there, here + last)]
        ends.append(lax.ppermute(field, ("lat", "lon"), pairs))

    strip = (all_rows * SIDE, channels)
    strip_scratch = pltpu.VMEM((all_rows, STRIP, channels), f32)
    near, far = call(
        functools.partial(strip_kernel, nlat),
        [strip, strip],
        tiles,
        [strip_scratch, strip_scratch],
    )
    near = swap(near, 1)
    odd = range(1, nlon - 1, 2)
    far = lax.ppermute(far, "lon", [p for j in odd for p in ((j, j + 1), (j + 1, j))])

    def padded(width):
        return pltpu.VMEM((all_rows + 2 * HALO, width, channels), f32)

    def scratch(count):
        kept = pltpu.VMEM((all_rows * count, channels), bf16)
        return [pltpu.VMEM(dw_weight.shape, f32), kept, kept]

    work = 4 * all_rows * columns * channels * w_expand.shape[1]
    weights = (w_expand, w_reduce, lat_attn, lon_attn)
    inner = (rows * (cols - columns), channels)
    inner_two, inner_in, expand, reduce, lat_proj, lon_proj = call(
        functools.partial(inner_kernel, nlat),
        [inner, inner] + [w.shape for w in weights],
        [*tiles, dw_weight, *weights],
        [padded(cols), pltpu.SemaphoreType.DMA((len(weights), STAGES)), *scratch(cols - columns)],
        kept=len(weights),
        flops=work,
        grant=STAGE_BYTES,
    )
    piece = (some * cols, channels)
    outer_two, *parts = call(
        functools.partial(outer_kernel, nlat, levels),
        [(rows * columns, channels)] + [piece] * levels,
        [*tiles, near, far, inner_in, *ends, dw_weight, expand, reduce, lat_proj],
        [pltpu.VMEM((rows, cols, channels), bf16), padded(cols + 2 * STRIP), *scratch(columns)],
        flops=work,
    )

    parts = exchange(parts)
    circle = [jnp.concatenate(parts, axis=0)]
    mask = column // 2
    while mask:
        circle = circle + [swap(part, mask + mask // 2) for part in circle]
        mask //= 2
    mixes = call(
        functools.partial(circle_kernel, levels, some), [piece] * levels, [*circle, lon_proj]
    )
    mixes = exchange(mixes)
    (out,) = call(
        functools.partial(last_kernel, levels),
        [(rows, cols, channels)],
        [*mixes, inner_two, outer_two, lon_proj],
    )
    return out


def solution(mesh):
    return jax.shard_map(
        shards,
        mesh=mesh,
        in_specs=(P("lat", "lon", None), P(), P(), P(), P(), P()),
        out_specs=P("lat", "lon", None),
        check_vma=False,
    )
```

```python
import functools

import jax
import jax.numpy as jnp
from jax import lax
from jax.experimental import pallas as pl
from jax.experimental.pallas import tpu as pltpu
from jax.sharding import PartitionSpec as P

HEADS = 8
HALO = 3
TAPS = 2 * HALO + 1
STRIP = 8
SIDE = 4
LANES = 128
LEVELS = 4
EPSILON = 1e-06
VMEM_BYTES = 24 * 1024 * 1024
STAGE_BYTES = 103 * 512 * 1024
bf16, f32 = jnp.bfloat16, jnp.float32


def layer_norm(values):
    average = jnp.mean(values, axis=-1, keepdims=True)
    centered = values - average
    variance = jnp.mean(centered * centered, axis=-1, keepdims=True)
    return centered * lax.rsqrt(variance + EPSILON)


def dot(rows, matrix):
    return jnp.dot(rows, matrix, preferred_element_type=f32)


def dot_t(rows, matrix):
    return lax.dot_general(rows, matrix, (((1,), (1,)), ((), ())), preferred_element_type=f32)


def gelu(values):
    size = jnp.abs(values)
    t = 1.0 / (1.0 + (0.3275911 * 0.5**0.5) * size)
    tail = 1.061405429 * t - 1.453152027
    for coefficient in (1.421413741, -0.284496736, 0.254829592):
        tail = tail * t + coefficient
    tail = (0.5 * size * t) * tail * jnp.exp(-0.5 * values * values)
    return jnp.maximum(values, 0.0) - tail


def attend(queries, keys, values, mask):
    count, channels = queries.shape
    head_size = channels // HEADS
    lane_head = lax.broadcasted_iota(jnp.int32, (1, channels), 1) // head_size
    picks = [lane_head == h for h in range(HEADS)]
    none = jnp.zeros_like(queries)
    stacked = jnp.concatenate([jnp.where(pick, queries, none) for pick in picks], axis=0)
    scores = dot_t(stacked, keys) * head_size ** (-0.5)
    if mask is not None:
        scores = scores.reshape(HEADS, count, keys.shape[0])
        scores = jnp.where(mask[None], scores, -1e30).reshape(HEADS * count, keys.shape[0])
    top = jnp.max(scores, axis=-1, keepdims=True)
    probs = jnp.exp(scores - top)
    probs = probs.astype(bf16)
    totals = dot(probs, jnp.ones((keys.shape[0], LANES), bf16))
    share = 1.0 / totals
    mixed = dot(probs, values) * jnp.concatenate([share] * (channels // LANES), axis=-1)
    out = mixed[:count]
    for h in range(1, HEADS):
        out = jnp.where(picks[h], mixed[h * count : (h + 1) * count], out)
    return out.astype(bf16)


def stage_kernel(*refs):
    count = (len(refs) - 1) // 2
    sems = refs[-1]
    copies = []
    for i in range(count):
        source, target = refs[i], refs[count + i]
        pieces = sems.shape[1]
        size = source.shape[0] // pieces
        for k in range(pieces):
            part = pl.ds(k * size, size)
            copies.append(pltpu.make_async_copy(source.at[part], target.at[part], sems.at[i, k]))
    for copy in copies:
        copy.start()
    for copy in copies:
        copy.wait()


def peer(levels, k):
    level = lax.axis_index("lon") // (lax.axis_size("lon") // levels)
    return level ^ ((levels - k) % levels)


def strip_kernel(nlat, *refs):
    tiles = refs[:nlat]
    near_ref, far_ref, near, far = refs[nlat + 1 :]
    rows, cols, channels = tiles[0].shape
    even = lax.axis_index("lon") % 2 == 0
    for s in range(nlat):
        values = tiles[s][...].astype(f32)
        first, last = values[:, :STRIP], values[:, cols - STRIP :]
        where = pl.ds(lax.rem(lax.axis_index("lat") + s, nlat) * rows, rows)
        near[where] = jnp.where(even, last, first)
        far[where] = jnp.where(even, first, last)
    for strip, strip_ref, is_last in ((near, near_ref, even), (far, far_ref, ~even)):
        strip_ref[...] = pack(strip[...], is_last).reshape(strip_ref.shape).astype(bf16)


def lower_half():
    return lax.broadcasted_iota(jnp.int32, (1, STRIP, 1), 1) < SIDE


def turn(values):
    return jnp.concatenate([values[:, SIDE:], values[:, :SIDE]], axis=1)


def pack(strip, is_last):
    half = strip.shape[0] // 2
    turned = turn(strip)
    low = jnp.where(is_last, turned, strip)
    high = jnp.where(is_last, strip, turned)
    return jnp.where(lower_half(), low[:half], high[half:])


def unpack(packed, is_left):
    turned = turn(packed)
    low = jnp.where(is_left, turned, packed)
    high = jnp.where(is_left, packed, turned)
    return jnp.concatenate([low, high], axis=0)


def chain(my_lat, slab, shape, dw_ref, expand_ref, reduce_ref, attn_ref, center, scratch):
    taps, one, lat_in = scratch
    rows, all_rows, columns, channels = shape
    cells = all_rows * columns
    taps[...] = dw_ref[...].astype(f32)
    parts = []
    for c in range(0, channels, LANES):
        acc = jnp.zeros((all_rows, columns, LANES), f32)
        for b in range(TAPS):
            block = slab(b, c)
            for a in range(TAPS):
                tap = taps[a, b : b + 1, c : c + LANES].reshape(1, 1, LANES)
                acc = acc + block[a : a + all_rows] * tap
        parts.append(acc.reshape(cells, LANES))
    normed = layer_norm(jnp.concatenate(parts, axis=-1)).astype(bf16)

    def widen(k, total):
        part = slice(k * channels, (k + 1) * channels)
        wide = gelu(dot(normed, expand_ref[:, part])).astype(bf16)
        return total + dot(wide, reduce_ref[part])

    total = center.reshape(cells, channels)
    for k in range(expand_ref.shape[1] // channels):
        total = widen(k, total)
    block_one = total.astype(bf16)
    one[...] = block_one
    every = layer_norm(block_one.astype(f32)).astype(bf16)
    lat_in[...] = every
    count = rows * columns
    own = pl.ds(pl.multiple_of(my_lat * count, count), count)
    queries = dot(lat_in[own], attn_ref[0]).astype(bf16)
    keys = dot(every, attn_ref[1]).astype(bf16)
    values = dot(every, attn_ref[2]).astype(bf16)
    row_col = lax.broadcasted_iota(jnp.int32, (count, 1), 0) % columns
    key_col = lax.broadcasted_iota(jnp.int32, (1, cells), 1) % columns
    mix = attend(queries, keys, values, row_col == key_col)
    block_two = (one[own].astype(f32) + dot(mix, attn_ref[3])).astype(bf16)
    return block_two, layer_norm(block_two.astype(f32))


def fill(padded, all_rows, first, values):
    width = values.shape[1]
    padded[HALO : HALO + all_rows, first : first + width] = values


def fill_tiles(padded, my_lat, first, tiles):
    rows, cols = tiles[0].shape[:2]
    for s in range(len(tiles)):
        place = HALO + lax.rem(my_lat + s, len(tiles)) * rows
        padded[pl.ds(place, rows), first : first + cols] = tiles[s][...].astype(f32)


def clear(padded, all_rows):
    edge = jnp.zeros((HALO,) + padded.shape[1:], f32)
    padded[:HALO] = edge
    padded[HALO + all_rows :] = edge


def inner_kernel(nlat, *refs):
    tiles, refs = refs[:nlat], refs[nlat:]
    dw_ref, expand_ref, reduce_ref, attn_ref, two_ref, in_ref, padded, *scratch = refs
    rows, cols, channels = tiles[0].shape
    all_rows = rows * nlat
    columns = cols - 2 * SIDE
    clear(padded, all_rows)
    my_lat = lax.axis_index("lat")
    fill_tiles(padded, my_lat, 0, tiles)

    def slab(b, c):
        first = SIDE - HALO + b
        return padded[:, first : first + columns, c : c + LANES]

    center = padded[HALO : HALO + all_rows, SIDE : SIDE + columns]
    shape = (rows, all_rows, columns, channels)
    block_two, lon_in = chain(
        my_lat, slab, shape, dw_ref, expand_ref, reduce_ref, attn_ref, center, scratch
    )
    two_ref[...] = block_two
    in_ref[...] = lon_in.astype(bf16)


def outer_kernel(nlat, levels, *refs):
    tiles, refs = refs[:nlat], refs[nlat:]
    far_ref, near_ref, inner_in_ref, dw_ref, expand_ref, reduce_ref, attn_ref = refs[:7]
    two_ref, *refs = refs[7:]
    sent_refs, (sent, padded, *scratch) = refs[:levels], refs[levels:]
    rows, cols, channels = tiles[0].shape
    all_rows = rows * nlat
    columns = 2 * SIDE
    packed = (all_rows // 2, STRIP, channels)
    near = near_ref[...].astype(f32).reshape(packed)
    far = far_ref[...].astype(f32).reshape(packed)
    even = lax.axis_index("lon") % 2 == 0
    my_lat = lax.axis_index("lat")
    clear(padded, all_rows)
    fill(padded, all_rows, 0, unpack(jnp.where(even, far, near), True))
    fill_tiles(padded, my_lat, STRIP, tiles)
    fill(padded, all_rows, STRIP + cols, unpack(jnp.where(even, near, far), False))
    sublane = lax.broadcasted_iota(jnp.int32, (1, columns, 1), 1)

    def halves(shift, rows_of, c, width):
        right = STRIP + cols - SIDE + shift
        left = STRIP - SIDE + shift
        return jnp.where(
            sublane < SIDE,
            padded[rows_of, right : right + columns, c : c + width],
            padded[rows_of, left : left + columns, c : c + width],
        )

    def slab(b, c):
        return halves(b - HALO, slice(None), c, LANES)

    center = halves(0, slice(HALO, HALO + all_rows), 0, channels)
    shape = (rows, all_rows, columns, channels)
    block_two, lon_in = chain(
        my_lat, slab, shape, dw_ref, expand_ref, reduce_ref, attn_ref, center, scratch
    )
    two_ref[...] = block_two
    inner = inner_in_ref[...].astype(f32).reshape(rows, cols - columns, channels)
    outer = lon_in.reshape(rows, columns, channels)
    sent[...] = jnp.concatenate([inner, outer], axis=1).astype(bf16)
    some = rows // levels
    for k in range(levels):
        part = sent[pl.ds(peer(levels, k) * some, some)]
        sent_refs[k][...] = part.reshape(sent_refs[k].shape)


def circle_kernel(levels, some, *refs):
    attn_ref, mix_refs = refs[-levels - 1], refs[-levels:]
    parts = refs[: -levels - 1]
    count = parts[0].shape[0] // (some * levels)

    def latitude(part, r):
        starts = [(k * some + r) * count for k in range(levels)]
        return jnp.concatenate([part[start : start + count] for start in starts], axis=0)

    for r in range(some):
        own = latitude(parts[0], r)
        every = jnp.concatenate([own] + [latitude(part, r) for part in parts[1:]], axis=0)
        queries = dot(own, attn_ref[0]).astype(bf16)
        keys = dot(every, attn_ref[1]).astype(bf16)
        values = dot(every, attn_ref[2]).astype(bf16)
        mix = attend(queries, keys, values, None)
        for k in range(levels):
            mix_refs[k][r * count : (r + 1) * count] = mix[k * count : (k + 1) * count]


def last_kernel(levels, *refs):
    parts = refs[:levels]
    inner_ref, outer_ref, attn_ref, out_ref = refs[levels:]
    rows, cols, channels = out_ref.shape
    columns = 2 * SIDE
    some = rows // levels
    every = jnp.concatenate([part[...] for part in parts], axis=0)
    change = dot(every, attn_ref[3]).reshape(levels, some, cols, channels)
    for k in range(levels):
        start = peer(levels, k) * some

        def state(ref, width):
            count = some * width
            place = pl.ds(pl.multiple_of(start * width, count), count)
            return ref[place].astype(f32).reshape(some, width, channels)

        inner = state(inner_ref, cols - columns) + change[k, :, : cols - columns]
        outer = state(outer_ref, columns) + change[k, :, cols - columns :]
        total = jnp.concatenate([outer[:, SIDE:], inner, outer[:, :SIDE]], axis=1)
        out_ref[pl.ds(start, some)] = total.astype(bf16)


def call(
    kernel, outs, operands, scratch=(), any_space=False, flops=0, grant=VMEM_BYTES
):
    vmem = pl.BlockSpec(memory_space=pltpu.VMEM)
    given = pl.BlockSpec(memory_space=pl.ANY) if any_space else vmem
    shapes = [jax.ShapeDtypeStruct(shape, bf16) for shape in outs]
    moved = sum(x.size * x.dtype.itemsize for x in operands)
    result = pl.pallas_call(
        kernel,
        out_shape=shapes,
        in_specs=[given] * len(operands),
        out_specs=[vmem] * len(outs),
        scratch_shapes=list(scratch),
        compiler_params=pltpu.CompilerParams(vmem_limit_bytes=grant),
        cost_estimate=pl.CostEstimate(flops=flops, bytes_accessed=moved, transcendentals=0),
    )(*operands)
    return result


def shards(field, dw_weight, w_expand, w_reduce, lat_attn, lon_attn):
    rows, cols, channels = field.shape
    nlat, nlon = lax.axis_size("lat"), lax.axis_size("lon")
    levels = min(LEVELS, nlon)
    column = nlon // levels
    some = rows // levels
    all_rows = rows * nlat
    columns = 2 * SIDE

    def swap(piece, mask):
        return lax.ppermute(piece, "lon", [(j, j ^ mask) for j in range(nlon)])

    def exchange(pieces):
        moved = []
        for k in range(1, levels):
            level = levels - k
            moved.append(swap(pieces[k], level * column + level * 2 // levels))
        return [pieces[0]] + moved

    tiles = [field]
    for s in range(1, nlat):
        tiles.append(lax.ppermute(field, "lat", [((i + s) % nlat, i) for i in range(nlat)]))
    weights = (w_expand, w_reduce, lat_attn, lon_attn)
    staged = call(
        stage_kernel,
        [w.shape for w in weights],
        weights,
        [pltpu.SemaphoreType.DMA((len(weights), 4))],
        any_space=True,
        grant=STAGE_BYTES,
    )
    expand, reduce, lat_proj, lon_proj = staged

    strip = (all_rows * SIDE, channels)
    strip_scratch = pltpu.VMEM((all_rows, STRIP, channels), f32)
    near, far = call(
        functools.partial(strip_kernel, nlat),
        [strip, strip],
        [*tiles, reduce],
        [strip_scratch, strip_scratch],
    )
    far = lax.ppermute(
        far, "lon", [(j, (j - 1) % nlon if j % 2 == 0 else (j + 1) % nlon) for j in range(nlon)]
    )
    near = swap(near, 1)

    def scratch(width, count):
        return [
            pltpu.VMEM((all_rows + 2 * HALO, width, channels), f32),
            pltpu.VMEM(dw_weight.shape, f32),
            pltpu.VMEM((all_rows * count, channels), bf16),
            pltpu.VMEM((all_rows * count, channels), bf16),
        ]

    work = 4 * all_rows * columns * channels * w_expand.shape[1]
    inner_two, inner_in = call(
        functools.partial(inner_kernel, nlat),
        [(rows * (cols - columns), channels)] * 2,
        [*tiles, dw_weight, expand, reduce, lat_proj],
        scratch(cols, cols - columns),
        flops=work,
    )
    piece = (some * cols, channels)
    outer_two, *parts = call(
        functools.partial(outer_kernel, nlat, levels),
        [(rows * columns, channels)] + [piece] * levels,
        [*tiles, far, near, inner_in, dw_weight, expand, reduce, lat_proj],
        [pltpu.VMEM((rows, cols, channels), bf16)] + scratch(cols + 2 * STRIP, columns),
        flops=work,
    )

    parts = exchange(parts)
    circle = [jnp.concatenate(parts, axis=0)]
    mask = column // 2
    while mask:
        circle = circle + [swap(part, mask + mask // 2) for part in circle]
        mask //= 2
    mixes = call(
        functools.partial(circle_kernel, levels, some), [piece] * levels, [*circle, lon_proj]
    )
    mixes = exchange(mixes)
    (out,) = call(
        functools.partial(last_kernel, levels),
        [(rows, cols, channels)],
        [*mixes, inner_two, outer_two, lon_proj],
    )
    return out


def solution(mesh):
    return jax.shard_map(
        shards,
        mesh=mesh,
        in_specs=(P("lat", "lon", None), P(), P(), P(), P(), P()),
        out_specs=P("lat", "lon", None),
        check_vma=False,
    )
```

```python
import functools

import jax
import jax.numpy as jnp
from jax import lax
from jax.experimental import pallas as pl
from jax.experimental.pallas import tpu as pltpu
from jax.sharding import PartitionSpec as P

HEADS = 8
HALO = 3
TAPS = 2 * HALO + 1
STRIP = 8
SIDE = 4
LANES = 128
LEVELS = 4
STAGES = 4
EPSILON = 1e-06
VMEM_BYTES = 24 * 1024 * 1024
STAGE_BYTES = 103 * 512 * 1024
bf16, f32 = jnp.bfloat16, jnp.float32


def layer_norm(values):
    average = jnp.mean(values, axis=-1, keepdims=True)
    centered = values - average
    variance = jnp.mean(centered * centered, axis=-1, keepdims=True)
    return centered * lax.rsqrt(variance + EPSILON)


def dot(rows, matrix):
    return jnp.dot(rows, matrix, preferred_element_type=f32)


def dot_t(rows, matrix):
    return lax.dot_general(rows, matrix, (((1,), (1,)), ((), ())), preferred_element_type=f32)


def gelu(values):
    size = jnp.abs(values)
    t = 1.0 / (1.0 + (0.3275911 * 0.5**0.5) * size)
    tail = 1.061405429 * t - 1.453152027
    for coefficient in (1.421413741, -0.284496736, 0.254829592):
        tail = tail * t + coefficient
    tail = (0.5 * size * t) * tail * jnp.exp(-0.5 * values * values)
    return jnp.maximum(values, 0.0) - tail


def attend(queries, keys, values, mask):
    count, channels = queries.shape
    head_size = channels // HEADS
    lane_head = lax.broadcasted_iota(jnp.int32, (1, channels), 1) // head_size
    picks = [lane_head == h for h in range(HEADS)]
    none = jnp.zeros_like(queries)
    stacked = jnp.concatenate([jnp.where(pick, queries, none) for pick in picks], axis=0)
    scores = dot_t(stacked, keys) * head_size ** (-0.5)
    if mask is not None:
        scores = scores.reshape(HEADS, count, keys.shape[0])
        scores = jnp.where(mask[None], scores, -1e30).reshape(HEADS * count, keys.shape[0])
    top = jnp.max(scores, axis=-1, keepdims=True)
    probs = jnp.exp(scores - top)
    totals = jnp.sum(probs, axis=-1, keepdims=True)
    mixed = dot(probs.astype(bf16), values) * (1.0 / totals)
    out = mixed[:count]
    for h in range(1, HEADS):
        out = jnp.where(picks[h], mixed[h * count : (h + 1) * count], out)
    return out.astype(bf16)


def stage_kernel(count, *refs):
    sources, dw_ref = refs[:count], refs[count]
    targets, taps_ref, dw, sems = refs[count + 1 : 2 * count + 1], *refs[2 * count + 1 :]
    copies = [pltpu.make_async_copy(dw_ref, dw, sems.at[count, 0])]
    pieces = sems.shape[1]
    for i in range(count):
        source, target = sources[i], targets[i]
        size = source.shape[0] // pieces
        for k in range(pieces):
            part = pl.ds(k * size, size)
            copies.append(pltpu.make_async_copy(source.at[part], target.at[part], sems.at[i, k]))
    for copy in copies:
        copy.start()
    for copy in copies:
        copy.wait()
    taps_ref[...] = dw[...].astype(f32)


def peer(levels, k):
    level = lax.axis_index("lon") // (lax.axis_size("lon") // levels)
    return level ^ ((levels - k) % levels)


def strip_kernel(nlat, *refs):
    tiles = refs[:nlat]
    near_ref, far_ref, near, far = refs[nlat + 1 :]
    rows, cols, channels = tiles[0].shape
    even = lax.axis_index("lon") % 2 == 0
    for s in range(nlat):
        values = tiles[s][...].astype(f32)
        first, last = values[:, :STRIP], values[:, cols - STRIP :]
        where = pl.ds(lax.rem(lax.axis_index("lat") + s, nlat) * rows, rows)
        near[where] = jnp.where(even, last, first)
        far[where] = jnp.where(even, first, last)
    for strip, strip_ref, is_last in ((near, near_ref, even), (far, far_ref, ~even)):
        strip_ref[...] = pack(strip[...], is_last).reshape(strip_ref.shape).astype(bf16)


def lower_half():
    return lax.broadcasted_iota(jnp.int32, (1, STRIP, 1), 1) < SIDE


def turn(values):
    return jnp.concatenate([values[:, SIDE:], values[:, :SIDE]], axis=1)


def pack(strip, is_last):
    half = strip.shape[0] // 2
    turned = turn(strip)
    low = jnp.where(is_last, turned, strip)
    high = jnp.where(is_last, strip, turned)
    return jnp.where(lower_half(), low[:half], high[half:])


def unpack(packed, is_left):
    turned = turn(packed)
    low = jnp.where(is_left, turned, packed)
    high = jnp.where(is_left, packed, turned)
    return jnp.concatenate([low, high], axis=0)


def chain(my_lat, slab, shape, taps_ref, expand_ref, reduce_ref, attn_ref, center, scratch):
    one, lat_in = scratch
    rows, all_rows, columns, channels = shape
    cells = all_rows * columns
    parts = []
    for c in range(0, channels, LANES):
        acc = jnp.zeros((all_rows, columns, LANES), f32)
        for b in range(TAPS):
            block = slab(b, c)
            for a in range(TAPS):
                tap = taps_ref[a, b : b + 1, c : c + LANES].reshape(1, 1, LANES)
                acc = acc + block[a : a + all_rows] * tap
        parts.append(acc.reshape(cells, LANES))
    normed = layer_norm(jnp.concatenate(parts, axis=-1)).astype(bf16)

    def widen(k, total):
        part = slice(k * channels, (k + 1) * channels)
        wide = gelu(dot(normed, expand_ref[:, part])).astype(bf16)
        return total + dot(wide, reduce_ref[part])

    total = center.reshape(cells, channels)
    for k in range(expand_ref.shape[1] // channels):
        total = widen(k, total)
    block_one = total.astype(bf16)
    one[...] = block_one
    every = layer_norm(block_one.astype(f32)).astype(bf16)
    lat_in[...] = every
    count = rows * columns
    own = pl.ds(pl.multiple_of(my_lat * count, count), count)
    queries = dot(lat_in[own], attn_ref[0]).astype(bf16)
    keys = dot(every, attn_ref[1]).astype(bf16)
    values = dot(every, attn_ref[2]).astype(bf16)
    row_col = lax.broadcasted_iota(jnp.int32, (count, 1), 0) % columns
    key_col = lax.broadcasted_iota(jnp.int32, (1, cells), 1) % columns
    mix = attend(queries, keys, values, row_col == key_col)
    block_two = (one[own].astype(f32) + dot(mix, attn_ref[3])).astype(bf16)
    return block_two, layer_norm(block_two.astype(f32))


def fill(padded, all_rows, first, values):
    width = values.shape[1]
    padded[HALO : HALO + all_rows, first : first + width] = values


def fill_tiles(padded, my_lat, first, tiles):
    rows, cols = tiles[0].shape[:2]
    for s in range(len(tiles)):
        place = HALO + lax.rem(my_lat + s, len(tiles)) * rows
        padded[pl.ds(place, rows), first : first + cols] = tiles[s][...].astype(f32)


def clear(padded, all_rows):
    edge = jnp.zeros((HALO,) + padded.shape[1:], f32)
    padded[:HALO] = edge
    padded[HALO + all_rows :] = edge


def inner_kernel(nlat, *refs):
    tiles, refs = refs[:nlat], refs[nlat:]
    taps_ref, expand_ref, reduce_ref, attn_ref, two_ref, in_ref, padded, *scratch = refs
    rows, cols, channels = tiles[0].shape
    all_rows = rows * nlat
    columns = cols - 2 * SIDE
    clear(padded, all_rows)
    my_lat = lax.axis_index("lat")
    fill_tiles(padded, my_lat, 0, tiles)

    def slab(b, c):
        first = SIDE - HALO + b
        return padded[:, first : first + columns, c : c + LANES]

    center = padded[HALO : HALO + all_rows, SIDE : SIDE + columns]
    shape = (rows, all_rows, columns, channels)
    block_two, lon_in = chain(
        my_lat, slab, shape, taps_ref, expand_ref, reduce_ref, attn_ref, center, scratch
    )
    two_ref[...] = block_two
    in_ref[...] = lon_in.astype(bf16)


def outer_kernel(nlat, levels, *refs):
    tiles, refs = refs[:nlat], refs[nlat:]
    far_ref, near_ref, inner_in_ref, taps_ref, expand_ref, reduce_ref, attn_ref = refs[:7]
    two_ref, *refs = refs[7:]
    sent_refs, (sent, padded, *scratch) = refs[:levels], refs[levels:]
    rows, cols, channels = tiles[0].shape
    all_rows = rows * nlat
    columns = 2 * SIDE
    packed = (all_rows // 2, STRIP, channels)
    near = near_ref[...].astype(f32).reshape(packed)
    far = far_ref[...].astype(f32).reshape(packed)
    even = lax.axis_index("lon") % 2 == 0
    my_lat = lax.axis_index("lat")
    clear(padded, all_rows)
    fill(padded, all_rows, 0, unpack(jnp.where(even, far, near), True))
    fill_tiles(padded, my_lat, STRIP, tiles)
    fill(padded, all_rows, STRIP + cols, unpack(jnp.where(even, near, far), False))
    sublane = lax.broadcasted_iota(jnp.int32, (1, columns, 1), 1)

    def halves(shift, rows_of, c, width):
        right = STRIP + cols - SIDE + shift
        left = STRIP - SIDE + shift
        return jnp.where(
            sublane < SIDE,
            padded[rows_of, right : right + columns, c : c + width],
            padded[rows_of, left : left + columns, c : c + width],
        )

    def slab(b, c):
        return halves(b - HALO, slice(None), c, LANES)

    center = halves(0, slice(HALO, HALO + all_rows), 0, channels)
    shape = (rows, all_rows, columns, channels)
    block_two, lon_in = chain(
        my_lat, slab, shape, taps_ref, expand_ref, reduce_ref, attn_ref, center, scratch
    )
    two_ref[...] = block_two
    inner = inner_in_ref[...].astype(f32).reshape(rows, cols - columns, channels)
    outer = lon_in.reshape(rows, columns, channels)
    sent[...] = jnp.concatenate([inner, outer], axis=1).astype(bf16)
    some = rows // levels
    for k in range(levels):
        part = sent[pl.ds(peer(levels, k) * some, some)]
        sent_refs[k][...] = part.reshape(sent_refs[k].shape)


def circle_kernel(levels, some, *refs):
    attn_ref, mix_refs = refs[-levels - 1], refs[-levels:]
    parts = refs[: -levels - 1]
    count = parts[0].shape[0] // (some * levels)

    def latitude(part, r):
        starts = [(k * some + r) * count for k in range(levels)]
        return jnp.concatenate([part[start : start + count] for start in starts], axis=0)

    for r in range(some):
        own = latitude(parts[0], r)
        every = jnp.concatenate([own] + [latitude(part, r) for part in parts[1:]], axis=0)
        queries = dot(own, attn_ref[0]).astype(bf16)
        keys = dot(every, attn_ref[1]).astype(bf16)
        values = dot(every, attn_ref[2]).astype(bf16)
        mix = attend(queries, keys, values, None)
        for k in range(levels):
            mix_refs[k][r * count : (r + 1) * count] = mix[k * count : (k + 1) * count]


def last_kernel(levels, *refs):
    parts = refs[:levels]
    inner_ref, outer_ref, attn_ref, out_ref = refs[levels:]
    rows, cols, channels = out_ref.shape
    columns = 2 * SIDE
    some = rows // levels
    every = jnp.concatenate([part[...] for part in parts], axis=0)
    change = dot(every, attn_ref[3]).reshape(levels, some, cols, channels)
    for k in range(levels):
        start = peer(levels, k) * some

        def state(ref, width):
            count = some * width
            place = pl.ds(pl.multiple_of(start * width, count), count)
            return ref[place].astype(f32).reshape(some, width, channels)

        inner = state(inner_ref, cols - columns) + change[k, :, : cols - columns]
        outer = state(outer_ref, columns) + change[k, :, cols - columns :]
        total = jnp.concatenate([outer[:, SIDE:], inner, outer[:, :SIDE]], axis=1)
        out_ref[pl.ds(start, some)] = total.astype(bf16)


def call(
    kernel, outs, operands, scratch=(), any_space=False, flops=0, grant=VMEM_BYTES
):
    vmem = pl.BlockSpec(memory_space=pltpu.VMEM)
    given = pl.BlockSpec(memory_space=pl.ANY) if any_space else vmem
    shapes = [
        out if isinstance(out, jax.ShapeDtypeStruct) else jax.ShapeDtypeStruct(out, bf16)
        for out in outs
    ]
    moved = sum(x.size * x.dtype.itemsize for x in operands)
    result = pl.pallas_call(
        kernel,
        out_shape=shapes,
        in_specs=[given] * len(operands),
        out_specs=[vmem] * len(outs),
        scratch_shapes=list(scratch),
        compiler_params=pltpu.CompilerParams(vmem_limit_bytes=grant),
        cost_estimate=pl.CostEstimate(flops=flops, bytes_accessed=moved, transcendentals=0),
    )(*operands)
    return result


def shards(field, dw_weight, w_expand, w_reduce, lat_attn, lon_attn):
    rows, cols, channels = field.shape
    nlat, nlon = lax.axis_size("lat"), lax.axis_size("lon")
    levels = min(LEVELS, nlon)
    column = nlon // levels
    some = rows // levels
    all_rows = rows * nlat
    columns = 2 * SIDE

    def swap(piece, mask):
        return lax.ppermute(piece, "lon", [(j, j ^ mask) for j in range(nlon)])

    def exchange(pieces):
        moved = []
        for k in range(1, levels):
            level = levels - k
            cross = (level ^ (level >> 1)) & 1 if column > 1 else 0
            moved.append(swap(pieces[k], level * column + cross))
        return [pieces[0]] + moved

    tiles = [field]
    for s in range(1, nlat):
        tiles.append(lax.ppermute(field, "lat", [((i + s) % nlat, i) for i in range(nlat)]))
    weights = (w_expand, w_reduce, lat_attn, lon_attn)
    expand, reduce, lat_proj, lon_proj, taps = call(
        functools.partial(stage_kernel, len(weights)),
        [w.shape for w in weights] + [jax.ShapeDtypeStruct(dw_weight.shape, f32)],
        [*weights, dw_weight],
        [
            pltpu.VMEM(dw_weight.shape, bf16),
            pltpu.SemaphoreType.DMA((len(weights) + 1, STAGES)),
        ],
        any_space=True,
        grant=STAGE_BYTES,
    )

    strip = (all_rows * SIDE, channels)
    strip_scratch = pltpu.VMEM((all_rows, STRIP, channels), f32)
    near, far = call(
        functools.partial(strip_kernel, nlat),
        [strip, strip],
        [*tiles, reduce],
        [strip_scratch, strip_scratch],
    )
    far = lax.ppermute(
        far, "lon", [(j, (j - 1) % nlon if j % 2 == 0 else (j + 1) % nlon) for j in range(nlon)]
    )
    near = swap(near, 1)

    def scratch(width, count):
        return [
            pltpu.VMEM((all_rows + 2 * HALO, width, channels), f32),
            pltpu.VMEM((all_rows * count, channels), bf16),
            pltpu.VMEM((all_rows * count, channels), bf16),
        ]

    work = 4 * all_rows * columns * channels * w_expand.shape[1]
    inner_two, inner_in = call(
        functools.partial(inner_kernel, nlat),
        [(rows * (cols - columns), channels)] * 2,
        [*tiles, taps, expand, reduce, lat_proj],
        scratch(cols, cols - columns),
        flops=work,
    )
    piece = (some * cols, channels)
    outer_two, *parts = call(
        functools.partial(outer_kernel, nlat, levels),
        [(rows * columns, channels)] + [piece] * levels,
        [*tiles, far, near, inner_in, taps, expand, reduce, lat_proj],
        [pltpu.VMEM((rows, cols, channels), bf16)] + scratch(cols + 2 * STRIP, columns),
        flops=work,
    )

    parts = exchange(parts)
    circle = [jnp.concatenate(parts, axis=0)]
    mask = column // 2
    while mask:
        circle = circle + [swap(part, mask + mask // 2) for part in circle]
        mask //= 2
    mixes = call(
        functools.partial(circle_kernel, levels, some), [piece] * levels, [*circle, lon_proj]
    )
    mixes = exchange(mixes)
    (out,) = call(
        functools.partial(last_kernel, levels),
        [(rows, cols, channels)],
        [*mixes, inner_two, outer_two, lon_proj],
    )
    return out


def solution(mesh):
    return jax.shard_map(
        shards,
        mesh=mesh,
        in_specs=(P("lat", "lon", None), P(), P(), P(), P(), P()),
        out_specs=P("lat", "lon", None),
        check_vma=False,
    )
```

```python
import functools

import jax
import jax.numpy as jnp
from jax import lax
from jax.experimental import pallas as pl
from jax.experimental.pallas import tpu as pltpu
from jax.sharding import PartitionSpec as P

HEADS = 8
HALO = 3
TAPS = 2 * HALO + 1
STRIP = 8
SIDE = 4
LANES = 128
LEVELS = 4
HALVES = 2
STAGES = 4
EPSILON = 1e-06
VMEM_BYTES = 24 * 1024 * 1024
STAGE_BYTES = 103 * 512 * 1024
bf16, f32 = jnp.bfloat16, jnp.float32


def layer_norm(values):
    average = jnp.mean(values, axis=-1, keepdims=True)
    centered = values - average
    variance = jnp.mean(centered * centered, axis=-1, keepdims=True)
    return centered * lax.rsqrt(variance + EPSILON)


def dot(rows, matrix):
    return jnp.dot(rows, matrix, preferred_element_type=f32)


def dot_t(rows, matrix):
    return lax.dot_general(rows, matrix, (((1,), (1,)), ((), ())), preferred_element_type=f32)


def gelu(values):
    size = jnp.abs(values)
    t = 1.0 / (1.0 + (0.3275911 * 0.5**0.5) * size)
    tail = 1.061405429 * t - 1.453152027
    for coefficient in (1.421413741, -0.284496736, 0.254829592):
        tail = tail * t + coefficient
    tail = (0.5 * size * t) * tail * jnp.exp(-0.5 * values * values)
    return jnp.maximum(values, 0.0) - tail


def attend(queries, keys, values, mask):
    count, channels = queries.shape
    head_size = channels // HEADS
    lane_head = lax.broadcasted_iota(jnp.int32, (1, channels), 1) // head_size
    picks = [lane_head == h for h in range(HEADS)]
    none = jnp.zeros_like(queries)
    stacked = jnp.concatenate([jnp.where(pick, queries, none) for pick in picks], axis=0)
    scores = dot_t(stacked, keys) * head_size ** (-0.5)
    if mask is not None:
        scores = scores.reshape(HEADS, count, keys.shape[0])
        scores = jnp.where(mask[None], scores, -1e30).reshape(HEADS * count, keys.shape[0])
    top = jnp.max(scores, axis=-1, keepdims=True)
    probs = jnp.exp(scores - top)
    totals = jnp.sum(probs, axis=-1, keepdims=True)
    mixed = dot(probs.astype(bf16), values) * (1.0 / totals)
    out = mixed[:count]
    for h in range(1, HEADS):
        out = jnp.where(picks[h], mixed[h * count : (h + 1) * count], out)
    return out.astype(bf16)


def stage_kernel(count, *refs):
    sources, dw_ref = refs[:count], refs[count]
    targets, taps_ref, dw, sems = refs[count + 1 : 2 * count + 1], *refs[2 * count + 1 :]
    copies = [pltpu.make_async_copy(dw_ref, dw, sems.at[count, 0])]
    pieces = sems.shape[1]
    for i in range(count):
        source, target = sources[i], targets[i]
        size = source.shape[0] // pieces
        for k in range(pieces):
            part = pl.ds(k * size, size)
            copies.append(pltpu.make_async_copy(source.at[part], target.at[part], sems.at[i, k]))
    for copy in copies:
        copy.start()
    for copy in copies:
        copy.wait()
    taps_ref[...] = dw[...].astype(f32)


def peer(levels, k):
    level = lax.axis_index("lon") // (lax.axis_size("lon") // levels)
    return level ^ ((levels - k) % levels)


def strip_kernel(nlat, *refs):
    tiles = refs[:nlat]
    near_ref, far_ref, near, far = refs[nlat + 1 :]
    rows, cols, channels = tiles[0].shape
    even = lax.axis_index("lon") % 2 == 0
    for s in range(nlat):
        values = tiles[s][...].astype(f32)
        first, last = values[:, :STRIP], values[:, cols - STRIP :]
        where = pl.ds(lax.rem(lax.axis_index("lat") + s, nlat) * rows, rows)
        near[where] = jnp.where(even, last, first)
        far[where] = jnp.where(even, first, last)
    for strip, strip_ref, is_last in ((near, near_ref, even), (far, far_ref, ~even)):
        strip_ref[...] = pack(strip[...], is_last).reshape(strip_ref.shape).astype(bf16)


def lower_half():
    return lax.broadcasted_iota(jnp.int32, (1, STRIP, 1), 1) < SIDE


def turn(values):
    return jnp.concatenate([values[:, SIDE:], values[:, :SIDE]], axis=1)


def pack(strip, is_last):
    half = strip.shape[0] // 2
    turned = turn(strip)
    low = jnp.where(is_last, turned, strip)
    high = jnp.where(is_last, strip, turned)
    return jnp.where(lower_half(), low[:half], high[half:])


def unpack(packed, is_left):
    turned = turn(packed)
    low = jnp.where(is_left, turned, packed)
    high = jnp.where(is_left, packed, turned)
    return jnp.concatenate([low, high], axis=0)


def chain(my_lat, slab, shape, taps_ref, expand_ref, reduce_ref, attn_ref, center, scratch):
    one, lat_in = scratch
    rows, all_rows, columns, channels = shape
    cells = all_rows * columns
    half = all_rows // HALVES

    def convolve(start):
        parts = []
        for c in range(0, channels, LANES):
            acc = jnp.zeros((half, columns, LANES), f32)
            for b in range(TAPS):
                block = slab(start, half + 2 * HALO, b, c)
                for a in range(TAPS):
                    tap = taps_ref[a, b : b + 1, c : c + LANES].reshape(1, 1, LANES)
                    acc = acc + block[a : a + half] * tap
            parts.append(acc.reshape(half * columns, LANES))
        return layer_norm(jnp.concatenate(parts, axis=-1)).astype(bf16)

    def widen(normed, total):
        for k in range(0, expand_ref.shape[1], channels):
            part = slice(k, k + channels)
            wide = gelu(dot(normed, expand_ref[:, part])).astype(bf16)
            total = total + dot(wide, reduce_ref[part])
        return total

    blocks = []
    for start in range(0, all_rows, half):
        total = widen(convolve(start), center(start, half).reshape(half * columns, channels))
        block_one = total.astype(bf16)
        place = slice(start * columns, (start + half) * columns)
        one[place] = block_one
        blocks.append(layer_norm(block_one.astype(f32)).astype(bf16))
        lat_in[place] = blocks[-1]
    every = jnp.concatenate(blocks, axis=0)
    count = rows * columns
    own = pl.ds(pl.multiple_of(my_lat * count, count), count)
    queries = dot(lat_in[own], attn_ref[0]).astype(bf16)
    keys = dot(every, attn_ref[1]).astype(bf16)
    values = dot(every, attn_ref[2]).astype(bf16)
    row_col = lax.broadcasted_iota(jnp.int32, (count, 1), 0) % columns
    key_col = lax.broadcasted_iota(jnp.int32, (1, cells), 1) % columns
    mix = attend(queries, keys, values, row_col == key_col)
    block_two = (one[own].astype(f32) + dot(mix, attn_ref[3])).astype(bf16)
    return block_two, layer_norm(block_two.astype(f32))


def fill(padded, all_rows, first, values):
    width = values.shape[1]
    padded[HALO : HALO + all_rows, first : first + width] = values


def fill_tiles(padded, my_lat, first, tiles):
    rows, cols = tiles[0].shape[:2]
    for s in range(len(tiles)):
        place = HALO + lax.rem(my_lat + s, len(tiles)) * rows
        padded[pl.ds(place, rows), first : first + cols] = tiles[s][...].astype(f32)


def clear(padded, all_rows):
    edge = jnp.zeros((HALO,) + padded.shape[1:], f32)
    padded[:HALO] = edge
    padded[HALO + all_rows :] = edge


def inner_kernel(nlat, *refs):
    tiles, refs = refs[:nlat], refs[nlat:]
    taps_ref, expand_ref, reduce_ref, attn_ref, two_ref, in_ref, padded, *scratch = refs
    rows, cols, channels = tiles[0].shape
    all_rows = rows * nlat
    columns = cols - 2 * SIDE
    clear(padded, all_rows)
    my_lat = lax.axis_index("lat")
    fill_tiles(padded, my_lat, 0, tiles)

    def slab(start, size, b, c):
        first = SIDE - HALO + b
        return padded[start : start + size, first : first + columns, c : c + LANES]

    def center(start, size):
        return padded[HALO + start : HALO + start + size, SIDE : SIDE + columns]

    shape = (rows, all_rows, columns, channels)
    block_two, lon_in = chain(
        my_lat, slab, shape, taps_ref, expand_ref, reduce_ref, attn_ref, center, scratch
    )
    two_ref[...] = block_two
    in_ref[...] = lon_in.astype(bf16)


def outer_kernel(nlat, levels, *refs):
    tiles, refs = refs[:nlat], refs[nlat:]
    far_ref, near_ref, inner_in_ref, taps_ref, expand_ref, reduce_ref, attn_ref = refs[:7]
    two_ref, *refs = refs[7:]
    sent_refs, (sent, padded, *scratch) = refs[:levels], refs[levels:]
    rows, cols, channels = tiles[0].shape
    all_rows = rows * nlat
    columns = 2 * SIDE
    packed = (all_rows // 2, STRIP, channels)
    near = near_ref[...].astype(f32).reshape(packed)
    far = far_ref[...].astype(f32).reshape(packed)
    even = lax.axis_index("lon") % 2 == 0
    my_lat = lax.axis_index("lat")
    clear(padded, all_rows)
    fill(padded, all_rows, 0, unpack(jnp.where(even, far, near), True))
    fill_tiles(padded, my_lat, STRIP, tiles)
    fill(padded, all_rows, STRIP + cols, unpack(jnp.where(even, near, far), False))
    sublane = lax.broadcasted_iota(jnp.int32, (1, columns, 1), 1)

    def halves(shift, rows_of, c, width):
        right = STRIP + cols - SIDE + shift
        left = STRIP - SIDE + shift
        return jnp.where(
            sublane < SIDE,
            padded[rows_of, right : right + columns, c : c + width],
            padded[rows_of, left : left + columns, c : c + width],
        )

    def slab(start, size, b, c):
        return halves(b - HALO, slice(start, start + size), c, LANES)

    def center(start, size):
        return halves(0, slice(HALO + start, HALO + start + size), 0, channels)

    shape = (rows, all_rows, columns, channels)
    block_two, lon_in = chain(
        my_lat, slab, shape, taps_ref, expand_ref, reduce_ref, attn_ref, center, scratch
    )
    two_ref[...] = block_two
    inner = inner_in_ref[...].astype(f32).reshape(rows, cols - columns, channels)
    outer = lon_in.reshape(rows, columns, channels)
    sent[...] = jnp.concatenate([inner, outer], axis=1).astype(bf16)
    some = rows // levels
    for k in range(levels):
        part = sent[pl.ds(peer(levels, k) * some, some)]
        sent_refs[k][...] = part.reshape(sent_refs[k].shape)


def circle_kernel(levels, some, *refs):
    attn_ref, mix_refs = refs[-levels - 1], refs[-levels:]
    parts = refs[: -levels - 1]
    count = parts[0].shape[0] // (some * levels)

    def latitude(part, r):
        starts = [(k * some + r) * count for k in range(levels)]
        return jnp.concatenate([part[start : start + count] for start in starts], axis=0)

    for r in range(some):
        own = latitude(parts[0], r)
        every = jnp.concatenate([own] + [latitude(part, r) for part in parts[1:]], axis=0)
        queries = dot(own, attn_ref[0]).astype(bf16)
        keys = dot(every, attn_ref[1]).astype(bf16)
        values = dot(every, attn_ref[2]).astype(bf16)
        mix = attend(queries, keys, values, None)
        for k in range(levels):
            mix_refs[k][r * count : (r + 1) * count] = mix[k * count : (k + 1) * count]


def last_kernel(levels, *refs):
    parts = refs[:levels]
    inner_ref, outer_ref, attn_ref, out_ref = refs[levels:]
    rows, cols, channels = out_ref.shape
    columns = 2 * SIDE
    some = rows // levels
    every = jnp.concatenate([part[...] for part in parts], axis=0)
    change = dot(every, attn_ref[3]).reshape(levels, some, cols, channels)
    for k in range(levels):
        start = peer(levels, k) * some

        def state(ref, width):
            count = some * width
            place = pl.ds(pl.multiple_of(start * width, count), count)
            return ref[place].astype(f32).reshape(some, width, channels)

        inner = state(inner_ref, cols - columns) + change[k, :, : cols - columns]
        outer = state(outer_ref, columns) + change[k, :, cols - columns :]
        total = jnp.concatenate([outer[:, SIDE:], inner, outer[:, :SIDE]], axis=1)
        out_ref[pl.ds(start, some)] = total.astype(bf16)


def call(
    kernel, outs, operands, scratch=(), any_space=False, flops=0, grant=VMEM_BYTES
):
    vmem = pl.BlockSpec(memory_space=pltpu.VMEM)
    given = pl.BlockSpec(memory_space=pl.ANY) if any_space else vmem
    shapes = [
        out if isinstance(out, jax.ShapeDtypeStruct) else jax.ShapeDtypeStruct(out, bf16)
        for out in outs
    ]
    moved = sum(x.size * x.dtype.itemsize for x in operands)
    result = pl.pallas_call(
        kernel,
        out_shape=shapes,
        in_specs=[given] * len(operands),
        out_specs=[vmem] * len(outs),
        scratch_shapes=list(scratch),
        compiler_params=pltpu.CompilerParams(vmem_limit_bytes=grant),
        cost_estimate=pl.CostEstimate(flops=flops, bytes_accessed=moved, transcendentals=0),
    )(*operands)
    return result


def shards(field, dw_weight, w_expand, w_reduce, lat_attn, lon_attn):
    rows, cols, channels = field.shape
    nlat, nlon = lax.axis_size("lat"), lax.axis_size("lon")
    levels = min(LEVELS, nlon)
    column = nlon // levels
    some = rows // levels
    all_rows = rows * nlat
    columns = 2 * SIDE

    def swap(piece, mask):
        return lax.ppermute(piece, "lon", [(j, j ^ mask) for j in range(nlon)])

    def exchange(pieces):
        moved = []
        for k in range(1, levels):
            level = levels - k
            cross = (level ^ (level >> 1)) & 1 if column > 1 else 0
            moved.append(swap(pieces[k], level * column + cross))
        return [pieces[0]] + moved

    tiles = [field]
    for s in range(1, nlat):
        tiles.append(lax.ppermute(field, "lat", [((i + s) % nlat, i) for i in range(nlat)]))
    weights = (w_expand, w_reduce, lat_attn, lon_attn)
    expand, reduce, lat_proj, lon_proj, taps = call(
        functools.partial(stage_kernel, len(weights)),
        [w.shape for w in weights] + [jax.ShapeDtypeStruct(dw_weight.shape, f32)],
        [*weights, dw_weight],
        [
            pltpu.VMEM(dw_weight.shape, bf16),
            pltpu.SemaphoreType.DMA((len(weights) + 1, STAGES)),
        ],
        any_space=True,
        grant=STAGE_BYTES,
    )

    strip = (all_rows * SIDE, channels)
    strip_scratch = pltpu.VMEM((all_rows, STRIP, channels), f32)
    near, far = call(
        functools.partial(strip_kernel, nlat),
        [strip, strip],
        [*tiles, reduce],
        [strip_scratch, strip_scratch],
    )
    far = lax.ppermute(
        far, "lon", [(j, (j - 1) % nlon if j % 2 == 0 else (j + 1) % nlon) for j in range(nlon)]
    )
    near = swap(near, 1)

    def scratch(width, count):
        return [
            pltpu.VMEM((all_rows + 2 * HALO, width, channels), f32),
            pltpu.VMEM((all_rows * count, channels), bf16),
            pltpu.VMEM((all_rows * count, channels), bf16),
        ]

    work = 4 * all_rows * columns * channels * w_expand.shape[1]
    inner_two, inner_in = call(
        functools.partial(inner_kernel, nlat),
        [(rows * (cols - columns), channels)] * 2,
        [*tiles, taps, expand, reduce, lat_proj],
        scratch(cols, cols - columns),
        flops=work,
    )
    piece = (some * cols, channels)
    outer_two, *parts = call(
        functools.partial(outer_kernel, nlat, levels),
        [(rows * columns, channels)] + [piece] * levels,
        [*tiles, far, near, inner_in, taps, expand, reduce, lat_proj],
        [pltpu.VMEM((rows, cols, channels), bf16)] + scratch(cols + 2 * STRIP, columns),
        flops=work,
    )

    parts = exchange(parts)
    circle = [jnp.concatenate(parts, axis=0)]
    mask = column // 2
    while mask:
        circle = circle + [swap(part, mask + mask // 2) for part in circle]
        mask //= 2
    mixes = call(
        functools.partial(circle_kernel, levels, some), [piece] * levels, [*circle, lon_proj]
    )
    mixes = exchange(mixes)
    (out,) = call(
        functools.partial(last_kernel, levels),
        [(rows, cols, channels)],
        [*mixes, inner_two, outer_two, lon_proj],
    )
    return out


def solution(mesh):
    return jax.shard_map(
        shards,
        mesh=mesh,
        in_specs=(P("lat", "lon", None), P(), P(), P(), P(), P()),
        out_specs=P("lat", "lon", None),
        check_vma=False,
    )
```

```python
import functools

import jax
import jax.numpy as jnp
from jax import lax
from jax.experimental import pallas as pl
from jax.experimental.pallas import tpu as pltpu
from jax.sharding import PartitionSpec as P

HEADS = 8
HALO = 3
TAPS = 2 * HALO + 1
STRIP = 8
SIDE = 4
LANES = 128
LEVELS = 4
STAGES = 4
EPSILON = 1e-06
VMEM_BYTES = 24 * 1024 * 1024
STAGE_BYTES = 103 * 512 * 1024
bf16, f32 = jnp.bfloat16, jnp.float32


def layer_norm(values):
    average = jnp.mean(values, axis=-1, keepdims=True)
    centered = values - average
    variance = jnp.mean(centered * centered, axis=-1, keepdims=True)
    return centered * lax.rsqrt(variance + EPSILON)


def dot(rows, matrix):
    return jnp.dot(rows, matrix, preferred_element_type=f32)


def dot_t(rows, matrix):
    return lax.dot_general(rows, matrix, (((1,), (1,)), ((), ())), preferred_element_type=f32)


def gelu(values):
    size = jnp.abs(values)
    t = 1.0 / (1.0 + (0.3275911 * 0.5**0.5) * size)
    tail = 1.061405429 * t - 1.453152027
    for coefficient in (1.421413741, -0.284496736, 0.254829592):
        tail = tail * t + coefficient
    tail = (0.5 * size * t) * tail * jnp.exp(-0.5 * values * values)
    return jnp.maximum(values, 0.0) - tail


def attend(queries, keys, values, mask):
    count, channels = queries.shape
    head_size = channels // HEADS
    lane_head = lax.broadcasted_iota(jnp.int32, (1, channels), 1) // head_size
    picks = [lane_head == h for h in range(HEADS)]
    none = jnp.zeros_like(queries)
    stacked = jnp.concatenate([jnp.where(pick, queries, none) for pick in picks], axis=0)
    scores = dot_t(stacked, keys) * head_size ** (-0.5)
    if mask is not None:
        scores = scores.reshape(HEADS, count, keys.shape[0])
        scores = jnp.where(mask[None], scores, -1e30).reshape(HEADS * count, keys.shape[0])
    top = jnp.max(scores, axis=-1, keepdims=True)
    probs = jnp.exp(scores - top)
    totals = jnp.sum(probs, axis=-1, keepdims=True)
    mixed = dot(probs.astype(bf16), values) * (1.0 / totals)
    out = mixed[:count]
    for h in range(1, HEADS):
        out = jnp.where(picks[h], mixed[h * count : (h + 1) * count], out)
    return out.astype(bf16)


def stage_kernel(count, *refs):
    sources, dw_ref = refs[:count], refs[count]
    targets, taps_ref, dw, sems = refs[count + 1 : 2 * count + 1], *refs[2 * count + 1 :]
    copies = [pltpu.make_async_copy(dw_ref, dw, sems.at[count, 0])]
    pieces = sems.shape[1]
    for i in range(count):
        source, target = sources[i], targets[i]
        size = source.shape[0] // pieces
        for k in range(pieces):
            part = pl.ds(k * size, size)
            copies.append(pltpu.make_async_copy(source.at[part], target.at[part], sems.at[i, k]))
    for copy in copies:
        copy.start()
    for copy in copies:
        copy.wait()
    taps_ref[...] = dw[...].astype(f32)


def peer(levels, k):
    level = lax.axis_index("lon") // (lax.axis_size("lon") // levels)
    return level ^ ((levels - k) % levels)


def strip_kernel(nlat, *refs):
    tiles = refs[:nlat]
    near_ref, far_ref, near, far = refs[nlat + 1 :]
    rows, cols, channels = tiles[0].shape
    even = lax.axis_index("lon") % 2 == 0
    for s in range(nlat):
        values = tiles[s][...].astype(f32)
        first, last = values[:, :STRIP], values[:, cols - STRIP :]
        where = pl.ds(lax.rem(lax.axis_index("lat") + s, nlat) * rows, rows)
        near[where] = jnp.where(even, last, first)
        far[where] = jnp.where(even, first, last)
    for strip, strip_ref, is_last in ((near, near_ref, even), (far, far_ref, ~even)):
        strip_ref[...] = pack(strip[...], is_last).reshape(strip_ref.shape).astype(bf16)


def lower_half():
    return lax.broadcasted_iota(jnp.int32, (1, STRIP, 1), 1) < SIDE


def turn(values):
    return jnp.concatenate([values[:, SIDE:], values[:, :SIDE]], axis=1)


def pack(strip, is_last):
    half = strip.shape[0] // 2
    turned = turn(strip)
    low = jnp.where(is_last, turned, strip)
    high = jnp.where(is_last, strip, turned)
    return jnp.where(lower_half(), low[:half], high[half:])


def unpack(packed, is_left):
    turned = turn(packed)
    low = jnp.where(is_left, turned, packed)
    high = jnp.where(is_left, packed, turned)
    return jnp.concatenate([low, high], axis=0)


def chain(my_lat, slab, shape, taps_ref, expand_ref, reduce_ref, attn_ref, center, scratch):
    one, lat_in, conv = scratch
    rows, all_rows, columns, channels = shape
    cells = all_rows * columns

    def convolve(i, carry):
        place = pl.ds(pl.multiple_of(i * LANES, LANES), LANES)
        acc = jnp.zeros((all_rows, columns, LANES), f32)
        for b in range(TAPS):
            block = slab(b, place)
            for a in range(TAPS):
                tap = taps_ref[a, b : b + 1, place].reshape(1, 1, LANES)
                acc = acc + block[a : a + all_rows] * tap
        conv[:, place] = acc.reshape(cells, LANES)
        return carry

    lax.fori_loop(0, channels // LANES, convolve, 0)
    normed = layer_norm(conv[...]).astype(bf16)

    def widen(k, total):
        part = slice(k * channels, (k + 1) * channels)
        wide = gelu(dot(normed, expand_ref[:, part])).astype(bf16)
        return total + dot(wide, reduce_ref[part])

    total = center.reshape(cells, channels)
    for k in range(expand_ref.shape[1] // channels):
        total = widen(k, total)
    block_one = total.astype(bf16)
    one[...] = block_one
    every = layer_norm(block_one.astype(f32)).astype(bf16)
    lat_in[...] = every
    count = rows * columns
    own = pl.ds(pl.multiple_of(my_lat * count, count), count)
    queries = dot(lat_in[own], attn_ref[0]).astype(bf16)
    keys = dot(every, attn_ref[1]).astype(bf16)
    values = dot(every, attn_ref[2]).astype(bf16)
    row_col = lax.broadcasted_iota(jnp.int32, (count, 1), 0) % columns
    key_col = lax.broadcasted_iota(jnp.int32, (1, cells), 1) % columns
    mix = attend(queries, keys, values, row_col == key_col)
    block_two = (one[own].astype(f32) + dot(mix, attn_ref[3])).astype(bf16)
    return block_two, layer_norm(block_two.astype(f32))


def fill(padded, all_rows, first, values):
    width = values.shape[1]
    padded[HALO : HALO + all_rows, first : first + width] = values


def fill_tiles(padded, my_lat, first, tiles):
    rows, cols = tiles[0].shape[:2]
    for s in range(len(tiles)):
        place = HALO + lax.rem(my_lat + s, len(tiles)) * rows
        padded[pl.ds(place, rows), first : first + cols] = tiles[s][...].astype(f32)


def clear(padded, all_rows):
    edge = jnp.zeros((HALO,) + padded.shape[1:], f32)
    padded[:HALO] = edge
    padded[HALO + all_rows :] = edge


def inner_kernel(nlat, *refs):
    tiles, refs = refs[:nlat], refs[nlat:]
    taps_ref, expand_ref, reduce_ref, attn_ref, two_ref, in_ref, padded, *scratch = refs
    rows, cols, channels = tiles[0].shape
    all_rows = rows * nlat
    columns = cols - 2 * SIDE
    clear(padded, all_rows)
    my_lat = lax.axis_index("lat")
    fill_tiles(padded, my_lat, 0, tiles)

    def slab(b, c):
        first = SIDE - HALO + b
        return padded[:, first : first + columns, c]

    center = padded[HALO : HALO + all_rows, SIDE : SIDE + columns]
    shape = (rows, all_rows, columns, channels)
    block_two, lon_in = chain(
        my_lat, slab, shape, taps_ref, expand_ref, reduce_ref, attn_ref, center, scratch
    )
    two_ref[...] = block_two
    in_ref[...] = lon_in.astype(bf16)


def outer_kernel(nlat, levels, *refs):
    tiles, refs = refs[:nlat], refs[nlat:]
    far_ref, near_ref, inner_in_ref, taps_ref, expand_ref, reduce_ref, attn_ref = refs[:7]
    two_ref, *refs = refs[7:]
    sent_refs, (sent, padded, *scratch) = refs[:levels], refs[levels:]
    rows, cols, channels = tiles[0].shape
    all_rows = rows * nlat
    columns = 2 * SIDE
    packed = (all_rows // 2, STRIP, channels)
    near = near_ref[...].astype(f32).reshape(packed)
    far = far_ref[...].astype(f32).reshape(packed)
    even = lax.axis_index("lon") % 2 == 0
    my_lat = lax.axis_index("lat")
    clear(padded, all_rows)
    fill(padded, all_rows, 0, unpack(jnp.where(even, far, near), True))
    fill_tiles(padded, my_lat, STRIP, tiles)
    fill(padded, all_rows, STRIP + cols, unpack(jnp.where(even, near, far), False))
    sublane = lax.broadcasted_iota(jnp.int32, (1, columns, 1), 1)

    def halves(shift, rows_of, c):
        right = STRIP + cols - SIDE + shift
        left = STRIP - SIDE + shift
        return jnp.where(
            sublane < SIDE,
            padded[rows_of, right : right + columns, c],
            padded[rows_of, left : left + columns, c],
        )

    def slab(b, c):
        return halves(b - HALO, slice(None), c)

    center = halves(0, slice(HALO, HALO + all_rows), slice(None))
    shape = (rows, all_rows, columns, channels)
    block_two, lon_in = chain(
        my_lat, slab, shape, taps_ref, expand_ref, reduce_ref, attn_ref, center, scratch
    )
    two_ref[...] = block_two
    inner = inner_in_ref[...].astype(f32).reshape(rows, cols - columns, channels)
    outer = lon_in.reshape(rows, columns, channels)
    sent[...] = jnp.concatenate([inner, outer], axis=1).astype(bf16)
    some = rows // levels
    for k in range(levels):
        part = sent[pl.ds(peer(levels, k) * some, some)]
        sent_refs[k][...] = part.reshape(sent_refs[k].shape)


def circle_kernel(levels, some, *refs):
    attn_ref, mix_refs = refs[-levels - 1], refs[-levels:]
    parts = refs[: -levels - 1]
    count = parts[0].shape[0] // (some * levels)

    def latitude(part, r):
        starts = [(k * some + r) * count for k in range(levels)]
        return jnp.concatenate([part[start : start + count] for start in starts], axis=0)

    for r in range(some):
        own = latitude(parts[0], r)
        every = jnp.concatenate([own] + [latitude(part, r) for part in parts[1:]], axis=0)
        queries = dot(own, attn_ref[0]).astype(bf16)
        keys = dot(every, attn_ref[1]).astype(bf16)
        values = dot(every, attn_ref[2]).astype(bf16)
        mix = attend(queries, keys, values, None)
        for k in range(levels):
            mix_refs[k][r * count : (r + 1) * count] = mix[k * count : (k + 1) * count]


def last_kernel(levels, *refs):
    parts = refs[:levels]
    inner_ref, outer_ref, attn_ref, out_ref = refs[levels:]
    rows, cols, channels = out_ref.shape
    columns = 2 * SIDE
    some = rows // levels
    every = jnp.concatenate([part[...] for part in parts], axis=0)
    change = dot(every, attn_ref[3]).reshape(levels, some, cols, channels)
    for k in range(levels):
        start = peer(levels, k) * some

        def state(ref, width):
            count = some * width
            place = pl.ds(pl.multiple_of(start * width, count), count)
            return ref[place].astype(f32).reshape(some, width, channels)

        inner = state(inner_ref, cols - columns) + change[k, :, : cols - columns]
        outer = state(outer_ref, columns) + change[k, :, cols - columns :]
        total = jnp.concatenate([outer[:, SIDE:], inner, outer[:, :SIDE]], axis=1)
        out_ref[pl.ds(start, some)] = total.astype(bf16)


def call(
    kernel, outs, operands, scratch=(), any_space=False, flops=0, grant=VMEM_BYTES
):
    vmem = pl.BlockSpec(memory_space=pltpu.VMEM)
    given = pl.BlockSpec(memory_space=pl.ANY) if any_space else vmem
    shapes = [
        out if isinstance(out, jax.ShapeDtypeStruct) else jax.ShapeDtypeStruct(out, bf16)
        for out in outs
    ]
    moved = sum(x.size * x.dtype.itemsize for x in operands)
    result = pl.pallas_call(
        kernel,
        out_shape=shapes,
        in_specs=[given] * len(operands),
        out_specs=[vmem] * len(outs),
        scratch_shapes=list(scratch),
        compiler_params=pltpu.CompilerParams(vmem_limit_bytes=grant),
        cost_estimate=pl.CostEstimate(flops=flops, bytes_accessed=moved, transcendentals=0),
    )(*operands)
    return result


def shards(field, dw_weight, w_expand, w_reduce, lat_attn, lon_attn):
    rows, cols, channels = field.shape
    nlat, nlon = lax.axis_size("lat"), lax.axis_size("lon")
    levels = min(LEVELS, nlon)
    column = nlon // levels
    some = rows // levels
    all_rows = rows * nlat
    columns = 2 * SIDE

    def swap(piece, mask):
        return lax.ppermute(piece, "lon", [(j, j ^ mask) for j in range(nlon)])

    def exchange(pieces):
        moved = []
        for k in range(1, levels):
            level = levels - k
            cross = (level ^ (level >> 1)) & 1 if column > 1 else 0
            moved.append(swap(pieces[k], level * column + cross))
        return [pieces[0]] + moved

    tiles = [field]
    for s in range(1, nlat):
        tiles.append(lax.ppermute(field, "lat", [((i + s) % nlat, i) for i in range(nlat)]))
    weights = (w_expand, w_reduce, lat_attn, lon_attn)
    expand, reduce, lat_proj, lon_proj, taps = call(
        functools.partial(stage_kernel, len(weights)),
        [w.shape for w in weights] + [jax.ShapeDtypeStruct(dw_weight.shape, f32)],
        [*weights, dw_weight],
        [
            pltpu.VMEM(dw_weight.shape, bf16),
            pltpu.SemaphoreType.DMA((len(weights) + 1, STAGES)),
        ],
        any_space=True,
        grant=STAGE_BYTES,
    )

    strip = (all_rows * SIDE, channels)
    strip_scratch = pltpu.VMEM((all_rows, STRIP, channels), f32)
    near, far = call(
        functools.partial(strip_kernel, nlat),
        [strip, strip],
        [*tiles, reduce],
        [strip_scratch, strip_scratch],
    )
    far = lax.ppermute(
        far, "lon", [(j, (j - 1) % nlon if j % 2 == 0 else (j + 1) % nlon) for j in range(nlon)]
    )
    near = swap(near, 1)

    def scratch(width, count):
        return [
            pltpu.VMEM((all_rows + 2 * HALO, width, channels), f32),
            pltpu.VMEM((all_rows * count, channels), bf16),
            pltpu.VMEM((all_rows * count, channels), bf16),
            pltpu.VMEM((all_rows * count, channels), f32),
        ]

    work = 4 * all_rows * columns * channels * w_expand.shape[1]
    inner_two, inner_in = call(
        functools.partial(inner_kernel, nlat),
        [(rows * (cols - columns), channels)] * 2,
        [*tiles, taps, expand, reduce, lat_proj],
        scratch(cols, cols - columns),
        flops=work,
    )
    piece = (some * cols, channels)
    outer_two, *parts = call(
        functools.partial(outer_kernel, nlat, levels),
        [(rows * columns, channels)] + [piece] * levels,
        [*tiles, far, near, inner_in, taps, expand, reduce, lat_proj],
        [pltpu.VMEM((rows, cols, channels), bf16)] + scratch(cols + 2 * STRIP, columns),
        flops=work,
    )

    parts = exchange(parts)
    circle = [jnp.concatenate(parts, axis=0)]
    mask = column // 2
    while mask:
        circle = circle + [swap(part, mask + mask // 2) for part in circle]
        mask //= 2
    mixes = call(
        functools.partial(circle_kernel, levels, some), [piece] * levels, [*circle, lon_proj]
    )
    mixes = exchange(mixes)
    (out,) = call(
        functools.partial(last_kernel, levels),
        [(rows, cols, channels)],
        [*mixes, inner_two, outer_two, lon_proj],
    )
    return out


def solution(mesh):
    return jax.shard_map(
        shards,
        mesh=mesh,
        in_specs=(P("lat", "lon", None), P(), P(), P(), P(), P()),
        out_specs=P("lat", "lon", None),
        check_vma=False,
    )
```

```python
import functools

import jax
import jax.numpy as jnp
from jax import lax
from jax.experimental import pallas as pl
from jax.experimental.pallas import tpu as pltpu
from jax.sharding import PartitionSpec as P

HEADS = 8
HALO = 3
TAPS = 2 * HALO + 1
STRIP = 8
SIDE = 4
LANES = 128
LEVELS = 4
STAGES = 4
EPSILON = 1e-06
VMEM_BYTES = 24 * 1024 * 1024
STAGE_BYTES = 103 * 512 * 1024
bf16, f32 = jnp.bfloat16, jnp.float32


def layer_norm(values):
    average = jnp.mean(values, axis=-1, keepdims=True)
    centered = values - average
    variance = jnp.mean(centered * centered, axis=-1, keepdims=True)
    return centered * lax.rsqrt(variance + EPSILON)


def dot(rows, matrix):
    return jnp.dot(rows, matrix, preferred_element_type=f32)


def dot_t(rows, matrix):
    return lax.dot_general(rows, matrix, (((1,), (1,)), ((), ())), preferred_element_type=f32)


def gelu(values):
    size = jnp.abs(values)
    t = 1.0 / (1.0 + (0.3275911 * 0.5**0.5) * size)
    tail = 1.061405429 * t - 1.453152027
    for coefficient in (1.421413741, -0.284496736, 0.254829592):
        tail = tail * t + coefficient
    tail = (0.5 * size * t) * tail * jnp.exp(-0.5 * values * values)
    return jnp.maximum(values, 0.0) - tail


def attend(queries, keys, values, mask):
    count, channels = queries.shape
    head_size = channels // HEADS
    lane_head = lax.broadcasted_iota(jnp.int32, (1, channels), 1) // head_size
    picks = [lane_head == h for h in range(HEADS)]
    none = jnp.zeros_like(queries)
    stacked = jnp.concatenate([jnp.where(pick, queries, none) for pick in picks], axis=0)
    scores = dot_t(stacked, keys) * head_size ** (-0.5)
    if mask is not None:
        scores = scores.reshape(HEADS, count, keys.shape[0])
        scores = jnp.where(mask[None], scores, -1e30).reshape(HEADS * count, keys.shape[0])
    top = jnp.max(scores, axis=-1, keepdims=True)
    probs = jnp.exp(scores - top)
    totals = jnp.sum(probs, axis=-1, keepdims=True)
    mixed = dot(probs.astype(bf16), values) * (1.0 / totals)
    out = mixed[:count]
    for h in range(1, HEADS):
        out = jnp.where(picks[h], mixed[h * count : (h + 1) * count], out)
    return out.astype(bf16)


def stage_kernel(count, *refs):
    sources, dw_ref = refs[:count], refs[count]
    targets, taps_ref, dw, sems = refs[count + 1 : 2 * count + 1], *refs[2 * count + 1 :]
    copies = [pltpu.make_async_copy(dw_ref, dw, sems.at[count, 0])]
    pieces = sems.shape[1]
    for i in range(count):
        source, target = sources[i], targets[i]
        size = source.shape[0] // pieces
        for k in range(pieces):
            part = pl.ds(k * size, size)
            copies.append(pltpu.make_async_copy(source.at[part], target.at[part], sems.at[i, k]))
    for copy in copies:
        copy.start()
    for copy in copies:
        copy.wait()
    taps_ref[...] = dw[...].astype(f32)


def peer(levels, k):
    level = lax.axis_index("lon") // (lax.axis_size("lon") // levels)
    return level ^ ((levels - k) % levels)


def strip_kernel(nlat, *refs):
    tiles = refs[:nlat]
    near_ref, far_ref, near, far = refs[nlat + 1 :]
    rows, cols, channels = tiles[0].shape
    even = lax.axis_index("lon") % 2 == 0
    for s in range(nlat):
        values = tiles[s][...].astype(f32)
        first, last = values[:, :STRIP], values[:, cols - STRIP :]
        where = pl.ds(lax.rem(lax.axis_index("lat") + s, nlat) * rows, rows)
        near[where] = jnp.where(even, last, first)
        far[where] = jnp.where(even, first, last)
    for strip, strip_ref, is_last in ((near, near_ref, even), (far, far_ref, ~even)):
        strip_ref[...] = pack(strip[...], is_last).reshape(strip_ref.shape).astype(bf16)


def lower_half():
    return lax.broadcasted_iota(jnp.int32, (1, STRIP, 1), 1) < SIDE


def turn(values):
    return jnp.concatenate([values[:, SIDE:], values[:, :SIDE]], axis=1)


def pack(strip, is_last):
    half = strip.shape[0] // 2
    turned = turn(strip)
    low = jnp.where(is_last, turned, strip)
    high = jnp.where(is_last, strip, turned)
    return jnp.where(lower_half(), low[:half], high[half:])


def unpack(packed, is_left):
    turned = turn(packed)
    low = jnp.where(is_left, turned, packed)
    high = jnp.where(is_left, packed, turned)
    return jnp.concatenate([low, high], axis=0)


def chain(my_lat, slab, shape, taps_ref, expand_ref, reduce_ref, attn_ref, center, scratch):
    one, lat_in = scratch
    rows, all_rows, columns, channels = shape
    cells = all_rows * columns
    parts = []
    for c in range(0, channels, LANES):
        acc = jnp.zeros((all_rows, columns, LANES), f32)
        for b in range(TAPS):
            block = slab(b, c)
            for a in range(TAPS):
                tap = taps_ref[a, b : b + 1, c : c + LANES].reshape(1, 1, LANES)
                acc = acc + block[a : a + all_rows] * tap
        parts.append(acc.reshape(cells, LANES))
    normed = layer_norm(jnp.concatenate(parts, axis=-1)).astype(bf16)

    def widen(k, total):
        part = slice(k * channels, (k + 1) * channels)
        wide = gelu(dot(normed, expand_ref[:, part])).astype(bf16)
        return total + dot(wide, reduce_ref[part])

    total = center.reshape(cells, channels)
    for k in range(expand_ref.shape[1] // channels):
        total = widen(k, total)
    block_one = total.astype(bf16)
    one[...] = block_one
    every = layer_norm(block_one.astype(f32)).astype(bf16)
    lat_in[...] = every
    count = rows * columns
    own = pl.ds(pl.multiple_of(my_lat * count, count), count)
    queries = dot(lat_in[own], attn_ref[0]).astype(bf16)
    keys = dot(every, attn_ref[1]).astype(bf16)
    values = dot(every, attn_ref[2]).astype(bf16)
    row_col = lax.broadcasted_iota(jnp.int32, (count, 1), 0) % columns
    key_col = lax.broadcasted_iota(jnp.int32, (1, cells), 1) % columns
    mix = attend(queries, keys, values, row_col == key_col)
    block_two = (one[own].astype(f32) + dot(mix, attn_ref[3])).astype(bf16)
    return block_two, layer_norm(block_two.astype(f32))


def fill(padded, all_rows, first, values):
    width = values.shape[1]
    padded[HALO : HALO + all_rows, first : first + width] = values


def fill_tiles(padded, my_lat, first, tiles):
    rows, cols = tiles[0].shape[:2]
    for s in range(len(tiles)):
        place = HALO + lax.rem(my_lat + s, len(tiles)) * rows
        padded[pl.ds(place, rows), first : first + cols] = tiles[s][...].astype(f32)


def clear(padded, all_rows):
    edge = jnp.zeros((HALO,) + padded.shape[1:], f32)
    padded[:HALO] = edge
    padded[HALO + all_rows :] = edge


def inner_kernel(nlat, *refs):
    tiles, refs = refs[:nlat], refs[nlat:]
    taps_ref, expand_ref, reduce_ref, attn_ref, two_ref, in_ref, padded, *scratch = refs
    rows, cols, channels = tiles[0].shape
    all_rows = rows * nlat
    columns = cols - 2 * SIDE
    clear(padded, all_rows)
    my_lat = lax.axis_index("lat")
    fill_tiles(padded, my_lat, 0, tiles)

    def slab(b, c):
        first = SIDE - HALO + b
        return padded[:, first : first + columns, c : c + LANES]

    center = padded[HALO : HALO + all_rows, SIDE : SIDE + columns]
    shape = (rows, all_rows, columns, channels)
    block_two, lon_in = chain(
        my_lat, slab, shape, taps_ref, expand_ref, reduce_ref, attn_ref, center, scratch
    )
    two_ref[...] = block_two
    in_ref[...] = lon_in.astype(bf16)


def outer_kernel(nlat, levels, *refs):
    tiles, refs = refs[:nlat], refs[nlat:]
    far_ref, near_ref, inner_in_ref, taps_ref, expand_ref, reduce_ref, attn_ref = refs[:7]
    two_ref, *refs = refs[7:]
    sent_refs, (sent, padded, *scratch) = refs[:levels], refs[levels:]
    rows, cols, channels = tiles[0].shape
    all_rows = rows * nlat
    columns = 2 * SIDE
    packed = (all_rows // 2, STRIP, channels)
    near = near_ref[...].astype(f32).reshape(packed)
    far = far_ref[...].astype(f32).reshape(packed)
    even = lax.axis_index("lon") % 2 == 0
    my_lat = lax.axis_index("lat")
    clear(padded, all_rows)
    fill(padded, all_rows, 0, unpack(jnp.where(even, far, near), True))
    fill_tiles(padded, my_lat, STRIP, tiles)
    fill(padded, all_rows, STRIP + cols, unpack(jnp.where(even, near, far), False))
    sublane = lax.broadcasted_iota(jnp.int32, (1, columns, 1), 1)

    def halves(shift, rows_of, c, width):
        right = STRIP + cols - SIDE + shift
        left = STRIP - SIDE + shift
        return jnp.where(
            sublane < SIDE,
            padded[rows_of, right : right + columns, c : c + width],
            padded[rows_of, left : left + columns, c : c + width],
        )

    def slab(b, c):
        return halves(b - HALO, slice(None), c, LANES)

    center = halves(0, slice(HALO, HALO + all_rows), 0, channels)
    shape = (rows, all_rows, columns, channels)
    block_two, lon_in = chain(
        my_lat, slab, shape, taps_ref, expand_ref, reduce_ref, attn_ref, center, scratch
    )
    two_ref[...] = block_two
    inner = inner_in_ref[...].astype(f32).reshape(rows, cols - columns, channels)
    outer = lon_in.reshape(rows, columns, channels)
    sent[...] = jnp.concatenate([inner, outer], axis=1).astype(bf16)
    some = rows // levels
    for k in range(levels):
        part = sent[pl.ds(peer(levels, k) * some, some)]
        sent_refs[k][...] = part.reshape(sent_refs[k].shape)


def join_kernel(levels, some, *refs):
    parts, joined = refs[:levels], refs[levels:]
    cols = parts[0].shape[0] // some
    for r in range(some):
        for k in range(levels):
            joined[r][k * cols : (k + 1) * cols] = parts[k][r * cols : (r + 1) * cols]


def circle_kernel(levels, before, *refs):
    attn_ref, refs = refs[0], refs[1:]
    done, refs = refs[:before], refs[before:]
    parts, mix_refs = refs[:-levels], refs[-levels:]
    own = parts[0][...]
    every = jnp.concatenate([own] + [part[...] for part in parts[1:]], axis=0)
    queries = dot(own, attn_ref[0]).astype(bf16)
    keys = dot(every, attn_ref[1]).astype(bf16)
    values = dot(every, attn_ref[2]).astype(bf16)
    mix = attend(queries, keys, values, None)
    cols = own.shape[0] // levels
    for k in range(levels):
        for r in range(before // levels):
            mix_refs[k][r * cols : (r + 1) * cols] = done[r * levels + k][...]
        mix_refs[k][before // levels * cols :] = mix[k * cols : (k + 1) * cols]


def last_kernel(levels, *refs):
    parts = refs[:levels]
    inner_ref, outer_ref, attn_ref, out_ref = refs[levels:]
    rows, cols, channels = out_ref.shape
    columns = 2 * SIDE
    some = rows // levels
    every = jnp.concatenate([part[...] for part in parts], axis=0)
    change = dot(every, attn_ref[3]).reshape(levels, some, cols, channels)
    for k in range(levels):
        start = peer(levels, k) * some

        def state(ref, width):
            count = some * width
            place = pl.ds(pl.multiple_of(start * width, count), count)
            return ref[place].astype(f32).reshape(some, width, channels)

        inner = state(inner_ref, cols - columns) + change[k, :, : cols - columns]
        outer = state(outer_ref, columns) + change[k, :, cols - columns :]
        total = jnp.concatenate([outer[:, SIDE:], inner, outer[:, :SIDE]], axis=1)
        out_ref[pl.ds(start, some)] = total.astype(bf16)


def call(
    kernel, outs, operands, scratch=(), any_space=False, flops=0, grant=VMEM_BYTES
):
    vmem = pl.BlockSpec(memory_space=pltpu.VMEM)
    given = pl.BlockSpec(memory_space=pl.ANY) if any_space else vmem
    shapes = [
        out if isinstance(out, jax.ShapeDtypeStruct) else jax.ShapeDtypeStruct(out, bf16)
        for out in outs
    ]
    moved = sum(x.size * x.dtype.itemsize for x in operands)
    result = pl.pallas_call(
        kernel,
        out_shape=shapes,
        in_specs=[given] * len(operands),
        out_specs=[vmem] * len(outs),
        scratch_shapes=list(scratch),
        compiler_params=pltpu.CompilerParams(vmem_limit_bytes=grant),
        cost_estimate=pl.CostEstimate(flops=flops, bytes_accessed=moved, transcendentals=0),
    )(*operands)
    return result


def shards(field, dw_weight, w_expand, w_reduce, lat_attn, lon_attn):
    rows, cols, channels = field.shape
    nlat, nlon = lax.axis_size("lat"), lax.axis_size("lon")
    levels = min(LEVELS, nlon)
    column = nlon // levels
    some = rows // levels
    all_rows = rows * nlat
    columns = 2 * SIDE

    def swap(piece, mask):
        return lax.ppermute(piece, "lon", [(j, j ^ mask) for j in range(nlon)])

    def exchange(pieces):
        moved = []
        for k in range(1, levels):
            level = levels - k
            cross = (level ^ (level >> 1)) & 1 if column > 1 else 0
            moved.append(swap(pieces[k], level * column + cross))
        return [pieces[0]] + moved

    tiles = [field]
    for s in range(1, nlat):
        tiles.append(lax.ppermute(field, "lat", [((i + s) % nlat, i) for i in range(nlat)]))
    weights = (w_expand, w_reduce, lat_attn, lon_attn)
    expand, reduce, lat_proj, lon_proj, taps = call(
        functools.partial(stage_kernel, len(weights)),
        [w.shape for w in weights] + [jax.ShapeDtypeStruct(dw_weight.shape, f32)],
        [*weights, dw_weight],
        [
            pltpu.VMEM(dw_weight.shape, bf16),
            pltpu.SemaphoreType.DMA((len(weights) + 1, STAGES)),
        ],
        any_space=True,
        grant=STAGE_BYTES,
    )

    strip = (all_rows * SIDE, channels)
    strip_scratch = pltpu.VMEM((all_rows, STRIP, channels), f32)
    near, far = call(
        functools.partial(strip_kernel, nlat),
        [strip, strip],
        [*tiles, reduce],
        [strip_scratch, strip_scratch],
    )
    far = lax.ppermute(
        far, "lon", [(j, (j - 1) % nlon if j % 2 == 0 else (j + 1) % nlon) for j in range(nlon)]
    )
    near = swap(near, 1)

    def scratch(width, count):
        return [
            pltpu.VMEM((all_rows + 2 * HALO, width, channels), f32),
            pltpu.VMEM((all_rows * count, channels), bf16),
            pltpu.VMEM((all_rows * count, channels), bf16),
        ]

    work = 4 * all_rows * columns * channels * w_expand.shape[1]
    inner_two, inner_in = call(
        functools.partial(inner_kernel, nlat),
        [(rows * (cols - columns), channels)] * 2,
        [*tiles, taps, expand, reduce, lat_proj],
        scratch(cols, cols - columns),
        flops=work,
    )
    piece = (some * cols, channels)
    outer_two, *parts = call(
        functools.partial(outer_kernel, nlat, levels),
        [(rows * columns, channels)] + [piece] * levels,
        [*tiles, far, near, inner_in, taps, expand, reduce, lat_proj],
        [pltpu.VMEM((rows, cols, channels), bf16)] + scratch(cols + 2 * STRIP, columns),
        flops=work,
    )

    parts = exchange(parts)
    joined = call(
        functools.partial(join_kernel, levels, some), [(levels * cols, channels)] * some, parts
    )
    circles = [[part] for part in joined]
    mask = column // 2
    while mask:
        for circle in circles:
            circle += [swap(part, mask + mask // 2) for part in circle]
        mask //= 2
    done = []
    for r, circle in enumerate(circles):
        last_one = r == some - 1
        mixes = call(
            functools.partial(circle_kernel, levels, len(done) if last_one else 0),
            [piece if last_one else (cols, channels)] * levels,
            [lon_proj, *(done if last_one else []), *circle],
            flops=work // 4,
        )
        done = done + list(mixes)
    mixes = exchange(mixes)
    (out,) = call(
        functools.partial(last_kernel, levels),
        [(rows, cols, channels)],
        [*mixes, inner_two, outer_two, lon_proj],
    )
    return out


def solution(mesh):
    return jax.shard_map(
        shards,
        mesh=mesh,
        in_specs=(P("lat", "lon", None), P(), P(), P(), P(), P()),
        out_specs=P("lat", "lon", None),
        check_vma=False,
    )
```

```python
import functools

import jax
import jax.numpy as jnp
from jax import lax
from jax.experimental import pallas as pl
from jax.experimental.pallas import tpu as pltpu
from jax.sharding import PartitionSpec as P

HEADS = 8
HALO = 3
TAPS = 2 * HALO + 1
STRIP = 8
SIDE = 4
LANES = 128
LEVELS = 4
STAGES = 4
EPSILON = 1e-06
VMEM_BYTES = 24 * 1024 * 1024
STAGE_BYTES = 103 * 512 * 1024
bf16, f32 = jnp.bfloat16, jnp.float32


def layer_norm(values):
    average = jnp.mean(values, axis=-1, keepdims=True)
    centered = values - average
    variance = jnp.mean(centered * centered, axis=-1, keepdims=True)
    return centered * lax.rsqrt(variance + EPSILON)


def dot(rows, matrix):
    return jnp.dot(rows, matrix, preferred_element_type=f32)


def dot_t(rows, matrix):
    return lax.dot_general(rows, matrix, (((1,), (1,)), ((), ())), preferred_element_type=f32)


def gelu(values):
    size = jnp.abs(values)
    t = 1.0 / (1.0 + (0.3275911 * 0.5**0.5) * size)
    tail = 1.061405429 * t - 1.453152027
    for coefficient in (1.421413741, -0.284496736, 0.254829592):
        tail = tail * t + coefficient
    tail = (0.5 * size * t) * tail * jnp.exp(-0.5 * values * values)
    return jnp.maximum(values, 0.0) - tail


def attend(queries, keys, values, mask):
    count, channels = queries.shape
    head_size = channels // HEADS
    lane_head = lax.broadcasted_iota(jnp.int32, (1, channels), 1) // head_size
    picks = [lane_head == h for h in range(HEADS)]
    none = jnp.zeros_like(queries)
    stacked = jnp.concatenate([jnp.where(pick, queries, none) for pick in picks], axis=0)
    scores = dot_t(stacked, keys) * head_size ** (-0.5)
    if mask is not None:
        scores = scores.reshape(HEADS, count, keys.shape[0])
        scores = jnp.where(mask[None], scores, -1e30).reshape(HEADS * count, keys.shape[0])
    top = jnp.max(scores, axis=-1, keepdims=True)
    probs = jnp.exp(scores - top)
    totals = jnp.sum(probs, axis=-1, keepdims=True)
    mixed = dot(probs.astype(bf16), values) * (1.0 / totals)
    out = mixed[:count]
    for h in range(1, HEADS):
        out = jnp.where(picks[h], mixed[h * count : (h + 1) * count], out)
    return out.astype(bf16)


def stage_kernel(count, *refs):
    sources, dw_ref = refs[:count], refs[count]
    targets, taps_ref, dw, sems = refs[count + 1 : 2 * count + 1], *refs[2 * count + 1 :]
    copies = [pltpu.make_async_copy(dw_ref, dw, sems.at[count, 0])]
    pieces = sems.shape[1]
    for i in range(count):
        source, target = sources[i], targets[i]
        size = source.shape[0] // pieces
        for k in range(pieces):
            part = pl.ds(k * size, size)
            copies.append(pltpu.make_async_copy(source.at[part], target.at[part], sems.at[i, k]))
    for copy in copies:
        copy.start()
    for copy in copies:
        copy.wait()
    taps_ref[...] = dw[...].astype(f32)


def peer(levels, k):
    level = lax.axis_index("lon") // (lax.axis_size("lon") // levels)
    return level ^ ((levels - k) % levels)


def strip_kernel(nlat, *refs):
    tiles = refs[:nlat]
    near_ref, far_ref, near, far = refs[nlat + 1 :]
    rows, cols, channels = tiles[0].shape
    even = lax.axis_index("lon") % 2 == 0
    for s in range(nlat):
        values = tiles[s][...].astype(f32)
        first, last = values[:, :STRIP], values[:, cols - STRIP :]
        where = pl.ds(lax.rem(lax.axis_index("lat") + s, nlat) * rows, rows)
        near[where] = jnp.where(even, last, first)
        far[where] = jnp.where(even, first, last)
    for strip, strip_ref, is_last in ((near, near_ref, even), (far, far_ref, ~even)):
        strip_ref[...] = pack(strip[...], is_last).reshape(strip_ref.shape).astype(bf16)


def lower_half():
    return lax.broadcasted_iota(jnp.int32, (1, STRIP, 1), 1) < SIDE


def turn(values):
    return jnp.concatenate([values[:, SIDE:], values[:, :SIDE]], axis=1)


def pack(strip, is_last):
    half = strip.shape[0] // 2
    turned = turn(strip)
    low = jnp.where(is_last, turned, strip)
    high = jnp.where(is_last, strip, turned)
    return jnp.where(lower_half(), low[:half], high[half:])


def unpack(packed, is_left):
    turned = turn(packed)
    low = jnp.where(is_left, turned, packed)
    high = jnp.where(is_left, packed, turned)
    return jnp.concatenate([low, high], axis=0)


def chain(my_lat, slab, shape, taps_ref, expand_ref, reduce_ref, attn_ref, center, scratch):
    one, lat_in = scratch
    rows, all_rows, columns, channels = shape
    cells = all_rows * columns
    parts = []
    for c in range(0, channels, LANES):
        acc = jnp.zeros((all_rows, columns, LANES), f32)
        for b in range(TAPS):
            block = slab(b, c)
            for a in range(TAPS):
                tap = taps_ref[a, b : b + 1, c : c + LANES].reshape(1, 1, LANES)
                acc = acc + block[a : a + all_rows] * tap
        parts.append(acc.reshape(cells, LANES))
    normed = layer_norm(jnp.concatenate(parts, axis=-1)).astype(bf16)

    def widen(k, total):
        part = slice(k * channels, (k + 1) * channels)
        wide = gelu(dot(normed, expand_ref[:, part])).astype(bf16)
        return total + dot(wide, reduce_ref[part])

    total = center.reshape(cells, channels)
    for k in range(expand_ref.shape[1] // channels):
        total = widen(k, total)
    block_one = total.astype(bf16)
    one[...] = block_one
    every = layer_norm(block_one.astype(f32)).astype(bf16)
    lat_in[...] = every
    count = rows * columns
    own = pl.ds(pl.multiple_of(my_lat * count, count), count)
    queries = dot(lat_in[own], attn_ref[0]).astype(bf16)
    keys = dot(every, attn_ref[1]).astype(bf16)
    values = dot(every, attn_ref[2]).astype(bf16)
    row_col = lax.broadcasted_iota(jnp.int32, (count, 1), 0) % columns
    key_col = lax.broadcasted_iota(jnp.int32, (1, cells), 1) % columns
    mix = attend(queries, keys, values, row_col == key_col)
    block_two = (one[own].astype(f32) + dot(mix, attn_ref[3])).astype(bf16)
    return block_two, layer_norm(block_two.astype(f32))


def fill(padded, all_rows, first, values):
    width = values.shape[1]
    padded[HALO : HALO + all_rows, first : first + width] = values


def fill_tiles(padded, my_lat, first, tiles):
    rows, cols = tiles[0].shape[:2]
    for s in range(len(tiles)):
        place = HALO + lax.rem(my_lat + s, len(tiles)) * rows
        padded[pl.ds(place, rows), first : first + cols] = tiles[s][...].astype(f32)


def clear(padded, all_rows):
    edge = jnp.zeros((HALO,) + padded.shape[1:], f32)
    padded[:HALO] = edge
    padded[HALO + all_rows :] = edge


def inner_kernel(nlat, *refs):
    tiles, refs = refs[:nlat], refs[nlat:]
    taps_ref, expand_ref, reduce_ref, attn_ref, two_ref, in_ref, padded, *scratch = refs
    rows, cols, channels = tiles[0].shape
    all_rows = rows * nlat
    columns = cols - 2 * SIDE
    clear(padded, all_rows)
    my_lat = lax.axis_index("lat")
    fill_tiles(padded, my_lat, 0, tiles)

    def slab(b, c):
        first = SIDE - HALO + b
        return padded[:, first : first + columns, c : c + LANES]

    center = padded[HALO : HALO + all_rows, SIDE : SIDE + columns]
    shape = (rows, all_rows, columns, channels)
    block_two, lon_in = chain(
        my_lat, slab, shape, taps_ref, expand_ref, reduce_ref, attn_ref, center, scratch
    )
    two_ref[...] = block_two
    in_ref[...] = lon_in.astype(bf16)


def outer_kernel(nlat, levels, *refs):
    tiles, refs = refs[:nlat], refs[nlat:]
    far_ref, near_ref, inner_in_ref, taps_ref, expand_ref, reduce_ref, attn_ref = refs[:7]
    two_ref, *refs = refs[7:]
    sent_refs, (sent, padded, *scratch) = refs[:levels], refs[levels:]
    rows, cols, channels = tiles[0].shape
    all_rows = rows * nlat
    columns = 2 * SIDE
    packed = (all_rows // 2, STRIP, channels)
    near = near_ref[...].astype(f32).reshape(packed)
    far = far_ref[...].astype(f32).reshape(packed)
    even = lax.axis_index("lon") % 2 == 0
    my_lat = lax.axis_index("lat")
    clear(padded, all_rows)
    fill(padded, all_rows, 0, unpack(jnp.where(even, far, near), True))
    fill_tiles(padded, my_lat, STRIP, tiles)
    fill(padded, all_rows, STRIP + cols, unpack(jnp.where(even, near, far), False))
    sublane = lax.broadcasted_iota(jnp.int32, (1, columns, 1), 1)

    def halves(shift, rows_of, c, width):
        right = STRIP + cols - SIDE + shift
        left = STRIP - SIDE + shift
        return jnp.where(
            sublane < SIDE,
            padded[rows_of, right : right + columns, c : c + width],
            padded[rows_of, left : left + columns, c : c + width],
        )

    def slab(b, c):
        return halves(b - HALO, slice(None), c, LANES)

    center = halves(0, slice(HALO, HALO + all_rows), 0, channels)
    shape = (rows, all_rows, columns, channels)
    block_two, lon_in = chain(
        my_lat, slab, shape, taps_ref, expand_ref, reduce_ref, attn_ref, center, scratch
    )
    two_ref[...] = block_two
    inner = inner_in_ref[...].astype(f32).reshape(rows, cols - columns, channels)
    outer = lon_in.reshape(rows, columns, channels)
    sent[...] = jnp.concatenate([inner, outer], axis=1).astype(bf16)
    some = rows // levels
    for k in range(levels):
        part = sent[pl.ds(peer(levels, k) * some, some)]
        sent_refs[k][...] = part.reshape(sent_refs[k].shape)


def join_kernel(levels, some, *refs):
    parts, joined = refs[:levels], refs[levels:]
    cols = parts[0].shape[0] // some
    for r in range(some):
        for k in range(levels):
            joined[r][k * cols : (k + 1) * cols] = parts[k][r * cols : (r + 1) * cols]


def circle_kernel(levels, before, *refs):
    attn_ref, refs = refs[0], refs[1:]
    done, refs = refs[:before], refs[before:]
    parts, mix_refs = refs[:-levels], refs[-levels:]
    own = parts[0][...]
    every = jnp.concatenate([own] + [part[...] for part in parts[1:]], axis=0)
    queries = dot(own, attn_ref[0]).astype(bf16)
    keys = dot(every, attn_ref[1]).astype(bf16)
    values = dot(every, attn_ref[2]).astype(bf16)
    mix = attend(queries, keys, values, None)
    cols = own.shape[0] // levels
    for k in range(levels):
        for r in range(before // levels):
            mix_refs[k][r * cols : (r + 1) * cols] = done[r * levels + k][...]
        mix_refs[k][before // levels * cols :] = mix[k * cols : (k + 1) * cols]


def last_kernel(levels, *refs):
    parts = refs[:levels]
    inner_ref, outer_ref, attn_ref, out_ref = refs[levels:]
    rows, cols, channels = out_ref.shape
    columns = 2 * SIDE
    some = rows // levels
    every = jnp.concatenate([part[...] for part in parts], axis=0)
    change = dot(every, attn_ref[3]).reshape(levels, some, cols, channels)
    for k in range(levels):
        start = peer(levels, k) * some

        def state(ref, width):
            count = some * width
            place = pl.ds(pl.multiple_of(start * width, count), count)
            return ref[place].astype(f32).reshape(some, width, channels)

        inner = state(inner_ref, cols - columns) + change[k, :, : cols - columns]
        outer = state(outer_ref, columns) + change[k, :, cols - columns :]
        total = jnp.concatenate([outer[:, SIDE:], inner, outer[:, :SIDE]], axis=1)
        out_ref[pl.ds(start, some)] = total.astype(bf16)


def call(
    kernel, outs, operands, scratch=(), any_space=False, flops=0, grant=VMEM_BYTES
):
    vmem = pl.BlockSpec(memory_space=pltpu.VMEM)
    given = pl.BlockSpec(memory_space=pl.ANY) if any_space else vmem
    shapes = [
        out if isinstance(out, jax.ShapeDtypeStruct) else jax.ShapeDtypeStruct(out, bf16)
        for out in outs
    ]
    moved = sum(x.size * x.dtype.itemsize for x in operands)
    result = pl.pallas_call(
        kernel,
        out_shape=shapes,
        in_specs=[given] * len(operands),
        out_specs=[vmem] * len(outs),
        scratch_shapes=list(scratch),
        compiler_params=pltpu.CompilerParams(vmem_limit_bytes=grant),
        cost_estimate=pl.CostEstimate(flops=flops, bytes_accessed=moved, transcendentals=0),
    )(*operands)
    return result


def shards(field, dw_weight, w_expand, w_reduce, lat_attn, lon_attn):
    rows, cols, channels = field.shape
    nlat, nlon = lax.axis_size("lat"), lax.axis_size("lon")
    levels = min(LEVELS, nlon)
    column = nlon // levels
    some = rows // levels
    all_rows = rows * nlat
    columns = 2 * SIDE

    def swap(piece, mask):
        return lax.ppermute(piece, "lon", [(j, j ^ mask) for j in range(nlon)])

    def exchange(pieces):
        moved = []
        for k in range(1, levels):
            level = levels - k
            moved.append(swap(pieces[k], level * column + min(1, column - 1)))
        return [pieces[0]] + moved

    tiles = [field]
    for s in range(1, nlat):
        tiles.append(lax.ppermute(field, "lat", [((i + s) % nlat, i) for i in range(nlat)]))
    weights = (w_expand, w_reduce, lat_attn, lon_attn)
    expand, reduce, lat_proj, lon_proj, taps = call(
        functools.partial(stage_kernel, len(weights)),
        [w.shape for w in weights] + [jax.ShapeDtypeStruct(dw_weight.shape, f32)],
        [*weights, dw_weight],
        [
            pltpu.VMEM(dw_weight.shape, bf16),
            pltpu.SemaphoreType.DMA((len(weights) + 1, STAGES)),
        ],
        any_space=True,
        grant=STAGE_BYTES,
    )

    strip = (all_rows * SIDE, channels)
    strip_scratch = pltpu.VMEM((all_rows, STRIP, channels), f32)
    near, far = call(
        functools.partial(strip_kernel, nlat),
        [strip, strip],
        [*tiles, reduce],
        [strip_scratch, strip_scratch],
    )
    far = lax.ppermute(
        far, "lon", [(j, (j - 1) % nlon if j % 2 == 0 else (j + 1) % nlon) for j in range(nlon)]
    )
    near = swap(near, 1)

    def scratch(width, count):
        return [
            pltpu.VMEM((all_rows + 2 * HALO, width, channels), f32),
            pltpu.VMEM((all_rows * count, channels), bf16),
            pltpu.VMEM((all_rows * count, channels), bf16),
        ]

    work = 4 * all_rows * columns * channels * w_expand.shape[1]
    inner_two, inner_in = call(
        functools.partial(inner_kernel, nlat),
        [(rows * (cols - columns), channels)] * 2,
        [*tiles, taps, expand, reduce, lat_proj],
        scratch(cols, cols - columns),
        flops=work,
    )
    piece = (some * cols, channels)
    outer_two, *parts = call(
        functools.partial(outer_kernel, nlat, levels),
        [(rows * columns, channels)] + [piece] * levels,
        [*tiles, far, near, inner_in, taps, expand, reduce, lat_proj],
        [pltpu.VMEM((rows, cols, channels), bf16)] + scratch(cols + 2 * STRIP, columns),
        flops=work,
    )

    parts = exchange(parts)
    joined = call(
        functools.partial(join_kernel, levels, some), [(levels * cols, channels)] * some, parts
    )
    circles = [[part] for part in joined]
    mask = column // 2
    while mask:
        for circle in circles:
            circle += [swap(part, mask + mask // 2) for part in circle]
        mask //= 2
    done = []
    for r, circle in enumerate(circles):
        last_one = r == some - 1
        mixes = call(
            functools.partial(circle_kernel, levels, len(done) if last_one else 0),
            [piece if last_one else (cols, channels)] * levels,
            [lon_proj, *(done if last_one else []), *circle],
            flops=work // 4,
        )
        done = done + list(mixes)
    mixes = exchange(mixes)
    (out,) = call(
        functools.partial(last_kernel, levels),
        [(rows, cols, channels)],
        [*mixes, inner_two, outer_two, lon_proj],
    )
    return out


def solution(mesh):
    return jax.shard_map(
        shards,
        mesh=mesh,
        in_specs=(P("lat", "lon", None), P(), P(), P(), P(), P()),
        out_specs=P("lat", "lon", None),
        check_vma=False,
    )
```

```python
import functools

import jax
import jax.numpy as jnp
from jax import lax
from jax.experimental import pallas as pl
from jax.experimental.pallas import tpu as pltpu
from jax.sharding import PartitionSpec as P

HEADS = 8
HALO = 3
TAPS = 2 * HALO + 1
STRIP = 8
SIDE = 4
LANES = 128
LEVELS = 4
STAGES = 4
EPSILON = 1e-06
VMEM_BYTES = 24 * 1024 * 1024
STAGE_BYTES = 103 * 512 * 1024
bf16, f32 = jnp.bfloat16, jnp.float32


def layer_norm(values):
    average = jnp.mean(values, axis=-1, keepdims=True)
    centered = values - average
    variance = jnp.mean(centered * centered, axis=-1, keepdims=True)
    return centered * lax.rsqrt(variance + EPSILON)


def dot(rows, matrix):
    return jnp.dot(rows, matrix, preferred_element_type=f32)


def dot_t(rows, matrix):
    return lax.dot_general(rows, matrix, (((1,), (1,)), ((), ())), preferred_element_type=f32)


def gelu(values):
    size = jnp.abs(values)
    t = pl.reciprocal(1.0 + (0.3275911 * 0.5**0.5) * size, approx=True)
    tail = 1.061405429 * t - 1.453152027
    for coefficient in (1.421413741, -0.284496736, 0.254829592):
        tail = tail * t + coefficient
    tail = (0.5 * size * t) * tail * jnp.exp(-0.5 * values * values)
    return jnp.maximum(values, 0.0) - tail


def attend(queries, keys, values, mask):
    count, channels = queries.shape
    head_size = channels // HEADS
    lane_head = lax.broadcasted_iota(jnp.int32, (1, channels), 1) // head_size
    picks = [lane_head == h for h in range(HEADS)]
    none = jnp.zeros_like(queries)
    stacked = jnp.concatenate([jnp.where(pick, queries, none) for pick in picks], axis=0)
    scores = dot_t(stacked, keys) * head_size ** (-0.5)
    if mask is not None:
        scores = scores.reshape(HEADS, count, keys.shape[0])
        scores = jnp.where(mask[None], scores, -1e30).reshape(HEADS * count, keys.shape[0])
    top = jnp.max(scores, axis=-1, keepdims=True)
    probs = jnp.exp(scores - top)
    totals = jnp.sum(probs, axis=-1, keepdims=True)
    mixed = dot(probs.astype(bf16), values) * pl.reciprocal(totals, approx=True)
    out = mixed[:count]
    for h in range(1, HEADS):
        out = jnp.where(picks[h], mixed[h * count : (h + 1) * count], out)
    return out.astype(bf16)


def stage_kernel(count, *refs):
    sources, dw_ref = refs[:count], refs[count]
    targets, taps_ref, dw, sems = refs[count + 1 : 2 * count + 1], *refs[2 * count + 1 :]
    copies = [pltpu.make_async_copy(dw_ref, dw, sems.at[count, 0])]
    pieces = sems.shape[1]
    for i in range(count):
        source, target = sources[i], targets[i]
        size = source.shape[0] // pieces
        for k in range(pieces):
            part = pl.ds(k * size, size)
            copies.append(pltpu.make_async_copy(source.at[part], target.at[part], sems.at[i, k]))
    for copy in copies:
        copy.start()
    for copy in copies:
        copy.wait()
    taps_ref[...] = dw[...].astype(f32)


def peer(levels, k):
    level = lax.axis_index("lon") // (lax.axis_size("lon") // levels)
    return level ^ ((levels - k) % levels)


def strip_kernel(nlat, *refs):
    tiles = refs[:nlat]
    near_ref, far_ref, near, far = refs[nlat + 1 :]
    rows, cols, channels = tiles[0].shape
    even = lax.axis_index("lon") % 2 == 0
    for s in range(nlat):
        values = tiles[s][...].astype(f32)
        first, last = values[:, :STRIP], values[:, cols - STRIP :]
        where = pl.ds(lax.rem(lax.axis_index("lat") + s, nlat) * rows, rows)
        near[where] = jnp.where(even, last, first)
        far[where] = jnp.where(even, first, last)
    for strip, strip_ref, is_last in ((near, near_ref, even), (far, far_ref, ~even)):
        strip_ref[...] = pack(strip[...], is_last).reshape(strip_ref.shape).astype(bf16)


def lower_half():
    return lax.broadcasted_iota(jnp.int32, (1, STRIP, 1), 1) < SIDE


def turn(values):
    return jnp.concatenate([values[:, SIDE:], values[:, :SIDE]], axis=1)


def pack(strip, is_last):
    half = strip.shape[0] // 2
    turned = turn(strip)
    low = jnp.where(is_last, turned, strip)
    high = jnp.where(is_last, strip, turned)
    return jnp.where(lower_half(), low[:half], high[half:])


def unpack(packed, is_left):
    turned = turn(packed)
    low = jnp.where(is_left, turned, packed)
    high = jnp.where(is_left, packed, turned)
    return jnp.concatenate([low, high], axis=0)


def chain(my_lat, slab, shape, taps_ref, expand_ref, reduce_ref, attn_ref, center, scratch):
    one, lat_in = scratch
    rows, all_rows, columns, channels = shape
    cells = all_rows * columns
    parts = []
    for c in range(0, channels, LANES):
        acc = jnp.zeros((all_rows, columns, LANES), f32)
        for b in range(TAPS):
            block = slab(b, c)
            for a in range(TAPS):
                tap = taps_ref[a, b : b + 1, c : c + LANES].reshape(1, 1, LANES)
                acc = acc + block[a : a + all_rows] * tap
        parts.append(acc.reshape(cells, LANES))
    normed = layer_norm(jnp.concatenate(parts, axis=-1)).astype(bf16)

    def widen(k, total):
        part = slice(k * channels, (k + 1) * channels)
        wide = gelu(dot(normed, expand_ref[:, part])).astype(bf16)
        return total + dot(wide, reduce_ref[part])

    total = center.reshape(cells, channels)
    for k in range(expand_ref.shape[1] // channels):
        total = widen(k, total)
    block_one = total.astype(bf16)
    one[...] = block_one
    every = layer_norm(block_one.astype(f32)).astype(bf16)
    lat_in[...] = every
    count = rows * columns
    own = pl.ds(pl.multiple_of(my_lat * count, count), count)
    queries = dot(lat_in[own], attn_ref[0]).astype(bf16)
    keys = dot(every, attn_ref[1]).astype(bf16)
    values = dot(every, attn_ref[2]).astype(bf16)
    row_col = lax.broadcasted_iota(jnp.int32, (count, 1), 0) % columns
    key_col = lax.broadcasted_iota(jnp.int32, (1, cells), 1) % columns
    mix = attend(queries, keys, values, row_col == key_col)
    block_two = (one[own].astype(f32) + dot(mix, attn_ref[3])).astype(bf16)
    return block_two, layer_norm(block_two.astype(f32))


def fill(padded, all_rows, first, values):
    width = values.shape[1]
    padded[HALO : HALO + all_rows, first : first + width] = values


def fill_tiles(padded, my_lat, first, tiles):
    rows, cols = tiles[0].shape[:2]
    for s in range(len(tiles)):
        place = HALO + lax.rem(my_lat + s, len(tiles)) * rows
        padded[pl.ds(place, rows), first : first + cols] = tiles[s][...].astype(f32)


def clear(padded, all_rows):
    edge = jnp.zeros((HALO,) + padded.shape[1:], f32)
    padded[:HALO] = edge
    padded[HALO + all_rows :] = edge


def inner_kernel(nlat, *refs):
    tiles, refs = refs[:nlat], refs[nlat:]
    taps_ref, expand_ref, reduce_ref, attn_ref, two_ref, in_ref, padded, *scratch = refs
    rows, cols, channels = tiles[0].shape
    all_rows = rows * nlat
    columns = cols - 2 * SIDE
    clear(padded, all_rows)
    my_lat = lax.axis_index("lat")
    fill_tiles(padded, my_lat, 0, tiles)

    def slab(b, c):
        first = SIDE - HALO + b
        return padded[:, first : first + columns, c : c + LANES]

    center = padded[HALO : HALO + all_rows, SIDE : SIDE + columns]
    shape = (rows, all_rows, columns, channels)
    block_two, lon_in = chain(
        my_lat, slab, shape, taps_ref, expand_ref, reduce_ref, attn_ref, center, scratch
    )
    two_ref[...] = block_two
    in_ref[...] = lon_in.astype(bf16)


def outer_kernel(nlat, levels, *refs):
    tiles, refs = refs[:nlat], refs[nlat:]
    far_ref, near_ref, inner_in_ref, taps_ref, expand_ref, reduce_ref, attn_ref = refs[:7]
    two_ref, *refs = refs[7:]
    sent_refs, (sent, padded, *scratch) = refs[:levels], refs[levels:]
    rows, cols, channels = tiles[0].shape
    all_rows = rows * nlat
    columns = 2 * SIDE
    packed = (all_rows // 2, STRIP, channels)
    near = near_ref[...].astype(f32).reshape(packed)
    far = far_ref[...].astype(f32).reshape(packed)
    even = lax.axis_index("lon") % 2 == 0
    my_lat = lax.axis_index("lat")
    clear(padded, all_rows)
    fill(padded, all_rows, 0, unpack(jnp.where(even, far, near), True))
    fill_tiles(padded, my_lat, STRIP, tiles)
    fill(padded, all_rows, STRIP + cols, unpack(jnp.where(even, near, far), False))
    sublane = lax.broadcasted_iota(jnp.int32, (1, columns, 1), 1)

    def halves(shift, rows_of, c, width):
        right = STRIP + cols - SIDE + shift
        left = STRIP - SIDE + shift
        return jnp.where(
            sublane < SIDE,
            padded[rows_of, right : right + columns, c : c + width],
            padded[rows_of, left : left + columns, c : c + width],
        )

    def slab(b, c):
        return halves(b - HALO, slice(None), c, LANES)

    center = halves(0, slice(HALO, HALO + all_rows), 0, channels)
    shape = (rows, all_rows, columns, channels)
    block_two, lon_in = chain(
        my_lat, slab, shape, taps_ref, expand_ref, reduce_ref, attn_ref, center, scratch
    )
    two_ref[...] = block_two
    inner = inner_in_ref[...].astype(f32).reshape(rows, cols - columns, channels)
    outer = lon_in.reshape(rows, columns, channels)
    sent[...] = jnp.concatenate([inner, outer], axis=1).astype(bf16)
    some = rows // levels
    for k in range(levels):
        part = sent[pl.ds(peer(levels, k) * some, some)]
        sent_refs[k][...] = part.reshape(sent_refs[k].shape)


def join_kernel(levels, some, *refs):
    parts, joined = refs[:levels], refs[levels:]
    cols = parts[0].shape[0] // some
    for r in range(some):
        for k in range(levels):
            joined[r][k * cols : (k + 1) * cols] = parts[k][r * cols : (r + 1) * cols]


def circle_kernel(levels, before, *refs):
    attn_ref, refs = refs[0], refs[1:]
    done, refs = refs[:before], refs[before:]
    parts, mix_refs = refs[:-levels], refs[-levels:]
    own = parts[0][...]
    every = jnp.concatenate([own] + [part[...] for part in parts[1:]], axis=0)
    queries = dot(own, attn_ref[0]).astype(bf16)
    keys = dot(every, attn_ref[1]).astype(bf16)
    values = dot(every, attn_ref[2]).astype(bf16)
    mix = attend(queries, keys, values, None)
    cols = own.shape[0] // levels
    for k in range(levels):
        for r in range(before // levels):
            mix_refs[k][r * cols : (r + 1) * cols] = done[r * levels + k][...]
        mix_refs[k][before // levels * cols :] = mix[k * cols : (k + 1) * cols]


def last_kernel(levels, *refs):
    parts = refs[:levels]
    inner_ref, outer_ref, attn_ref, out_ref = refs[levels:]
    rows, cols, channels = out_ref.shape
    columns = 2 * SIDE
    some = rows // levels
    every = jnp.concatenate([part[...] for part in parts], axis=0)
    change = dot(every, attn_ref[3]).reshape(levels, some, cols, channels)
    for k in range(levels):
        start = peer(levels, k) * some

        def state(ref, width):
            count = some * width
            place = pl.ds(pl.multiple_of(start * width, count), count)
            return ref[place].astype(f32).reshape(some, width, channels)

        inner = state(inner_ref, cols - columns) + change[k, :, : cols - columns]
        outer = state(outer_ref, columns) + change[k, :, cols - columns :]
        total = jnp.concatenate([outer[:, SIDE:], inner, outer[:, :SIDE]], axis=1)
        out_ref[pl.ds(start, some)] = total.astype(bf16)


def call(
    kernel, outs, operands, scratch=(), any_space=False, flops=0, grant=VMEM_BYTES
):
    vmem = pl.BlockSpec(memory_space=pltpu.VMEM)
    given = pl.BlockSpec(memory_space=pl.ANY) if any_space else vmem
    shapes = [
        out if isinstance(out, jax.ShapeDtypeStruct) else jax.ShapeDtypeStruct(out, bf16)
        for out in outs
    ]
    moved = sum(x.size * x.dtype.itemsize for x in operands)
    result = pl.pallas_call(
        kernel,
        out_shape=shapes,
        in_specs=[given] * len(operands),
        out_specs=[vmem] * len(outs),
        scratch_shapes=list(scratch),
        compiler_params=pltpu.CompilerParams(vmem_limit_bytes=grant),
        cost_estimate=pl.CostEstimate(flops=flops, bytes_accessed=moved, transcendentals=0),
    )(*operands)
    return result


def shards(field, dw_weight, w_expand, w_reduce, lat_attn, lon_attn):
    rows, cols, channels = field.shape
    nlat, nlon = lax.axis_size("lat"), lax.axis_size("lon")
    levels = min(LEVELS, nlon)
    column = nlon // levels
    some = rows // levels
    all_rows = rows * nlat
    columns = 2 * SIDE

    def swap(piece, mask):
        return lax.ppermute(piece, "lon", [(j, j ^ mask) for j in range(nlon)])

    def exchange(pieces):
        moved = []
        for k in range(1, levels):
            level = levels - k
            moved.append(swap(pieces[k], level * column + min(1, column - 1)))
        return [pieces[0]] + moved

    tiles = [field]
    for s in range(1, nlat):
        tiles.append(lax.ppermute(field, "lat", [((i + s) % nlat, i) for i in range(nlat)]))
    weights = (w_expand, w_reduce, lat_attn, lon_attn)
    expand, reduce, lat_proj, lon_proj, taps = call(
        functools.partial(stage_kernel, len(weights)),
        [w.shape for w in weights] + [jax.ShapeDtypeStruct(dw_weight.shape, f32)],
        [*weights, dw_weight],
        [
            pltpu.VMEM(dw_weight.shape, bf16),
            pltpu.SemaphoreType.DMA((len(weights) + 1, STAGES)),
        ],
        any_space=True,
        grant=STAGE_BYTES,
    )

    strip = (all_rows * SIDE, channels)
    strip_scratch = pltpu.VMEM((all_rows, STRIP, channels), f32)
    near, far = call(
        functools.partial(strip_kernel, nlat),
        [strip, strip],
        [*tiles, reduce],
        [strip_scratch, strip_scratch],
    )
    far = lax.ppermute(
        far, "lon", [(j, (j - 1) % nlon if j % 2 == 0 else (j + 1) % nlon) for j in range(nlon)]
    )
    near = swap(near, 1)

    def scratch(width, count):
        return [
            pltpu.VMEM((all_rows + 2 * HALO, width, channels), f32),
            pltpu.VMEM((all_rows * count, channels), bf16),
            pltpu.VMEM((all_rows * count, channels), bf16),
        ]

    work = 4 * all_rows * columns * channels * w_expand.shape[1]
    inner_two, inner_in = call(
        functools.partial(inner_kernel, nlat),
        [(rows * (cols - columns), channels)] * 2,
        [*tiles, taps, expand, reduce, lat_proj],
        scratch(cols, cols - columns),
        flops=work,
    )
    piece = (some * cols, channels)
    outer_two, *parts = call(
        functools.partial(outer_kernel, nlat, levels),
        [(rows * columns, channels)] + [piece] * levels,
        [*tiles, far, near, inner_in, taps, expand, reduce, lat_proj],
        [pltpu.VMEM((rows, cols, channels), bf16)] + scratch(cols + 2 * STRIP, columns),
        flops=work,
    )

    parts = exchange(parts)
    joined = call(
        functools.partial(join_kernel, levels, some), [(levels * cols, channels)] * some, parts
    )
    circles = [[part] for part in joined]
    mask = column // 2
    while mask:
        for circle in circles:
            circle += [swap(part, mask + mask // 2) for part in circle]
        mask //= 2
    done = []
    for r, circle in enumerate(circles):
        last_one = r == some - 1
        mixes = call(
            functools.partial(circle_kernel, levels, len(done) if last_one else 0),
            [piece if last_one else (cols, channels)] * levels,
            [lon_proj, *(done if last_one else []), *circle],
            flops=work // 4,
        )
        done = done + list(mixes)
    mixes = exchange(mixes)
    (out,) = call(
        functools.partial(last_kernel, levels),
        [(rows, cols, channels)],
        [*mixes, inner_two, outer_two, lon_proj],
    )
    return out


def solution(mesh):
    return jax.shard_map(
        shards,
        mesh=mesh,
        in_specs=(P("lat", "lon", None), P(), P(), P(), P(), P()),
        out_specs=P("lat", "lon", None),
        check_vma=False,
    )
```

```python
import functools

import jax
import jax.numpy as jnp
from jax import lax
from jax.experimental import pallas as pl
from jax.experimental.pallas import tpu as pltpu
from jax.sharding import PartitionSpec as P

HEADS = 8
HALO = 3
TAPS = 2 * HALO + 1
STRIP = 8
SIDE = 4
LANES = 128
LEVELS = 4
STAGES = 4
EPSILON = 1e-06
VMEM_BYTES = 24 * 1024 * 1024
STAGE_BYTES = 103 * 512 * 1024
bf16, f32 = jnp.bfloat16, jnp.float32


def layer_norm(values):
    average = jnp.mean(values, axis=-1, keepdims=True)
    centered = values - average
    variance = jnp.mean(centered * centered, axis=-1, keepdims=True)
    return centered * lax.rsqrt(variance + EPSILON)


def dot(rows, matrix):
    return jnp.dot(rows, matrix, preferred_element_type=f32)


def dot_t(rows, matrix):
    return lax.dot_general(rows, matrix, (((1,), (1,)), ((), ())), preferred_element_type=f32)


def gelu(values):
    size = jnp.abs(values)
    t = 1.0 / (1.0 + (0.3275911 * 0.5**0.5) * size)
    tail = 1.061405429 * t - 1.453152027
    for coefficient in (1.421413741, -0.284496736, 0.254829592):
        tail = tail * t + coefficient
    tail = (0.5 * size * t) * tail * jnp.exp(-0.5 * values * values)
    return jnp.maximum(values, 0.0) - tail


def attend(queries, keys, values, mask):
    count, channels = queries.shape
    head_size = channels // HEADS
    lane_head = lax.broadcasted_iota(jnp.int32, (1, channels), 1) // head_size
    picks = [lane_head == h for h in range(HEADS)]
    none = jnp.zeros_like(queries)
    stacked = jnp.concatenate([jnp.where(pick, queries, none) for pick in picks], axis=0)
    scores = dot_t(stacked, keys) * head_size ** (-0.5)
    if mask is not None:
        scores = scores.reshape(HEADS, count, keys.shape[0])
        scores = jnp.where(mask[None], scores, -1e30).reshape(HEADS * count, keys.shape[0])
    top = jnp.max(scores, axis=-1, keepdims=True)
    probs = jnp.exp(scores - top)
    totals = jnp.sum(probs, axis=-1, keepdims=True)
    mixed = dot(probs.astype(bf16), values) * (1.0 / totals)
    out = mixed[:count]
    for h in range(1, HEADS):
        out = jnp.where(picks[h], mixed[h * count : (h + 1) * count], out)
    return out.astype(bf16)


def stage_kernel(count, *refs):
    sources, dw_ref = refs[:count], refs[count]
    targets, taps_ref, dw, sems = refs[count + 1 : 2 * count + 1], *refs[2 * count + 1 :]
    copies = [pltpu.make_async_copy(dw_ref, dw, sems.at[count, 0])]
    pieces = sems.shape[1]
    for i in range(count):
        source, target = sources[i], targets[i]
        size = source.shape[0] // pieces
        for k in range(pieces):
            part = pl.ds(k * size, size)
            copies.append(pltpu.make_async_copy(source.at[part], target.at[part], sems.at[i, k]))
    for copy in copies:
        copy.start()
    for copy in copies:
        copy.wait()
    taps_ref[...] = dw[...].astype(f32)


def peer(levels, k):
    level = lax.axis_index("lon") // (lax.axis_size("lon") // levels)
    return level ^ ((levels - k) % levels)


def strip_kernel(nlat, *refs):
    tiles = refs[:nlat]
    near_ref, far_ref, near, far = refs[nlat + 1 :]
    rows, cols, channels = tiles[0].shape
    even = lax.axis_index("lon") % 2 == 0
    for s in range(nlat):
        values = tiles[s][...].astype(f32)
        first, last = values[:, :STRIP], values[:, cols - STRIP :]
        where = pl.ds(lax.rem(lax.axis_index("lat") + s, nlat) * rows, rows)
        near[where] = jnp.where(even, last, first)
        far[where] = jnp.where(even, first, last)
    for strip, strip_ref, is_last in ((near, near_ref, even), (far, far_ref, ~even)):
        strip_ref[...] = pack(strip[...], is_last).reshape(strip_ref.shape).astype(bf16)


def lower_half():
    return lax.broadcasted_iota(jnp.int32, (1, STRIP, 1), 1) < SIDE


def turn(values):
    return jnp.concatenate([values[:, SIDE:], values[:, :SIDE]], axis=1)


def pack(strip, is_last):
    half = strip.shape[0] // 2
    turned = turn(strip)
    low = jnp.where(is_last, turned, strip)
    high = jnp.where(is_last, strip, turned)
    return jnp.where(lower_half(), low[:half], high[half:])


def unpack(packed, is_left):
    turned = turn(packed)
    low = jnp.where(is_left, turned, packed)
    high = jnp.where(is_left, packed, turned)
    return jnp.concatenate([low, high], axis=0)


def chain(my_lat, slab, shape, taps_ref, expand_ref, reduce_ref, attn_ref, center, scratch):
    one, lat_in = scratch
    rows, all_rows, columns, channels = shape
    cells = all_rows * columns
    parts = []
    for c in range(0, channels, LANES):
        acc = jnp.zeros((all_rows, columns, LANES), f32)
        for b in range(TAPS):
            block = slab(b, c)
            for a in range(TAPS):
                tap = taps_ref[a, b : b + 1, c : c + LANES].reshape(1, 1, LANES)
                acc = acc + block[a : a + all_rows] * tap
        parts.append(acc.reshape(cells, LANES))
    normed = layer_norm(jnp.concatenate(parts, axis=-1)).astype(bf16)

    def widen(k, total):
        part = slice(k * channels, (k + 1) * channels)
        wide = gelu(dot(normed, expand_ref[:, part]).astype(bf16))
        return total + dot(wide, reduce_ref[part])

    total = center.reshape(cells, channels)
    for k in range(expand_ref.shape[1] // channels):
        total = widen(k, total)
    block_one = total.astype(bf16)
    one[...] = block_one
    every = layer_norm(block_one.astype(f32)).astype(bf16)
    lat_in[...] = every
    count = rows * columns
    own = pl.ds(pl.multiple_of(my_lat * count, count), count)
    queries = dot(lat_in[own], attn_ref[0]).astype(bf16)
    keys = dot(every, attn_ref[1]).astype(bf16)
    values = dot(every, attn_ref[2]).astype(bf16)
    row_col = lax.broadcasted_iota(jnp.int32, (count, 1), 0) % columns
    key_col = lax.broadcasted_iota(jnp.int32, (1, cells), 1) % columns
    mix = attend(queries, keys, values, row_col == key_col)
    block_two = (one[own].astype(f32) + dot(mix, attn_ref[3])).astype(bf16)
    return block_two, layer_norm(block_two.astype(f32))


def fill(padded, all_rows, first, values):
    width = values.shape[1]
    padded[HALO : HALO + all_rows, first : first + width] = values


def fill_tiles(padded, my_lat, first, tiles):
    rows, cols = tiles[0].shape[:2]
    for s in range(len(tiles)):
        place = HALO + lax.rem(my_lat + s, len(tiles)) * rows
        padded[pl.ds(place, rows), first : first + cols] = tiles[s][...].astype(f32)


def clear(padded, all_rows):
    edge = jnp.zeros((HALO,) + padded.shape[1:], f32)
    padded[:HALO] = edge
    padded[HALO + all_rows :] = edge


def inner_kernel(nlat, *refs):
    tiles, refs = refs[:nlat], refs[nlat:]
    taps_ref, expand_ref, reduce_ref, attn_ref, two_ref, in_ref, padded, *scratch = refs
    rows, cols, channels = tiles[0].shape
    all_rows = rows * nlat
    columns = cols - 2 * SIDE
    clear(padded, all_rows)
    my_lat = lax.axis_index("lat")
    fill_tiles(padded, my_lat, 0, tiles)

    def slab(b, c):
        first = SIDE - HALO + b
        return padded[:, first : first + columns, c : c + LANES]

    center = padded[HALO : HALO + all_rows, SIDE : SIDE + columns]
    shape = (rows, all_rows, columns, channels)
    block_two, lon_in = chain(
        my_lat, slab, shape, taps_ref, expand_ref, reduce_ref, attn_ref, center, scratch
    )
    two_ref[...] = block_two
    in_ref[...] = lon_in.astype(bf16)


def outer_kernel(nlat, levels, *refs):
    tiles, refs = refs[:nlat], refs[nlat:]
    far_ref, near_ref, inner_in_ref, taps_ref, expand_ref, reduce_ref, attn_ref = refs[:7]
    two_ref, *refs = refs[7:]
    sent_refs, (sent, padded, *scratch) = refs[:levels], refs[levels:]
    rows, cols, channels = tiles[0].shape
    all_rows = rows * nlat
    columns = 2 * SIDE
    packed = (all_rows // 2, STRIP, channels)
    near = near_ref[...].astype(f32).reshape(packed)
    far = far_ref[...].astype(f32).reshape(packed)
    even = lax.axis_index("lon") % 2 == 0
    my_lat = lax.axis_index("lat")
    clear(padded, all_rows)
    fill(padded, all_rows, 0, unpack(jnp.where(even, far, near), True))
    fill_tiles(padded, my_lat, STRIP, tiles)
    fill(padded, all_rows, STRIP + cols, unpack(jnp.where(even, near, far), False))
    sublane = lax.broadcasted_iota(jnp.int32, (1, columns, 1), 1)

    def halves(shift, rows_of, c, width):
        right = STRIP + cols - SIDE + shift
        left = STRIP - SIDE + shift
        return jnp.where(
            sublane < SIDE,
            padded[rows_of, right : right + columns, c : c + width],
            padded[rows_of, left : left + columns, c : c + width],
        )

    def slab(b, c):
        return halves(b - HALO, slice(None), c, LANES)

    center = halves(0, slice(HALO, HALO + all_rows), 0, channels)
    shape = (rows, all_rows, columns, channels)
    block_two, lon_in = chain(
        my_lat, slab, shape, taps_ref, expand_ref, reduce_ref, attn_ref, center, scratch
    )
    two_ref[...] = block_two
    inner = inner_in_ref[...].astype(f32).reshape(rows, cols - columns, channels)
    outer = lon_in.reshape(rows, columns, channels)
    sent[...] = jnp.concatenate([inner, outer], axis=1).astype(bf16)
    some = rows // levels
    for k in range(levels):
        part = sent[pl.ds(peer(levels, k) * some, some)]
        sent_refs[k][...] = part.reshape(sent_refs[k].shape)


def join_kernel(levels, some, *refs):
    parts, joined = refs[:levels], refs[levels:]
    cols = parts[0].shape[0] // some
    for r in range(some):
        for k in range(levels):
            joined[r][k * cols : (k + 1) * cols] = parts[k][r * cols : (r + 1) * cols]


def circle_kernel(levels, before, *refs):
    attn_ref, refs = refs[0], refs[1:]
    done, refs = refs[:before], refs[before:]
    parts, mix_refs = refs[:-levels], refs[-levels:]
    own = parts[0][...]
    every = jnp.concatenate([own] + [part[...] for part in parts[1:]], axis=0)
    queries = dot(own, attn_ref[0]).astype(bf16)
    keys = dot(every, attn_ref[1]).astype(bf16)
    values = dot(every, attn_ref[2]).astype(bf16)
    mix = attend(queries, keys, values, None)
    cols = own.shape[0] // levels
    for k in range(levels):
        for r in range(before // levels):
            mix_refs[k][r * cols : (r + 1) * cols] = done[r * levels + k][...]
        mix_refs[k][before // levels * cols :] = mix[k * cols : (k + 1) * cols]


def last_kernel(levels, *refs):
    parts = refs[:levels]
    inner_ref, outer_ref, attn_ref, out_ref = refs[levels:]
    rows, cols, channels = out_ref.shape
    columns = 2 * SIDE
    some = rows // levels
    every = jnp.concatenate([part[...] for part in parts], axis=0)
    change = dot(every, attn_ref[3]).reshape(levels, some, cols, channels)
    for k in range(levels):
        start = peer(levels, k) * some

        def state(ref, width):
            count = some * width
            place = pl.ds(pl.multiple_of(start * width, count), count)
            return ref[place].astype(f32).reshape(some, width, channels)

        inner = state(inner_ref, cols - columns) + change[k, :, : cols - columns]
        outer = state(outer_ref, columns) + change[k, :, cols - columns :]
        total = jnp.concatenate([outer[:, SIDE:], inner, outer[:, :SIDE]], axis=1)
        out_ref[pl.ds(start, some)] = total.astype(bf16)


def call(
    kernel, outs, operands, scratch=(), any_space=False, flops=0, grant=VMEM_BYTES
):
    vmem = pl.BlockSpec(memory_space=pltpu.VMEM)
    given = pl.BlockSpec(memory_space=pl.ANY) if any_space else vmem
    shapes = [
        out if isinstance(out, jax.ShapeDtypeStruct) else jax.ShapeDtypeStruct(out, bf16)
        for out in outs
    ]
    moved = sum(x.size * x.dtype.itemsize for x in operands)
    result = pl.pallas_call(
        kernel,
        out_shape=shapes,
        in_specs=[given] * len(operands),
        out_specs=[vmem] * len(outs),
        scratch_shapes=list(scratch),
        compiler_params=pltpu.CompilerParams(vmem_limit_bytes=grant),
        cost_estimate=pl.CostEstimate(flops=flops, bytes_accessed=moved, transcendentals=0),
    )(*operands)
    return result


def shards(field, dw_weight, w_expand, w_reduce, lat_attn, lon_attn):
    rows, cols, channels = field.shape
    nlat, nlon = lax.axis_size("lat"), lax.axis_size("lon")
    levels = min(LEVELS, nlon)
    column = nlon // levels
    some = rows // levels
    all_rows = rows * nlat
    columns = 2 * SIDE

    def swap(piece, mask):
        return lax.ppermute(piece, "lon", [(j, j ^ mask) for j in range(nlon)])

    def exchange(pieces):
        moved = []
        for k in range(1, levels):
            level = levels - k
            moved.append(swap(pieces[k], level * column + min(1, column - 1)))
        return [pieces[0]] + moved

    tiles = [field]
    for s in range(1, nlat):
        tiles.append(lax.ppermute(field, "lat", [((i + s) % nlat, i) for i in range(nlat)]))
    weights = (w_expand, w_reduce, lat_attn, lon_attn)
    expand, reduce, lat_proj, lon_proj, taps = call(
        functools.partial(stage_kernel, len(weights)),
        [w.shape for w in weights] + [jax.ShapeDtypeStruct(dw_weight.shape, f32)],
        [*weights, dw_weight],
        [
            pltpu.VMEM(dw_weight.shape, bf16),
            pltpu.SemaphoreType.DMA((len(weights) + 1, STAGES)),
        ],
        any_space=True,
        grant=STAGE_BYTES,
    )

    strip = (all_rows * SIDE, channels)
    strip_scratch = pltpu.VMEM((all_rows, STRIP, channels), f32)
    near, far = call(
        functools.partial(strip_kernel, nlat),
        [strip, strip],
        [*tiles, reduce],
        [strip_scratch, strip_scratch],
    )
    far = lax.ppermute(
        far, "lon", [(j, (j - 1) % nlon if j % 2 == 0 else (j + 1) % nlon) for j in range(nlon)]
    )
    near = swap(near, 1)

    def scratch(width, count):
        return [
            pltpu.VMEM((all_rows + 2 * HALO, width, channels), f32),
            pltpu.VMEM((all_rows * count, channels), bf16),
            pltpu.VMEM((all_rows * count, channels), bf16),
        ]

    work = 4 * all_rows * columns * channels * w_expand.shape[1]
    inner_two, inner_in = call(
        functools.partial(inner_kernel, nlat),
        [(rows * (cols - columns), channels)] * 2,
        [*tiles, taps, expand, reduce, lat_proj],
        scratch(cols, cols - columns),
        flops=work,
    )
    piece = (some * cols, channels)
    outer_two, *parts = call(
        functools.partial(outer_kernel, nlat, levels),
        [(rows * columns, channels)] + [piece] * levels,
        [*tiles, far, near, inner_in, taps, expand, reduce, lat_proj],
        [pltpu.VMEM((rows, cols, channels), bf16)] + scratch(cols + 2 * STRIP, columns),
        flops=work,
    )

    parts = exchange(parts)
    joined = call(
        functools.partial(join_kernel, levels, some), [(levels * cols, channels)] * some, parts
    )
    circles = [[part] for part in joined]
    mask = column // 2
    while mask:
        for circle in circles:
            circle += [swap(part, mask + mask // 2) for part in circle]
        mask //= 2
    done = []
    for r, circle in enumerate(circles):
        last_one = r == some - 1
        mixes = call(
            functools.partial(circle_kernel, levels, len(done) if last_one else 0),
            [piece if last_one else (cols, channels)] * levels,
            [lon_proj, *(done if last_one else []), *circle],
            flops=work // 4,
        )
        done = done + list(mixes)
    mixes = exchange(mixes)
    (out,) = call(
        functools.partial(last_kernel, levels),
        [(rows, cols, channels)],
        [*mixes, inner_two, outer_two, lon_proj],
    )
    return out


def solution(mesh):
    return jax.shard_map(
        shards,
        mesh=mesh,
        in_specs=(P("lat", "lon", None), P(), P(), P(), P(), P()),
        out_specs=P("lat", "lon", None),
        check_vma=False,
    )
```

```python
import functools

import jax
import jax.numpy as jnp
from jax import lax
from jax.experimental import pallas as pl
from jax.experimental.pallas import tpu as pltpu
from jax.sharding import PartitionSpec as P

HEADS = 8
HALO = 3
TAPS = 2 * HALO + 1
STRIP = 8
SIDE = 4
LANES = 128
LEVELS = 4
STAGES = 4
EPSILON = 1e-06
VMEM_BYTES = 24 * 1024 * 1024
STAGE_BYTES = 103 * 512 * 1024
bf16, f32 = jnp.bfloat16, jnp.float32


def layer_norm(values):
    average = jnp.mean(values, axis=-1, keepdims=True)
    centered = values - average
    variance = jnp.mean(centered * centered, axis=-1, keepdims=True)
    return centered * lax.rsqrt(variance + EPSILON)


def dot(rows, matrix):
    return jnp.dot(rows, matrix, preferred_element_type=f32)


def dot_t(rows, matrix):
    return lax.dot_general(rows, matrix, (((1,), (1,)), ((), ())), preferred_element_type=f32)


def gelu(values):
    size = jnp.abs(values)
    t = 1.0 / (1.0 + (0.3275911 * 0.5**0.5) * size)
    tail = 1.061405429 * t - 1.453152027
    for coefficient in (1.421413741, -0.284496736, 0.254829592):
        tail = tail * t + coefficient
    tail = (0.5 * size * t) * tail * jnp.exp(-0.5 * values * values)
    return jnp.maximum(values, 0.0) - tail


def attend(queries, keys, values, mask):
    count, channels = queries.shape
    head_size = channels // HEADS
    lane_head = lax.broadcasted_iota(jnp.int32, (1, channels), 1) // head_size
    picks = [lane_head == h for h in range(HEADS)]
    none = jnp.zeros_like(queries)
    stacked = jnp.concatenate([jnp.where(pick, queries, none) for pick in picks], axis=0)
    scores = dot_t(stacked, keys) * head_size ** (-0.5)
    if mask is not None:
        scores = scores.reshape(HEADS, count, keys.shape[0])
        scores = jnp.where(mask[None], scores, -1e30).reshape(HEADS * count, keys.shape[0])
    top = jnp.max(scores, axis=-1, keepdims=True)
    probs = jnp.exp(scores - top)
    totals = jnp.sum(probs, axis=-1, keepdims=True)
    mixed = dot(probs.astype(bf16), values) * (1.0 / totals)
    out = mixed[:count]
    for h in range(1, HEADS):
        out = jnp.where(picks[h], mixed[h * count : (h + 1) * count], out)
    return out.astype(bf16)


def stage_kernel(count, *refs):
    sources, dw_ref = refs[:count], refs[count]
    targets, taps_ref, dw, sems = refs[count + 1 : 2 * count + 1], *refs[2 * count + 1 :]
    copies = [pltpu.make_async_copy(dw_ref, dw, sems.at[count, 0])]
    pieces = sems.shape[1]
    for i in range(count):
        source, target = sources[i], targets[i]
        size = source.shape[0] // pieces
        for k in range(pieces):
            part = pl.ds(k * size, size)
            copies.append(pltpu.make_async_copy(source.at[part], target.at[part], sems.at[i, k]))
    for copy in copies:
        copy.start()
    for copy in copies:
        copy.wait()
    taps_ref[...] = dw[...].astype(f32)


def peer(levels, k):
    level = lax.axis_index("lon") // (lax.axis_size("lon") // levels)
    return level ^ ((levels - k) % levels)


def strip_kernel(nlat, *refs):
    tiles = refs[:nlat]
    near_ref, far_ref, near, far = refs[nlat + 1 :]
    rows, cols, channels = tiles[0].shape
    even = lax.axis_index("lon") % 2 == 0
    for s in range(nlat):
        values = tiles[s][...].astype(f32)
        first, last = values[:, :STRIP], values[:, cols - STRIP :]
        where = pl.ds(lax.rem(lax.axis_index("lat") + s, nlat) * rows, rows)
        near[where] = jnp.where(even, last, first)
        far[where] = jnp.where(even, first, last)
    for strip, strip_ref, is_last in ((near, near_ref, even), (far, far_ref, ~even)):
        strip_ref[...] = pack(strip[...], is_last).reshape(strip_ref.shape).astype(bf16)


def lower_half():
    return lax.broadcasted_iota(jnp.int32, (1, STRIP, 1), 1) < SIDE


def turn(values):
    return jnp.concatenate([values[:, SIDE:], values[:, :SIDE]], axis=1)


def pack(strip, is_last):
    half = strip.shape[0] // 2
    turned = turn(strip)
    low = jnp.where(is_last, turned, strip)
    high = jnp.where(is_last, strip, turned)
    return jnp.where(lower_half(), low[:half], high[half:])


def unpack(packed, is_left):
    turned = turn(packed)
    low = jnp.where(is_left, turned, packed)
    high = jnp.where(is_left, packed, turned)
    return jnp.concatenate([low, high], axis=0)


def chain(my_lat, slab, shape, taps_ref, expand_ref, reduce_ref, attn_ref, center, scratch):
    one, lat_in = scratch
    rows, all_rows, columns, channels = shape
    cells = all_rows * columns
    parts = []
    for c in range(0, channels, LANES):
        acc = jnp.zeros((all_rows, columns, LANES), f32)
        for b in range(TAPS):
            block = slab(b, c)
            for a in range(TAPS):
                tap = taps_ref[a, b : b + 1, c : c + LANES].reshape(1, 1, LANES)
                acc = acc + block[a : a + all_rows] * tap
        parts.append(acc.reshape(cells, LANES))
    normed = layer_norm(jnp.concatenate(parts, axis=-1)).astype(bf16)

    def widen(k, total):
        part = slice(k * channels, (k + 1) * channels)
        wide = gelu(dot(normed, expand_ref[:, part])).astype(bf16)
        return total + dot(wide, reduce_ref[part])

    total = center.reshape(cells, channels)
    for k in range(expand_ref.shape[1] // channels):
        total = widen(k, total)
    block_one = total.astype(bf16)
    one[...] = block_one
    every = layer_norm(block_one.astype(f32)).astype(bf16)
    lat_in[...] = every
    count = rows * columns
    own = pl.ds(pl.multiple_of(my_lat * count, count), count)
    queries = dot(lat_in[own], attn_ref[0]).astype(bf16)
    keys = dot(every, attn_ref[1]).astype(bf16)
    values = dot(every, attn_ref[2]).astype(bf16)
    row_col = lax.broadcasted_iota(jnp.int32, (count, 1), 0) % columns
    key_col = lax.broadcasted_iota(jnp.int32, (1, cells), 1) % columns
    mix = attend(queries, keys, values, row_col == key_col)
    block_two = (one[own].astype(f32) + dot(mix, attn_ref[3])).astype(bf16)
    return block_two, layer_norm(block_two.astype(f32))


def fill(padded, all_rows, first, values):
    width = values.shape[1]
    padded[HALO : HALO + all_rows, first : first + width] = values


def fill_tiles(padded, my_lat, first, tiles):
    rows, cols = tiles[0].shape[:2]
    for s in range(len(tiles)):
        place = HALO + lax.rem(my_lat + s, len(tiles)) * rows
        padded[pl.ds(place, rows), first : first + cols] = tiles[s][...].astype(f32)


def clear(padded, all_rows):
    edge = jnp.zeros((HALO,) + padded.shape[1:], f32)
    padded[:HALO] = edge
    padded[HALO + all_rows :] = edge


def inner_kernel(nlat, *refs):
    tiles, refs = refs[:nlat], refs[nlat:]
    taps_ref, expand_ref, reduce_ref, attn_ref, two_ref, in_ref, padded, *scratch = refs
    rows, cols, channels = tiles[0].shape
    all_rows = rows * nlat
    columns = cols - 2 * SIDE
    clear(padded, all_rows)
    my_lat = lax.axis_index("lat")
    fill_tiles(padded, my_lat, 0, tiles)

    def slab(b, c):
        first = SIDE - HALO + b
        return padded[:, first : first + columns, c : c + LANES]

    center = padded[HALO : HALO + all_rows, SIDE : SIDE + columns]
    shape = (rows, all_rows, columns, channels)
    block_two, lon_in = chain(
        my_lat, slab, shape, taps_ref, expand_ref, reduce_ref, attn_ref, center, scratch
    )
    two_ref[...] = block_two
    in_ref[...] = lon_in.astype(bf16)


def outer_kernel(nlat, levels, *refs):
    tiles, refs = refs[:nlat], refs[nlat:]
    far_ref, near_ref, inner_in_ref, taps_ref, expand_ref, reduce_ref, attn_ref = refs[:7]
    two_ref, *refs = refs[7:]
    sent_refs, (sent, padded, *scratch) = refs[:levels], refs[levels:]
    rows, cols, channels = tiles[0].shape
    all_rows = rows * nlat
    columns = 2 * SIDE
    packed = (all_rows // 2, STRIP, channels)
    near = near_ref[...].astype(f32).reshape(packed)
    far = far_ref[...].astype(f32).reshape(packed)
    even = lax.axis_index("lon") % 2 == 0
    my_lat = lax.axis_index("lat")
    clear(padded, all_rows)
    fill(padded, all_rows, 0, unpack(jnp.where(even, far, near), True))
    fill_tiles(padded, my_lat, STRIP, tiles)
    fill(padded, all_rows, STRIP + cols, unpack(jnp.where(even, near, far), False))
    sublane = lax.broadcasted_iota(jnp.int32, (1, columns, 1), 1)

    def halves(shift, rows_of, c, width):
        right = STRIP + cols - SIDE + shift
        left = STRIP - SIDE + shift
        return jnp.where(
            sublane < SIDE,
            padded[rows_of, right : right + columns, c : c + width],
            padded[rows_of, left : left + columns, c : c + width],
        )

    def slab(b, c):
        return halves(b - HALO, slice(None), c, LANES)

    center = halves(0, slice(HALO, HALO + all_rows), 0, channels)
    shape = (rows, all_rows, columns, channels)
    block_two, lon_in = chain(
        my_lat, slab, shape, taps_ref, expand_ref, reduce_ref, attn_ref, center, scratch
    )
    two_ref[...] = block_two
    inner = inner_in_ref[...].astype(f32).reshape(rows, cols - columns, channels)
    outer = lon_in.reshape(rows, columns, channels)
    sent[...] = jnp.concatenate([inner, outer], axis=1).astype(bf16)
    some = rows // levels
    for k in range(levels):
        part = sent[pl.ds(peer(levels, k) * some, some)]
        sent_refs[k][...] = part.reshape(sent_refs[k].shape)


def join_kernel(levels, some, *refs):
    parts, joined, whole_ref = refs[:levels], refs[levels:-1], refs[-1]
    cols = parts[0].shape[0] // some
    for r in range(some):
        for k in range(levels):
            part = parts[k][r * cols : (r + 1) * cols]
            start = (r * levels + k) * cols
            joined[r][k * cols : (k + 1) * cols] = part
            whole_ref[start : start + cols] = part


def circle_kernel(levels, r, before, beside, *refs):
    attn_ref, refs = refs[0], refs[1:]
    done, refs = refs[:before], refs[before:]
    parts, mix_refs = refs[:-levels], refs[-levels:]
    own = parts[0][...]
    pieces = [own] + [part[...] for part in parts[1 + beside :]]
    if beside:
        pieces.append(parts[1][r * own.shape[0] : (r + 1) * own.shape[0]])
    every = jnp.concatenate(pieces, axis=0)
    queries = dot(own, attn_ref[0]).astype(bf16)
    keys = dot(every, attn_ref[1]).astype(bf16)
    values = dot(every, attn_ref[2]).astype(bf16)
    mix = attend(queries, keys, values, None)
    cols = own.shape[0] // levels
    for k in range(levels):
        for i in range(before // levels):
            mix_refs[k][i * cols : (i + 1) * cols] = done[i * levels + k][...]
        mix_refs[k][before // levels * cols :] = mix[k * cols : (k + 1) * cols]


def last_kernel(levels, *refs):
    parts = refs[:levels]
    inner_ref, outer_ref, attn_ref, out_ref = refs[levels:]
    rows, cols, channels = out_ref.shape
    columns = 2 * SIDE
    some = rows // levels
    every = jnp.concatenate([part[...] for part in parts], axis=0)
    change = dot(every, attn_ref[3]).reshape(levels, some, cols, channels)
    for k in range(levels):
        start = peer(levels, k) * some

        def state(ref, width):
            count = some * width
            place = pl.ds(pl.multiple_of(start * width, count), count)
            return ref[place].astype(f32).reshape(some, width, channels)

        inner = state(inner_ref, cols - columns) + change[k, :, : cols - columns]
        outer = state(outer_ref, columns) + change[k, :, cols - columns :]
        total = jnp.concatenate([outer[:, SIDE:], inner, outer[:, :SIDE]], axis=1)
        out_ref[pl.ds(start, some)] = total.astype(bf16)


def call(
    kernel, outs, operands, scratch=(), any_space=False, flops=0, grant=VMEM_BYTES
):
    vmem = pl.BlockSpec(memory_space=pltpu.VMEM)
    given = pl.BlockSpec(memory_space=pl.ANY) if any_space else vmem
    shapes = [
        out if isinstance(out, jax.ShapeDtypeStruct) else jax.ShapeDtypeStruct(out, bf16)
        for out in outs
    ]
    moved = sum(x.size * x.dtype.itemsize for x in operands)
    result = pl.pallas_call(
        kernel,
        out_shape=shapes,
        in_specs=[given] * len(operands),
        out_specs=[vmem] * len(outs),
        scratch_shapes=list(scratch),
        compiler_params=pltpu.CompilerParams(vmem_limit_bytes=grant),
        cost_estimate=pl.CostEstimate(flops=flops, bytes_accessed=moved, transcendentals=0),
    )(*operands)
    return result


def shards(field, dw_weight, w_expand, w_reduce, lat_attn, lon_attn):
    rows, cols, channels = field.shape
    nlat, nlon = lax.axis_size("lat"), lax.axis_size("lon")
    levels = min(LEVELS, nlon)
    column = nlon // levels
    some = rows // levels
    all_rows = rows * nlat
    columns = 2 * SIDE

    def swap(piece, mask):
        return lax.ppermute(piece, "lon", [(j, j ^ mask) for j in range(nlon)])

    def exchange(pieces):
        moved = []
        for k in range(1, levels):
            level = levels - k
            moved.append(swap(pieces[k], level * column + min(1, column - 1)))
        return [pieces[0]] + moved

    tiles = [field]
    for s in range(1, nlat):
        tiles.append(lax.ppermute(field, "lat", [((i + s) % nlat, i) for i in range(nlat)]))
    weights = (w_expand, w_reduce, lat_attn, lon_attn)
    expand, reduce, lat_proj, lon_proj, taps = call(
        functools.partial(stage_kernel, len(weights)),
        [w.shape for w in weights] + [jax.ShapeDtypeStruct(dw_weight.shape, f32)],
        [*weights, dw_weight],
        [
            pltpu.VMEM(dw_weight.shape, bf16),
            pltpu.SemaphoreType.DMA((len(weights) + 1, STAGES)),
        ],
        any_space=True,
        grant=STAGE_BYTES,
    )

    strip = (all_rows * SIDE, channels)
    strip_scratch = pltpu.VMEM((all_rows, STRIP, channels), f32)
    near, far = call(
        functools.partial(strip_kernel, nlat),
        [strip, strip],
        [*tiles, reduce],
        [strip_scratch, strip_scratch],
    )
    far = lax.ppermute(
        far, "lon", [(j, (j - 1) % nlon if j % 2 == 0 else (j + 1) % nlon) for j in range(nlon)]
    )
    near = swap(near, 1)

    def scratch(width, count):
        return [
            pltpu.VMEM((all_rows + 2 * HALO, width, channels), f32),
            pltpu.VMEM((all_rows * count, channels), bf16),
            pltpu.VMEM((all_rows * count, channels), bf16),
        ]

    work = 4 * all_rows * columns * channels * w_expand.shape[1]
    inner_two, inner_in = call(
        functools.partial(inner_kernel, nlat),
        [(rows * (cols - columns), channels)] * 2,
        [*tiles, taps, expand, reduce, lat_proj],
        scratch(cols, cols - columns),
        flops=work,
    )
    piece = (some * cols, channels)
    outer_two, *parts = call(
        functools.partial(outer_kernel, nlat, levels),
        [(rows * columns, channels)] + [piece] * levels,
        [*tiles, far, near, inner_in, taps, expand, reduce, lat_proj],
        [pltpu.VMEM((rows, cols, channels), bf16)] + scratch(cols + 2 * STRIP, columns),
        flops=work,
    )

    parts = exchange(parts)
    block = (levels * cols, channels)
    *joined, whole = call(
        functools.partial(join_kernel, levels, some),
        [block] * some + [(some * levels * cols, channels)],
        parts,
    )
    circles = [[part] for part in joined]
    mask = column // 2
    while mask > 1:
        for circle in circles:
            circle += [swap(part, mask + mask // 2) for part in circle]
        mask //= 2
    beside = [swap(whole, 1)] if column > 1 else []
    done = []
    for r, circle in enumerate(circles):
        if beside:
            circle += [swap(part, 1) for part in circle[1:]]
        earlier = done if r == some - 1 else []
        mixes = call(
            functools.partial(circle_kernel, levels, r, len(earlier), len(beside)),
            [piece if r == some - 1 else (cols, channels)] * levels,
            [lon_proj, *earlier, circle[0], *beside, *circle[1:]],
            flops=work // 4,
        )
        done = done + list(mixes)
    mixes = exchange(mixes)
    (out,) = call(
        functools.partial(last_kernel, levels),
        [(rows, cols, channels)],
        [*mixes, inner_two, outer_two, lon_proj],
    )
    return out


def solution(mesh):
    return jax.shard_map(
        shards,
        mesh=mesh,
        in_specs=(P("lat", "lon", None), P(), P(), P(), P(), P()),
        out_specs=P("lat", "lon", None),
        check_vma=False,
    )
```

```python
import functools

import jax
import jax.numpy as jnp
from jax import lax
from jax.experimental import pallas as pl
from jax.experimental.pallas import tpu as pltpu
from jax.sharding import PartitionSpec as P

HEADS = 8
HALO = 3
TAPS = 2 * HALO + 1
STRIP = 8
SIDE = 4
LANES = 128
LEVELS = 4
STAGES = 4
EPSILON = 1e-06
VMEM_BYTES = 24 * 1024 * 1024
STAGE_BYTES = 103 * 512 * 1024
bf16, f32 = jnp.bfloat16, jnp.float32


def layer_norm(values):
    average = jnp.mean(values, axis=-1, keepdims=True)
    centered = values - average
    variance = jnp.mean(centered * centered, axis=-1, keepdims=True)
    return centered * lax.rsqrt(variance + EPSILON)


def dot(rows, matrix):
    return jnp.dot(rows, matrix, preferred_element_type=f32)


def dot_t(rows, matrix):
    return lax.dot_general(rows, matrix, (((1,), (1,)), ((), ())), preferred_element_type=f32)


def gelu(values):
    size = jnp.abs(values)
    t = 1.0 / (1.0 + (0.3275911 * 0.5**0.5) * size)
    tail = 1.061405429 * t - 1.453152027
    for coefficient in (1.421413741, -0.284496736, 0.254829592):
        tail = tail * t + coefficient
    tail = (0.5 * size * t) * tail * jnp.exp(-0.5 * values * values)
    return jnp.maximum(values, 0.0) - tail


def attend(queries, keys, values, mask):
    count, channels = queries.shape
    head_size = channels // HEADS
    lane_head = lax.broadcasted_iota(jnp.int32, (1, channels), 1) // head_size
    picks = [lane_head == h for h in range(HEADS)]
    none = jnp.zeros_like(queries)
    stacked = jnp.concatenate([jnp.where(pick, queries, none) for pick in picks], axis=0)
    scores = dot_t(stacked, keys) * head_size ** (-0.5)
    if mask is not None:
        scores = scores.reshape(HEADS, count, keys.shape[0])
        scores = jnp.where(mask[None], scores, -1e30).reshape(HEADS * count, keys.shape[0])
    top = jnp.max(scores, axis=-1, keepdims=True)
    probs = jnp.exp(scores - top)
    totals = jnp.sum(probs, axis=-1, keepdims=True)
    mixed = dot(probs.astype(bf16), values) * (1.0 / totals)
    out = mixed[:count]
    for h in range(1, HEADS):
        out = jnp.where(picks[h], mixed[h * count : (h + 1) * count], out)
    return out.astype(bf16)


def stage_kernel(count, *refs):
    sources, dw_ref = refs[:count], refs[count]
    targets, taps_ref, dw, sems = refs[count + 1 : 2 * count + 1], *refs[2 * count + 1 :]
    copies = [pltpu.make_async_copy(dw_ref, dw, sems.at[count, 0])]
    pieces = sems.shape[1]
    for i in range(count):
        source, target = sources[i], targets[i]
        size = source.shape[0] // pieces
        for k in range(pieces):
            part = pl.ds(k * size, size)
            copies.append(pltpu.make_async_copy(source.at[part], target.at[part], sems.at[i, k]))
    for copy in copies:
        copy.start()
    for copy in copies:
        copy.wait()
    taps_ref[...] = dw[...].astype(f32)


def peer(levels, k):
    level = lax.axis_index("lon") // (lax.axis_size("lon") // levels)
    return level ^ ((levels - k) % levels)


def strip_kernel(nlat, *refs):
    tiles = refs[:nlat]
    near_ref, far_ref, near, far = refs[nlat + 1 :]
    rows, cols, channels = tiles[0].shape
    even = lax.axis_index("lon") % 2 == 0
    for s in range(nlat):
        values = tiles[s][...].astype(f32)
        first, last = values[:, :STRIP], values[:, cols - STRIP :]
        where = pl.ds(lax.rem(lax.axis_index("lat") + s, nlat) * rows, rows)
        near[where] = jnp.where(even, last, first)
        far[where] = jnp.where(even, first, last)
    for strip, strip_ref, is_last in ((near, near_ref, even), (far, far_ref, ~even)):
        strip_ref[...] = pack(strip[...], is_last).reshape(strip_ref.shape).astype(bf16)


def lower_half():
    return lax.broadcasted_iota(jnp.int32, (1, STRIP, 1), 1) < SIDE


def turn(values):
    return pltpu.roll(values, SIDE, axis=1)


def pack(strip, is_last):
    half = strip.shape[0] // 2
    turned = turn(strip)
    low = jnp.where(is_last, turned, strip)
    high = jnp.where(is_last, strip, turned)
    return jnp.where(lower_half(), low[:half], high[half:])


def unpack(packed, is_left):
    turned = turn(packed)
    low = jnp.where(is_left, turned, packed)
    high = jnp.where(is_left, packed, turned)
    return jnp.concatenate([low, high], axis=0)


def chain(my_lat, slab, shape, taps_ref, expand_ref, reduce_ref, attn_ref, center, scratch):
    one, lat_in = scratch
    rows, all_rows, columns, channels = shape
    cells = all_rows * columns
    parts = []
    for c in range(0, channels, LANES):
        acc = jnp.zeros((all_rows, columns, LANES), f32)
        for b in range(TAPS):
            block = slab(b, c)
            for a in range(TAPS):
                tap = taps_ref[a, b : b + 1, c : c + LANES].reshape(1, 1, LANES)
                acc = acc + block[a : a + all_rows] * tap
        parts.append(acc.reshape(cells, LANES))
    normed = layer_norm(jnp.concatenate(parts, axis=-1)).astype(bf16)

    def widen(k, total):
        part = slice(k * channels, (k + 1) * channels)
        wide = gelu(dot(normed, expand_ref[:, part])).astype(bf16)
        return total + dot(wide, reduce_ref[part])

    total = center.reshape(cells, channels)
    for k in range(expand_ref.shape[1] // channels):
        total = widen(k, total)
    block_one = total.astype(bf16)
    one[...] = block_one
    every = layer_norm(block_one.astype(f32)).astype(bf16)
    lat_in[...] = every
    count = rows * columns
    own = pl.ds(pl.multiple_of(my_lat * count, count), count)
    queries = dot(lat_in[own], attn_ref[0]).astype(bf16)
    keys = dot(every, attn_ref[1]).astype(bf16)
    values = dot(every, attn_ref[2]).astype(bf16)
    row_col = lax.broadcasted_iota(jnp.int32, (count, 1), 0) % columns
    key_col = lax.broadcasted_iota(jnp.int32, (1, cells), 1) % columns
    mix = attend(queries, keys, values, row_col == key_col)
    block_two = (one[own].astype(f32) + dot(mix, attn_ref[3])).astype(bf16)
    return block_two, layer_norm(block_two.astype(f32))


def fill(padded, all_rows, first, values):
    width = values.shape[1]
    padded[HALO : HALO + all_rows, first : first + width] = values


def fill_tiles(padded, my_lat, first, tiles):
    rows, cols = tiles[0].shape[:2]
    for s in range(len(tiles)):
        place = HALO + lax.rem(my_lat + s, len(tiles)) * rows
        padded[pl.ds(place, rows), first : first + cols] = tiles[s][...].astype(f32)


def clear(padded, all_rows):
    edge = jnp.zeros((HALO,) + padded.shape[1:], f32)
    padded[:HALO] = edge
    padded[HALO + all_rows :] = edge


def inner_kernel(nlat, *refs):
    tiles, refs = refs[:nlat], refs[nlat:]
    taps_ref, expand_ref, reduce_ref, attn_ref, two_ref, in_ref, padded, *scratch = refs
    rows, cols, channels = tiles[0].shape
    all_rows = rows * nlat
    columns = cols - 2 * SIDE
    clear(padded, all_rows)
    my_lat = lax.axis_index("lat")
    fill_tiles(padded, my_lat, 0, tiles)

    def slab(b, c):
        first = SIDE - HALO + b
        return padded[:, first : first + columns, c : c + LANES]

    center = padded[HALO : HALO + all_rows, SIDE : SIDE + columns]
    shape = (rows, all_rows, columns, channels)
    block_two, lon_in = chain(
        my_lat, slab, shape, taps_ref, expand_ref, reduce_ref, attn_ref, center, scratch
    )
    two_ref[...] = block_two
    in_ref[...] = lon_in.astype(bf16)


def outer_kernel(nlat, levels, *refs):
    tiles, refs = refs[:nlat], refs[nlat:]
    far_ref, near_ref, inner_in_ref, taps_ref, expand_ref, reduce_ref, attn_ref = refs[:7]
    two_ref, *refs = refs[7:]
    sent_refs, (sent, padded, *scratch) = refs[:levels], refs[levels:]
    rows, cols, channels = tiles[0].shape
    all_rows = rows * nlat
    columns = 2 * SIDE
    packed = (all_rows // 2, STRIP, channels)
    near = near_ref[...].astype(f32).reshape(packed)
    far = far_ref[...].astype(f32).reshape(packed)
    even = lax.axis_index("lon") % 2 == 0
    my_lat = lax.axis_index("lat")
    clear(padded, all_rows)
    fill(padded, all_rows, 0, unpack(jnp.where(even, far, near), True))
    fill_tiles(padded, my_lat, STRIP, tiles)
    fill(padded, all_rows, STRIP + cols, unpack(jnp.where(even, near, far), False))
    sublane = lax.broadcasted_iota(jnp.int32, (1, columns, 1), 1)

    def halves(shift, rows_of, c, width):
        right = STRIP + cols - SIDE + shift
        left = STRIP - SIDE + shift
        return jnp.where(
            sublane < SIDE,
            padded[rows_of, right : right + columns, c : c + width],
            padded[rows_of, left : left + columns, c : c + width],
        )

    def slab(b, c):
        return halves(b - HALO, slice(None), c, LANES)

    center = halves(0, slice(HALO, HALO + all_rows), 0, channels)
    shape = (rows, all_rows, columns, channels)
    block_two, lon_in = chain(
        my_lat, slab, shape, taps_ref, expand_ref, reduce_ref, attn_ref, center, scratch
    )
    two_ref[...] = block_two
    inner = inner_in_ref[...].astype(f32).reshape(rows, cols - columns, channels)
    outer = lon_in.reshape(rows, columns, channels)
    sent[...] = jnp.concatenate([inner, outer], axis=1).astype(bf16)
    some = rows // levels
    for k in range(levels):
        part = sent[pl.ds(peer(levels, k) * some, some)]
        sent_refs[k][...] = part.reshape(sent_refs[k].shape)


def join_kernel(levels, some, *refs):
    parts, joined = refs[:levels], refs[levels:]
    cols = parts[0].shape[0] // some
    for r in range(some):
        for k in range(levels):
            joined[r][k * cols : (k + 1) * cols] = parts[k][r * cols : (r + 1) * cols]


def circle_kernel(levels, before, *refs):
    attn_ref, refs = refs[0], refs[1:]
    done, refs = refs[:before], refs[before:]
    parts, mix_refs = refs[:-levels], refs[-levels:]
    own = parts[0][...]
    every = jnp.concatenate([own] + [part[...] for part in parts[1:]], axis=0)
    queries = dot(own, attn_ref[0]).astype(bf16)
    keys = dot(every, attn_ref[1]).astype(bf16)
    values = dot(every, attn_ref[2]).astype(bf16)
    mix = attend(queries, keys, values, None)
    cols = own.shape[0] // levels
    for k in range(levels):
        for r in range(before // levels):
            mix_refs[k][r * cols : (r + 1) * cols] = done[r * levels + k][...]
        mix_refs[k][before // levels * cols :] = mix[k * cols : (k + 1) * cols]


def last_kernel(levels, *refs):
    parts = refs[:levels]
    inner_ref, outer_ref, attn_ref, out_ref = refs[levels:]
    rows, cols, channels = out_ref.shape
    columns = 2 * SIDE
    some = rows // levels
    every = jnp.concatenate([part[...] for part in parts], axis=0)
    change = dot(every, attn_ref[3]).reshape(levels, some, cols, channels)
    for k in range(levels):
        start = peer(levels, k) * some

        def state(ref, width):
            count = some * width
            place = pl.ds(pl.multiple_of(start * width, count), count)
            return ref[place].astype(f32).reshape(some, width, channels)

        before = jnp.concatenate(
            [state(inner_ref, cols - columns), state(outer_ref, columns)], axis=1
        )
        total = pltpu.roll(before + change[k], SIDE, axis=1)
        out_ref[pl.ds(start, some)] = total.astype(bf16)


def call(
    kernel, outs, operands, scratch=(), any_space=False, flops=0, grant=VMEM_BYTES
):
    vmem = pl.BlockSpec(memory_space=pltpu.VMEM)
    given = pl.BlockSpec(memory_space=pl.ANY) if any_space else vmem
    shapes = [
        out if isinstance(out, jax.ShapeDtypeStruct) else jax.ShapeDtypeStruct(out, bf16)
        for out in outs
    ]
    moved = sum(x.size * x.dtype.itemsize for x in operands)
    result = pl.pallas_call(
        kernel,
        out_shape=shapes,
        in_specs=[given] * len(operands),
        out_specs=[vmem] * len(outs),
        scratch_shapes=list(scratch),
        compiler_params=pltpu.CompilerParams(vmem_limit_bytes=grant),
        cost_estimate=pl.CostEstimate(flops=flops, bytes_accessed=moved, transcendentals=0),
    )(*operands)
    return result


def shards(field, dw_weight, w_expand, w_reduce, lat_attn, lon_attn):
    rows, cols, channels = field.shape
    nlat, nlon = lax.axis_size("lat"), lax.axis_size("lon")
    levels = min(LEVELS, nlon)
    column = nlon // levels
    some = rows // levels
    all_rows = rows * nlat
    columns = 2 * SIDE

    def swap(piece, mask):
        return lax.ppermute(piece, "lon", [(j, j ^ mask) for j in range(nlon)])

    def exchange(pieces):
        moved = []
        for k in range(1, levels):
            level = levels - k
            moved.append(swap(pieces[k], level * column + min(1, column - 1)))
        return [pieces[0]] + moved

    tiles = [field]
    for s in range(1, nlat):
        tiles.append(lax.ppermute(field, "lat", [((i + s) % nlat, i) for i in range(nlat)]))
    weights = (w_expand, w_reduce, lat_attn, lon_attn)
    expand, reduce, lat_proj, lon_proj, taps = call(
        functools.partial(stage_kernel, len(weights)),
        [w.shape for w in weights] + [jax.ShapeDtypeStruct(dw_weight.shape, f32)],
        [*weights, dw_weight],
        [
            pltpu.VMEM(dw_weight.shape, bf16),
            pltpu.SemaphoreType.DMA((len(weights) + 1, STAGES)),
        ],
        any_space=True,
        grant=STAGE_BYTES,
    )

    strip = (all_rows * SIDE, channels)
    strip_scratch = pltpu.VMEM((all_rows, STRIP, channels), f32)
    near, far = call(
        functools.partial(strip_kernel, nlat),
        [strip, strip],
        [*tiles, reduce],
        [strip_scratch, strip_scratch],
    )
    far = lax.ppermute(
        far, "lon", [(j, (j - 1) % nlon if j % 2 == 0 else (j + 1) % nlon) for j in range(nlon)]
    )
    near = swap(near, 1)

    def scratch(width, count):
        return [
            pltpu.VMEM((all_rows + 2 * HALO, width, channels), f32),
            pltpu.VMEM((all_rows * count, channels), bf16),
            pltpu.VMEM((all_rows * count, channels), bf16),
        ]

    work = 4 * all_rows * columns * channels * w_expand.shape[1]
    inner_two, inner_in = call(
        functools.partial(inner_kernel, nlat),
        [(rows * (cols - columns), channels)] * 2,
        [*tiles, taps, expand, reduce, lat_proj],
        scratch(cols, cols - columns),
        flops=work,
    )
    piece = (some * cols, channels)
    outer_two, *parts = call(
        functools.partial(outer_kernel, nlat, levels),
        [(rows * columns, channels)] + [piece] * levels,
        [*tiles, far, near, inner_in, taps, expand, reduce, lat_proj],
        [pltpu.VMEM((rows, cols, channels), bf16)] + scratch(cols + 2 * STRIP, columns),
        flops=work,
    )

    parts = exchange(parts)
    joined = call(
        functools.partial(join_kernel, levels, some), [(levels * cols, channels)] * some, parts
    )
    circles = [[part] for part in joined]
    mask = column // 2
    while mask:
        for circle in circles:
            circle += [swap(part, mask + mask // 2) for part in circle]
        mask //= 2
    done = []
    for r, circle in enumerate(circles):
        last_one = r == some - 1
        mixes = call(
            functools.partial(circle_kernel, levels, len(done) if last_one else 0),
            [piece if last_one else (cols, channels)] * levels,
            [lon_proj, *(done if last_one else []), *circle],
            flops=work // 4,
        )
        done = done + list(mixes)
    mixes = exchange(mixes)
    (out,) = call(
        functools.partial(last_kernel, levels),
        [(rows, cols, channels)],
        [*mixes, inner_two, outer_two, lon_proj],
    )
    return out


def solution(mesh):
    return jax.shard_map(
        shards,
        mesh=mesh,
        in_specs=(P("lat", "lon", None), P(), P(), P(), P(), P()),
        out_specs=P("lat", "lon", None),
        check_vma=False,
    )
```

```python
import functools

import jax
import jax.numpy as jnp
from jax import lax
from jax.experimental import pallas as pl
from jax.experimental.pallas import tpu as pltpu
from jax.sharding import PartitionSpec as P

HEADS = 8
HALO = 3
TAPS = 2 * HALO + 1
STRIP = 8
SIDE = 4
LANES = 128
LEVELS = 4
STAGES = 4
EPSILON = 1e-06
VMEM_BYTES = 24 * 1024 * 1024
STAGE_BYTES = 103 * 512 * 1024
bf16, f32 = jnp.bfloat16, jnp.float32


def layer_norm(values):
    average = jnp.mean(values, axis=-1, keepdims=True)
    centered = values - average
    variance = jnp.mean(centered * centered, axis=-1, keepdims=True)
    return centered * lax.rsqrt(variance + EPSILON)


def dot(rows, matrix):
    return jnp.dot(rows, matrix, preferred_element_type=f32)


def dot_t(rows, matrix):
    return lax.dot_general(rows, matrix, (((1,), (1,)), ((), ())), preferred_element_type=f32)


def gelu(values):
    size = jnp.abs(values)
    t = 1.0 / (1.0 + (0.3275911 * 0.5**0.5) * size)
    tail = 1.061405429 * t - 1.453152027
    for coefficient in (1.421413741, -0.284496736, 0.254829592):
        tail = tail * t + coefficient
    tail = (0.5 * size * t) * tail * jnp.exp(-0.5 * values * values)
    return jnp.maximum(values, 0.0) - tail


def attend(queries, keys, values, mask):
    count, channels = queries.shape
    head_size = channels // HEADS
    lane_head = lax.broadcasted_iota(jnp.int32, (1, channels), 1) // head_size
    picks = [lane_head == h for h in range(HEADS)]
    none = jnp.zeros_like(queries)
    stacked = jnp.concatenate([jnp.where(pick, queries, none) for pick in picks], axis=0)
    scores = dot_t(stacked, keys) * head_size ** (-0.5)
    if mask is not None:
        scores = scores.reshape(HEADS, count, keys.shape[0])
        scores = jnp.where(mask[None], scores, -1e30).reshape(HEADS * count, keys.shape[0])
    top = jnp.max(scores, axis=-1, keepdims=True)
    probs = jnp.exp(scores - top)
    totals = jnp.sum(probs, axis=-1, keepdims=True)
    mixed = dot(probs.astype(bf16), values) * (1.0 / totals)
    out = mixed[:count]
    for h in range(1, HEADS):
        out = jnp.where(picks[h], mixed[h * count : (h + 1) * count], out)
    return out.astype(bf16)


def stage_kernel(count, *refs):
    sources, dw_ref = refs[:count], refs[count]
    targets, taps_ref, dw, sems = refs[count + 1 : 2 * count + 1], *refs[2 * count + 1 :]
    copies = [pltpu.make_async_copy(dw_ref, dw, sems.at[count, 0])]
    pieces = sems.shape[1]
    for i in range(count):
        source, target = sources[i], targets[i]
        size = source.shape[0] // pieces
        for k in range(pieces):
            part = pl.ds(k * size, size)
            copies.append(pltpu.make_async_copy(source.at[part], target.at[part], sems.at[i, k]))
    for copy in copies:
        copy.start()
    for copy in copies:
        copy.wait()
    taps_ref[...] = dw[...].astype(f32)


def hops_of(levels):
    return [0] + [h for h in (*range(levels // 2, levels), *range(1, levels // 2)) if h]


def peer(levels, k):
    level = lax.axis_index("lon") // (lax.axis_size("lon") // levels)
    return level ^ hops_of(levels)[k]


def strip_kernel(nlat, *refs):
    tiles = refs[:nlat]
    near_ref, far_ref, near, far = refs[nlat + 1 :]
    rows, cols, channels = tiles[0].shape
    even = lax.axis_index("lon") % 2 == 0
    for s in range(nlat):
        values = tiles[s][...].astype(f32)
        first, last = values[:, :STRIP], values[:, cols - STRIP :]
        where = pl.ds(lax.rem(lax.axis_index("lat") + s, nlat) * rows, rows)
        near[where] = jnp.where(even, last, first)
        far[where] = jnp.where(even, first, last)
    for strip, strip_ref, is_last in ((near, near_ref, even), (far, far_ref, ~even)):
        strip_ref[...] = pack(strip[...], is_last).reshape(strip_ref.shape).astype(bf16)


def lower_half():
    return lax.broadcasted_iota(jnp.int32, (1, STRIP, 1), 1) < SIDE


def turn(values):
    return pltpu.roll(values, SIDE, axis=1)


def pack(strip, is_last):
    half = strip.shape[0] // 2
    turned = turn(strip)
    low = jnp.where(is_last, turned, strip)
    high = jnp.where(is_last, strip, turned)
    return jnp.where(lower_half(), low[:half], high[half:])


def unpack(packed, is_left):
    turned = turn(packed)
    low = jnp.where(is_left, turned, packed)
    high = jnp.where(is_left, packed, turned)
    return jnp.concatenate([low, high], axis=0)


def chain(my_lat, slab, shape, taps_ref, expand_ref, reduce_ref, attn_ref, center, scratch):
    one, lat_in = scratch
    rows, all_rows, columns, channels = shape
    cells = all_rows * columns
    parts = []
    for c in range(0, channels, LANES):
        acc = jnp.zeros((all_rows, columns, LANES), f32)
        for b in range(TAPS):
            block = slab(b, c)
            for a in range(TAPS):
                tap = taps_ref[a, b : b + 1, c : c + LANES].reshape(1, 1, LANES)
                acc = acc + block[a : a + all_rows] * tap
        parts.append(acc.reshape(cells, LANES))
    normed = layer_norm(jnp.concatenate(parts, axis=-1)).astype(bf16)

    def widen(k, total):
        part = slice(k * channels, (k + 1) * channels)
        wide = gelu(dot(normed, expand_ref[:, part])).astype(bf16)
        return total + dot(wide, reduce_ref[part])

    total = center.reshape(cells, channels)
    for k in range(expand_ref.shape[1] // channels):
        total = widen(k, total)
    block_one = total.astype(bf16)
    one[...] = block_one
    every = layer_norm(block_one.astype(f32)).astype(bf16)
    lat_in[...] = every
    count = rows * columns
    own = pl.ds(pl.multiple_of(my_lat * count, count), count)
    queries = dot(lat_in[own], attn_ref[0]).astype(bf16)
    keys = dot(every, attn_ref[1]).astype(bf16)
    values = dot(every, attn_ref[2]).astype(bf16)
    row_col = lax.broadcasted_iota(jnp.int32, (count, 1), 0) % columns
    key_col = lax.broadcasted_iota(jnp.int32, (1, cells), 1) % columns
    mix = attend(queries, keys, values, row_col == key_col)
    block_two = (one[own].astype(f32) + dot(mix, attn_ref[3])).astype(bf16)
    return block_two, layer_norm(block_two.astype(f32))


def fill(padded, all_rows, first, values):
    width = values.shape[1]
    padded[HALO : HALO + all_rows, first : first + width] = values


def fill_tiles(padded, my_lat, first, tiles):
    rows, cols = tiles[0].shape[:2]
    for s in range(len(tiles)):
        place = HALO + lax.rem(my_lat + s, len(tiles)) * rows
        padded[pl.ds(place, rows), first : first + cols] = tiles[s][...].astype(f32)


def clear(padded, all_rows):
    edge = jnp.zeros((HALO,) + padded.shape[1:], f32)
    padded[:HALO] = edge
    padded[HALO + all_rows :] = edge


def inner_kernel(nlat, *refs):
    tiles, refs = refs[:nlat], refs[nlat:]
    taps_ref, expand_ref, reduce_ref, attn_ref, two_ref, in_ref, padded, *scratch = refs
    rows, cols, channels = tiles[0].shape
    all_rows = rows * nlat
    columns = cols - 2 * SIDE
    clear(padded, all_rows)
    my_lat = lax.axis_index("lat")
    fill_tiles(padded, my_lat, 0, tiles)

    def slab(b, c):
        first = SIDE - HALO + b
        return padded[:, first : first + columns, c : c + LANES]

    center = padded[HALO : HALO + all_rows, SIDE : SIDE + columns]
    shape = (rows, all_rows, columns, channels)
    block_two, lon_in = chain(
        my_lat, slab, shape, taps_ref, expand_ref, reduce_ref, attn_ref, center, scratch
    )
    two_ref[...] = block_two
    in_ref[...] = lon_in.astype(bf16)


def outer_kernel(nlat, levels, *refs):
    tiles, refs = refs[:nlat], refs[nlat:]
    far_ref, near_ref, inner_in_ref, taps_ref, expand_ref, reduce_ref, attn_ref = refs[:7]
    two_ref, *refs = refs[7:]
    sent_refs, (sent, padded, *scratch) = refs[:levels], refs[levels:]
    rows, cols, channels = tiles[0].shape
    all_rows = rows * nlat
    columns = 2 * SIDE
    packed = (all_rows // 2, STRIP, channels)
    near = near_ref[...].astype(f32).reshape(packed)
    far = far_ref[...].astype(f32).reshape(packed)
    even = lax.axis_index("lon") % 2 == 0
    my_lat = lax.axis_index("lat")
    clear(padded, all_rows)
    fill(padded, all_rows, 0, unpack(jnp.where(even, far, near), True))
    fill_tiles(padded, my_lat, STRIP, tiles)
    fill(padded, all_rows, STRIP + cols, unpack(jnp.where(even, near, far), False))
    sublane = lax.broadcasted_iota(jnp.int32, (1, columns, 1), 1)

    def halves(shift, rows_of, c, width):
        right = STRIP + cols - SIDE + shift
        left = STRIP - SIDE + shift
        return jnp.where(
            sublane < SIDE,
            padded[rows_of, right : right + columns, c : c + width],
            padded[rows_of, left : left + columns, c : c + width],
        )

    def slab(b, c):
        return halves(b - HALO, slice(None), c, LANES)

    center = halves(0, slice(HALO, HALO + all_rows), 0, channels)
    shape = (rows, all_rows, columns, channels)
    block_two, lon_in = chain(
        my_lat, slab, shape, taps_ref, expand_ref, reduce_ref, attn_ref, center, scratch
    )
    two_ref[...] = block_two
    inner = inner_in_ref[...].astype(f32).reshape(rows, cols - columns, channels)
    outer = lon_in.reshape(rows, columns, channels)
    sent[...] = jnp.concatenate([inner, outer], axis=1).astype(bf16)
    some = rows // levels
    for k in range(levels):
        part = sent[pl.ds(peer(levels, k) * some, some)]
        sent_refs[k][...] = part.reshape(sent_refs[k].shape)


def join_kernel(levels, some, *refs):
    parts, joined = refs[:levels], refs[levels:]
    cols = parts[0].shape[0] // some
    for r in range(some):
        for k in range(levels):
            joined[r][k * cols : (k + 1) * cols] = parts[k][r * cols : (r + 1) * cols]


def circle_kernel(levels, before, *refs):
    attn_ref, refs = refs[0], refs[1:]
    done, refs = refs[:before], refs[before:]
    parts, mix_refs = refs[:-levels], refs[-levels:]
    own = parts[0][...]
    every = jnp.concatenate([own] + [part[...] for part in parts[1:]], axis=0)
    queries = dot(own, attn_ref[0]).astype(bf16)
    keys = dot(every, attn_ref[1]).astype(bf16)
    values = dot(every, attn_ref[2]).astype(bf16)
    mix = attend(queries, keys, values, None)
    cols = own.shape[0] // levels
    for k in range(levels):
        for r in range(before // levels):
            mix_refs[k][r * cols : (r + 1) * cols] = done[r * levels + k][...]
        mix_refs[k][before // levels * cols :] = mix[k * cols : (k + 1) * cols]


def last_kernel(levels, *refs):
    parts = refs[:levels]
    inner_ref, outer_ref, attn_ref, out_ref = refs[levels:]
    rows, cols, channels = out_ref.shape
    columns = 2 * SIDE
    some = rows // levels
    every = jnp.concatenate([part[...] for part in parts], axis=0)
    change = dot(every, attn_ref[3]).reshape(levels, some, cols, channels)
    for k in range(levels):
        start = peer(levels, k) * some

        def state(ref, width):
            count = some * width
            place = pl.ds(pl.multiple_of(start * width, count), count)
            return ref[place].astype(f32).reshape(some, width, channels)

        before = jnp.concatenate(
            [state(inner_ref, cols - columns), state(outer_ref, columns)], axis=1
        )
        total = pltpu.roll(before + change[k], SIDE, axis=1)
        out_ref[pl.ds(start, some)] = total.astype(bf16)


def call(
    kernel, outs, operands, scratch=(), any_space=False, flops=0, grant=VMEM_BYTES
):
    vmem = pl.BlockSpec(memory_space=pltpu.VMEM)
    given = pl.BlockSpec(memory_space=pl.ANY) if any_space else vmem
    shapes = [
        out if isinstance(out, jax.ShapeDtypeStruct) else jax.ShapeDtypeStruct(out, bf16)
        for out in outs
    ]
    moved = sum(x.size * x.dtype.itemsize for x in operands)
    result = pl.pallas_call(
        kernel,
        out_shape=shapes,
        in_specs=[given] * len(operands),
        out_specs=[vmem] * len(outs),
        scratch_shapes=list(scratch),
        compiler_params=pltpu.CompilerParams(vmem_limit_bytes=grant),
        cost_estimate=pl.CostEstimate(flops=flops, bytes_accessed=moved, transcendentals=0),
    )(*operands)
    return result


def shards(field, dw_weight, w_expand, w_reduce, lat_attn, lon_attn):
    rows, cols, channels = field.shape
    nlat, nlon = lax.axis_size("lat"), lax.axis_size("lon")
    levels = min(LEVELS, nlon)
    column = nlon // levels
    some = rows // levels
    all_rows = rows * nlat
    columns = 2 * SIDE

    def swap(piece, mask):
        return lax.ppermute(piece, "lon", [(j, j ^ mask) for j in range(nlon)])

    def exchange(pieces):
        cross = min(1, column - 1)
        return [
            swap(piece, hops * column + cross) if hops else piece
            for piece, hops in zip(pieces, hops_of(levels))
        ]

    tiles = [field]
    for s in range(1, nlat):
        tiles.append(lax.ppermute(field, "lat", [((i + s) % nlat, i) for i in range(nlat)]))
    weights = (w_expand, w_reduce, lat_attn, lon_attn)
    expand, reduce, lat_proj, lon_proj, taps = call(
        functools.partial(stage_kernel, len(weights)),
        [w.shape for w in weights] + [jax.ShapeDtypeStruct(dw_weight.shape, f32)],
        [*weights, dw_weight],
        [
            pltpu.VMEM(dw_weight.shape, bf16),
            pltpu.SemaphoreType.DMA((len(weights) + 1, STAGES)),
        ],
        any_space=True,
        grant=STAGE_BYTES,
    )

    strip = (all_rows * SIDE, channels)
    strip_scratch = pltpu.VMEM((all_rows, STRIP, channels), f32)
    near, far = call(
        functools.partial(strip_kernel, nlat),
        [strip, strip],
        [*tiles, reduce],
        [strip_scratch, strip_scratch],
    )
    far = lax.ppermute(
        far, "lon", [(j, (j - 1) % nlon if j % 2 == 0 else (j + 1) % nlon) for j in range(nlon)]
    )
    near = swap(near, 1)

    def scratch(width, count):
        return [
            pltpu.VMEM((all_rows + 2 * HALO, width, channels), f32),
            pltpu.VMEM((all_rows * count, channels), bf16),
            pltpu.VMEM((all_rows * count, channels), bf16),
        ]

    work = 4 * all_rows * columns * channels * w_expand.shape[1]
    inner_two, inner_in = call(
        functools.partial(inner_kernel, nlat),
        [(rows * (cols - columns), channels)] * 2,
        [*tiles, taps, expand, reduce, lat_proj],
        scratch(cols, cols - columns),
        flops=work,
    )
    piece = (some * cols, channels)
    outer_two, *parts = call(
        functools.partial(outer_kernel, nlat, levels),
        [(rows * columns, channels)] + [piece] * levels,
        [*tiles, far, near, inner_in, taps, expand, reduce, lat_proj],
        [pltpu.VMEM((rows, cols, channels), bf16)] + scratch(cols + 2 * STRIP, columns),
        flops=work,
    )

    parts = exchange(parts)
    joined = call(
        functools.partial(join_kernel, levels, some), [(levels * cols, channels)] * some, parts
    )
    circles = [[part] for part in joined]
    mask = column // 2
    while mask:
        for circle in circles:
            circle += [swap(part, mask + mask // 2) for part in circle]
        mask //= 2
    done = []
    for r, circle in enumerate(circles):
        last_one = r == some - 1
        mixes = call(
            functools.partial(circle_kernel, levels, len(done) if last_one else 0),
            [piece if last_one else (cols, channels)] * levels,
            [lon_proj, *(done if last_one else []), *circle],
            flops=work // 4,
        )
        done = done + list(mixes)
    mixes = exchange(mixes)
    (out,) = call(
        functools.partial(last_kernel, levels),
        [(rows, cols, channels)],
        [*mixes, inner_two, outer_two, lon_proj],
    )
    return out


def solution(mesh):
    return jax.shard_map(
        shards,
        mesh=mesh,
        in_specs=(P("lat", "lon", None), P(), P(), P(), P(), P()),
        out_specs=P("lat", "lon", None),
        check_vma=False,
    )
```

```python
import functools

import jax
import jax.numpy as jnp
from jax import lax
from jax.experimental import pallas as pl
from jax.experimental.pallas import tpu as pltpu
from jax.sharding import PartitionSpec as P

HEADS = 8
HALO = 3
TAPS = 2 * HALO + 1
STRIP = 8
SIDE = 4
LANES = 128
LEVELS = 4
STAGES = 4
EPSILON = 1e-06
VMEM_BYTES = 24 * 1024 * 1024
STAGE_BYTES = 103 * 512 * 1024
bf16, f32 = jnp.bfloat16, jnp.float32


def layer_norm(values):
    average = jnp.mean(values, axis=-1, keepdims=True)
    centered = values - average
    variance = jnp.mean(centered * centered, axis=-1, keepdims=True)
    return centered * lax.rsqrt(variance + EPSILON)


def dot(rows, matrix):
    return jnp.dot(rows, matrix, preferred_element_type=f32)


def dot_t(rows, matrix):
    return lax.dot_general(rows, matrix, (((1,), (1,)), ((), ())), preferred_element_type=f32)


def gelu(values):
    size = jnp.abs(values)
    t = 1.0 / (1.0 + (0.3275911 * 0.5**0.5) * size)
    tail = 1.061405429 * t - 1.453152027
    for coefficient in (1.421413741, -0.284496736, 0.254829592):
        tail = tail * t + coefficient
    tail = (0.5 * size * t) * tail * jnp.exp(-0.5 * values * values)
    return jnp.maximum(values, 0.0) - tail


def attend(queries, keys, values, mask):
    count, channels = queries.shape
    head_size = channels // HEADS
    lane_head = lax.broadcasted_iota(jnp.int32, (1, channels), 1) // head_size
    picks = [lane_head == h for h in range(HEADS)]
    none = jnp.zeros_like(queries)
    stacked = jnp.concatenate([jnp.where(pick, queries, none) for pick in picks], axis=0)
    scores = dot_t(stacked, keys) * head_size ** (-0.5)
    if mask is not None:
        scores = scores.reshape(HEADS, count, keys.shape[0])
        scores = jnp.where(mask[None], scores, -1e30).reshape(HEADS * count, keys.shape[0])
    top = jnp.max(scores, axis=-1, keepdims=True)
    probs = jnp.exp(scores - top)
    totals = jnp.sum(probs, axis=-1, keepdims=True)
    mixed = dot(probs.astype(bf16), values) * (1.0 / totals)
    out = mixed[:count]
    for h in range(1, HEADS):
        out = jnp.where(picks[h], mixed[h * count : (h + 1) * count], out)
    return out.astype(bf16)


def stage_kernel(count, *refs):
    sources, dw_ref = refs[:count], refs[count]
    targets, taps_ref, dw, sems = refs[count + 1 : 2 * count + 1], *refs[2 * count + 1 :]
    copies = [pltpu.make_async_copy(dw_ref, dw, sems.at[count, 0])]
    pieces = sems.shape[1]
    for i in range(count):
        source, target = sources[i], targets[i]
        size = source.shape[0] // pieces
        for k in range(pieces):
            part = pl.ds(k * size, size)
            copies.append(pltpu.make_async_copy(source.at[part], target.at[part], sems.at[i, k]))
    for copy in copies:
        copy.start()
    for copy in copies:
        copy.wait()
    taps_ref[...] = dw[...].astype(f32)


def hops_in(levels):
    return [0, *range(levels - 1, 0, -1)]


def hops_back(levels):
    return [0] + [h for h in (*range(levels // 2, levels), *range(1, levels // 2)) if h]


def peer(levels, hops):
    return (lax.axis_index("lon") // (lax.axis_size("lon") // levels)) ^ hops


def strip_kernel(nlat, *refs):
    tiles = refs[:nlat]
    near_ref, far_ref, near, far = refs[nlat + 1 :]
    rows, cols, channels = tiles[0].shape
    even = lax.axis_index("lon") % 2 == 0
    for s in range(nlat):
        values = tiles[s][...].astype(f32)
        first, last = values[:, :STRIP], values[:, cols - STRIP :]
        where = pl.ds(lax.rem(lax.axis_index("lat") + s, nlat) * rows, rows)
        near[where] = jnp.where(even, last, first)
        far[where] = jnp.where(even, first, last)
    for strip, strip_ref, is_last in ((near, near_ref, even), (far, far_ref, ~even)):
        strip_ref[...] = pack(strip[...], is_last).reshape(strip_ref.shape).astype(bf16)


def lower_half():
    return lax.broadcasted_iota(jnp.int32, (1, STRIP, 1), 1) < SIDE


def turn(values):
    return pltpu.roll(values, SIDE, axis=1)


def pack(strip, is_last):
    half = strip.shape[0] // 2
    turned = turn(strip)
    low = jnp.where(is_last, turned, strip)
    high = jnp.where(is_last, strip, turned)
    return jnp.where(lower_half(), low[:half], high[half:])


def unpack(packed, is_left):
    turned = turn(packed)
    low = jnp.where(is_left, turned, packed)
    high = jnp.where(is_left, packed, turned)
    return jnp.concatenate([low, high], axis=0)


def chain(my_lat, slab, shape, taps_ref, expand_ref, reduce_ref, attn_ref, center, scratch):
    one, lat_in = scratch
    rows, all_rows, columns, channels = shape
    cells = all_rows * columns
    parts = []
    for c in range(0, channels, LANES):
        acc = jnp.zeros((all_rows, columns, LANES), f32)
        for b in range(TAPS):
            block = slab(b, c)
            for a in range(TAPS):
                tap = taps_ref[a, b : b + 1, c : c + LANES].reshape(1, 1, LANES)
                acc = acc + block[a : a + all_rows] * tap
        parts.append(acc.reshape(cells, LANES))
    normed = layer_norm(jnp.concatenate(parts, axis=-1)).astype(bf16)

    def widen(k, total):
        part = slice(k * channels, (k + 1) * channels)
        wide = gelu(dot(normed, expand_ref[:, part])).astype(bf16)
        return total + dot(wide, reduce_ref[part])

    total = center.reshape(cells, channels)
    for k in range(expand_ref.shape[1] // channels):
        total = widen(k, total)
    block_one = total.astype(bf16)
    one[...] = block_one
    every = layer_norm(block_one.astype(f32)).astype(bf16)
    lat_in[...] = every
    count = rows * columns
    own = pl.ds(pl.multiple_of(my_lat * count, count), count)
    queries = dot(lat_in[own], attn_ref[0]).astype(bf16)
    keys = dot(every, attn_ref[1]).astype(bf16)
    values = dot(every, attn_ref[2]).astype(bf16)
    row_col = lax.broadcasted_iota(jnp.int32, (count, 1), 0) % columns
    key_col = lax.broadcasted_iota(jnp.int32, (1, cells), 1) % columns
    mix = attend(queries, keys, values, row_col == key_col)
    block_two = (one[own].astype(f32) + dot(mix, attn_ref[3])).astype(bf16)
    return block_two, layer_norm(block_two.astype(f32))


def fill(padded, all_rows, first, values):
    width = values.shape[1]
    padded[HALO : HALO + all_rows, first : first + width] = values


def fill_tiles(padded, my_lat, first, tiles):
    rows, cols = tiles[0].shape[:2]
    for s in range(len(tiles)):
        place = HALO + lax.rem(my_lat + s, len(tiles)) * rows
        padded[pl.ds(place, rows), first : first + cols] = tiles[s][...].astype(f32)


def clear(padded, all_rows):
    edge = jnp.zeros((HALO,) + padded.shape[1:], f32)
    padded[:HALO] = edge
    padded[HALO + all_rows :] = edge


def inner_kernel(nlat, *refs):
    tiles, refs = refs[:nlat], refs[nlat:]
    taps_ref, expand_ref, reduce_ref, attn_ref, two_ref, in_ref, padded, *scratch = refs
    rows, cols, channels = tiles[0].shape
    all_rows = rows * nlat
    columns = cols - 2 * SIDE
    clear(padded, all_rows)
    my_lat = lax.axis_index("lat")
    fill_tiles(padded, my_lat, 0, tiles)

    def slab(b, c):
        first = SIDE - HALO + b
        return padded[:, first : first + columns, c : c + LANES]

    center = padded[HALO : HALO + all_rows, SIDE : SIDE + columns]
    shape = (rows, all_rows, columns, channels)
    block_two, lon_in = chain(
        my_lat, slab, shape, taps_ref, expand_ref, reduce_ref, attn_ref, center, scratch
    )
    two_ref[...] = block_two
    in_ref[...] = lon_in.astype(bf16)


def outer_kernel(nlat, levels, *refs):
    tiles, refs = refs[:nlat], refs[nlat:]
    far_ref, near_ref, inner_in_ref, taps_ref, expand_ref, reduce_ref, attn_ref = refs[:7]
    two_ref, *refs = refs[7:]
    sent_refs, (sent, padded, *scratch) = refs[:levels], refs[levels:]
    rows, cols, channels = tiles[0].shape
    all_rows = rows * nlat
    columns = 2 * SIDE
    packed = (all_rows // 2, STRIP, channels)
    near = near_ref[...].astype(f32).reshape(packed)
    far = far_ref[...].astype(f32).reshape(packed)
    even = lax.axis_index("lon") % 2 == 0
    my_lat = lax.axis_index("lat")
    clear(padded, all_rows)
    fill(padded, all_rows, 0, unpack(jnp.where(even, far, near), True))
    fill_tiles(padded, my_lat, STRIP, tiles)
    fill(padded, all_rows, STRIP + cols, unpack(jnp.where(even, near, far), False))
    sublane = lax.broadcasted_iota(jnp.int32, (1, columns, 1), 1)

    def halves(shift, rows_of, c, width):
        right = STRIP + cols - SIDE + shift
        left = STRIP - SIDE + shift
        return jnp.where(
            sublane < SIDE,
            padded[rows_of, right : right + columns, c : c + width],
            padded[rows_of, left : left + columns, c : c + width],
        )

    def slab(b, c):
        return halves(b - HALO, slice(None), c, LANES)

    center = halves(0, slice(HALO, HALO + all_rows), 0, channels)
    shape = (rows, all_rows, columns, channels)
    block_two, lon_in = chain(
        my_lat, slab, shape, taps_ref, expand_ref, reduce_ref, attn_ref, center, scratch
    )
    two_ref[...] = block_two
    inner = inner_in_ref[...].astype(f32).reshape(rows, cols - columns, channels)
    outer = lon_in.reshape(rows, columns, channels)
    sent[...] = jnp.concatenate([inner, outer], axis=1).astype(bf16)
    some = rows // levels
    for k in range(levels):
        part = sent[pl.ds(peer(levels, hops_in(levels)[k]) * some, some)]
        sent_refs[k][...] = part.reshape(sent_refs[k].shape)


def join_kernel(levels, some, *refs):
    parts, joined = refs[:levels], refs[levels:]
    cols = parts[0].shape[0] // some
    for r in range(some):
        for k in range(levels):
            joined[r][k * cols : (k + 1) * cols] = parts[k][r * cols : (r + 1) * cols]


def circle_kernel(levels, before, *refs):
    attn_ref, refs = refs[0], refs[1:]
    done, refs = refs[:before], refs[before:]
    parts, mix_refs = refs[:-levels], refs[-levels:]
    own = parts[0][...]
    every = jnp.concatenate([own] + [part[...] for part in parts[1:]], axis=0)
    queries = dot(own, attn_ref[0]).astype(bf16)
    keys = dot(every, attn_ref[1]).astype(bf16)
    values = dot(every, attn_ref[2]).astype(bf16)
    mix = attend(queries, keys, values, None)
    cols = own.shape[0] // levels
    for k in range(levels):
        for r in range(before // levels):
            mix_refs[k][r * cols : (r + 1) * cols] = done[r * levels + k][...]
        mix_refs[k][before // levels * cols :] = mix[k * cols : (k + 1) * cols]


def last_kernel(levels, *refs):
    parts = refs[:levels]
    inner_ref, outer_ref, attn_ref, out_ref = refs[levels:]
    rows, cols, channels = out_ref.shape
    columns = 2 * SIDE
    some = rows // levels
    every = jnp.concatenate([part[...] for part in parts], axis=0)
    change = dot(every, attn_ref[3]).reshape(levels, some, cols, channels)
    for k in range(levels):
        start = peer(levels, hops_back(levels)[k]) * some

        def state(ref, width):
            count = some * width
            place = pl.ds(pl.multiple_of(start * width, count), count)
            return ref[place].astype(f32).reshape(some, width, channels)

        before = jnp.concatenate(
            [state(inner_ref, cols - columns), state(outer_ref, columns)], axis=1
        )
        total = pltpu.roll(before + change[k], SIDE, axis=1)
        out_ref[pl.ds(start, some)] = total.astype(bf16)


def call(
    kernel, outs, operands, scratch=(), any_space=False, flops=0, grant=VMEM_BYTES
):
    vmem = pl.BlockSpec(memory_space=pltpu.VMEM)
    given = pl.BlockSpec(memory_space=pl.ANY) if any_space else vmem
    shapes = [
        out if isinstance(out, jax.ShapeDtypeStruct) else jax.ShapeDtypeStruct(out, bf16)
        for out in outs
    ]
    moved = sum(x.size * x.dtype.itemsize for x in operands)
    result = pl.pallas_call(
        kernel,
        out_shape=shapes,
        in_specs=[given] * len(operands),
        out_specs=[vmem] * len(outs),
        scratch_shapes=list(scratch),
        compiler_params=pltpu.CompilerParams(vmem_limit_bytes=grant),
        cost_estimate=pl.CostEstimate(flops=flops, bytes_accessed=moved, transcendentals=0),
    )(*operands)
    return result


def shards(field, dw_weight, w_expand, w_reduce, lat_attn, lon_attn):
    rows, cols, channels = field.shape
    nlat, nlon = lax.axis_size("lat"), lax.axis_size("lon")
    levels = min(LEVELS, nlon)
    column = nlon // levels
    some = rows // levels
    all_rows = rows * nlat
    columns = 2 * SIDE

    def swap(piece, mask):
        return lax.ppermute(piece, "lon", [(j, j ^ mask) for j in range(nlon)])

    def exchange(pieces, hops):
        cross = min(1, column - 1)
        return [swap(p, h * column + cross) if h else p for p, h in zip(pieces, hops)]

    tiles = [field]
    for s in range(1, nlat):
        tiles.append(lax.ppermute(field, "lat", [((i + s) % nlat, i) for i in range(nlat)]))
    weights = (w_expand, w_reduce, lat_attn, lon_attn)
    expand, reduce, lat_proj, lon_proj, taps = call(
        functools.partial(stage_kernel, len(weights)),
        [w.shape for w in weights] + [jax.ShapeDtypeStruct(dw_weight.shape, f32)],
        [*weights, dw_weight],
        [
            pltpu.VMEM(dw_weight.shape, bf16),
            pltpu.SemaphoreType.DMA((len(weights) + 1, STAGES)),
        ],
        any_space=True,
        grant=STAGE_BYTES,
    )

    strip = (all_rows * SIDE, channels)
    strip_scratch = pltpu.VMEM((all_rows, STRIP, channels), f32)
    near, far = call(
        functools.partial(strip_kernel, nlat),
        [strip, strip],
        [*tiles, reduce],
        [strip_scratch, strip_scratch],
    )
    far = lax.ppermute(
        far, "lon", [(j, (j - 1) % nlon if j % 2 == 0 else (j + 1) % nlon) for j in range(nlon)]
    )
    near = swap(near, 1)

    def scratch(width, count):
        return [
            pltpu.VMEM((all_rows + 2 * HALO, width, channels), f32),
            pltpu.VMEM((all_rows * count, channels), bf16),
            pltpu.VMEM((all_rows * count, channels), bf16),
        ]

    work = 4 * all_rows * columns * channels * w_expand.shape[1]
    inner_two, inner_in = call(
        functools.partial(inner_kernel, nlat),
        [(rows * (cols - columns), channels)] * 2,
        [*tiles, taps, expand, reduce, lat_proj],
        scratch(cols, cols - columns),
        flops=work,
    )
    piece = (some * cols, channels)
    outer_two, *parts = call(
        functools.partial(outer_kernel, nlat, levels),
        [(rows * columns, channels)] + [piece] * levels,
        [*tiles, far, near, inner_in, taps, expand, reduce, lat_proj],
        [pltpu.VMEM((rows, cols, channels), bf16)] + scratch(cols + 2 * STRIP, columns),
        flops=work,
    )

    parts = exchange(parts, hops_in(levels))
    joined = call(
        functools.partial(join_kernel, levels, some), [(levels * cols, channels)] * some, parts
    )
    circles = [[part] for part in joined]
    mask = column // 2
    while mask:
        for circle in circles:
            circle += [swap(part, mask + mask // 2) for part in circle]
        mask //= 2
    done = []
    for r, circle in enumerate(circles):
        last_one = r == some - 1
        mixes = call(
            functools.partial(circle_kernel, levels, len(done) if last_one else 0),
            [piece if last_one else (cols, channels)] * levels,
            [lon_proj, *(done if last_one else []), *circle],
            flops=work // 4,
        )
        done = done + list(mixes)
    mixes = dict(zip(hops_in(levels), mixes))
    mixes = exchange([mixes[h] for h in hops_back(levels)], hops_back(levels))
    (out,) = call(
        functools.partial(last_kernel, levels),
        [(rows, cols, channels)],
        [*mixes, inner_two, outer_two, lon_proj],
    )
    return out


def solution(mesh):
    return jax.shard_map(
        shards,
        mesh=mesh,
        in_specs=(P("lat", "lon", None), P(), P(), P(), P(), P()),
        out_specs=P("lat", "lon", None),
        check_vma=False,
    )
```

```python
import functools

import jax
import jax.numpy as jnp
from jax import lax
from jax.experimental import pallas as pl
from jax.experimental.pallas import tpu as pltpu
from jax.sharding import PartitionSpec as P

HEADS = 8
HALO = 3
TAPS = 2 * HALO + 1
STRIP = 8
SIDE = 4
LANES = 128
LEVELS = 4
STAGES = 4
EPSILON = 1e-06
VMEM_BYTES = 24 * 1024 * 1024
STAGE_BYTES = 103 * 512 * 1024
bf16, f32 = jnp.bfloat16, jnp.float32


def layer_norm(values):
    average = jnp.mean(values, axis=-1, keepdims=True)
    centered = values - average
    variance = jnp.mean(centered * centered, axis=-1, keepdims=True)
    return centered * lax.rsqrt(variance + EPSILON)


def dot(rows, matrix):
    return jnp.dot(rows, matrix, preferred_element_type=f32)


def dot_t(rows, matrix):
    return lax.dot_general(rows, matrix, (((1,), (1,)), ((), ())), preferred_element_type=f32)


def gelu(values):
    size = jnp.abs(values)
    t = 1.0 / (1.0 + (0.3275911 * 0.5**0.5) * size)
    tail = 1.061405429 * t - 1.453152027
    for coefficient in (1.421413741, -0.284496736, 0.254829592):
        tail = tail * t + coefficient
    tail = (0.5 * size * t) * tail * jnp.exp(-0.5 * values * values)
    return jnp.maximum(values, 0.0) - tail


def attend(queries, keys, values, mask):
    count, channels = queries.shape
    head_size = channels // HEADS
    lane_head = lax.broadcasted_iota(jnp.int32, (1, channels), 1) // head_size
    picks = [lane_head == h for h in range(HEADS)]
    none = jnp.zeros_like(queries)
    stacked = jnp.concatenate([jnp.where(pick, queries, none) for pick in picks], axis=0)
    scores = dot_t(stacked, keys) * head_size ** (-0.5)
    if mask is not None:
        scores = scores.reshape(HEADS, count, keys.shape[0])
        scores = jnp.where(mask[None], scores, -1e30).reshape(HEADS * count, keys.shape[0])
    top = jnp.max(scores, axis=-1, keepdims=True)
    probs = jnp.exp(scores - top)
    totals = jnp.sum(probs, axis=-1, keepdims=True)
    mixed = dot(probs.astype(bf16), values) * (1.0 / totals)
    out = mixed[:count]
    for h in range(1, HEADS):
        out = jnp.where(picks[h], mixed[h * count : (h + 1) * count], out)
    return out.astype(bf16)


def stage_kernel(count, *refs):
    sources, dw_ref = refs[:count], refs[count]
    targets, taps_ref, dw, sems = refs[count + 1 : 2 * count + 1], *refs[2 * count + 1 :]
    copies = [pltpu.make_async_copy(dw_ref, dw, sems.at[count, 0])]
    pieces = sems.shape[1]
    for i in range(count):
        source, target = sources[i], targets[i]
        size = source.shape[0] // pieces
        for k in range(pieces):
            part = pl.ds(k * size, size)
            copies.append(pltpu.make_async_copy(source.at[part], target.at[part], sems.at[i, k]))
    for copy in copies:
        copy.start()
    for copy in copies:
        copy.wait()
    taps_ref[...] = dw[...].astype(f32)


def hops_back(levels):
    return [0, *range(levels - 1, 0, -1)]


def hops_in(levels):
    return [0] + [h for h in (*range(levels // 2, levels), *range(1, levels // 2)) if h]


def peer(levels, hops):
    return (lax.axis_index("lon") // (lax.axis_size("lon") // levels)) ^ hops


def strip_kernel(nlat, *refs):
    tiles = refs[:nlat]
    near_ref, far_ref, near, far = refs[nlat + 1 :]
    rows, cols, channels = tiles[0].shape
    even = lax.axis_index("lon") % 2 == 0
    for s in range(nlat):
        values = tiles[s][...].astype(f32)
        first, last = values[:, :STRIP], values[:, cols - STRIP :]
        where = pl.ds(lax.rem(lax.axis_index("lat") + s, nlat) * rows, rows)
        near[where] = jnp.where(even, last, first)
        far[where] = jnp.where(even, first, last)
    for strip, strip_ref, is_last in ((near, near_ref, even), (far, far_ref, ~even)):
        strip_ref[...] = pack(strip[...], is_last).reshape(strip_ref.shape).astype(bf16)


def lower_half():
    return lax.broadcasted_iota(jnp.int32, (1, STRIP, 1), 1) < SIDE


def turn(values):
    return pltpu.roll(values, SIDE, axis=1)


def pack(strip, is_last):
    half = strip.shape[0] // 2
    turned = turn(strip)
    low = jnp.where(is_last, turned, strip)
    high = jnp.where(is_last, strip, turned)
    return jnp.where(lower_half(), low[:half], high[half:])


def unpack(packed, is_left):
    turned = turn(packed)
    low = jnp.where(is_left, turned, packed)
    high = jnp.where(is_left, packed, turned)
    return jnp.concatenate([low, high], axis=0)


def chain(my_lat, slab, shape, taps_ref, expand_ref, reduce_ref, attn_ref, center, scratch):
    one, lat_in = scratch
    rows, all_rows, columns, channels = shape
    cells = all_rows * columns
    parts = []
    for c in range(0, channels, LANES):
        acc = jnp.zeros((all_rows, columns, LANES), f32)
        for b in range(TAPS):
            block = slab(b, c)
            for a in range(TAPS):
                tap = taps_ref[a, b : b + 1, c : c + LANES].reshape(1, 1, LANES)
                acc = acc + block[a : a + all_rows] * tap
        parts.append(acc.reshape(cells, LANES))
    normed = layer_norm(jnp.concatenate(parts, axis=-1)).astype(bf16)

    def widen(k, total):
        part = slice(k * channels, (k + 1) * channels)
        wide = gelu(dot(normed, expand_ref[:, part])).astype(bf16)
        return total + dot(wide, reduce_ref[part])

    total = center.reshape(cells, channels)
    for k in range(expand_ref.shape[1] // channels):
        total = widen(k, total)
    block_one = total.astype(bf16)
    one[...] = block_one
    every = layer_norm(block_one.astype(f32)).astype(bf16)
    lat_in[...] = every
    count = rows * columns
    own = pl.ds(pl.multiple_of(my_lat * count, count), count)
    queries = dot(lat_in[own], attn_ref[0]).astype(bf16)
    keys = dot(every, attn_ref[1]).astype(bf16)
    values = dot(every, attn_ref[2]).astype(bf16)
    row_col = lax.broadcasted_iota(jnp.int32, (count, 1), 0) % columns
    key_col = lax.broadcasted_iota(jnp.int32, (1, cells), 1) % columns
    mix = attend(queries, keys, values, row_col == key_col)
    block_two = (one[own].astype(f32) + dot(mix, attn_ref[3])).astype(bf16)
    return block_two, layer_norm(block_two.astype(f32))


def fill(padded, all_rows, first, values):
    width = values.shape[1]
    padded[HALO : HALO + all_rows, first : first + width] = values


def fill_tiles(padded, my_lat, first, tiles):
    rows, cols = tiles[0].shape[:2]
    for s in range(len(tiles)):
        place = HALO + lax.rem(my_lat + s, len(tiles)) * rows
        padded[pl.ds(place, rows), first : first + cols] = tiles[s][...].astype(f32)


def clear(padded, all_rows):
    edge = jnp.zeros((HALO,) + padded.shape[1:], f32)
    padded[:HALO] = edge
    padded[HALO + all_rows :] = edge


def inner_kernel(nlat, *refs):
    tiles, refs = refs[:nlat], refs[nlat:]
    taps_ref, expand_ref, reduce_ref, attn_ref, two_ref, in_ref, padded, *scratch = refs
    rows, cols, channels = tiles[0].shape
    all_rows = rows * nlat
    columns = cols - 2 * SIDE
    clear(padded, all_rows)
    my_lat = lax.axis_index("lat")
    fill_tiles(padded, my_lat, 0, tiles)

    def slab(b, c):
        first = SIDE - HALO + b
        return padded[:, first : first + columns, c : c + LANES]

    center = padded[HALO : HALO + all_rows, SIDE : SIDE + columns]
    shape = (rows, all_rows, columns, channels)
    block_two, lon_in = chain(
        my_lat, slab, shape, taps_ref, expand_ref, reduce_ref, attn_ref, center, scratch
    )
    two_ref[...] = block_two
    in_ref[...] = lon_in.astype(bf16)


def outer_kernel(nlat, levels, *refs):
    tiles, refs = refs[:nlat], refs[nlat:]
    far_ref, near_ref, inner_in_ref, taps_ref, expand_ref, reduce_ref, attn_ref = refs[:7]
    two_ref, *refs = refs[7:]
    sent_refs, (sent, padded, *scratch) = refs[:levels], refs[levels:]
    rows, cols, channels = tiles[0].shape
    all_rows = rows * nlat
    columns = 2 * SIDE
    packed = (all_rows // 2, STRIP, channels)
    near = near_ref[...].astype(f32).reshape(packed)
    far = far_ref[...].astype(f32).reshape(packed)
    even = lax.axis_index("lon") % 2 == 0
    my_lat = lax.axis_index("lat")
    clear(padded, all_rows)
    fill(padded, all_rows, 0, unpack(jnp.where(even, far, near), True))
    fill_tiles(padded, my_lat, STRIP, tiles)
    fill(padded, all_rows, STRIP + cols, unpack(jnp.where(even, near, far), False))
    sublane = lax.broadcasted_iota(jnp.int32, (1, columns, 1), 1)

    def halves(shift, rows_of, c, width):
        right = STRIP + cols - SIDE + shift
        left = STRIP - SIDE + shift
        return jnp.where(
            sublane < SIDE,
            padded[rows_of, right : right + columns, c : c + width],
            padded[rows_of, left : left + columns, c : c + width],
        )

    def slab(b, c):
        return halves(b - HALO, slice(None), c, LANES)

    center = halves(0, slice(HALO, HALO + all_rows), 0, channels)
    shape = (rows, all_rows, columns, channels)
    block_two, lon_in = chain(
        my_lat, slab, shape, taps_ref, expand_ref, reduce_ref, attn_ref, center, scratch
    )
    two_ref[...] = block_two
    inner = inner_in_ref[...].astype(f32).reshape(rows, cols - columns, channels)
    outer = lon_in.reshape(rows, columns, channels)
    sent[...] = jnp.concatenate([inner, outer], axis=1).astype(bf16)
    some = rows // levels
    for k in range(levels):
        part = sent[pl.ds(peer(levels, hops_in(levels)[k]) * some, some)]
        sent_refs[k][...] = part.reshape(sent_refs[k].shape)


def join_kernel(levels, some, *refs):
    parts, joined = refs[:levels], refs[levels:]
    cols = parts[0].shape[0] // some
    for r in range(some):
        for k in range(levels):
            joined[r][k * cols : (k + 1) * cols] = parts[k][r * cols : (r + 1) * cols]


def circle_kernel(levels, before, *refs):
    attn_ref, refs = refs[0], refs[1:]
    done, refs = refs[:before], refs[before:]
    parts, mix_refs = refs[:-levels], refs[-levels:]
    own = parts[0][...]
    every = jnp.concatenate([own] + [part[...] for part in parts[1:]], axis=0)
    queries = dot(own, attn_ref[0]).astype(bf16)
    keys = dot(every, attn_ref[1]).astype(bf16)
    values = dot(every, attn_ref[2]).astype(bf16)
    mix = attend(queries, keys, values, None)
    cols = own.shape[0] // levels
    for k in range(levels):
        for r in range(before // levels):
            mix_refs[k][r * cols : (r + 1) * cols] = done[r * levels + k][...]
        mix_refs[k][before // levels * cols :] = mix[k * cols : (k + 1) * cols]


def last_kernel(levels, *refs):
    parts = refs[:levels]
    inner_ref, outer_ref, attn_ref, out_ref = refs[levels:]
    rows, cols, channels = out_ref.shape
    columns = 2 * SIDE
    some = rows // levels
    every = jnp.concatenate([part[...] for part in parts], axis=0)
    change = dot(every, attn_ref[3]).reshape(levels, some, cols, channels)
    for k in range(levels):
        start = peer(levels, hops_back(levels)[k]) * some

        def state(ref, width):
            count = some * width
            place = pl.ds(pl.multiple_of(start * width, count), count)
            return ref[place].astype(f32).reshape(some, width, channels)

        before = jnp.concatenate(
            [state(inner_ref, cols - columns), state(outer_ref, columns)], axis=1
        )
        total = pltpu.roll(before + change[k], SIDE, axis=1)
        out_ref[pl.ds(start, some)] = total.astype(bf16)


def call(
    kernel, outs, operands, scratch=(), any_space=False, flops=0, grant=VMEM_BYTES
):
    vmem = pl.BlockSpec(memory_space=pltpu.VMEM)
    given = pl.BlockSpec(memory_space=pl.ANY) if any_space else vmem
    shapes = [
        out if isinstance(out, jax.ShapeDtypeStruct) else jax.ShapeDtypeStruct(out, bf16)
        for out in outs
    ]
    moved = sum(x.size * x.dtype.itemsize for x in operands)
    result = pl.pallas_call(
        kernel,
        out_shape=shapes,
        in_specs=[given] * len(operands),
        out_specs=[vmem] * len(outs),
        scratch_shapes=list(scratch),
        compiler_params=pltpu.CompilerParams(vmem_limit_bytes=grant),
        cost_estimate=pl.CostEstimate(flops=flops, bytes_accessed=moved, transcendentals=0),
    )(*operands)
    return result


def shards(field, dw_weight, w_expand, w_reduce, lat_attn, lon_attn):
    rows, cols, channels = field.shape
    nlat, nlon = lax.axis_size("lat"), lax.axis_size("lon")
    levels = min(LEVELS, nlon)
    column = nlon // levels
    some = rows // levels
    all_rows = rows * nlat
    columns = 2 * SIDE

    def swap(piece, mask):
        return lax.ppermute(piece, "lon", [(j, j ^ mask) for j in range(nlon)])

    def exchange(pieces, hops):
        cross = min(1, column - 1)
        return [swap(p, h * column + cross) if h else p for p, h in zip(pieces, hops)]

    tiles = [field]
    for s in range(1, nlat):
        tiles.append(lax.ppermute(field, "lat", [((i + s) % nlat, i) for i in range(nlat)]))
    weights = (w_expand, w_reduce, lat_attn, lon_attn)
    expand, reduce, lat_proj, lon_proj, taps = call(
        functools.partial(stage_kernel, len(weights)),
        [w.shape for w in weights] + [jax.ShapeDtypeStruct(dw_weight.shape, f32)],
        [*weights, dw_weight],
        [
            pltpu.VMEM(dw_weight.shape, bf16),
            pltpu.SemaphoreType.DMA((len(weights) + 1, STAGES)),
        ],
        any_space=True,
        grant=STAGE_BYTES,
    )

    strip = (all_rows * SIDE, channels)
    strip_scratch = pltpu.VMEM((all_rows, STRIP, channels), f32)
    near, far = call(
        functools.partial(strip_kernel, nlat),
        [strip, strip],
        [*tiles, reduce],
        [strip_scratch, strip_scratch],
    )
    far = lax.ppermute(
        far, "lon", [(j, (j - 1) % nlon if j % 2 == 0 else (j + 1) % nlon) for j in range(nlon)]
    )
    near = swap(near, 1)

    def scratch(width, count):
        return [
            pltpu.VMEM((all_rows + 2 * HALO, width, channels), f32),
            pltpu.VMEM((all_rows * count, channels), bf16),
            pltpu.VMEM((all_rows * count, channels), bf16),
        ]

    work = 4 * all_rows * columns * channels * w_expand.shape[1]
    inner_two, inner_in = call(
        functools.partial(inner_kernel, nlat),
        [(rows * (cols - columns), channels)] * 2,
        [*tiles, taps, expand, reduce, lat_proj],
        scratch(cols, cols - columns),
        flops=work,
    )
    piece = (some * cols, channels)
    outer_two, *parts = call(
        functools.partial(outer_kernel, nlat, levels),
        [(rows * columns, channels)] + [piece] * levels,
        [*tiles, far, near, inner_in, taps, expand, reduce, lat_proj],
        [pltpu.VMEM((rows, cols, channels), bf16)] + scratch(cols + 2 * STRIP, columns),
        flops=work,
    )

    parts = exchange(parts, hops_in(levels))
    joined = call(
        functools.partial(join_kernel, levels, some), [(levels * cols, channels)] * some, parts
    )
    circles = [[part] for part in joined]
    mask = column // 2
    while mask:
        for circle in circles:
            circle += [swap(part, mask + mask // 2) for part in circle]
        mask //= 2
    done = []
    for r, circle in enumerate(circles):
        last_one = r == some - 1
        mixes = call(
            functools.partial(circle_kernel, levels, len(done) if last_one else 0),
            [piece if last_one else (cols, channels)] * levels,
            [lon_proj, *(done if last_one else []), *circle],
            flops=work // 4,
        )
        done = done + list(mixes)
    mixes = dict(zip(hops_in(levels), mixes))
    mixes = exchange([mixes[h] for h in hops_back(levels)], hops_back(levels))
    (out,) = call(
        functools.partial(last_kernel, levels),
        [(rows, cols, channels)],
        [*mixes, inner_two, outer_two, lon_proj],
    )
    return out


def solution(mesh):
    return jax.shard_map(
        shards,
        mesh=mesh,
        in_specs=(P("lat", "lon", None), P(), P(), P(), P(), P()),
        out_specs=P("lat", "lon", None),
        check_vma=False,
    )
```

```python
import functools

import jax
import jax.numpy as jnp
from jax import lax
from jax.experimental import pallas as pl
from jax.experimental.pallas import tpu as pltpu
from jax.sharding import PartitionSpec as P

HEADS = 8
HALO = 3
TAPS = 2 * HALO + 1
STRIP = 8
SIDE = 4
LANES = 128
LEVELS = 4
STAGES = 4
EPSILON = 1e-06
VMEM_BYTES = 24 * 1024 * 1024
STAGE_BYTES = 103 * 512 * 1024
bf16, f32 = jnp.bfloat16, jnp.float32


def layer_norm(values):
    average = jnp.mean(values, axis=-1, keepdims=True)
    centered = values - average
    variance = jnp.mean(centered * centered, axis=-1, keepdims=True)
    return centered * lax.rsqrt(variance + EPSILON)


def dot(rows, matrix):
    return jnp.dot(rows, matrix, preferred_element_type=f32)


def dot_t(rows, matrix):
    return lax.dot_general(rows, matrix, (((1,), (1,)), ((), ())), preferred_element_type=f32)


def gelu(values):
    size = jnp.abs(values)
    t = 1.0 / (1.0 + (0.3275911 * 0.5**0.5) * size)
    tail = 1.061405429 * t - 1.453152027
    for coefficient in (1.421413741, -0.284496736, 0.254829592):
        tail = tail * t + coefficient
    tail = (0.5 * size * t) * tail * jnp.exp(-0.5 * values * values)
    return jnp.maximum(values, 0.0) - tail


def attend(queries, keys, values, mask):
    count, channels = queries.shape
    head_size = channels // HEADS
    lane_head = lax.broadcasted_iota(jnp.int32, (1, channels), 1) // head_size
    picks = [lane_head == h for h in range(HEADS)]
    none = jnp.zeros_like(queries)
    stacked = jnp.concatenate([jnp.where(pick, queries, none) for pick in picks], axis=0)
    scores = dot_t(stacked, keys) * head_size ** (-0.5)
    if mask is not None:
        scores = scores.reshape(HEADS, count, keys.shape[0])
        scores = jnp.where(mask[None], scores, -1e30).reshape(HEADS * count, keys.shape[0])
    top = jnp.max(scores, axis=-1, keepdims=True)
    probs = jnp.exp(scores - top)
    totals = jnp.sum(probs, axis=-1, keepdims=True)
    mixed = dot(probs.astype(bf16), values) * (1.0 / totals)
    out = mixed[:count]
    for h in range(1, HEADS):
        out = jnp.where(picks[h], mixed[h * count : (h + 1) * count], out)
    return out.astype(bf16)


def stage_kernel(count, *refs):
    sources, targets, sems = refs[:count], refs[count : 2 * count], refs[-1]
    copies = []
    for i in range(count):
        source, target = sources[i], targets[i]
        pieces = sems.shape[1] if source.shape[0] % sems.shape[1] == 0 else 1
        size = source.shape[0] // pieces
        for k in range(pieces):
            part = pl.ds(k * size, size)
            copies.append(pltpu.make_async_copy(source.at[part], target.at[part], sems.at[i, k]))
    for copy in copies:
        copy.start()
    for copy in copies:
        copy.wait()


def hops_of(levels):
    return [0] + [h for h in (*range(levels // 2, levels), *range(1, levels // 2)) if h]


def peer(levels, k):
    level = lax.axis_index("lon") // (lax.axis_size("lon") // levels)
    return level ^ hops_of(levels)[k]


def strip_kernel(nlat, *refs):
    tiles = refs[:nlat]
    near_ref, far_ref, near, far = refs[nlat + 1 :]
    rows, cols, channels = tiles[0].shape
    even = lax.axis_index("lon") % 2 == 0
    for s in range(nlat):
        values = tiles[s][...].astype(f32)
        first, last = values[:, :STRIP], values[:, cols - STRIP :]
        where = pl.ds(lax.rem(lax.axis_index("lat") + s, nlat) * rows, rows)
        near[where] = jnp.where(even, last, first)
        far[where] = jnp.where(even, first, last)
    for strip, strip_ref, is_last in ((near, near_ref, even), (far, far_ref, ~even)):
        strip_ref[...] = pack(strip[...], is_last).reshape(strip_ref.shape).astype(bf16)


def lower_half():
    return lax.broadcasted_iota(jnp.int32, (1, STRIP, 1), 1) < SIDE


def turn(values):
    return pltpu.roll(values, SIDE, axis=1)


def pack(strip, is_last):
    half = strip.shape[0] // 2
    turned = turn(strip)
    low = jnp.where(is_last, turned, strip)
    high = jnp.where(is_last, strip, turned)
    return jnp.where(lower_half(), low[:half], high[half:])


def unpack(packed, is_left):
    turned = turn(packed)
    low = jnp.where(is_left, turned, packed)
    high = jnp.where(is_left, packed, turned)
    return jnp.concatenate([low, high], axis=0)


def chain(my_lat, slab, shape, dw_ref, expand_ref, reduce_ref, attn_ref, center, scratch):
    taps, one, lat_in = scratch
    taps[...] = dw_ref[...].astype(f32)
    rows, all_rows, columns, channels = shape
    cells = all_rows * columns
    parts = []
    for c in range(0, channels, LANES):
        acc = jnp.zeros((all_rows, columns, LANES), f32)
        for b in range(TAPS):
            block = slab(b, c)
            for a in range(TAPS):
                tap = taps[a, b : b + 1, c : c + LANES].reshape(1, 1, LANES)
                acc = acc + block[a : a + all_rows] * tap
        parts.append(acc.reshape(cells, LANES))
    normed = layer_norm(jnp.concatenate(parts, axis=-1)).astype(bf16)

    def widen(k, total):
        part = slice(k * channels, (k + 1) * channels)
        wide = gelu(dot(normed, expand_ref[:, part])).astype(bf16)
        return total + dot(wide, reduce_ref[part])

    total = center.reshape(cells, channels)
    for k in range(expand_ref.shape[1] // channels):
        total = widen(k, total)
    block_one = total.astype(bf16)
    one[...] = block_one
    every = layer_norm(block_one.astype(f32)).astype(bf16)
    lat_in[...] = every
    count = rows * columns
    own = pl.ds(pl.multiple_of(my_lat * count, count), count)
    queries = dot(lat_in[own], attn_ref[0]).astype(bf16)
    keys = dot(every, attn_ref[1]).astype(bf16)
    values = dot(every, attn_ref[2]).astype(bf16)
    row_col = lax.broadcasted_iota(jnp.int32, (count, 1), 0) % columns
    key_col = lax.broadcasted_iota(jnp.int32, (1, cells), 1) % columns
    mix = attend(queries, keys, values, row_col == key_col)
    block_two = (one[own].astype(f32) + dot(mix, attn_ref[3])).astype(bf16)
    return block_two, layer_norm(block_two.astype(f32))


def fill(padded, all_rows, first, values):
    width = values.shape[1]
    padded[HALO : HALO + all_rows, first : first + width] = values


def fill_tiles(padded, my_lat, first, tiles):
    rows, cols = tiles[0].shape[:2]
    for s in range(len(tiles)):
        place = HALO + lax.rem(my_lat + s, len(tiles)) * rows
        padded[pl.ds(place, rows), first : first + cols] = tiles[s][...].astype(f32)


def clear(padded, all_rows):
    edge = jnp.zeros((HALO,) + padded.shape[1:], f32)
    padded[:HALO] = edge
    padded[HALO + all_rows :] = edge


def inner_kernel(nlat, *refs):
    tiles, refs = refs[:nlat], refs[nlat:]
    dw_ref, expand_ref, reduce_ref, attn_ref, two_ref, in_ref, padded, *scratch = refs
    rows, cols, channels = tiles[0].shape
    all_rows = rows * nlat
    columns = cols - 2 * SIDE
    clear(padded, all_rows)
    my_lat = lax.axis_index("lat")
    fill_tiles(padded, my_lat, 0, tiles)

    def slab(b, c):
        first = SIDE - HALO + b
        return padded[:, first : first + columns, c : c + LANES]

    center = padded[HALO : HALO + all_rows, SIDE : SIDE + columns]
    shape = (rows, all_rows, columns, channels)
    block_two, lon_in = chain(
        my_lat, slab, shape, dw_ref, expand_ref, reduce_ref, attn_ref, center, scratch
    )
    two_ref[...] = block_two
    in_ref[...] = lon_in.astype(bf16)


def outer_kernel(nlat, levels, *refs):
    tiles, refs = refs[:nlat], refs[nlat:]
    far_ref, near_ref, inner_in_ref, dw_ref, expand_ref, reduce_ref, attn_ref = refs[:7]
    two_ref, *refs = refs[7:]
    sent_refs, (sent, padded, *scratch) = refs[:levels], refs[levels:]
    rows, cols, channels = tiles[0].shape
    all_rows = rows * nlat
    columns = 2 * SIDE
    packed = (all_rows // 2, STRIP, channels)
    near = near_ref[...].astype(f32).reshape(packed)
    far = far_ref[...].astype(f32).reshape(packed)
    even = lax.axis_index("lon") % 2 == 0
    my_lat = lax.axis_index("lat")
    clear(padded, all_rows)
    fill(padded, all_rows, 0, unpack(jnp.where(even, far, near), True))
    fill_tiles(padded, my_lat, STRIP, tiles)
    fill(padded, all_rows, STRIP + cols, unpack(jnp.where(even, near, far), False))
    sublane = lax.broadcasted_iota(jnp.int32, (1, columns, 1), 1)

    def halves(shift, rows_of, c, width):
        right = STRIP + cols - SIDE + shift
        left = STRIP - SIDE + shift
        return jnp.where(
            sublane < SIDE,
            padded[rows_of, right : right + columns, c : c + width],
            padded[rows_of, left : left + columns, c : c + width],
        )

    def slab(b, c):
        return halves(b - HALO, slice(None), c, LANES)

    center = halves(0, slice(HALO, HALO + all_rows), 0, channels)
    shape = (rows, all_rows, columns, channels)
    block_two, lon_in = chain(
        my_lat, slab, shape, dw_ref, expand_ref, reduce_ref, attn_ref, center, scratch
    )
    two_ref[...] = block_two
    inner = inner_in_ref[...].astype(f32).reshape(rows, cols - columns, channels)
    outer = lon_in.reshape(rows, columns, channels)
    sent[...] = jnp.concatenate([inner, outer], axis=1).astype(bf16)
    some = rows // levels
    for k in range(levels):
        part = sent[pl.ds(peer(levels, k) * some, some)]
        sent_refs[k][...] = part.reshape(sent_refs[k].shape)


def join_kernel(levels, some, *refs):
    parts, joined = refs[:levels], refs[levels:]
    cols = parts[0].shape[0] // some
    for r in range(some):
        for k in range(levels):
            joined[r][k * cols : (k + 1) * cols] = parts[k][r * cols : (r + 1) * cols]


def circle_kernel(levels, before, *refs):
    attn_ref, refs = refs[0], refs[1:]
    done, refs = refs[:before], refs[before:]
    parts, mix_refs = refs[:-levels], refs[-levels:]
    own = parts[0][...]
    every = jnp.concatenate([own] + [part[...] for part in parts[1:]], axis=0)
    queries = dot(own, attn_ref[0]).astype(bf16)
    keys = dot(every, attn_ref[1]).astype(bf16)
    values = dot(every, attn_ref[2]).astype(bf16)
    mix = attend(queries, keys, values, None)
    cols = own.shape[0] // levels
    for k in range(levels):
        for r in range(before // levels):
            mix_refs[k][r * cols : (r + 1) * cols] = done[r * levels + k][...]
        mix_refs[k][before // levels * cols :] = mix[k * cols : (k + 1) * cols]


def last_kernel(levels, *refs):
    parts = refs[:levels]
    inner_ref, outer_ref, attn_ref, out_ref = refs[levels:]
    rows, cols, channels = out_ref.shape
    columns = 2 * SIDE
    some = rows // levels
    every = jnp.concatenate([part[...] for part in parts], axis=0)
    change = dot(every, attn_ref[3]).reshape(levels, some, cols, channels)
    for k in range(levels):
        start = peer(levels, k) * some

        def state(ref, width):
            count = some * width
            place = pl.ds(pl.multiple_of(start * width, count), count)
            return ref[place].astype(f32).reshape(some, width, channels)

        before = jnp.concatenate(
            [state(inner_ref, cols - columns), state(outer_ref, columns)], axis=1
        )
        total = pltpu.roll(before + change[k], SIDE, axis=1)
        out_ref[pl.ds(start, some)] = total.astype(bf16)


def call(
    kernel, outs, operands, scratch=(), any_space=False, flops=0, grant=VMEM_BYTES
):
    vmem = pl.BlockSpec(memory_space=pltpu.VMEM)
    given = pl.BlockSpec(memory_space=pl.ANY) if any_space else vmem
    shapes = [
        out if isinstance(out, jax.ShapeDtypeStruct) else jax.ShapeDtypeStruct(out, bf16)
        for out in outs
    ]
    moved = sum(x.size * x.dtype.itemsize for x in operands)
    result = pl.pallas_call(
        kernel,
        out_shape=shapes,
        in_specs=[given] * len(operands),
        out_specs=[vmem] * len(outs),
        scratch_shapes=list(scratch),
        compiler_params=pltpu.CompilerParams(vmem_limit_bytes=grant),
        cost_estimate=pl.CostEstimate(flops=flops, bytes_accessed=moved, transcendentals=0),
    )(*operands)
    return result


def shards(field, dw_weight, w_expand, w_reduce, lat_attn, lon_attn):
    rows, cols, channels = field.shape
    nlat, nlon = lax.axis_size("lat"), lax.axis_size("lon")
    levels = min(LEVELS, nlon)
    column = nlon // levels
    some = rows // levels
    all_rows = rows * nlat
    columns = 2 * SIDE

    def swap(piece, mask):
        return lax.ppermute(piece, "lon", [(j, j ^ mask) for j in range(nlon)])

    def exchange(pieces):
        cross = min(1, column - 1)
        return [
            swap(piece, hops * column + cross) if hops else piece
            for piece, hops in zip(pieces, hops_of(levels))
        ]

    tiles = [field]
    for s in range(1, nlat):
        tiles.append(lax.ppermute(field, "lat", [((i + s) % nlat, i) for i in range(nlat)]))
    weights = (dw_weight, w_expand, w_reduce, lat_attn, lon_attn)
    taps, expand, reduce, lat_proj, lon_proj = call(
        functools.partial(stage_kernel, len(weights)),
        [w.shape for w in weights],
        weights,
        [pltpu.SemaphoreType.DMA((len(weights), STAGES))],
        any_space=True,
        grant=STAGE_BYTES,
    )

    strip = (all_rows * SIDE, channels)
    strip_scratch = pltpu.VMEM((all_rows, STRIP, channels), f32)
    near, far = call(
        functools.partial(strip_kernel, nlat),
        [strip, strip],
        [*tiles, reduce],
        [strip_scratch, strip_scratch],
    )
    far = lax.ppermute(
        far, "lon", [(j, (j - 1) % nlon if j % 2 == 0 else (j + 1) % nlon) for j in range(nlon)]
    )
    near = swap(near, 1)

    def scratch(width, count):
        return [
            pltpu.VMEM((all_rows + 2 * HALO, width, channels), f32),
            pltpu.VMEM(dw_weight.shape, f32),
            pltpu.VMEM((all_rows * count, channels), bf16),
            pltpu.VMEM((all_rows * count, channels), bf16),
        ]

    work = 4 * all_rows * columns * channels * w_expand.shape[1]
    inner_two, inner_in = call(
        functools.partial(inner_kernel, nlat),
        [(rows * (cols - columns), channels)] * 2,
        [*tiles, taps, expand, reduce, lat_proj],
        scratch(cols, cols - columns),
        flops=work,
    )
    piece = (some * cols, channels)
    outer_two, *parts = call(
        functools.partial(outer_kernel, nlat, levels),
        [(rows * columns, channels)] + [piece] * levels,
        [*tiles, far, near, inner_in, taps, expand, reduce, lat_proj],
        [pltpu.VMEM((rows, cols, channels), bf16)] + scratch(cols + 2 * STRIP, columns),
        flops=work,
    )

    parts = exchange(parts)
    joined = call(
        functools.partial(join_kernel, levels, some), [(levels * cols, channels)] * some, parts
    )
    circles = [[part] for part in joined]
    mask = column // 2
    while mask:
        for circle in circles:
            circle += [swap(part, mask + mask // 2) for part in circle]
        mask //= 2
    done = []
    for r, circle in enumerate(circles):
        last_one = r == some - 1
        mixes = call(
            functools.partial(circle_kernel, levels, len(done) if last_one else 0),
            [piece if last_one else (cols, channels)] * levels,
            [lon_proj, *(done if last_one else []), *circle],
            flops=work // 4,
        )
        done = done + list(mixes)
    mixes = exchange(mixes)
    (out,) = call(
        functools.partial(last_kernel, levels),
        [(rows, cols, channels)],
        [*mixes, inner_two, outer_two, lon_proj],
    )
    return out


def solution(mesh):
    return jax.shard_map(
        shards,
        mesh=mesh,
        in_specs=(P("lat", "lon", None), P(), P(), P(), P(), P()),
        out_specs=P("lat", "lon", None),
        check_vma=False,
    )
```

```python
import functools

import jax
import jax.numpy as jnp
from jax import lax
from jax.experimental import pallas as pl
from jax.experimental.pallas import tpu as pltpu
from jax.sharding import PartitionSpec as P

HEADS = 8
HALO = 3
TAPS = 2 * HALO + 1
STRIP = 8
SIDE = 4
LANES = 128
LEVELS = 4
STAGES = 4
EPSILON = 1e-06
VMEM_BYTES = 24 * 1024 * 1024
STAGE_BYTES = 103 * 512 * 1024
bf16, f32 = jnp.bfloat16, jnp.float32


def layer_norm(values):
    average = jnp.mean(values, axis=-1, keepdims=True)
    centered = values - average
    variance = jnp.mean(centered * centered, axis=-1, keepdims=True)
    return centered * lax.rsqrt(variance + EPSILON)


def dot(rows, matrix):
    return jnp.dot(rows, matrix, preferred_element_type=f32)


def dot_t(rows, matrix):
    return lax.dot_general(rows, matrix, (((1,), (1,)), ((), ())), preferred_element_type=f32)


def gelu(values):
    size = jnp.abs(values)
    t = 1.0 / (1.0 + (0.3275911 * 0.5**0.5) * size)
    tail = 1.061405429 * t - 1.453152027
    for coefficient in (1.421413741, -0.284496736, 0.254829592):
        tail = tail * t + coefficient
    tail = (0.5 * size * t) * tail * jnp.exp(-0.5 * values * values)
    return jnp.maximum(values, 0.0) - tail


def attend(queries, keys, values, mask):
    count, channels = queries.shape
    head_size = channels // HEADS
    lane_head = lax.broadcasted_iota(jnp.int32, (1, channels), 1) // head_size
    picks = [lane_head == h for h in range(HEADS)]
    none = jnp.zeros_like(queries)
    stacked = jnp.concatenate([jnp.where(pick, queries, none) for pick in picks], axis=0)
    scores = dot_t(stacked, keys) * head_size ** (-0.5)
    if mask is not None:
        scores = scores.reshape(HEADS, count, keys.shape[0])
        scores = jnp.where(mask[None], scores, -1e30).reshape(HEADS * count, keys.shape[0])
    top = jnp.max(scores, axis=-1, keepdims=True)
    probs = jnp.exp(scores - top)
    totals = jnp.sum(probs, axis=-1, keepdims=True)
    mixed = dot(probs.astype(bf16), values) * (1.0 / totals)
    out = mixed[:count]
    for h in range(1, HEADS):
        out = jnp.where(picks[h], mixed[h * count : (h + 1) * count], out)
    return out.astype(bf16)


def stage_kernel(count, *refs):
    sources, targets, sems = refs[:count], refs[count : 2 * count], refs[-1]
    copies = []
    for i in range(count):
        source, target = sources[i], targets[i]
        pieces = sems.shape[1] if source.shape[0] % sems.shape[1] == 0 else 1
        size = source.shape[0] // pieces
        for k in range(pieces):
            part = pl.ds(k * size, size)
            copies.append(pltpu.make_async_copy(source.at[part], target.at[part], sems.at[i, k]))
    for copy in copies:
        copy.start()
    for copy in copies:
        copy.wait()


def hops_of(levels):
    return [0] + [h for h in (*range(levels // 2, levels), *range(1, levels // 2)) if h]


def peer(levels, k):
    level = lax.axis_index("lon") // (lax.axis_size("lon") // levels)
    return level ^ hops_of(levels)[k]


def strip_kernel(nlat, *refs):
    tiles = refs[:nlat]
    near_ref, far_ref, near, far = refs[nlat + 1 :]
    rows, cols, channels = tiles[0].shape
    even = lax.axis_index("lon") % 2 == 0
    for s in range(nlat):
        values = tiles[s][...].astype(f32)
        first, last = values[:, :STRIP], values[:, cols - STRIP :]
        where = pl.ds(lax.rem(lax.axis_index("lat") + s, nlat) * rows, rows)
        near[where] = jnp.where(even, last, first)
        far[where] = jnp.where(even, first, last)
    for strip, strip_ref, is_last in ((near, near_ref, even), (far, far_ref, ~even)):
        strip_ref[...] = pack(strip[...], is_last).reshape(strip_ref.shape).astype(bf16)


def lower_half():
    return lax.broadcasted_iota(jnp.int32, (1, STRIP, 1), 1) < SIDE


def turn(values):
    return pltpu.roll(values, SIDE, axis=1)


def pack(strip, is_last):
    half = strip.shape[0] // 2
    turned = turn(strip)
    low = jnp.where(is_last, turned, strip)
    high = jnp.where(is_last, strip, turned)
    return jnp.where(lower_half(), low[:half], high[half:])


def unpack(packed, is_left):
    turned = turn(packed)
    low = jnp.where(is_left, turned, packed)
    high = jnp.where(is_left, packed, turned)
    return jnp.concatenate([low, high], axis=0)


def chain(my_lat, slab, shape, dw_ref, expand_ref, reduce_ref, attn_ref, center, scratch):
    taps, one, lat_in = scratch
    taps[...] = dw_ref[...].astype(f32)
    rows, all_rows, columns, channels = shape
    cells = all_rows * columns
    parts = []
    for c in range(0, channels, LANES):
        acc = jnp.zeros((all_rows, columns, LANES), f32)
        for b in range(TAPS):
            block = slab(b, c)
            for a in range(TAPS):
                tap = taps[a, b : b + 1, c : c + LANES].reshape(1, 1, LANES)
                acc = acc + block[a : a + all_rows] * tap
        parts.append(acc.reshape(cells, LANES))
    normed = layer_norm(jnp.concatenate(parts, axis=-1)).astype(bf16)

    def widen(k, total):
        part = slice(k * channels, (k + 1) * channels)
        wide = gelu(dot(normed, expand_ref[:, part])).astype(bf16)
        return total + dot(wide, reduce_ref[part])

    total = center.reshape(cells, channels)
    for k in range(expand_ref.shape[1] // channels):
        total = widen(k, total)
    block_one = total.astype(bf16)
    one[...] = block_one
    every = layer_norm(block_one.astype(f32)).astype(bf16)
    lat_in[...] = every
    count = rows * columns
    own = pl.ds(pl.multiple_of(my_lat * count, count), count)
    queries = dot(lat_in[own], attn_ref[0]).astype(bf16)
    keys = dot(every, attn_ref[1]).astype(bf16)
    values = dot(every, attn_ref[2]).astype(bf16)
    row_col = lax.broadcasted_iota(jnp.int32, (count, 1), 0) % columns
    key_col = lax.broadcasted_iota(jnp.int32, (1, cells), 1) % columns
    mix = attend(queries, keys, values, row_col == key_col)
    block_two = (one[own].astype(f32) + dot(mix, attn_ref[3])).astype(bf16)
    return block_two, layer_norm(block_two.astype(f32))


def fill(padded, all_rows, first, values):
    width = values.shape[1]
    padded[HALO : HALO + all_rows, first : first + width] = values


def fill_tiles(padded, my_lat, first, tiles):
    rows, cols = tiles[0].shape[:2]
    for s in range(len(tiles)):
        place = HALO + lax.rem(my_lat + s, len(tiles)) * rows
        padded[pl.ds(place, rows), first : first + cols] = tiles[s][...].astype(f32)


def clear(padded, all_rows):
    edge = jnp.zeros((HALO,) + padded.shape[1:], f32)
    padded[:HALO] = edge
    padded[HALO + all_rows :] = edge


def inner_kernel(nlat, *refs):
    tiles, refs = refs[:nlat], refs[nlat:]
    dw_ref, expand_ref, reduce_ref, attn_ref, two_ref, in_ref, padded, *scratch = refs
    rows, cols, channels = tiles[0].shape
    all_rows = rows * nlat
    columns = cols - 2 * SIDE
    clear(padded, all_rows)
    my_lat = lax.axis_index("lat")
    fill_tiles(padded, my_lat, 0, tiles)

    def slab(b, c):
        first = SIDE - HALO + b
        return padded[:, first : first + columns, c : c + LANES]

    center = padded[HALO : HALO + all_rows, SIDE : SIDE + columns]
    shape = (rows, all_rows, columns, channels)
    block_two, lon_in = chain(
        my_lat, slab, shape, dw_ref, expand_ref, reduce_ref, attn_ref, center, scratch
    )
    two_ref[...] = block_two
    in_ref[...] = lon_in.astype(bf16)


def outer_kernel(nlat, levels, *refs):
    tiles, refs = refs[:nlat], refs[nlat:]
    far_ref, near_ref, inner_in_ref, dw_ref, expand_ref, reduce_ref, attn_ref = refs[:7]
    two_ref, *refs = refs[7:]
    sent_refs, (sent, padded, *scratch) = refs[:levels], refs[levels:]
    rows, cols, channels = tiles[0].shape
    all_rows = rows * nlat
    columns = 2 * SIDE
    packed = (all_rows // 2, STRIP, channels)
    near = near_ref[...].astype(f32).reshape(packed)
    far = far_ref[...].astype(f32).reshape(packed)
    even = lax.axis_index("lon") % 2 == 0
    my_lat = lax.axis_index("lat")
    clear(padded, all_rows)
    fill(padded, all_rows, 0, unpack(jnp.where(even, far, near), True))
    fill_tiles(padded, my_lat, STRIP, tiles)
    fill(padded, all_rows, STRIP + cols, unpack(jnp.where(even, near, far), False))
    sublane = lax.broadcasted_iota(jnp.int32, (1, columns, 1), 1)

    def halves(shift, rows_of, c, width):
        right = STRIP + cols - SIDE + shift
        left = STRIP - SIDE + shift
        return jnp.where(
            sublane < SIDE,
            padded[rows_of, right : right + columns, c : c + width],
            padded[rows_of, left : left + columns, c : c + width],
        )

    def slab(b, c):
        return halves(b - HALO, slice(None), c, LANES)

    center = halves(0, slice(HALO, HALO + all_rows), 0, channels)
    shape = (rows, all_rows, columns, channels)
    block_two, lon_in = chain(
        my_lat, slab, shape, dw_ref, expand_ref, reduce_ref, attn_ref, center, scratch
    )
    two_ref[...] = block_two
    inner = inner_in_ref[...].astype(f32).reshape(rows, cols - columns, channels)
    outer = lon_in.reshape(rows, columns, channels)
    sent[...] = jnp.concatenate([inner, outer], axis=1).astype(bf16)
    some = rows // levels
    for k in range(levels):
        part = sent[pl.ds(peer(levels, k) * some, some)]
        sent_refs[k][...] = part.reshape(sent_refs[k].shape)


def join_kernel(levels, some, *refs):
    parts, joined = refs[:levels], refs[levels:]
    cols = parts[0].shape[0] // some
    for r in range(some):
        for k in range(levels):
            joined[r][k * cols : (k + 1) * cols] = parts[k][r * cols : (r + 1) * cols]


def circle_kernel(levels, before, *refs):
    attn_ref, refs = refs[0], refs[1:]
    done, refs = refs[:before], refs[before:]
    parts, mix_refs = refs[:-levels], refs[-levels:]
    own = parts[0][...]
    every = jnp.concatenate([own] + [part[...] for part in parts[1:]], axis=0)
    queries = dot(own, attn_ref[0]).astype(bf16)
    keys = dot(every, attn_ref[1]).astype(bf16)
    values = dot(every, attn_ref[2]).astype(bf16)
    mix = attend(queries, keys, values, None)
    cols = own.shape[0] // levels
    for k in range(levels):
        for r in range(before // levels):
            mix_refs[k][r * cols : (r + 1) * cols] = done[r * levels + k][...]
        mix_refs[k][before // levels * cols :] = mix[k * cols : (k + 1) * cols]


def last_kernel(levels, *refs):
    parts = refs[:levels]
    inner_ref, outer_ref, attn_ref, out_ref, ready, sems = refs[levels:]
    rows, cols, channels = out_ref.shape
    columns = 2 * SIDE
    some = rows // levels
    every = jnp.concatenate([part[...] for part in parts], axis=0)
    change = dot(every, attn_ref[3]).reshape(levels, some, cols, channels)
    copies = []
    for k in range(levels):
        start = peer(levels, k) * some

        def state(ref, width):
            count = some * width
            place = pl.ds(pl.multiple_of(start * width, count), count)
            return ref[place].astype(f32).reshape(some, width, channels)

        before = jnp.concatenate(
            [state(inner_ref, cols - columns), state(outer_ref, columns)], axis=1
        )
        total = pltpu.roll(before + change[k], SIDE, axis=1)
        ready[k] = total.astype(bf16)
        place = out_ref.at[pl.ds(start, some)]
        copies.append(pltpu.make_async_copy(ready.at[k], place, sems.at[k]))
        copies[-1].start()
    for copy in copies:
        copy.wait()


def call(
    kernel, outs, operands, scratch=(), any_space=False, far_out=False, flops=0, grant=VMEM_BYTES
):
    vmem = pl.BlockSpec(memory_space=pltpu.VMEM)
    given = pl.BlockSpec(memory_space=pl.ANY) if any_space else vmem
    shapes = [
        out if isinstance(out, jax.ShapeDtypeStruct) else jax.ShapeDtypeStruct(out, bf16)
        for out in outs
    ]
    moved = sum(x.size * x.dtype.itemsize for x in operands)
    result = pl.pallas_call(
        kernel,
        out_shape=shapes,
        in_specs=[given] * len(operands),
        out_specs=[pl.BlockSpec(memory_space=pl.ANY) if far_out else vmem] * len(outs),
        scratch_shapes=list(scratch),
        compiler_params=pltpu.CompilerParams(vmem_limit_bytes=grant),
        cost_estimate=pl.CostEstimate(flops=flops, bytes_accessed=moved, transcendentals=0),
    )(*operands)
    return result


def shards(field, dw_weight, w_expand, w_reduce, lat_attn, lon_attn):
    rows, cols, channels = field.shape
    nlat, nlon = lax.axis_size("lat"), lax.axis_size("lon")
    levels = min(LEVELS, nlon)
    column = nlon // levels
    some = rows // levels
    all_rows = rows * nlat
    columns = 2 * SIDE

    def swap(piece, mask):
        return lax.ppermute(piece, "lon", [(j, j ^ mask) for j in range(nlon)])

    def exchange(pieces):
        cross = min(1, column - 1)
        return [
            swap(piece, hops * column + cross) if hops else piece
            for piece, hops in zip(pieces, hops_of(levels))
        ]

    tiles = [field]
    for s in range(1, nlat):
        tiles.append(lax.ppermute(field, "lat", [((i + s) % nlat, i) for i in range(nlat)]))
    weights = (dw_weight, w_expand, w_reduce, lat_attn, lon_attn)
    taps, expand, reduce, lat_proj, lon_proj = call(
        functools.partial(stage_kernel, len(weights)),
        [w.shape for w in weights],
        weights,
        [pltpu.SemaphoreType.DMA((len(weights), STAGES))],
        any_space=True,
        grant=STAGE_BYTES,
    )

    strip = (all_rows * SIDE, channels)
    strip_scratch = pltpu.VMEM((all_rows, STRIP, channels), f32)
    near, far = call(
        functools.partial(strip_kernel, nlat),
        [strip, strip],
        [*tiles, reduce],
        [strip_scratch, strip_scratch],
    )
    far = lax.ppermute(
        far, "lon", [(j, (j - 1) % nlon if j % 2 == 0 else (j + 1) % nlon) for j in range(nlon)]
    )
    near = swap(near, 1)

    def scratch(width, count):
        return [
            pltpu.VMEM((all_rows + 2 * HALO, width, channels), f32),
            pltpu.VMEM(dw_weight.shape, f32),
            pltpu.VMEM((all_rows * count, channels), bf16),
            pltpu.VMEM((all_rows * count, channels), bf16),
        ]

    work = 4 * all_rows * columns * channels * w_expand.shape[1]
    inner_two, inner_in = call(
        functools.partial(inner_kernel, nlat),
        [(rows * (cols - columns), channels)] * 2,
        [*tiles, taps, expand, reduce, lat_proj],
        scratch(cols, cols - columns),
        flops=work,
    )
    piece = (some * cols, channels)
    outer_two, *parts = call(
        functools.partial(outer_kernel, nlat, levels),
        [(rows * columns, channels)] + [piece] * levels,
        [*tiles, far, near, inner_in, taps, expand, reduce, lat_proj],
        [pltpu.VMEM((rows, cols, channels), bf16)] + scratch(cols + 2 * STRIP, columns),
        flops=work,
    )

    parts = exchange(parts)
    joined = call(
        functools.partial(join_kernel, levels, some), [(levels * cols, channels)] * some, parts
    )
    circles = [[part] for part in joined]
    mask = column // 2
    while mask:
        for circle in circles:
            circle += [swap(part, mask + mask // 2) for part in circle]
        mask //= 2
    done = []
    for r, circle in enumerate(circles):
        last_one = r == some - 1
        mixes = call(
            functools.partial(circle_kernel, levels, len(done) if last_one else 0),
            [piece if last_one else (cols, channels)] * levels,
            [lon_proj, *(done if last_one else []), *circle],
            flops=work // 4,
        )
        done = done + list(mixes)
    mixes = exchange(mixes)
    (out,) = call(
        functools.partial(last_kernel, levels),
        [(rows, cols, channels)],
        [*mixes, inner_two, outer_two, lon_proj],
        [
            pltpu.VMEM((levels, some, cols, channels), bf16),
            pltpu.SemaphoreType.DMA((levels,)),
        ],
        far_out=True,
    )
    return out


def solution(mesh):
    return jax.shard_map(
        shards,
        mesh=mesh,
        in_specs=(P("lat", "lon", None), P(), P(), P(), P(), P()),
        out_specs=P("lat", "lon", None),
        check_vma=False,
    )
```

```python
import functools

import jax
import jax.numpy as jnp
from jax import lax
from jax.experimental import pallas as pl
from jax.experimental.pallas import tpu as pltpu
from jax.sharding import PartitionSpec as P

HEADS = 8
HALO = 3
TAPS = 2 * HALO + 1
STRIP = 8
SIDE = 4
LANES = 128
LEVELS = 4
STAGES = 4
EPSILON = 1e-06
VMEM_BYTES = 24 * 1024 * 1024
STAGE_BYTES = 103 * 512 * 1024
bf16, f32 = jnp.bfloat16, jnp.float32


def layer_norm(values):
    average = jnp.mean(values, axis=-1, keepdims=True)
    centered = values - average
    variance = jnp.mean(centered * centered, axis=-1, keepdims=True)
    return centered * lax.rsqrt(variance + EPSILON)


def dot(rows, matrix):
    return jnp.dot(rows, matrix, preferred_element_type=f32)


def dot_t(rows, matrix):
    return lax.dot_general(rows, matrix, (((1,), (1,)), ((), ())), preferred_element_type=f32)


def gelu(values):
    size = jnp.abs(values)
    t = 1.0 / (1.0 + (0.3275911 * 0.5**0.5) * size)
    tail = 1.061405429 * t - 1.453152027
    for coefficient in (1.421413741, -0.284496736, 0.254829592):
        tail = tail * t + coefficient
    tail = (0.5 * size * t) * tail * jnp.exp(-0.5 * values * values)
    return jnp.maximum(values, 0.0) - tail


def attend(queries, keys, values, mask):
    count, channels = queries.shape
    head_size = channels // HEADS
    lane_head = lax.broadcasted_iota(jnp.int32, (1, channels), 1) // head_size
    picks = [lane_head == h for h in range(HEADS)]
    none = jnp.zeros_like(queries)
    stacked = jnp.concatenate([jnp.where(pick, queries, none) for pick in picks], axis=0)
    scores = dot_t(stacked, keys) * head_size ** (-0.5)
    if mask is not None:
        scores = scores.reshape(HEADS, count, keys.shape[0])
        scores = jnp.where(mask[None], scores, -1e30).reshape(HEADS * count, keys.shape[0])
    top = jnp.max(scores, axis=-1, keepdims=True)
    probs = jnp.exp(scores - top)
    totals = jnp.sum(probs, axis=-1, keepdims=True)
    mixed = dot(probs.astype(bf16), values) * (1.0 / totals)
    out = mixed[:count]
    for h in range(1, HEADS):
        out = jnp.where(picks[h], mixed[h * count : (h + 1) * count], out)
    return out.astype(bf16)


def stage_kernel(count, *refs):
    sources, targets, sems = refs[:count], refs[count : 2 * count], refs[-1]
    copies = []
    for i in range(count):
        source, target = sources[i], targets[i]
        pieces = sems.shape[1] if source.shape[0] % sems.shape[1] == 0 else 1
        size = source.shape[0] // pieces
        for k in range(pieces):
            part = pl.ds(k * size, size)
            copies.append(pltpu.make_async_copy(source.at[part], target.at[part], sems.at[i, k]))
    for copy in copies:
        copy.start()
    for copy in copies:
        copy.wait()


def hops_of(levels):
    return [0] + [h for h in (*range(levels // 2, levels), *range(1, levels // 2)) if h]


def peer(levels, k):
    level = lax.axis_index("lon") // (lax.axis_size("lon") // levels)
    return level ^ hops_of(levels)[k]


def strip_kernel(nlat, *refs):
    tiles = refs[:nlat]
    near_ref, far_ref, near, far = refs[nlat + 1 :]
    rows, cols, channels = tiles[0].shape
    even = lax.axis_index("lon") % 2 == 0
    for s in range(nlat):
        values = tiles[s][...].astype(f32)
        first, last = values[:, :STRIP], values[:, cols - STRIP :]
        where = pl.ds(lax.rem(lax.axis_index("lat") + s, nlat) * rows, rows)
        near[where] = jnp.where(even, last, first)
        far[where] = jnp.where(even, first, last)
    for strip, strip_ref, is_last in ((near, near_ref, even), (far, far_ref, ~even)):
        strip_ref[...] = pack(strip[...], is_last).reshape(strip_ref.shape).astype(bf16)


def lower_half():
    return lax.broadcasted_iota(jnp.int32, (1, STRIP, 1), 1) < SIDE


def turn(values):
    return pltpu.roll(values, SIDE, axis=1)


def pack(strip, is_last):
    half = strip.shape[0] // 2
    turned = turn(strip)
    low = jnp.where(is_last, turned, strip)
    high = jnp.where(is_last, strip, turned)
    return jnp.where(lower_half(), low[:half], high[half:])


def unpack(packed, is_left):
    turned = turn(packed)
    low = jnp.where(is_left, turned, packed)
    high = jnp.where(is_left, packed, turned)
    return jnp.concatenate([low, high], axis=0)


def chain(my_lat, slab, shape, dw_ref, expand_ref, reduce_ref, attn_ref, center, scratch):
    taps, one, lat_in = scratch
    taps[...] = dw_ref[...].astype(f32)
    rows, all_rows, columns, channels = shape
    cells = all_rows * columns
    parts = []
    for c in range(0, channels, LANES):
        acc = jnp.zeros((all_rows, columns, LANES), f32)
        for b in range(TAPS):
            block = slab(b, c)
            for a in range(TAPS):
                tap = taps[a, b : b + 1, c : c + LANES].reshape(1, 1, LANES)
                acc = acc + block[a : a + all_rows] * tap
        parts.append(acc.reshape(cells, LANES))
    normed = layer_norm(jnp.concatenate(parts, axis=-1)).astype(bf16)

    def widen(k, total):
        part = slice(k * channels, (k + 1) * channels)
        wide = gelu(dot(normed, expand_ref[:, part])).astype(bf16)
        return total + dot(wide, reduce_ref[part])

    total = center.reshape(cells, channels)
    for k in range(expand_ref.shape[1] // channels):
        total = widen(k, total)
    block_one = total.astype(bf16)
    one[...] = block_one
    every = layer_norm(block_one.astype(f32)).astype(bf16)
    lat_in[...] = every
    count = rows * columns
    own = pl.ds(pl.multiple_of(my_lat * count, count), count)
    queries = dot(lat_in[own], attn_ref[0]).astype(bf16)
    keys = dot(every, attn_ref[1]).astype(bf16)
    values = dot(every, attn_ref[2]).astype(bf16)
    row_col = lax.broadcasted_iota(jnp.int32, (count, 1), 0) % columns
    key_col = lax.broadcasted_iota(jnp.int32, (1, cells), 1) % columns
    mix = attend(queries, keys, values, row_col == key_col)
    block_two = (one[own].astype(f32) + dot(mix, attn_ref[3])).astype(bf16)
    return block_two, layer_norm(block_two.astype(f32))


def fill(padded, all_rows, first, values):
    width = values.shape[1]
    padded[HALO : HALO + all_rows, first : first + width] = values


def fill_tiles(padded, my_lat, first, tiles):
    rows, cols = tiles[0].shape[:2]
    for s in range(len(tiles)):
        place = HALO + lax.rem(my_lat + s, len(tiles)) * rows
        padded[pl.ds(place, rows), first : first + cols] = tiles[s][...].astype(f32)


def clear(padded, all_rows):
    edge = jnp.zeros((HALO,) + padded.shape[1:], f32)
    padded[:HALO] = edge
    padded[HALO + all_rows :] = edge


def inner_kernel(nlat, *refs):
    tiles, refs = refs[:nlat], refs[nlat:]
    dw_ref, expand_ref, reduce_ref, attn_ref, two_ref, in_ref, padded, *scratch = refs
    rows, cols, channels = tiles[0].shape
    all_rows = rows * nlat
    columns = cols - 2 * SIDE
    clear(padded, all_rows)
    my_lat = lax.axis_index("lat")
    fill_tiles(padded, my_lat, 0, tiles)

    def slab(b, c):
        first = SIDE - HALO + b
        return padded[:, first : first + columns, c : c + LANES]

    center = padded[HALO : HALO + all_rows, SIDE : SIDE + columns]
    shape = (rows, all_rows, columns, channels)
    block_two, lon_in = chain(
        my_lat, slab, shape, dw_ref, expand_ref, reduce_ref, attn_ref, center, scratch
    )
    two_ref[...] = block_two
    in_ref[...] = lon_in.astype(bf16)


def outer_kernel(nlat, levels, *refs):
    tiles, refs = refs[:nlat], refs[nlat:]
    far_ref, near_ref, inner_in_ref, dw_ref, expand_ref, reduce_ref, attn_ref = refs[:7]
    two_ref, *refs = refs[7:]
    sent_refs, (sent, padded, *scratch) = refs[:levels], refs[levels:]
    rows, cols, channels = tiles[0].shape
    all_rows = rows * nlat
    columns = 2 * SIDE
    packed = (all_rows // 2, STRIP, channels)
    near = near_ref[...].astype(f32).reshape(packed)
    far = far_ref[...].astype(f32).reshape(packed)
    even = lax.axis_index("lon") % 2 == 0
    my_lat = lax.axis_index("lat")
    clear(padded, all_rows)
    fill(padded, all_rows, 0, unpack(jnp.where(even, far, near), True))
    fill_tiles(padded, my_lat, STRIP, tiles)
    fill(padded, all_rows, STRIP + cols, unpack(jnp.where(even, near, far), False))
    sublane = lax.broadcasted_iota(jnp.int32, (1, columns, 1), 1)

    def halves(shift, rows_of, c, width):
        right = STRIP + cols - SIDE + shift
        left = STRIP - SIDE + shift
        return jnp.where(
            sublane < SIDE,
            padded[rows_of, right : right + columns, c : c + width],
            padded[rows_of, left : left + columns, c : c + width],
        )

    def slab(b, c):
        return halves(b - HALO, slice(None), c, LANES)

    center = halves(0, slice(HALO, HALO + all_rows), 0, channels)
    shape = (rows, all_rows, columns, channels)
    block_two, lon_in = chain(
        my_lat, slab, shape, dw_ref, expand_ref, reduce_ref, attn_ref, center, scratch
    )
    two_ref[...] = block_two
    inner = inner_in_ref[...].astype(f32).reshape(rows, cols - columns, channels)
    outer = lon_in.reshape(rows, columns, channels)
    sent[...] = jnp.concatenate([inner, outer], axis=1).astype(bf16)
    some = rows // levels
    for k in range(levels):
        part = sent[pl.ds(peer(levels, k) * some, some)]
        sent_refs[k][...] = part.reshape(sent_refs[k].shape)


def join_kernel(levels, some, *refs):
    parts, whole_ref = refs[:levels], refs[levels]
    cols = parts[0].shape[0] // some
    for r in range(some):
        for k in range(levels):
            start = (r * levels + k) * cols
            whole_ref[start : start + cols] = parts[k][r * cols : (r + 1) * cols]


def circle_kernel(levels, before, *refs):
    attn_ref, refs = refs[0], refs[1:]
    done, refs = refs[:before], refs[before:]
    parts, mix_refs = refs[:-levels], refs[-levels:]
    own = parts[0][...]
    every = jnp.concatenate([own] + [part[...] for part in parts[1:]], axis=0)
    queries = dot(own, attn_ref[0]).astype(bf16)
    keys = dot(every, attn_ref[1]).astype(bf16)
    values = dot(every, attn_ref[2]).astype(bf16)
    mix = attend(queries, keys, values, None)
    cols = own.shape[0] // levels
    for k in range(levels):
        for r in range(before // levels):
            mix_refs[k][r * cols : (r + 1) * cols] = done[r * levels + k][...]
        mix_refs[k][before // levels * cols :] = mix[k * cols : (k + 1) * cols]


def last_kernel(levels, *refs):
    parts = refs[:levels]
    inner_ref, outer_ref, attn_ref, out_ref = refs[levels:]
    rows, cols, channels = out_ref.shape
    columns = 2 * SIDE
    some = rows // levels
    every = jnp.concatenate([part[...] for part in parts], axis=0)
    change = dot(every, attn_ref[3]).reshape(levels, some, cols, channels)
    for k in range(levels):
        start = peer(levels, k) * some

        def state(ref, width):
            count = some * width
            place = pl.ds(pl.multiple_of(start * width, count), count)
            return ref[place].astype(f32).reshape(some, width, channels)

        before = jnp.concatenate(
            [state(inner_ref, cols - columns), state(outer_ref, columns)], axis=1
        )
        total = pltpu.roll(before + change[k], SIDE, axis=1)
        out_ref[pl.ds(start, some)] = total.astype(bf16)


def call(
    kernel, outs, operands, scratch=(), any_space=False, flops=0, grant=VMEM_BYTES
):
    vmem = pl.BlockSpec(memory_space=pltpu.VMEM)
    given = pl.BlockSpec(memory_space=pl.ANY) if any_space else vmem
    shapes = [
        out if isinstance(out, jax.ShapeDtypeStruct) else jax.ShapeDtypeStruct(out, bf16)
        for out in outs
    ]
    moved = sum(x.size * x.dtype.itemsize for x in operands)
    result = pl.pallas_call(
        kernel,
        out_shape=shapes,
        in_specs=[given] * len(operands),
        out_specs=[vmem] * len(outs),
        scratch_shapes=list(scratch),
        compiler_params=pltpu.CompilerParams(vmem_limit_bytes=grant),
        cost_estimate=pl.CostEstimate(flops=flops, bytes_accessed=moved, transcendentals=0),
    )(*operands)
    return result


def shards(field, dw_weight, w_expand, w_reduce, lat_attn, lon_attn):
    rows, cols, channels = field.shape
    nlat, nlon = lax.axis_size("lat"), lax.axis_size("lon")
    levels = min(LEVELS, nlon)
    column = nlon // levels
    some = rows // levels
    all_rows = rows * nlat
    columns = 2 * SIDE

    def swap(piece, mask):
        return lax.ppermute(piece, "lon", [(j, j ^ mask) for j in range(nlon)])

    def exchange(pieces):
        cross = min(1, column - 1)
        return [
            swap(piece, hops * column + cross) if hops else piece
            for piece, hops in zip(pieces, hops_of(levels))
        ]

    tiles = [field]
    for s in range(1, nlat):
        tiles.append(lax.ppermute(field, "lat", [((i + s) % nlat, i) for i in range(nlat)]))
    weights = (dw_weight, w_expand, w_reduce, lat_attn, lon_attn)
    taps, expand, reduce, lat_proj, lon_proj = call(
        functools.partial(stage_kernel, len(weights)),
        [w.shape for w in weights],
        weights,
        [pltpu.SemaphoreType.DMA((len(weights), STAGES))],
        any_space=True,
        grant=STAGE_BYTES,
    )

    strip = (all_rows * SIDE, channels)
    strip_scratch = pltpu.VMEM((all_rows, STRIP, channels), f32)
    near, far = call(
        functools.partial(strip_kernel, nlat),
        [strip, strip],
        [*tiles, reduce],
        [strip_scratch, strip_scratch],
    )
    far = lax.ppermute(
        far, "lon", [(j, (j - 1) % nlon if j % 2 == 0 else (j + 1) % nlon) for j in range(nlon)]
    )
    near = swap(near, 1)

    def scratch(width, count):
        return [
            pltpu.VMEM((all_rows + 2 * HALO, width, channels), f32),
            pltpu.VMEM(dw_weight.shape, f32),
            pltpu.VMEM((all_rows * count, channels), bf16),
            pltpu.VMEM((all_rows * count, channels), bf16),
        ]

    work = 4 * all_rows * columns * channels * w_expand.shape[1]
    inner_two, inner_in = call(
        functools.partial(inner_kernel, nlat),
        [(rows * (cols - columns), channels)] * 2,
        [*tiles, taps, expand, reduce, lat_proj],
        scratch(cols, cols - columns),
        flops=work,
    )
    piece = (some * cols, channels)
    outer_two, *parts = call(
        functools.partial(outer_kernel, nlat, levels),
        [(rows * columns, channels)] + [piece] * levels,
        [*tiles, far, near, inner_in, taps, expand, reduce, lat_proj],
        [pltpu.VMEM((rows, cols, channels), bf16)] + scratch(cols + 2 * STRIP, columns),
        flops=work,
    )

    parts = exchange(parts)
    block = levels * cols
    wholes = list(call(
        functools.partial(join_kernel, levels, some), [(some * block, channels)], parts
    ))
    mask = column // 2
    while mask > 1:
        wholes = wholes + [swap(part, mask + mask // 2) for part in wholes]
        mask //= 2
    circles = []
    for r in range(some):
        circle = [whole[r * block : (r + 1) * block] for whole in wholes]
        circles.append(circle + ([swap(part, 1) for part in circle] if mask else []))
    done = []
    for r, circle in enumerate(circles):
        last_one = r == some - 1
        mixes = call(
            functools.partial(circle_kernel, levels, len(done) if last_one else 0),
            [piece if last_one else (cols, channels)] * levels,
            [lon_proj, *(done if last_one else []), *circle],
            flops=work // 4,
        )
        done = done + list(mixes)
    mixes = exchange(mixes)
    (out,) = call(
        functools.partial(last_kernel, levels),
        [(rows, cols, channels)],
        [*mixes, inner_two, outer_two, lon_proj],
    )
    return out


def solution(mesh):
    return jax.shard_map(
        shards,
        mesh=mesh,
        in_specs=(P("lat", "lon", None), P(), P(), P(), P(), P()),
        out_specs=P("lat", "lon", None),
        check_vma=False,
    )
```
